32 devices in a mesh: parts: 2 (over y), expert: 2 (over x), col: 4 (over z), row: 2 (over core).
Axes of the slice: x: 2, y: 2, z: 4, core: 2. Of those that a mesh axis runs over, the one named last changes fastest.
Arguments:
- tokens: bfloat16 [1024, 6144], P(('parts', 'col'), ('expert', 'row')), parts along dimension 0, may hold values from -6 to 6
- routes: int32 [1024, 2], P(('parts', 'col')), parts along dimension 0, may hold values from 0 to 7, as said below
- route_weight: float32 [1024, 2], P(('parts', 'col')), parts along dimension 0, may hold values from 0.2 to 1
- pad_mask: int32 [1024], P(('parts', 'col')), parts along dimension 0, may hold values 0 or 1
- gate_up: bfloat16 [6144, 2, 12288], P(('expert', 'row'), None, 'col'), may hold values from -0.078125 to 0.078125
- down: bfloat16 [12288, 6144], P('col', ('expert', 'row')), may hold values from -0.0546875 to 0.0546875
Outputs:
- expert_out: bfloat16 [1024, 6144], P(('parts', 'col'), ('expert', 'row')), parts along dimension 0
- gram: float32 [24576, 12288], P(('parts', 'expert', 'row'), 'col'), parts along dimension 0
The draws below stay inside these ranges and needn't reach their ends.
There are 2 independent parts, one for each index of `parts`. The reference program is written for one: setup_inputs(seed, part) draws one part's arguments, and reference() takes and returns one part's arrays. A program takes and returns all parts, laid end to end along the dimension named above; an argument that names none is the same for every part. Nothing has to cross between parts.
Inputs may be any that keep to these rules, and one draw needn't show every extreme that they name: `routes`: each row names two different experts. In each aligned block of 128 rows at most 32 rows name expert 0, and some block has exactly 32.
All inputs are finite; a program needn't handle non-finite values. No bound on the sum of `pad_mask` on one device may be relied on, other than what follows from the above.
Results may differ from the reference program's by a relative error of at most 0.005.
Values may be sent and summed in bfloat16 or wider, within the bound.
No kernel may reach another device: no remote copies, remote signals or barrier semaphores. Data moves between devices by JAX's collectives and lax.ppermute only.
A program may use at most 192 MiB of HBM per device.

```python
import jax
import jax.numpy as jnp

D = 6144
FF = 12288
ROUTED = 8
TOK_GRP = 128
CAP = 128
TOKENS = 512


def draw_routes(key, part):
    key = jax.random.fold_in(key, 11)
    groups = TOKENS // TOK_GRP
    slot_count = TOK_GRP // 4
    streams = jax.random.split(key, 6)
    counts = jax.random.randint(streams[0], (groups,), slot_count // 4, slot_count + 1)
    full_group = jax.random.randint(streams[1], (), 0, groups)
    counts = jnp.where(jnp.arange(groups) == full_group, slot_count, counts)
    shuffled = jax.vmap(lambda stream: jax.random.permutation(stream, TOK_GRP))(jax.random.split(streams[2], groups))
    position = jnp.argsort(shuffled, axis=1, stable=True)
    routed = (position < counts[:, None]).reshape(TOKENS)
    first_pick = jax.random.randint(streams[3], (TOKENS,), 1, ROUTED)
    offset_pick = jax.random.randint(streams[4], (TOKENS,), 1, ROUTED - 1)
    second_pick = 1 + (first_pick - 1 + offset_pick) % (ROUTED - 1)
    partner = jnp.where(routed, 0, second_pick)
    flipped = jax.random.randint(streams[5], (TOKENS,), 0, 2) == 1
    column_one = jnp.where(flipped, partner, first_pick)
    column_two = jnp.where(flipped, first_pick, partner)
    return jnp.stack([column_one, column_two], axis=1).astype(jnp.int32)


def touch_ends(drawn, key, least, largest):
    shape = drawn.shape
    index_at = [jax.random.randint(jax.random.fold_in(key, axis), (), 0, shape[axis]) for axis in range(len(shape))]
    drawn = drawn.at[tuple(index_at)].set(least)
    longest = shape.index(max(shape))
    index_at[longest] = (index_at[longest] + 1) % shape[longest]
    return drawn.at[tuple(index_at)].set(largest)


def block_scale(own_key, dims, cuts, smallest, high):
    level = 1.0
    for axis_at, parts in cuts:
        heights = jax.random.uniform(jax.random.fold_in(jax.random.fold_in(own_key, 6), axis_at), (parts,), jnp.float32, smallest / len(cuts), high / len(cuts))
        level = level * jnp.repeat(jnp.exp(heights), dims[axis_at] // parts).reshape((-1,) + (1,) * (len(dims) - 1 - axis_at))
    return level


def centred(key, dims, spread, most, pieces=(), kind=jnp.bfloat16):
    drawn = spread * jax.random.normal(key, dims, jnp.float32)
    if pieces:
        drawn = drawn * block_scale(key, dims, pieces, -0.22, 0.18)
    return jnp.clip(drawn, -most, most).astype(kind)


def setup_inputs(seed: int = 0, part: int = 0) -> dict:
    arg_keys = jax.random.split(jax.random.key(seed), 7)
    own_keys = jax.random.split(jax.random.fold_in(arg_keys[6], part), 7)
    tokens = centred(own_keys[0], (TOKENS, D), 1.0, 6.0, ((0, 4), (1, 4)))
    routes = draw_routes(jax.random.fold_in(jax.random.fold_in(arg_keys[6], part), 71), part)
    route_weight = jnp.clip(0.2 + 0.8 * jax.random.uniform(own_keys[2], (TOKENS, 2), jnp.float32) ** block_scale(own_keys[2], (TOKENS, 2), ((0, 4),), -0.2, 0.2), 0.2, 1.0)
    pad_mask = touch_ends((jax.random.randint(own_keys[3], (TOKENS,), 0, 8) < 7).astype(jnp.int32), jax.random.fold_in(own_keys[3], 1), 0, 1)
    gate_up = centred(arg_keys[4], (D, 2, FF), D ** -0.5, 0.078125, ((0, 4), (2, 4)))
    down = centred(arg_keys[5], (FF, D), FF ** -0.5, 0.0546875, ((0, 4), (1, 4)))
    return dict(tokens=tokens, routes=routes, route_weight=route_weight, pad_mask=pad_mask, gate_up=gate_up, down=down)


def reference(tokens, routes, route_weight, pad_mask, gate_up, down):
    names_zero = routes == 0
    live_rows = (jnp.any(names_zero, axis=1) & (pad_mask == 1)).astype(jnp.float32)
    weight = jnp.sum(jnp.where(names_zero, route_weight, jnp.float32(0.0)), axis=1) * live_rows
    gate_out = jnp.dot(tokens, gate_up[:, 0, :], preferred_element_type=jnp.float32)
    up_out = jnp.dot(tokens, gate_up[:, 1, :], preferred_element_type=jnp.float32)
    hidden = (jax.nn.silu(gate_out) * up_out).astype(jnp.bfloat16)
    kept_rows = hidden * live_rows.astype(jnp.bfloat16)[:, None]
    gram = jnp.dot(kept_rows.T, kept_rows, preferred_element_type=jnp.float32) * jnp.float32(2.0 / CAP)
    projected = jnp.dot(hidden, down, preferred_element_type=jnp.float32)
    expert_out = (projected * weight[:, None]).astype(jnp.bfloat16)
    return expert_out, gram
```

```python
import functools

import jax
import jax.numpy as jnp
from jax import lax
from jax.experimental import pallas as pl
from jax.experimental.pallas import tpu as pltpu
from jax.sharding import PartitionSpec as P

F32 = jnp.float32
BF16 = jnp.bfloat16
MIB = 1 << 20


def spread(value, axis, source):
    kept = jnp.where(lax.axis_index(axis) == source, value, 0).astype(value.dtype)
    return lax.psum(kept, axis)


def activate(preacts):
    return (jax.nn.silu(preacts[:, 0, :]) * preacts[:, 1, :]).astype(jnp.bfloat16)


def on_any_device(tokens, routes, route_weight, pad_mask, gate_up, down):
    group_rows = tokens.shape[0]
    slot_count = group_rows // 4
    names_zero = routes == 0
    routed = jnp.any(names_zero, axis=1)
    live_rows = routed & (pad_mask == 1)
    factor = jnp.sum(
        jnp.where(names_zero, route_weight, jnp.float32(0.0)), axis=1
    ) * live_rows.astype(jnp.float32)
    position = jnp.cumsum(routed.astype(jnp.int32)) - 1
    slot_ids = lax.broadcasted_iota(jnp.int32, (slot_count, group_rows), 0)
    placing = ((position[None, :] == slot_ids) & routed[None, :]).astype(jnp.bfloat16)
    masked = tokens * live_rows.astype(jnp.bfloat16)[:, None]
    packed = jnp.dot(placing, masked, preferred_element_type=jnp.float32).astype(jnp.bfloat16)
    gathered = lax.all_gather(packed, "col", axis=0, tiled=True)
    anchor = lax.axis_index(("expert", "row"))
    preacts = lax.psum(
        jnp.einsum("rd,dgf->rgf", gathered, gate_up, preferred_element_type=jnp.float32),
        ("expert", "row"),
    )
    hidden = activate(preacts)
    mirrored = spread(hidden, "col", anchor)
    gram_block = lax.dot_general(
        mirrored, hidden, (((0,), (0,)), ((), ())), preferred_element_type=jnp.float32
    )
    gram_block = gram_block * jnp.float32(2.0 / hidden.shape[0])
    returned = lax.psum_scatter(
        jnp.dot(hidden, down, preferred_element_type=jnp.float32),
        "col",
        scatter_dimension=0,
        tiled=True,
    )
    unpacked = lax.dot_general(
        placing.astype(jnp.float32),
        returned,
        (((0,), (0,)), ((), ())),
        precision=lax.Precision.HIGHEST,
        preferred_element_type=jnp.float32,
    )
    expert_out = (unpacked * factor[:, None]).astype(jnp.bfloat16)
    return (expert_out, gram_block)


def cost(flops, moved):
    return pl.CostEstimate(flops=int(flops), bytes_accessed=int(moved), transcendentals=0)


def params(mib):
    return pltpu.CompilerParams(vmem_limit_bytes=mib * MIB)


def placing_of(routes_t, pad, slots):
    rows = routes_t.shape[1]
    routed = (routes_t[0:1, :] == 0) | (routes_t[1:2, :] == 0)
    live = jnp.where(routed & (pad == 1), 1.0, 0.0)
    before = lax.broadcasted_iota(jnp.int32, (rows, rows), 0)
    upto = lax.broadcasted_iota(jnp.int32, (rows, rows), 1)
    tri = jnp.where(before <= upto, 1.0, 0.0).astype(BF16)
    routed_rows = jnp.broadcast_to(jnp.where(routed, 1.0, 0.0), (8, rows)).astype(BF16)
    position = jnp.dot(routed_rows, tri, preferred_element_type=F32)[0:1, :] - 1.0
    slot_ids = lax.broadcasted_iota(jnp.int32, (slots, rows), 0).astype(F32)
    return jnp.where(position == slot_ids, jnp.broadcast_to(live, (slots, rows)), 0.0)


def pack_kernel(tokens_ref, routes_ref, pad_ref, packed_ref):
    placing = placing_of(routes_ref[...], pad_ref[...], packed_ref.shape[0])
    packed_ref[...] = jnp.dot(
        placing.astype(BF16), tokens_ref[...], preferred_element_type=F32
    ).astype(BF16)


def unpack_kernel(routes_ref, pad_ref, weight_ref, own_ref, r1_ref, r2_ref, r3_ref, out_ref):
    routes_t = routes_ref[...]
    placing = placing_of(routes_t, pad_ref[...], own_ref.shape[0])
    weight = jnp.sum(jnp.where(routes_t == 0, weight_ref[...], 0.0), axis=0, keepdims=True)
    factor = jnp.sum(placing * weight, axis=1, keepdims=True)
    total = own_ref[...] + r1_ref[...].astype(F32) + r2_ref[...].astype(F32) + r3_ref[...].astype(F32)
    scaled = (total * factor).astype(BF16)
    out_ref[...] = lax.dot_general(
        placing.astype(BF16), scaled, (((0,), (0,)), ((), ())), preferred_element_type=F32
    ).astype(BF16)


def preact_kernel(first, place_ref, *refs):
    if first:
        x0, x1, x2, x3, w0_ref, w1_ref, out_ref, wide_ref = refs
    else:
        wide_ref, w0_ref, w1_ref, out_ref = refs
    depth = w0_ref.shape[0]
    if first:

        @pl.when(pl.program_id(0) == 0)
        def _():
            slots = x0.shape[0]
            rows = 4 * slots
            here = place_ref[2]
            cut = 256
            into = lax.broadcasted_iota(jnp.int32, (cut, 2 * cut), 1)
            out_of = lax.broadcasted_iota(jnp.int32, (cut, 2 * cut), 0)
            for half in range(2):
                widen = jnp.where(into == 2 * out_of + half, 1.0, 0.0).astype(BF16)
                for slot, x_ref in enumerate((x0, x1, x2, x3)):
                    at = pl.multiple_of(half * rows + (here ^ slot) * slots, slots)
                    for k in range(depth // cut):
                        wide_ref[pl.ds(at, slots), 2 * cut * k : 2 * cut * (k + 1)] = jnp.dot(
                            x_ref[:, cut * k : cut * (k + 1)], widen, preferred_element_type=F32
                        ).astype(BF16)

    wide = wide_ref[...]
    lanes = w0_ref.shape[-1]
    for i, w_ref in enumerate((w0_ref, w1_ref)):
        w = w_ref.reshape(2 * depth, lanes)[...]
        out_ref[:, lanes * i : lanes * (i + 1)] = jnp.dot(
            wide, w, preferred_element_type=F32
        ).astype(out_ref.dtype)


def preacts_of(place, lefts, weights, row_flip, out_type):
    depth, tiles, _, lanes = weights.shape
    first = len(lefts) > 1
    rows = 4 * lefts[0].shape[0] if first else lefts[0].shape[0] // 2
    per = tiles // 4
    steps = per // 2

    def tile(i, j, place):
        quarter = (place[0] ^ (1 - j // steps)) * 2 + (place[1] ^ row_flip)
        return (0, quarter * per + (j % steps) * 2 + i, 0, 0)

    whole = lambda shape: pl.BlockSpec(shape, lambda j, place: (0,) * len(shape))
    out_shape = [jax.ShapeDtypeStruct((2, 2 * rows, per * lanes), out_type)]
    out_specs = [pl.BlockSpec((None, 2 * rows, 2 * lanes), lambda j, place: (j // steps, 0, j % steps))]
    if first:
        out_shape.append(jax.ShapeDtypeStruct((2 * rows, 2 * depth), BF16))
        out_specs.append(whole((2 * rows, 2 * depth)))
    return pl.pallas_call(
        functools.partial(preact_kernel, first),
        grid_spec=pltpu.PrefetchScalarGridSpec(
            num_scalar_prefetch=1,
            grid=(2 * steps,),
            in_specs=[whole(left.shape) for left in lefts]
            + [
                pl.BlockSpec((depth, None, 2, lanes), functools.partial(tile, 0)),
                pl.BlockSpec((depth, None, 2, lanes), functools.partial(tile, 1)),
            ],
            out_specs=out_specs,
        ),
        out_shape=out_shape,
        compiler_params=params(40),
        cost_estimate=cost(8 * rows * depth * per * 2 * lanes, depth * tiles * lanes * 2),
        name="preacts_sent" if first else "preacts_kept",
    )(place, *lefts, weights, weights)


def project_kernel(place_ref, h0, h1, h2, h3, down_ref, own_ref, s1_ref, s2_ref, s3_ref, total_ref):
    j = pl.program_id(0)
    slots = own_ref.shape[0]
    for k, h_ref in enumerate((h0, h1, h2, h3)):

        @pl.when(j == k)
        def _():
            part = jnp.dot(h_ref[...], down_ref[...], preferred_element_type=F32)
            total_ref[...] = part if k == 0 else total_ref[...] + part

    @pl.when(j == 3)
    def _():
        here = place_ref[2]
        for slot, out_ref in enumerate((own_ref, s1_ref, s2_ref, s3_ref)):
            at = pl.multiple_of((here ^ slot) * slots, slots)
            out_ref[...] = total_ref[pl.ds(at, slots), :].astype(out_ref.dtype)


def project(place, quarters, down):
    rows, units = quarters[0].shape
    width = down.shape[1]
    slots = rows // 4
    whole = lambda shape: pl.BlockSpec(shape, lambda j, place: (0, 0))

    def quarter(j, place):
        return ((place[0] ^ (j % 2)) * 2 + (place[1] ^ (j // 2)), 0)

    return pl.pallas_call(
        project_kernel,
        grid_spec=pltpu.PrefetchScalarGridSpec(
            num_scalar_prefetch=1,
            grid=(4,),
            in_specs=[whole((rows, units))] * 4 + [pl.BlockSpec((units, width), quarter)],
            out_specs=[whole((slots, width))] * 4,
            scratch_shapes=[pltpu.VMEM((rows, width), F32)],
        ),
        out_shape=[jax.ShapeDtypeStruct((slots, width), F32)]
        + [jax.ShapeDtypeStruct((slots, width), BF16)] * 3,
        compiler_params=params(32),
        cost_estimate=cost(2 * rows * 4 * units * width, down.size * 2),
        name="project",
    )(place, *quarters, down)


def gram_kernel(scale, halves, place_ref, a0, a1, a2, a3, c0, c1, c2, c3, out_ref, wide_ref):
    j = pl.program_id(0)
    units = a0.shape[1]
    take = units // halves

    @pl.when(j == 0)
    def _():
        for k, c_ref in enumerate((c0, c1, c2, c3)):
            q = (place_ref[0] ^ (k % 2)) * 2 + (place_ref[1] ^ (k // 2))
            wide_ref[:, pl.ds(pl.multiple_of(q * units, units), units)] = c_ref[...]

    for k, a_ref in enumerate((a0, a1, a2, a3)):
        for half in range(halves):

            @pl.when(j == k * halves + half)
            def _():
                left = a_ref[:, take * half : take * (half + 1)]
                cut = 256
                for n in range(4 * units // cut):
                    out_ref[:, cut * n : cut * (n + 1)] = scale * lax.dot_general(
                        left,
                        wide_ref[:, cut * n : cut * (n + 1)],
                        (((0,), (0,)), ((), ())),
                        preferred_element_type=F32,
                    )


def gram_of(place, a_quarters, c_quarters):
    rows, units = a_quarters[0].shape
    halves = 2
    whole = pl.BlockSpec((rows, units), lambda j, place: (0, 0))

    def block(j, place):
        k = j // halves
        quarter = (place[0] ^ (k % 2)) * 2 + (place[1] ^ (k // 2))
        return (quarter * halves + j % halves, 0)

    return pl.pallas_call(
        functools.partial(gram_kernel, 2.0 / rows, halves),
        grid_spec=pltpu.PrefetchScalarGridSpec(
            num_scalar_prefetch=1,
            grid=(4 * halves,),
            in_specs=[whole] * 8,
            out_specs=pl.BlockSpec((units // halves, 4 * units), block),
            scratch_shapes=[pltpu.VMEM((rows, 4 * units), BF16)],
        ),
        out_shape=jax.ShapeDtypeStruct((4 * units, 4 * units), F32),
        compiler_params=params(32),
        cost_estimate=cost(2 * rows * 16 * units * units, 64 * units * units),
        name="gram",
    )(place, *a_quarters, *c_quarters)


def swap(value, axis):
    return lax.ppermute(value, axis, [(0, 1), (1, 0)])


def across(value, slot):
    return lax.ppermute(value, "col", [(i, i ^ slot) for i in range(4)])


def on_device(tokens, routes, route_weight, pad_mask, gate_up, down):
    group_rows, depth = tokens.shape
    slots = group_rows // 4
    units = gate_up.shape[2]
    lanes = 128
    e = lax.axis_index("expert").astype(jnp.int32)
    r = lax.axis_index("row").astype(jnp.int32)
    c = lax.axis_index("col").astype(jnp.int32)
    place = jnp.stack([e, r, c])
    routes_t = routes.T
    pad = pad_mask[None, :]
    weights = gate_up.reshape(depth, 2, units // lanes, lanes).transpose(0, 2, 1, 3)

    packed = pl.pallas_call(
        pack_kernel,
        out_shape=jax.ShapeDtypeStruct((slots, depth), BF16),
        name="pack",
    )(tokens, routes_t, pad)
    lefts = [packed] + [across(packed, slot) for slot in (1, 2, 3)]
    sent, wide = preacts_of(place, lefts, weights, 1, BF16)
    got = swap(sent, "row")
    (kept,) = preacts_of(place, [wide], weights, 0, F32)
    got_x = swap((kept[0] + got[0].astype(F32)).astype(BF16), "expert")
    rows = 4 * slots
    preacts = kept[1] + got[1].astype(F32) + got_x.astype(F32)
    hidden = (jax.nn.silu(preacts[:rows]) * preacts[rows:]).astype(BF16)

    z1, z2, z3 = (across(hidden, slot) for slot in (1, 2, 3))
    near = (c // 2) == e
    hidden_x = swap(hidden, "expert")
    x2 = swap(jnp.where(near, z2, z1), "expert")
    x3 = lax.ppermute(
        z3,
        ("expert", "col"),
        [(ee * 4 + cc, (1 - ee) * 4 + cc) for ee in range(2) for cc in range(4) if cc // 2 == ee],
    )
    odd = (c % 2) != r

    def pick(flag):
        own = jnp.where(near, jnp.where(flag, z1, hidden), jnp.where(flag, z3, z2))
        other = jnp.where(near, jnp.where(flag, x2, hidden_x), jnp.where(flag, x3, x2))
        return own, other

    a_own, a_other = pick(odd)
    b_own, b_other = pick(~odd)
    a_quarters = [a_own, a_other, swap(b_own, "row"), swap(b_other, "row")]
    c_quarters = [hidden, hidden_x, swap(hidden, "row"), swap(hidden_x, "row")]

    own, s1, s2, s3 = project(place, c_quarters, down)
    returned = [across(value, slot) for slot, value in ((1, s1), (2, s2), (3, s3))]
    gram_block = gram_of(place, a_quarters, c_quarters)
    expert_out = pl.pallas_call(
        unpack_kernel,
        out_shape=jax.ShapeDtypeStruct((group_rows, depth), BF16),
        name="unpack",
    )(routes_t, pad, route_weight.T, own, *returned)
    return (expert_out, gram_block)


def solution(mesh):
    in_specs = (
        P(("parts", "col"), ("expert", "row")),
        P(("parts", "col"), None),
        P(("parts", "col"), None),
        P(("parts", "col")),
        P(("expert", "row"), None, "col"),
        P("col", ("expert", "row")),
    )
    out_specs = (P(("parts", "col"), ("expert", "row")), P(("parts", "expert", "row"), "col"))
    small = mesh.shape["expert"] == 2 and mesh.shape["row"] == 2 and mesh.shape["col"] == 4
    return jax.shard_map(
        on_device if small else on_any_device,
        mesh=mesh,
        in_specs=in_specs,
        out_specs=out_specs,
        check_vma=False,
    )
```

```python
import functools

import jax
import jax.numpy as jnp
from jax import lax
from jax.experimental import pallas as pl
from jax.experimental.pallas import tpu as pltpu
from jax.sharding import PartitionSpec as P

F32 = jnp.float32
BF16 = jnp.bfloat16
MIB = 1 << 20


def spread(value, axis, source):
    kept = jnp.where(lax.axis_index(axis) == source, value, 0).astype(value.dtype)
    return lax.psum(kept, axis)


def activate(preacts):
    return (jax.nn.silu(preacts[:, 0, :]) * preacts[:, 1, :]).astype(jnp.bfloat16)


def on_any_device(tokens, routes, route_weight, pad_mask, gate_up, down):
    group_rows = tokens.shape[0]
    slot_count = group_rows // 4
    names_zero = routes == 0
    routed = jnp.any(names_zero, axis=1)
    live_rows = routed & (pad_mask == 1)
    factor = jnp.sum(
        jnp.where(names_zero, route_weight, jnp.float32(0.0)), axis=1
    ) * live_rows.astype(jnp.float32)
    position = jnp.cumsum(routed.astype(jnp.int32)) - 1
    slot_ids = lax.broadcasted_iota(jnp.int32, (slot_count, group_rows), 0)
    placing = ((position[None, :] == slot_ids) & routed[None, :]).astype(jnp.bfloat16)
    masked = tokens * live_rows.astype(jnp.bfloat16)[:, None]
    packed = jnp.dot(placing, masked, preferred_element_type=jnp.float32).astype(jnp.bfloat16)
    gathered = lax.all_gather(packed, "col", axis=0, tiled=True)
    anchor = lax.axis_index(("expert", "row"))
    preacts = lax.psum(
        jnp.einsum("rd,dgf->rgf", gathered, gate_up, preferred_element_type=jnp.float32),
        ("expert", "row"),
    )
    hidden = activate(preacts)
    mirrored = spread(hidden, "col", anchor)
    gram_block = lax.dot_general(
        mirrored, hidden, (((0,), (0,)), ((), ())), preferred_element_type=jnp.float32
    )
    gram_block = gram_block * jnp.float32(2.0 / hidden.shape[0])
    returned = lax.psum_scatter(
        jnp.dot(hidden, down, preferred_element_type=jnp.float32),
        "col",
        scatter_dimension=0,
        tiled=True,
    )
    unpacked = lax.dot_general(
        placing.astype(jnp.float32),
        returned,
        (((0,), (0,)), ((), ())),
        precision=lax.Precision.HIGHEST,
        preferred_element_type=jnp.float32,
    )
    expert_out = (unpacked * factor[:, None]).astype(jnp.bfloat16)
    return (expert_out, gram_block)


def cost(flops, moved):
    return pl.CostEstimate(flops=int(flops), bytes_accessed=int(moved), transcendentals=0)


def params(mib):
    return pltpu.CompilerParams(vmem_limit_bytes=mib * MIB)


def placing_of(routes_t, pad, slots):
    rows = routes_t.shape[1]
    routed = (routes_t[0:1, :] == 0) | (routes_t[1:2, :] == 0)
    live = jnp.where(routed & (pad == 1), 1.0, 0.0)
    before = lax.broadcasted_iota(jnp.int32, (rows, rows), 0)
    upto = lax.broadcasted_iota(jnp.int32, (rows, rows), 1)
    tri = jnp.where(before <= upto, 1.0, 0.0).astype(BF16)
    routed_rows = jnp.broadcast_to(jnp.where(routed, 1.0, 0.0), (8, rows)).astype(BF16)
    position = jnp.dot(routed_rows, tri, preferred_element_type=F32)[0:1, :] - 1.0
    slot_ids = lax.broadcasted_iota(jnp.int32, (slots, rows), 0).astype(F32)
    return jnp.where(position == slot_ids, jnp.broadcast_to(live, (slots, rows)), 0.0)


def pack_kernel(tokens_ref, routes_ref, pad_ref, packed_ref):
    placing = placing_of(routes_ref[...], pad_ref[...], packed_ref.shape[0])
    packed_ref[...] = jnp.dot(
        placing.astype(BF16), tokens_ref[...], preferred_element_type=F32
    ).astype(BF16)


def unpack_kernel(
    after_ref, routes_ref, pad_ref, weight_ref, own_ref, r1_ref, r2_ref, r3_ref, out_ref
):
    del after_ref
    routes_t = routes_ref[...]
    placing = placing_of(routes_t, pad_ref[...], own_ref.shape[0])
    weight = jnp.sum(jnp.where(routes_t == 0, weight_ref[...], 0.0), axis=0, keepdims=True)
    factor = jnp.sum(placing * weight, axis=1, keepdims=True)
    total = own_ref[...] + r1_ref[...].astype(F32) + r2_ref[...].astype(F32) + r3_ref[...].astype(F32)
    scaled = (total * factor).astype(BF16)
    out_ref[...] = lax.dot_general(
        placing.astype(BF16), scaled, (((0,), (0,)), ((), ())), preferred_element_type=F32
    ).astype(BF16)


def regroup_kernel(after_ref, weights_ref, out_ref, sems):
    del after_ref
    copies = [
        pltpu.make_async_copy(weights_ref.at[:, t], out_ref.at[t], sems.at[t])
        for t in range(out_ref.shape[0])
    ]
    for copy in copies:
        copy.start()
    for copy in copies:
        copy.wait()


def regroup(after, weights):
    depth, tiles, two, lanes = weights.shape
    grouped = pl.pallas_call(
        regroup_kernel,
        in_specs=[pl.BlockSpec(memory_space=pl.ANY), pl.BlockSpec(memory_space=pltpu.HBM)],
        out_specs=pl.BlockSpec(memory_space=pltpu.VMEM),
        out_shape=pltpu.VMEM((tiles, depth, two, lanes), BF16),
        scratch_shapes=[pltpu.SemaphoreType.DMA((tiles,))],
        compiler_params=params(8),
        cost_estimate=cost(0, 4 * weights.size),
        name="regroup",
    )(after, weights)
    return grouped.reshape(tiles, depth * two, lanes)


def widen_tokens(place_ref, x_refs, wide_ref):
    slots, depth = x_refs[0].shape
    rows = 4 * slots
    here = place_ref[2]
    cut = 256
    into = lax.broadcasted_iota(jnp.int32, (cut, 2 * cut), 1)
    out_of = lax.broadcasted_iota(jnp.int32, (cut, 2 * cut), 0)
    for half in range(2):
        widen = jnp.where(into == 2 * out_of + half, 1.0, 0.0).astype(BF16)
        for slot, x_ref in enumerate(x_refs):
            at = pl.multiple_of(half * rows + (here ^ slot) * slots, slots)
            for k in range(depth // cut):
                wide_ref[pl.ds(at, slots), 2 * cut * k : 2 * cut * (k + 1)] = jnp.dot(
                    x_ref[:, cut * k : cut * (k + 1)], widen, preferred_element_type=F32
                ).astype(BF16)


def preact_kernel(first, row_flip, place_ref, *refs):
    if first:
        x0, x1, x2, x3, w_ref, out_ref, wide_ref = refs
        widen_tokens(place_ref, (x0, x1, x2, x3), wide_ref)
    else:
        wide_ref, w_ref, out_ref = refs
    tiles, _, lanes = w_ref.shape
    per = tiles // 4
    for i in range(2):
        quarter = (place_ref[0] ^ (1 - i)) * 2 + (place_ref[1] ^ row_flip)
        for j in range(per // 2):
            at = quarter * per + 2 * j
            w = jnp.concatenate([w_ref[at], w_ref[at + 1]], axis=1)
            out_ref[i, :, 2 * lanes * j : 2 * lanes * (j + 1)] = jnp.dot(
                wide_ref[...], w, preferred_element_type=F32
            ).astype(out_ref.dtype)


def preacts_of(place, lefts, weights, row_flip, out_type):
    tiles, depth2, lanes = weights.shape
    first = len(lefts) > 1
    rows = 4 * lefts[0].shape[0] if first else lefts[0].shape[0] // 2
    per = tiles // 4
    vmem = pl.BlockSpec(memory_space=pltpu.VMEM)
    out_shape = [jax.ShapeDtypeStruct((2, 2 * rows, per * lanes), out_type)]
    if first:
        out_shape.append(jax.ShapeDtypeStruct((2 * rows, depth2), BF16))
    return pl.pallas_call(
        functools.partial(preact_kernel, first, row_flip),
        in_specs=[pl.BlockSpec(memory_space=pltpu.SMEM)] + [vmem] * (len(lefts) + 1),
        out_specs=[vmem] * len(out_shape),
        out_shape=out_shape,
        compiler_params=params(8),
        cost_estimate=cost(4 * rows * depth2 * per * 2 * lanes, 2 * weights.size // 2),
        name="preacts_sent" if first else "preacts_kept",
    )(place, *lefts, pltpu.with_memory_space_constraint(weights, pltpu.VMEM))


def project_kernel(place_ref, h0, h1, h2, h3, down_ref, own_ref, s1_ref, s2_ref, s3_ref, total_ref):
    j = pl.program_id(0)
    slots = own_ref.shape[0]
    for k, h_ref in enumerate((h0, h1, h2, h3)):

        @pl.when(j == k)
        def _():
            part = jnp.dot(h_ref[...], down_ref[...], preferred_element_type=F32)
            total_ref[...] = part if k == 0 else total_ref[...] + part

    @pl.when(j == 3)
    def _():
        here = place_ref[2]
        for slot, out_ref in enumerate((own_ref, s1_ref, s2_ref, s3_ref)):
            at = pl.multiple_of((here ^ slot) * slots, slots)
            out_ref[...] = total_ref[pl.ds(at, slots), :].astype(out_ref.dtype)


def project(place, quarters, down):
    rows, units = quarters[0].shape
    width = down.shape[1]
    slots = rows // 4
    whole = lambda shape: pl.BlockSpec(shape, lambda j, place: (0, 0))

    def quarter(j, place):
        return ((place[0] ^ (j % 2)) * 2 + (place[1] ^ (j // 2)), 0)

    return pl.pallas_call(
        project_kernel,
        grid_spec=pltpu.PrefetchScalarGridSpec(
            num_scalar_prefetch=1,
            grid=(4,),
            in_specs=[whole((rows, units))] * 4 + [pl.BlockSpec((units, width), quarter)],
            out_specs=[whole((slots, width))] * 4,
            scratch_shapes=[pltpu.VMEM((rows, width), F32)],
        ),
        out_shape=[jax.ShapeDtypeStruct((slots, width), F32)]
        + [jax.ShapeDtypeStruct((slots, width), BF16)] * 3,
        compiler_params=params(32),
        cost_estimate=cost(2 * rows * 4 * units * width, down.size * 2),
        name="project",
    )(place, *quarters, pltpu.with_memory_space_constraint(down, pltpu.HBM))


def gram_kernel(scale, halves, place_ref, a0, a1, a2, a3, c0, c1, c2, c3, out_ref, done_ref, wide_ref):
    j = pl.program_id(0)
    done_ref[...] = jnp.zeros_like(done_ref)
    units = a0.shape[1]
    take = units // halves

    @pl.when(j == 0)
    def _():
        for k, c_ref in enumerate((c0, c1, c2, c3)):
            q = (place_ref[0] ^ (k % 2)) * 2 + (place_ref[1] ^ (k // 2))
            wide_ref[:, pl.ds(pl.multiple_of(q * units, units), units)] = c_ref[...]

    for k, a_ref in enumerate((a0, a1, a2, a3)):
        for half in range(halves):

            @pl.when(j == k * halves + half)
            def _():
                left = a_ref[:, take * half : take * (half + 1)]
                cut = 256
                for n in range(4 * units // cut):
                    out_ref[:, cut * n : cut * (n + 1)] = scale * lax.dot_general(
                        left,
                        wide_ref[:, cut * n : cut * (n + 1)],
                        (((0,), (0,)), ((), ())),
                        preferred_element_type=F32,
                    )


def gram_of(place, a_quarters, c_quarters):
    rows, units = a_quarters[0].shape
    halves = 2
    whole = pl.BlockSpec((rows, units), lambda j, place: (0, 0))

    def block(j, place):
        k = j // halves
        quarter = (place[0] ^ (k % 2)) * 2 + (place[1] ^ (k // 2))
        return (quarter * halves + j % halves, 0)

    return pl.pallas_call(
        functools.partial(gram_kernel, 2.0 / rows, halves),
        grid_spec=pltpu.PrefetchScalarGridSpec(
            num_scalar_prefetch=1,
            grid=(4 * halves,),
            in_specs=[whole] * 8,
            out_specs=[
                pl.BlockSpec((units // halves, 4 * units), block),
                pl.BlockSpec((8, 128), lambda j, place: (0, 0)),
            ],
            scratch_shapes=[pltpu.VMEM((rows, 4 * units), BF16)],
        ),
        out_shape=[
            jax.ShapeDtypeStruct((4 * units, 4 * units), F32),
            jax.ShapeDtypeStruct((8, 128), F32),
        ],
        compiler_params=params(32),
        cost_estimate=cost(2 * rows * 16 * units * units, 64 * units * units),
        name="gram",
    )(place, *a_quarters, *c_quarters)


def swap(value, axis):
    return lax.ppermute(value, axis, [(0, 1), (1, 0)])


def across(value, slot):
    return lax.ppermute(value, "col", [(i, i ^ slot) for i in range(4)])


def on_device(tokens, routes, route_weight, pad_mask, gate_up, down):
    group_rows, depth = tokens.shape
    slots = group_rows // 4
    units = gate_up.shape[2]
    lanes = 128
    e = lax.axis_index("expert").astype(jnp.int32)
    r = lax.axis_index("row").astype(jnp.int32)
    c = lax.axis_index("col").astype(jnp.int32)
    place = jnp.stack([e, r, c])
    routes_t = routes.T
    pad = pad_mask[None, :]
    weights = gate_up.reshape(depth, 2, units // lanes, lanes).transpose(0, 2, 1, 3)

    packed = pl.pallas_call(
        pack_kernel,
        out_shape=jax.ShapeDtypeStruct((slots, depth), BF16),
        name="pack",
    )(tokens, routes_t, pad)
    lefts = [packed] + [across(packed, slot) for slot in (1, 2, 3)]
    grouped = regroup(packed, pltpu.with_memory_space_constraint(weights, pltpu.HBM))
    sent, wide = preacts_of(place, lefts, grouped, 1, F32)
    got = swap(sent, "row")
    (kept,) = preacts_of(place, [wide], grouped, 0, F32)
    got_x = swap((kept[0] + got[0]).astype(BF16), "expert")
    rows = 4 * slots
    preacts = kept[1] + got[1] + got_x.astype(F32)
    hidden = (jax.nn.silu(preacts[:rows]) * preacts[rows:]).astype(BF16)

    z2 = across(hidden, 2)
    z1 = across(hidden, 1)
    hidden_x = swap(hidden, "expert")

    near = (c // 2) == e
    z2, z1, hidden_x = lax.optimization_barrier((z2, z1, hidden_x))
    onward, x2 = lax.optimization_barrier((z2, jnp.where(near, z2, z1)))
    z3 = across(onward, 1)
    x2 = swap(x2, "expert")
    c_quarters = [hidden, hidden_x, swap(hidden, "row"), swap(hidden_x, "row")]
    own, s1, s2, s3 = project(place, c_quarters, down)
    z3, own = lax.optimization_barrier((z3, own))
    x3 = lax.ppermute(
        z3,
        ("expert", "col"),
        [(ee * 4 + cc, (1 - ee) * 4 + cc) for ee in range(2) for cc in range(4) if cc // 2 == ee],
    )
    odd = (c % 2) != r

    def pick(flag):
        own = jnp.where(near, jnp.where(flag, z1, hidden), jnp.where(flag, z3, z2))
        other = jnp.where(near, jnp.where(flag, x2, hidden_x), jnp.where(flag, x3, x2))
        return own, other

    a_own, a_other = pick(odd)
    b_own, b_other = pick(~odd)
    a_quarters = [a_own, a_other, swap(b_own, "row"), swap(b_other, "row")]

    returned = [across(value, slot) for slot, value in ((1, s1), (2, s2), (3, s3))]
    gram_block, done = gram_of(place, a_quarters, c_quarters)
    expert_out = pl.pallas_call(
        unpack_kernel,
        out_shape=jax.ShapeDtypeStruct((group_rows, depth), BF16),
        name="unpack",
    )(done, routes_t, pad, route_weight.T, own, *returned)
    return (expert_out, gram_block)


def solution(mesh):
    in_specs = (
        P(("parts", "col"), ("expert", "row")),
        P(("parts", "col"), None),
        P(("parts", "col"), None),
        P(("parts", "col")),
        P(("expert", "row"), None, "col"),
        P("col", ("expert", "row")),
    )
    out_specs = (P(("parts", "col"), ("expert", "row")), P(("parts", "expert", "row"), "col"))
    small = mesh.shape["expert"] == 2 and mesh.shape["row"] == 2 and mesh.shape["col"] == 4
    return jax.shard_map(
        on_device if small else on_any_device,
        mesh=mesh,
        in_specs=in_specs,
        out_specs=out_specs,
        check_vma=False,
    )
```

```python
import functools

import jax
import jax.numpy as jnp
from jax import lax
from jax.experimental import pallas as pl
from jax.experimental.pallas import tpu as pltpu
from jax.sharding import PartitionSpec as P

F32 = jnp.float32
BF16 = jnp.bfloat16
MIB = 1 << 20


def spread(value, axis, source):
    kept = jnp.where(lax.axis_index(axis) == source, value, 0).astype(value.dtype)
    return lax.psum(kept, axis)


def activate(preacts):
    return (jax.nn.silu(preacts[:, 0, :]) * preacts[:, 1, :]).astype(jnp.bfloat16)


def on_any_device(tokens, routes, route_weight, pad_mask, gate_up, down):
    group_rows = tokens.shape[0]
    slot_count = group_rows // 4
    names_zero = routes == 0
    routed = jnp.any(names_zero, axis=1)
    live_rows = routed & (pad_mask == 1)
    factor = jnp.sum(
        jnp.where(names_zero, route_weight, jnp.float32(0.0)), axis=1
    ) * live_rows.astype(jnp.float32)
    position = jnp.cumsum(routed.astype(jnp.int32)) - 1
    slot_ids = lax.broadcasted_iota(jnp.int32, (slot_count, group_rows), 0)
    placing = ((position[None, :] == slot_ids) & routed[None, :]).astype(jnp.bfloat16)
    masked = tokens * live_rows.astype(jnp.bfloat16)[:, None]
    packed = jnp.dot(placing, masked, preferred_element_type=jnp.float32).astype(jnp.bfloat16)
    gathered = lax.all_gather(packed, "col", axis=0, tiled=True)
    anchor = lax.axis_index(("expert", "row"))
    preacts = lax.psum(
        jnp.einsum("rd,dgf->rgf", gathered, gate_up, preferred_element_type=jnp.float32),
        ("expert", "row"),
    )
    hidden = activate(preacts)
    mirrored = spread(hidden, "col", anchor)
    gram_block = lax.dot_general(
        mirrored, hidden, (((0,), (0,)), ((), ())), preferred_element_type=jnp.float32
    )
    gram_block = gram_block * jnp.float32(2.0 / hidden.shape[0])
    returned = lax.psum_scatter(
        jnp.dot(hidden, down, preferred_element_type=jnp.float32),
        "col",
        scatter_dimension=0,
        tiled=True,
    )
    unpacked = lax.dot_general(
        placing.astype(jnp.float32),
        returned,
        (((0,), (0,)), ((), ())),
        precision=lax.Precision.HIGHEST,
        preferred_element_type=jnp.float32,
    )
    expert_out = (unpacked * factor[:, None]).astype(jnp.bfloat16)
    return (expert_out, gram_block)


def cost(flops, moved):
    return pl.CostEstimate(flops=int(flops), bytes_accessed=int(moved), transcendentals=0)


def params(mib):
    return pltpu.CompilerParams(vmem_limit_bytes=mib * MIB)


VMEM = pl.BlockSpec(memory_space=pltpu.VMEM)
HBM = pl.BlockSpec(memory_space=pltpu.HBM)
SMEM = pl.BlockSpec(memory_space=pltpu.SMEM)
ANY = pl.BlockSpec(memory_space=pl.ANY)


def in_vmem(value):
    return pltpu.with_memory_space_constraint(value, pltpu.VMEM)


def in_hbm(value):
    return pltpu.with_memory_space_constraint(value, pltpu.HBM)


def tie(*values):
    return lax.optimization_barrier(values)


def pack_kernel(
    tokens_ref, routes_ref, pad_ref, weight_ref, packed_ref, placing_ref, factor_ref, held_ref, sem
):
    copy = pltpu.make_async_copy(tokens_ref, held_ref, sem)
    copy.start()
    slots, rows = placing_ref.shape
    routes_t = routes_ref[...]
    routed = (routes_t[0:1, :] == 0) | (routes_t[1:2, :] == 0)
    live = jnp.where(routed & (pad_ref[...] == 1), 1.0, 0.0)
    before = lax.broadcasted_iota(jnp.int32, (rows, rows), 0)
    upto = lax.broadcasted_iota(jnp.int32, (rows, rows), 1)
    tri = jnp.where(before <= upto, 1.0, 0.0).astype(BF16)
    routed_rows = jnp.broadcast_to(jnp.where(routed, 1.0, 0.0), (8, rows)).astype(BF16)
    position = jnp.dot(routed_rows, tri, preferred_element_type=F32)[0:1, :] - 1.0
    slot_ids = lax.broadcasted_iota(jnp.int32, (slots, rows), 0).astype(F32)
    placing = jnp.where(position == slot_ids, jnp.broadcast_to(live, (slots, rows)), 0.0)
    placing_ref[...] = placing.astype(BF16)
    weight = jnp.sum(jnp.where(routes_t == 0, weight_ref[...], 0.0), axis=0, keepdims=True)
    factor = jnp.sum(placing * weight, axis=1, keepdims=True)
    factor_ref[...] = jnp.broadcast_to(factor, factor_ref.shape)
    copy.wait()
    packed_ref[...] = jnp.dot(
        placing.astype(BF16), held_ref[...], preferred_element_type=F32
    ).astype(BF16)


def pack(tokens, routes_t, pad, weight_t):
    rows, depth = tokens.shape
    slots = rows // 4
    return pl.pallas_call(
        pack_kernel,
        in_specs=[HBM, VMEM, VMEM, VMEM],
        out_specs=[VMEM] * 3,
        out_shape=[
            pltpu.VMEM((slots, depth), BF16),
            pltpu.VMEM((slots, rows), BF16),
            pltpu.VMEM((slots, 128), F32),
        ],
        scratch_shapes=[pltpu.VMEM((rows, depth), BF16), pltpu.SemaphoreType.DMA],
        compiler_params=params(4),
        name="pack",
    )(tokens, routes_t, pad, weight_t)


def unpack_kernel(after_ref, placing_ref, factor_ref, own_ref, r1_ref, r2_ref, r3_ref, out_ref):
    del after_ref
    total = own_ref[...] + r1_ref[...].astype(F32) + r2_ref[...].astype(F32) + r3_ref[...].astype(F32)
    scaled = (total * factor_ref[:, 0:1]).astype(BF16)
    out_ref[...] = lax.dot_general(
        placing_ref[...], scaled, (((0,), (0,)), ((), ())), preferred_element_type=F32
    ).astype(BF16)


def unpack(done, placing, factor, own, returned):
    slots, rows = placing.shape
    return pl.pallas_call(
        unpack_kernel,
        in_specs=[ANY] + [VMEM] * 6,
        out_specs=VMEM,
        out_shape=jax.ShapeDtypeStruct((rows, own.shape[1]), BF16),
        compiler_params=params(4),
        name="unpack",
    )(done, placing, factor, own, *returned)


def regroup_kernel(after_ref, weights_ref, out_ref, sems):
    del after_ref
    copies = [
        pltpu.make_async_copy(weights_ref.at[:, t], out_ref.at[t], sems.at[t])
        for t in range(out_ref.shape[0])
    ]
    for copy in copies:
        copy.start()
    for copy in copies:
        copy.wait()


def regroup(behind, weights):
    depth, tiles, two, lanes = weights.shape
    grouped = pl.pallas_call(
        regroup_kernel,
        in_specs=[ANY, HBM],
        out_specs=VMEM,
        out_shape=pltpu.VMEM((tiles, depth, two, lanes), BF16),
        scratch_shapes=[pltpu.SemaphoreType.DMA((tiles,))],
        compiler_params=params(4),
        cost_estimate=cost(0, 4 * weights.size),
        name="regroup",
    )(behind, in_hbm(weights))
    return grouped.reshape(tiles, depth * two, lanes)


def fetch_kernel(after_ref, down_ref, out_ref, done_ref, sems):
    del after_ref
    parts = sems.shape[0]
    size = down_ref.shape[0] // parts
    copies = [
        pltpu.make_async_copy(
            down_ref.at[pl.ds(size * i, size)], out_ref.at[pl.ds(size * i, size)], sems.at[i]
        )
        for i in range(parts)
    ]
    for copy in copies:
        copy.start()
    done_ref[...] = jnp.zeros_like(done_ref)
    for copy in copies:
        copy.wait()


def fetch(behind, down):
    return pl.pallas_call(
        fetch_kernel,
        in_specs=[ANY, HBM],
        out_specs=[VMEM, VMEM],
        out_shape=[pltpu.VMEM(down.shape, BF16), pltpu.VMEM((8, 128), F32)],
        scratch_shapes=[pltpu.SemaphoreType.DMA((4,))],
        compiler_params=params(4),
        cost_estimate=cost(0, 4 * down.size),
        name="fetch_down",
    )(behind, in_hbm(down))


def widen_tokens(place_ref, x_refs, wide_ref):
    slots, depth = x_refs[0].shape
    rows = 4 * slots
    here = place_ref[2]
    cut = 256
    into = lax.broadcasted_iota(jnp.int32, (cut, 4 * cut), 1)
    out_of = lax.broadcasted_iota(jnp.int32, (cut, 4 * cut), 0)
    half = jnp.where(into < 2 * cut, 0, 1)
    widen = jnp.where(into - 2 * cut * half == 2 * out_of + half, 1.0, 0.0).astype(BF16)
    for slot, x_ref in enumerate(x_refs):
        stacked = jnp.concatenate(
            [x_ref[:, cut * k : cut * (k + 1)] for k in range(depth // cut)], axis=0
        )
        spaced = jnp.dot(stacked, widen, preferred_element_type=F32).astype(BF16)
        for h in range(2):
            at = pl.multiple_of(h * rows + (here ^ slot) * slots, slots)
            for k in range(depth // cut):
                wide_ref[pl.ds(at, slots), 2 * cut * k : 2 * cut * (k + 1)] = spaced[
                    slots * k : slots * (k + 1), 2 * cut * h : 2 * cut * (h + 1)
                ]


def preact_kernel(first, row_flip, chunk, chunks, place_ref, *refs):
    if first:
        x0, x1, x2, x3, w_ref, out_ref, wide_ref = refs
        widen_tokens(place_ref, (x0, x1, x2, x3), wide_ref)
    else:
        wide_ref, w_ref, out_ref = refs
    tiles, _, lanes = w_ref.shape
    per = tiles // 4
    take = per // chunks
    at = []
    for i in range(2):
        quarter = (place_ref[0] ^ (1 - i)) * 2 + (place_ref[1] ^ row_flip)
        at += [quarter * per + chunk * take + j for j in range(take)]
    for j in range(take):
        w = jnp.concatenate([w_ref[at[2 * j]], w_ref[at[2 * j + 1]]], axis=1)
        out_ref[:, 2 * lanes * j : 2 * lanes * (j + 1)] = jnp.dot(
            wide_ref[...], w, preferred_element_type=F32
        )


def preacts_of(place, lefts, weights, row_flip, chunk, chunks):
    tiles, depth2, lanes = weights.shape
    first = len(lefts) > 1
    rows = 4 * lefts[0].shape[0] if first else lefts[0].shape[0] // 2
    units = tiles // 4 // chunks * lanes
    out_shape = [jax.ShapeDtypeStruct((2 * rows, 2 * units), F32)]
    if first:
        out_shape.append(pltpu.VMEM((2 * rows, depth2), BF16))
    return pl.pallas_call(
        functools.partial(preact_kernel, first, row_flip, chunk, chunks),
        in_specs=[SMEM] + [VMEM] * (len(lefts) + 1),
        out_specs=[VMEM] * len(out_shape),
        out_shape=out_shape,
        compiler_params=params(8),
        cost_estimate=cost(8 * rows * depth2 * units, 0),
        name="preacts_" + ("sent" if row_flip else "kept"),
    )(place, *lefts, in_vmem(weights))


def project_kernel(tick_ref, place_ref, hidden_ref, down_ref, own_ref, s1_ref, s2_ref, s3_ref, total_ref):
    del tick_ref
    slots, width = own_ref.shape
    cut = 512
    for n in range(width // cut):
        total_ref[:, cut * n : cut * (n + 1)] = jnp.dot(
            hidden_ref[...], down_ref[:, cut * n : cut * (n + 1)], preferred_element_type=F32
        )
    here = place_ref[2]
    for slot, out_ref in enumerate((own_ref, s1_ref, s2_ref, s3_ref)):
        at = pl.multiple_of((here ^ slot) * slots, slots)
        out_ref[...] = total_ref[pl.ds(at, slots), :].astype(out_ref.dtype)


def project(tick, place, hidden, down):
    rows, units = hidden.shape
    width = down.shape[1]
    slots = rows // 4
    return pl.pallas_call(
        project_kernel,
        in_specs=[ANY, SMEM, VMEM, VMEM],
        out_specs=[VMEM] * 4,
        out_shape=[jax.ShapeDtypeStruct((slots, width), F32)]
        + [jax.ShapeDtypeStruct((slots, width), BF16)] * 3,
        scratch_shapes=[pltpu.VMEM((rows, width), F32)],
        compiler_params=params(8),
        cost_estimate=cost(2 * rows * units * width, 0),
        name="project",
    )(tick, place, in_vmem(hidden), in_vmem(down))


def gram_kernel(scale, first, flip, chunk, chunks, tick_ref, place_ref, a0, a1, *refs):
    del tick_ref
    if first:
        c_refs = refs[: 4 * chunks]
        out_ref, done_ref, wide_ref, held_ref, sems = refs[4 * chunks :]
    else:
        wide_ref, _, out_ref, done_ref, held_ref, sems = refs
    done_ref[...] = jnp.zeros_like(done_ref)
    units = a0.shape[1]
    quarter = chunks * units
    if first:
        for k in range(4):
            q = (place_ref[0] ^ (k % 2)) * 2 + (place_ref[1] ^ (k // 2))
            for h in range(chunks):
                at = pl.multiple_of(q * quarter + h * units, units)
                wide_ref[:, pl.ds(at, units)] = c_refs[k * chunks + h][...]
    cut = held_ref.shape[-1]
    copies = []
    for k, a_ref in enumerate((a0, a1)):
        q = (place_ref[0] ^ flip) * 2 + (place_ref[1] ^ k)
        rows = pl.ds(pl.multiple_of(q * quarter + chunk * units, units), units)
        left = a_ref[...].T
        for n in range(4 * quarter // cut):
            columns = pl.ds(cut * n, cut)
            held_ref[k, n] = scale * jnp.dot(
                left, wide_ref[:, cut * n : cut * (n + 1)], preferred_element_type=F32
            )
            copy = pltpu.make_async_copy(
                held_ref.at[k, n], out_ref.at[rows, columns], sems.at[k, n]
            )
            copy.start()
            copies.append(copy)
    for copy in copies:
        copy.wait()


def gram_piece(tick, place, pieces, flip, chunk, chunks, c_parts=None, wide=None, gram=None):
    rows, units = pieces[0].shape
    quarter = chunks * units
    first = gram is None
    cut = 512
    steps = 4 * quarter // cut
    out_specs = [HBM, VMEM]
    out_shape = [
        jax.ShapeDtypeStruct((4 * quarter, 4 * quarter), F32),
        pltpu.VMEM((8, 128), F32),
    ]
    if first:
        operands = [tick, place, *pieces, *c_parts]
        in_specs = [ANY, SMEM] + [VMEM] * (2 + 4 * chunks)
        out_specs.append(VMEM)
        out_shape.append(pltpu.VMEM((rows, 4 * quarter), BF16))
        aliases = {}
    else:
        operands = [tick, place, *pieces, in_vmem(wide), gram]
        in_specs = [ANY, SMEM] + [VMEM] * 3 + [HBM]
        aliases = {5: 0}
    return pl.pallas_call(
        functools.partial(gram_kernel, 2.0 / rows, first, flip, chunk, chunks),
        in_specs=in_specs,
        out_specs=out_specs,
        out_shape=out_shape,
        input_output_aliases=aliases,
        scratch_shapes=[
            pltpu.VMEM((2, steps, units, cut), F32),
            pltpu.SemaphoreType.DMA((2, steps)),
        ],
        compiler_params=params(24),
        cost_estimate=cost(16 * rows * units * quarter, 32 * units * quarter),
        name="gram",
    )(*operands)


def swap(value, axis):
    return lax.ppermute(value, axis, [(0, 1), (1, 0)])


def across(value, slot):
    return lax.ppermute(value, "col", [(i, i ^ slot) for i in range(4)])


def on_device(tokens, routes, route_weight, pad_mask, gate_up, down):
    group_rows, depth = tokens.shape
    slots = group_rows // 4
    rows = 4 * slots
    units = gate_up.shape[2]
    lanes = 128
    chunks = 2
    width = units // 4 // chunks
    e = lax.axis_index("expert").astype(jnp.int32)
    r = lax.axis_index("row").astype(jnp.int32)
    c = lax.axis_index("col").astype(jnp.int32)
    place = jnp.stack([e, r, c])
    near = (c // 2) == e
    odd = (c % 2) != r
    weights = gate_up.reshape(depth, 2, units // lanes, lanes).transpose(0, 2, 1, 3)

    packed, placing, factor = pack(tokens, routes.T, pad_mask[None, :], route_weight.T)
    lefts = [packed] + [across(packed, slot) for slot in (1, 2, 3)]
    grouped = regroup(packed, weights)

    first_sent, wide = preacts_of(place, lefts, grouped, 1, 0, chunks)
    (last_sent,) = preacts_of(place, [wide], grouped, 1, 1, chunks)
    got = [swap(first_sent, "row"), swap(last_sent, "row")]
    sums, got_x = [], []
    for h in range(chunks):
        (kept,) = preacts_of(place, [wide], grouped, 0, h, chunks)
        leaves = (kept[:, :width] + got[h][:, :width]).astype(BF16)
        wide, leaves = tie(wide, leaves)
        sums.append(kept[:, width:] + got[h][:, width:])
        got_x.append(swap(leaves, "expert"))
    down_held, tick = fetch(wide, down)

    hidden, z1, z2, z3, hidden_x, x2, x3 = ([None] * chunks for _ in range(7))
    for h in range(chunks):
        tick, arrived = tie(tick, got_x[h])
        preacts = sums[h] + arrived.astype(F32)
        hidden[h] = (jax.nn.silu(preacts[:rows]) * preacts[rows:]).astype(BF16)
        z2[h] = across(hidden[h], 2)
        z1[h] = across(hidden[h], 1)
        hidden_x[h] = swap(hidden[h], "expert")

    def pass_on(tick, h):
        tick, z2[h], z1[h], hidden[-1] = tie(tick, z2[h], z1[h], hidden[-1])
        tick, onward, leaves = tie(tick, z2[h], jnp.where(near, z2[h], z1[h]))
        z3[h] = across(onward, 1)
        x2[h] = swap(leaves, "expert")
        return tick

    def pass_last(tick, h):
        tick, z3[h] = tie(tick, z3[h])
        x3[h] = lax.ppermute(
            z3[h],
            ("expert", "col"),
            [
                (ee * 4 + cc, (1 - ee) * 4 + cc)
                for ee in range(2)
                for cc in range(4)
                if cc // 2 == ee
            ],
        )
        return tick

    def own_plane(h, flag):
        return jnp.where(near, jnp.where(flag, z1[h], hidden[h]), jnp.where(flag, z3[h], z2[h]))

    def other_plane(h, flag):
        return jnp.where(near, jnp.where(flag, x2[h], hidden_x[h]), jnp.where(flag, x3[h], x2[h]))

    def pieces_of(plane, h):
        return [plane(h, odd), swap(plane(h, ~odd), "row")]

    tick = pass_on(tick, 0)
    tick, hidden_x[0] = tie(tick, hidden_x[0])
    c_parts = [*hidden, *hidden_x, swap(hidden[0], "row"), swap(hidden[1], "row")]
    c_parts.append(swap(hidden_x[0], "row"))
    tick = pass_last(tick, 0)
    own_first = pieces_of(own_plane, 0)
    tick = pass_on(tick, 1)
    tick, hidden_x[1] = tie(tick, hidden_x[1])
    c_parts[3] = hidden_x[1]
    c_parts.append(swap(hidden_x[1], "row"))
    gram, tick, hidden_c = gram_piece(tick, place, own_first, 0, 0, chunks, c_parts=c_parts)

    tick = pass_last(tick, 1)
    own_last = pieces_of(own_plane, 1)
    own, s1, s2, s3 = project(tick, place, hidden_c, down_held)
    tick, own = tie(tick, own)
    returned = [across(value, slot) for slot, value in ((1, s1), (2, s2), (3, s3))]
    tick, x2[0], x3[0] = tie(tick, x2[0], x3[0])
    other_first = pieces_of(other_plane, 0)
    gram, tick = gram_piece(tick, place, own_last, 0, 1, chunks, wide=hidden_c, gram=gram)
    tick, x2[1], x3[1] = tie(tick, x2[1], x3[1])
    other_last = pieces_of(other_plane, 1)
    gram, tick = gram_piece(tick, place, other_first, 1, 0, chunks, wide=hidden_c, gram=gram)
    gram, tick = gram_piece(tick, place, other_last, 1, 1, chunks, wide=hidden_c, gram=gram)
    return (unpack(tick, placing, factor, own, returned), gram)


def solution(mesh):
    in_specs = (
        P(("parts", "col"), ("expert", "row")),
        P(("parts", "col"), None),
        P(("parts", "col"), None),
        P(("parts", "col")),
        P(("expert", "row"), None, "col"),
        P("col", ("expert", "row")),
    )
    out_specs = (P(("parts", "col"), ("expert", "row")), P(("parts", "expert", "row"), "col"))
    small = mesh.shape["expert"] == 2 and mesh.shape["row"] == 2 and mesh.shape["col"] == 4
    return jax.shard_map(
        on_device if small else on_any_device,
        mesh=mesh,
        in_specs=in_specs,
        out_specs=out_specs,
        check_vma=False,
    )
```

```python
import functools

import jax
import jax.numpy as jnp
from jax import lax
from jax.experimental import pallas as pl
from jax.experimental.pallas import tpu as pltpu
from jax.sharding import PartitionSpec as P

F32 = jnp.float32
BF16 = jnp.bfloat16
MIB = 1 << 20


def spread(value, axis, source):
    kept = jnp.where(lax.axis_index(axis) == source, value, 0).astype(value.dtype)
    return lax.psum(kept, axis)


def activate(preacts):
    return (jax.nn.silu(preacts[:, 0, :]) * preacts[:, 1, :]).astype(jnp.bfloat16)


def on_any_device(tokens, routes, route_weight, pad_mask, gate_up, down):
    group_rows = tokens.shape[0]
    slot_count = group_rows // 4
    names_zero = routes == 0
    routed = jnp.any(names_zero, axis=1)
    live_rows = routed & (pad_mask == 1)
    factor = jnp.sum(
        jnp.where(names_zero, route_weight, jnp.float32(0.0)), axis=1
    ) * live_rows.astype(jnp.float32)
    position = jnp.cumsum(routed.astype(jnp.int32)) - 1
    slot_ids = lax.broadcasted_iota(jnp.int32, (slot_count, group_rows), 0)
    placing = ((position[None, :] == slot_ids) & routed[None, :]).astype(jnp.bfloat16)
    masked = tokens * live_rows.astype(jnp.bfloat16)[:, None]
    packed = jnp.dot(placing, masked, preferred_element_type=jnp.float32).astype(jnp.bfloat16)
    gathered = lax.all_gather(packed, "col", axis=0, tiled=True)
    anchor = lax.axis_index(("expert", "row"))
    preacts = lax.psum(
        jnp.einsum("rd,dgf->rgf", gathered, gate_up, preferred_element_type=jnp.float32),
        ("expert", "row"),
    )
    hidden = activate(preacts)
    mirrored = spread(hidden, "col", anchor)
    gram_block = lax.dot_general(
        mirrored, hidden, (((0,), (0,)), ((), ())), preferred_element_type=jnp.float32
    )
    gram_block = gram_block * jnp.float32(2.0 / hidden.shape[0])
    returned = lax.psum_scatter(
        jnp.dot(hidden, down, preferred_element_type=jnp.float32),
        "col",
        scatter_dimension=0,
        tiled=True,
    )
    unpacked = lax.dot_general(
        placing.astype(jnp.float32),
        returned,
        (((0,), (0,)), ((), ())),
        precision=lax.Precision.HIGHEST,
        preferred_element_type=jnp.float32,
    )
    expert_out = (unpacked * factor[:, None]).astype(jnp.bfloat16)
    return (expert_out, gram_block)


def cost(flops, moved):
    return pl.CostEstimate(flops=int(flops), bytes_accessed=int(moved), transcendentals=0)


def params(mib):
    return pltpu.CompilerParams(vmem_limit_bytes=mib * MIB)


VMEM = pl.BlockSpec(memory_space=pltpu.VMEM)
HBM = pl.BlockSpec(memory_space=pltpu.HBM)
SMEM = pl.BlockSpec(memory_space=pltpu.SMEM)
ANY = pl.BlockSpec(memory_space=pl.ANY)


def in_vmem(value):
    return pltpu.with_memory_space_constraint(value, pltpu.VMEM)


def in_hbm(value):
    return pltpu.with_memory_space_constraint(value, pltpu.HBM)


def quarter_of(expert_flip, row_flip):
    return (lax.axis_index("expert") ^ expert_flip) * 2 + (lax.axis_index("row") ^ row_flip)


def tie(*values):
    return lax.optimization_barrier(values)


def pack_kernel(
    tokens_ref, routes_ref, pad_ref, weight_ref, packed_ref, placing_ref, factor_ref,
    tokens_held, routes_held, pad_held, weight_held, sems,
):
    pairs = (
        (routes_ref, routes_held),
        (pad_ref, pad_held),
        (weight_ref, weight_held),
        (tokens_ref, tokens_held),
    )
    copies = [pltpu.make_async_copy(a, b, sems.at[i]) for i, (a, b) in enumerate(pairs)]
    for copy in copies:
        copy.start()
    slots, rows = placing_ref.shape
    before = lax.broadcasted_iota(jnp.int32, (rows, rows), 0)
    upto = lax.broadcasted_iota(jnp.int32, (rows, rows), 1)
    tri = jnp.where(before <= upto, 1.0, 0.0).astype(BF16)
    slot_ids = lax.broadcasted_iota(jnp.int32, (slots, rows), 0).astype(F32)
    for copy in copies[:3]:
        copy.wait()
    routes_t = routes_held[...]
    routed = (routes_t[0:1, :] == 0) | (routes_t[1:2, :] == 0)
    live = jnp.where(routed & (pad_held[...] == 1), 1.0, 0.0)
    routed_rows = jnp.broadcast_to(jnp.where(routed, 1.0, 0.0), (8, rows)).astype(BF16)
    position = jnp.dot(routed_rows, tri, preferred_element_type=F32)[0:1, :] - 1.0
    placing = jnp.where(position == slot_ids, jnp.broadcast_to(live, (slots, rows)), 0.0)
    placing_ref[...] = placing.astype(BF16)
    weight = jnp.sum(jnp.where(routes_t == 0, weight_held[...], 0.0), axis=0, keepdims=True)
    factor = jnp.sum(placing * weight, axis=1, keepdims=True)
    factor_ref[...] = jnp.broadcast_to(factor, factor_ref.shape)
    copies[3].wait()
    packed_ref[...] = jnp.dot(
        placing.astype(BF16), tokens_held[...], preferred_element_type=F32
    ).astype(BF16)


def pack(tokens, routes_t, pad, weight_t):
    rows, depth = tokens.shape
    slots = rows // 4
    operands = (tokens, routes_t, pad, weight_t)
    return pl.pallas_call(
        pack_kernel,
        in_specs=[HBM] * 4,
        out_specs=[VMEM] * 3,
        out_shape=[
            pltpu.VMEM((slots, depth), BF16),
            pltpu.VMEM((slots, rows), BF16),
            pltpu.VMEM((slots, 128), F32),
        ],
        scratch_shapes=[pltpu.VMEM(x.shape, x.dtype) for x in operands]
        + [pltpu.SemaphoreType.DMA((4,))],
        compiler_params=params(3),
        name="pack",
    )(*(in_hbm(x) for x in operands))


def unpack_kernel(after_ref, placing_ref, factor_ref, own_ref, r1_ref, r2_ref, r3_ref, out_ref):
    del after_ref
    total = own_ref[...] + r1_ref[...].astype(F32) + r2_ref[...].astype(F32) + r3_ref[...].astype(F32)
    scaled = (total * factor_ref[:, 0:1]).astype(BF16)
    out_ref[...] = lax.dot_general(
        placing_ref[...], scaled, (((0,), (0,)), ((), ())), preferred_element_type=F32
    ).astype(BF16)


def unpack(done, placing, factor, own, returned):
    slots, rows = placing.shape
    return pl.pallas_call(
        unpack_kernel,
        in_specs=[ANY] + [VMEM] * 6,
        out_specs=VMEM,
        out_shape=jax.ShapeDtypeStruct((rows, own.shape[1]), BF16),
        compiler_params=params(4),
        name="unpack",
    )(done, placing, factor, own, *returned)


def regroup_kernel(after_ref, weights_ref, out_ref, sems):
    del after_ref
    copies = [
        pltpu.make_async_copy(weights_ref.at[:, t], out_ref.at[t], sems.at[t])
        for t in range(out_ref.shape[0])
    ]
    for copy in copies:
        copy.start()
    for copy in copies:
        copy.wait()


def regroup(behind, weights):
    depth, tiles, two, lanes = weights.shape
    grouped = pl.pallas_call(
        regroup_kernel,
        in_specs=[ANY, HBM],
        out_specs=VMEM,
        out_shape=pltpu.VMEM((tiles, depth, two, lanes), BF16),
        scratch_shapes=[pltpu.SemaphoreType.DMA((tiles,))],
        compiler_params=params(4),
        cost_estimate=cost(0, 4 * weights.size),
        name="regroup",
    )(behind, in_hbm(weights))
    return grouped.reshape(tiles, depth * two, lanes)


def fetch_kernel(after_ref, down_ref, out_ref, done_ref, sems):
    del after_ref
    parts = sems.shape[0]
    size = down_ref.shape[0] // parts
    copies = [
        pltpu.make_async_copy(
            down_ref.at[pl.ds(size * i, size)], out_ref.at[pl.ds(size * i, size)], sems.at[i]
        )
        for i in range(parts)
    ]
    for copy in copies:
        copy.start()
    done_ref[...] = jnp.zeros_like(done_ref)
    for copy in copies:
        copy.wait()


def fetch(behind, down):
    return pl.pallas_call(
        fetch_kernel,
        in_specs=[ANY, HBM],
        out_specs=[VMEM, VMEM],
        out_shape=[pltpu.VMEM(down.shape, BF16), pltpu.VMEM((8, 128), F32)],
        scratch_shapes=[pltpu.SemaphoreType.DMA((4,))],
        compiler_params=params(4),
        cost_estimate=cost(0, 4 * down.size),
        name="fetch_down",
    )(behind, in_hbm(down))


def widen_tokens(x_refs, wide_ref):
    slots, depth = x_refs[0].shape
    rows = 4 * slots
    here = lax.axis_index("col")
    cut = 256
    into = lax.broadcasted_iota(jnp.int32, (cut, 4 * cut), 1)
    out_of = lax.broadcasted_iota(jnp.int32, (cut, 4 * cut), 0)
    half = jnp.where(into < 2 * cut, 0, 1)
    widen = jnp.where(into - 2 * cut * half == 2 * out_of + half, 1.0, 0.0).astype(BF16)
    for slot, x_ref in enumerate(x_refs):
        stacked = jnp.concatenate(
            [x_ref[:, cut * k : cut * (k + 1)] for k in range(depth // cut)], axis=0
        )
        spaced = jnp.dot(stacked, widen, preferred_element_type=F32).astype(BF16)
        for h in range(2):
            at = pl.multiple_of(h * rows + (here ^ slot) * slots, slots)
            for k in range(depth // cut):
                wide_ref[pl.ds(at, slots), 2 * cut * k : 2 * cut * (k + 1)] = spaced[
                    slots * k : slots * (k + 1), 2 * cut * h : 2 * cut * (h + 1)
                ]


def preact_kernel(first, row_flip, chunk, chunks, *refs):
    if first:
        x0, x1, x2, x3, w_ref, out_ref, wide_ref = refs
        widen_tokens((x0, x1, x2, x3), wide_ref)
    else:
        wide_ref, w_ref, out_ref = refs
    tiles, _, lanes = w_ref.shape
    per = tiles // 4
    take = per // chunks
    at = []
    for i in range(2):
        quarter = quarter_of(1 - i, row_flip)
        at += [quarter * per + chunk * take + j for j in range(take)]
    for j in range(take):
        w = jnp.concatenate([w_ref[at[2 * j]], w_ref[at[2 * j + 1]]], axis=1)
        out_ref[:, 2 * lanes * j : 2 * lanes * (j + 1)] = jnp.dot(
            wide_ref[...], w, preferred_element_type=F32
        )


def preacts_of(lefts, weights, row_flip, chunk, chunks):
    tiles, depth2, lanes = weights.shape
    first = len(lefts) > 1
    rows = 4 * lefts[0].shape[0] if first else lefts[0].shape[0] // 2
    units = tiles // 4 // chunks * lanes
    out_shape = [jax.ShapeDtypeStruct((2 * rows, 2 * units), F32)]
    if first:
        out_shape.append(pltpu.VMEM((2 * rows, depth2), BF16))
    return pl.pallas_call(
        functools.partial(preact_kernel, first, row_flip, chunk, chunks),
        in_specs=[VMEM] * (len(lefts) + 1),
        out_specs=[VMEM] * len(out_shape),
        out_shape=out_shape,
        compiler_params=params(4),
        cost_estimate=cost(8 * rows * depth2 * units, 0),
        name="preacts_" + ("sent" if row_flip else "kept"),
    )(*lefts, in_vmem(weights))


def leave_kernel(kept_ref, got_ref, leaves_ref, stays_ref):
    units = stays_ref.shape[1]
    leaves_ref[...] = (kept_ref[:, :units] + got_ref[:, :units]).astype(BF16)
    stays_ref[...] = kept_ref[:, units:] + got_ref[:, units:]


def leave(kept, got):
    rows, units = kept.shape[0], kept.shape[1] // 2
    return pl.pallas_call(
        leave_kernel,
        in_specs=[VMEM] * 2,
        out_specs=[VMEM] * 2,
        out_shape=[
            jax.ShapeDtypeStruct((rows, units), BF16),
            jax.ShapeDtypeStruct((rows, units), F32),
        ],
        compiler_params=params(2),
        name="leave",
    )(kept, got)


def act_kernel(tick_ref, stays_ref, got_ref, *refs):
    del tick_ref
    out_ref = refs[-1]
    rows = out_ref.shape[0]
    done = out_ref.shape[1] - stays_ref.shape[1]
    if done:
        out_ref[:, :done] = refs[0][...]
    gate = stays_ref[:rows, :] + got_ref[:rows, :].astype(F32)
    up = stays_ref[rows:, :] + got_ref[rows:, :].astype(F32)
    out_ref[:, done:] = (jax.nn.silu(gate) * up).astype(BF16)


def act(tick, stays, got, *before):
    rows, units = stays.shape
    units += sum(x.shape[1] for x in before)
    return pl.pallas_call(
        act_kernel,
        in_specs=[ANY] + [VMEM] * (2 + len(before)),
        out_specs=VMEM,
        out_shape=jax.ShapeDtypeStruct((rows // 2, units), BF16),
        compiler_params=params(2),
        name="act",
    )(tick, stays, got, *before)


def is_near():
    return (lax.axis_index("col") // 2) == lax.axis_index("expert")


def is_odd():
    return (lax.axis_index("col") % 2) != lax.axis_index("row")


def choose_kernel(near_ref, far_ref, out_ref):
    @pl.when(is_near())
    def _():
        out_ref[...] = near_ref[...]

    @pl.when(jnp.logical_not(is_near()))
    def _():
        out_ref[...] = far_ref[...]


def choose(if_near, if_far):
    return pl.pallas_call(
        choose_kernel,
        in_specs=[VMEM] * 2,
        out_specs=VMEM,
        out_shape=jax.ShapeDtypeStruct(if_near.shape, if_near.dtype),
        compiler_params=params(2),
        name="choose",
    )(if_near, if_far)


def pick_kernel(n0, n1, f2, f3, mine_ref, other_ref):
    for near, pair in ((True, (n0, n1)), (False, (f2, f3))):
        for odd in (False, True):

            @pl.when((is_near() == near) & (is_odd() == odd))
            def _():
                mine_ref[...] = pair[int(odd)][...]
                other_ref[...] = pair[1 - int(odd)][...]


def pick(*slots):
    same = jax.ShapeDtypeStruct(slots[0].shape, slots[0].dtype)
    return pl.pallas_call(
        pick_kernel,
        in_specs=[VMEM] * 4,
        out_specs=[VMEM] * 2,
        out_shape=[same, same],
        compiler_params=params(2),
        name="pick",
    )(*slots)


def project_kernel(
    tick_ref, h0, h1, h2, h3, down_ref, own_ref, s1_ref, s2_ref, s3_ref, wide_ref, done_ref, total_ref
):
    del tick_ref
    units = h0.shape[1]
    for k, h_ref in enumerate((h0, h1, h2, h3)):
        at = pl.multiple_of(quarter_of(k % 2, k // 2) * units, units)
        wide_ref[:, pl.ds(at, units)] = h_ref[...]
    done_ref[...] = jnp.zeros_like(done_ref)
    slots, width = own_ref.shape
    cut = 512
    for n in range(width // cut):
        total_ref[:, cut * n : cut * (n + 1)] = jnp.dot(
            wide_ref[...], down_ref[:, cut * n : cut * (n + 1)], preferred_element_type=F32
        )
    here = lax.axis_index("col")
    for slot, out_ref in enumerate((own_ref, s1_ref, s2_ref, s3_ref)):
        at = pl.multiple_of((here ^ slot) * slots, slots)
        out_ref[...] = total_ref[pl.ds(at, slots), :].astype(out_ref.dtype)


def project(tick, quarters, down):
    rows, units = quarters[0].shape
    width = down.shape[1]
    slots = rows // 4
    return pl.pallas_call(
        project_kernel,
        in_specs=[ANY] + [VMEM] * 5,
        out_specs=[VMEM] * 6,
        out_shape=[jax.ShapeDtypeStruct((slots, width), F32)]
        + [jax.ShapeDtypeStruct((slots, width), BF16)] * 3
        + [pltpu.VMEM((rows, 4 * units), BF16), pltpu.VMEM((8, 128), F32)],
        scratch_shapes=[pltpu.VMEM((rows, width), F32)],
        compiler_params=params(4),
        cost_estimate=cost(8 * rows * units * width, 0),
        name="project",
    )(tick, *quarters, in_vmem(down))


def gram_kernel(scale, flips, *refs):
    count = len(flips)
    pieces = refs[1 : 1 + count]
    wide_ref = refs[1 + count]
    out_ref, done_ref, ring_ref, sems = refs[-4:]
    done_ref[...] = jnp.zeros_like(done_ref)
    units = pieces[0].shape[1]
    depth, _, cut = ring_ref.shape
    copies = []
    for (expert_flip, row_flip), a_ref in zip(flips, pieces):
        at = pl.multiple_of(quarter_of(expert_flip, row_flip) * units, units)
        left = a_ref[...].T
        for n in range(4 * units // cut):
            spot = len(copies) % depth
            if len(copies) >= depth:
                copies[-depth].wait()
            ring_ref[spot] = scale * jnp.dot(
                left, wide_ref[:, cut * n : cut * (n + 1)], preferred_element_type=F32
            )
            copy = pltpu.make_async_copy(
                ring_ref.at[spot], out_ref.at[pl.ds(at, units), pl.ds(cut * n, cut)], sems.at[spot]
            )
            copy.start()
            copies.append(copy)
    for copy in copies[-depth:]:
        copy.wait()


def gram_piece(tick, pieces, flips, wide, gram=None):
    rows, units = pieces[0].shape
    cut, depth = 512, 4
    operands = [tick, *pieces, in_vmem(wide)]
    in_specs = [ANY] + [VMEM] * (len(pieces) + 1)
    aliases = {}
    if gram is not None:
        aliases = {len(operands): 0}
        operands.append(gram)
        in_specs.append(HBM)
    return pl.pallas_call(
        functools.partial(gram_kernel, 2.0 / rows, flips),
        in_specs=in_specs,
        out_specs=[HBM, VMEM],
        out_shape=[
            jax.ShapeDtypeStruct((4 * units, 4 * units), F32),
            pltpu.VMEM((8, 128), F32),
        ],
        input_output_aliases=aliases,
        scratch_shapes=[
            pltpu.VMEM((depth, units, cut), F32),
            pltpu.SemaphoreType.DMA((depth,)),
        ],
        compiler_params=params(10),
        cost_estimate=cost(8 * rows * units * units * len(pieces), 16 * units * units * len(pieces)),
        name="gram",
    )(*operands)


def swap(value, axis):
    return lax.ppermute(value, axis, [(0, 1), (1, 0)])


def across(value, slot):
    return lax.ppermute(value, "col", [(i, i ^ slot) for i in range(4)])


def on_device(tokens, routes, route_weight, pad_mask, gate_up, down):
    depth = tokens.shape[1]
    units = gate_up.shape[2]
    lanes = 128
    chunks = 2
    weights = gate_up.reshape(depth, 2, units // lanes, lanes).transpose(0, 2, 1, 3)

    packed, placing, factor = pack(tokens, routes.T, pad_mask[None, :], route_weight.T)
    lefts = [packed] + [across(packed, slot) for slot in (1, 2, 3)]
    grouped = regroup(packed, weights)

    first_sent, wide = preacts_of(lefts, grouped, 1, 0, chunks)
    (last_sent,) = preacts_of([wide], grouped, 1, 1, chunks)
    got = [swap(first_sent, "row"), swap(last_sent, "row")]
    stays, got_x = [], []
    for h in range(chunks):
        (kept,) = preacts_of([wide], grouped, 0, h, chunks)
        leaves, stay = leave(kept, got[h])
        wide, leaves = tie(wide, leaves)
        stays.append(stay)
        got_x.append(swap(leaves, "expert"))
    down_held, tick = fetch(wide, down)
    tick, got_x[0] = tie(tick, got_x[0])
    hidden = act(tick, stays[0], got_x[0])
    tick, got_x[1], hidden = tie(tick, got_x[1], hidden)
    hidden = act(tick, stays[1], got_x[1], hidden)

    z2 = across(hidden, 2)
    z1 = across(hidden, 1)
    hidden_x = swap(hidden, "expert")
    c_near = swap(hidden, "row")
    tick, z2, z1, hidden_x = tie(tick, z2, z1, hidden_x)

    tick, onward, leaves, sent_x = tie(tick, z2, choose(z2, z1), hidden_x)
    z3 = across(onward, 1)
    x2 = swap(leaves, "expert")
    c_far = swap(sent_x, "row")
    own, s1, s2, s3, hidden_c, tick = project(
        tick, [hidden, hidden_x, c_near, c_far], down_held
    )
    tick, z3 = tie(tick, z3)
    x3 = lax.ppermute(
        z3,
        ("expert", "col"),
        [(ee * 4 + cc, (1 - ee) * 4 + cc) for ee in range(2) for cc in range(4) if cc // 2 == ee],
    )
    mine, passed = pick(hidden, z1, z2, z3)
    mine_near = swap(passed, "row")
    tick, s1, s2, s3 = tie(tick, s1, s2, s3)
    returned = [across(value, slot) for slot, value in ((1, s1), (2, s2), (3, s3))]
    gram, tick = gram_piece(tick, [mine], [(0, 0)], hidden_c)
    tick, x2, x3 = tie(tick, x2, x3)
    mine_x, passed = pick(hidden_x, x2, x2, x3)
    mine_far = swap(passed, "row")
    tick, mine_near = tie(tick, mine_near)
    gram, tick = gram_piece(tick, [mine_near], [(0, 1)], hidden_c, gram)
    tick, mine_far = tie(tick, mine_far)
    gram, tick = gram_piece(tick, [mine_x, mine_far], [(1, 0), (1, 1)], hidden_c, gram)
    return (unpack(tick, placing, factor, own, returned), gram)


def solution(mesh):
    in_specs = (
        P(("parts", "col"), ("expert", "row")),
        P(("parts", "col"), None),
        P(("parts", "col"), None),
        P(("parts", "col")),
        P(("expert", "row"), None, "col"),
        P("col", ("expert", "row")),
    )
    out_specs = (P(("parts", "col"), ("expert", "row")), P(("parts", "expert", "row"), "col"))
    small = mesh.shape["expert"] == 2 and mesh.shape["row"] == 2 and mesh.shape["col"] == 4
    return jax.shard_map(
        on_device if small else on_any_device,
        mesh=mesh,
        in_specs=in_specs,
        out_specs=out_specs,
        check_vma=False,
    )
```

```python
import functools

import jax
import jax.numpy as jnp
from jax import lax
from jax.experimental import pallas as pl
from jax.experimental.pallas import tpu as pltpu
from jax.sharding import PartitionSpec as P

F32 = jnp.float32
BF16 = jnp.bfloat16
MIB = 1 << 20


def spread(value, axis, source):
    kept = jnp.where(lax.axis_index(axis) == source, value, 0).astype(value.dtype)
    return lax.psum(kept, axis)


def activate(preacts):
    return (jax.nn.silu(preacts[:, 0, :]) * preacts[:, 1, :]).astype(jnp.bfloat16)


def on_any_device(tokens, routes, route_weight, pad_mask, gate_up, down):
    group_rows = tokens.shape[0]
    slot_count = group_rows // 4
    names_zero = routes == 0
    routed = jnp.any(names_zero, axis=1)
    live_rows = routed & (pad_mask == 1)
    factor = jnp.sum(
        jnp.where(names_zero, route_weight, jnp.float32(0.0)), axis=1
    ) * live_rows.astype(jnp.float32)
    position = jnp.cumsum(routed.astype(jnp.int32)) - 1
    slot_ids = lax.broadcasted_iota(jnp.int32, (slot_count, group_rows), 0)
    placing = ((position[None, :] == slot_ids) & routed[None, :]).astype(jnp.bfloat16)
    masked = tokens * live_rows.astype(jnp.bfloat16)[:, None]
    packed = jnp.dot(placing, masked, preferred_element_type=jnp.float32).astype(jnp.bfloat16)
    gathered = lax.all_gather(packed, "col", axis=0, tiled=True)
    anchor = lax.axis_index(("expert", "row"))
    preacts = lax.psum(
        jnp.einsum("rd,dgf->rgf", gathered, gate_up, preferred_element_type=jnp.float32),
        ("expert", "row"),
    )
    hidden = activate(preacts)
    mirrored = spread(hidden, "col", anchor)
    gram_block = lax.dot_general(
        mirrored, hidden, (((0,), (0,)), ((), ())), preferred_element_type=jnp.float32
    )
    gram_block = gram_block * jnp.float32(2.0 / hidden.shape[0])
    returned = lax.psum_scatter(
        jnp.dot(hidden, down, preferred_element_type=jnp.float32),
        "col",
        scatter_dimension=0,
        tiled=True,
    )
    unpacked = lax.dot_general(
        placing.astype(jnp.float32),
        returned,
        (((0,), (0,)), ((), ())),
        precision=lax.Precision.HIGHEST,
        preferred_element_type=jnp.float32,
    )
    expert_out = (unpacked * factor[:, None]).astype(jnp.bfloat16)
    return (expert_out, gram_block)


def cost(flops, moved):
    return pl.CostEstimate(flops=int(flops), bytes_accessed=int(moved), transcendentals=0)


def params(mib):
    return pltpu.CompilerParams(vmem_limit_bytes=mib * MIB)


VMEM = pl.BlockSpec(memory_space=pltpu.VMEM)
HBM = pl.BlockSpec(memory_space=pltpu.HBM)
SMEM = pl.BlockSpec(memory_space=pltpu.SMEM)
ANY = pl.BlockSpec(memory_space=pl.ANY)


def in_vmem(value):
    return pltpu.with_memory_space_constraint(value, pltpu.VMEM)


def in_hbm(value):
    return pltpu.with_memory_space_constraint(value, pltpu.HBM)


def quarter_of(expert_flip, row_flip):
    return (lax.axis_index("expert") ^ expert_flip) * 2 + (lax.axis_index("row") ^ row_flip)


def tie(*values):
    return lax.optimization_barrier(values)


def pack_kernel(
    tokens_ref, routes_ref, pad_ref, weight_ref, packed_ref, placing_ref, factor_ref,
    tokens_held, routes_held, pad_held, weight_held, sems,
):
    pairs = (
        (routes_ref, routes_held),
        (pad_ref, pad_held),
        (weight_ref, weight_held),
        (tokens_ref, tokens_held),
    )
    copies = [pltpu.make_async_copy(a, b, sems.at[i]) for i, (a, b) in enumerate(pairs)]
    for copy in copies:
        copy.start()
    slots, rows = placing_ref.shape
    before = lax.broadcasted_iota(jnp.int32, (rows, rows), 0)
    upto = lax.broadcasted_iota(jnp.int32, (rows, rows), 1)
    tri = jnp.where(before <= upto, 1.0, 0.0).astype(BF16)
    slot_ids = lax.broadcasted_iota(jnp.int32, (slots, rows), 0).astype(F32)
    for copy in copies[:3]:
        copy.wait()
    routes_t = routes_held[...]
    routed = (routes_t[0:1, :] == 0) | (routes_t[1:2, :] == 0)
    live = jnp.where(routed & (pad_held[...] == 1), 1.0, 0.0)
    routed_rows = jnp.broadcast_to(jnp.where(routed, 1.0, 0.0), (8, rows)).astype(BF16)
    position = jnp.dot(routed_rows, tri, preferred_element_type=F32)[0:1, :] - 1.0
    placing = jnp.where(position == slot_ids, jnp.broadcast_to(live, (slots, rows)), 0.0)
    placing_ref[...] = placing.astype(BF16)
    weight = jnp.sum(jnp.where(routes_t == 0, weight_held[...], 0.0), axis=0, keepdims=True)
    factor = jnp.sum(placing * weight, axis=1, keepdims=True)
    factor_ref[...] = jnp.broadcast_to(factor, factor_ref.shape)
    copies[3].wait()
    packed_ref[...] = jnp.dot(
        placing.astype(BF16), tokens_held[...], preferred_element_type=F32
    ).astype(BF16)


def pack(tokens, routes_t, pad, weight_t):
    rows, depth = tokens.shape
    slots = rows // 4
    operands = (tokens, routes_t, pad, weight_t)
    return pl.pallas_call(
        pack_kernel,
        in_specs=[HBM] * 4,
        out_specs=[VMEM] * 3,
        out_shape=[
            pltpu.VMEM((slots, depth), BF16),
            pltpu.VMEM((slots, rows), BF16),
            pltpu.VMEM((slots, 128), F32),
        ],
        scratch_shapes=[pltpu.VMEM(x.shape, x.dtype) for x in operands]
        + [pltpu.SemaphoreType.DMA((4,))],
        compiler_params=params(3),
        name="pack",
    )(*(in_hbm(x) for x in operands))


def unpack_kernel(after_ref, placing_ref, factor_ref, own_ref, r1_ref, r2_ref, r3_ref, out_ref):
    del after_ref
    total = own_ref[...] + r1_ref[...].astype(F32) + r2_ref[...].astype(F32) + r3_ref[...].astype(F32)
    scaled = (total * factor_ref[:, 0:1]).astype(BF16)
    out_ref[...] = lax.dot_general(
        placing_ref[...], scaled, (((0,), (0,)), ((), ())), preferred_element_type=F32
    ).astype(BF16)


def unpack(done, placing, factor, own, returned):
    slots, rows = placing.shape
    return pl.pallas_call(
        unpack_kernel,
        in_specs=[ANY] + [VMEM] * 6,
        out_specs=VMEM,
        out_shape=jax.ShapeDtypeStruct((rows, own.shape[1]), BF16),
        compiler_params=params(4),
        name="unpack",
    )(done, placing, factor, own, *returned)


def regroup_kernel(after_ref, weights_ref, out_ref, sems):
    del after_ref
    copies = [
        pltpu.make_async_copy(weights_ref.at[:, t], out_ref.at[t], sems.at[t])
        for t in range(out_ref.shape[0])
    ]
    for copy in copies:
        copy.start()
    for copy in copies:
        copy.wait()


def regroup(behind, weights):
    depth, tiles, two, lanes = weights.shape
    grouped = pl.pallas_call(
        regroup_kernel,
        in_specs=[ANY, HBM],
        out_specs=VMEM,
        out_shape=pltpu.VMEM((tiles, depth, two, lanes), BF16),
        scratch_shapes=[pltpu.SemaphoreType.DMA((tiles,))],
        compiler_params=params(4),
        cost_estimate=cost(0, 4 * weights.size),
        name="regroup",
    )(behind, in_hbm(weights))
    return grouped.reshape(tiles, depth * two, lanes)


def fetch_kernel(after_ref, down_ref, out_ref, done_ref, sems):
    del after_ref
    parts = sems.shape[0]
    size = down_ref.shape[0] // parts
    copies = [
        pltpu.make_async_copy(
            down_ref.at[pl.ds(size * i, size)], out_ref.at[pl.ds(size * i, size)], sems.at[i]
        )
        for i in range(parts)
    ]
    for copy in copies:
        copy.start()
    done_ref[...] = jnp.zeros_like(done_ref)
    for copy in copies:
        copy.wait()


def fetch(behind, down):
    return pl.pallas_call(
        fetch_kernel,
        in_specs=[ANY, HBM],
        out_specs=[VMEM, VMEM],
        out_shape=[pltpu.VMEM(down.shape, BF16), pltpu.VMEM((8, 128), F32)],
        scratch_shapes=[pltpu.SemaphoreType.DMA((4,))],
        compiler_params=params(4),
        cost_estimate=cost(0, 4 * down.size),
        name="fetch_down",
    )(behind, in_hbm(down))


def widen_tokens(x_refs, wide_ref):
    slots, depth = x_refs[0].shape
    rows = 4 * slots
    here = lax.axis_index("col")
    cut = 256
    into = lax.broadcasted_iota(jnp.int32, (cut, 4 * cut), 1)
    out_of = lax.broadcasted_iota(jnp.int32, (cut, 4 * cut), 0)
    half = jnp.where(into < 2 * cut, 0, 1)
    widen = jnp.where(into - 2 * cut * half == 2 * out_of + half, 1.0, 0.0).astype(BF16)
    for slot, x_ref in enumerate(x_refs):
        stacked = jnp.concatenate(
            [x_ref[:, cut * k : cut * (k + 1)] for k in range(depth // cut)], axis=0
        )
        spaced = jnp.dot(stacked, widen, preferred_element_type=F32).astype(BF16)
        for h in range(2):
            at = pl.multiple_of(h * rows + (here ^ slot) * slots, slots)
            for k in range(depth // cut):
                wide_ref[pl.ds(at, slots), 2 * cut * k : 2 * cut * (k + 1)] = spaced[
                    slots * k : slots * (k + 1), 2 * cut * h : 2 * cut * (h + 1)
                ]


def preact_kernel(first, row_flip, chunk, chunks, *refs):
    if first:
        x0, x1, x2, x3, w_ref, out_ref, wide_ref = refs
        widen_tokens((x0, x1, x2, x3), wide_ref)
    else:
        wide_ref, w_ref, out_ref = refs
    tiles, _, lanes = w_ref.shape
    per = tiles // 4
    take = per // chunks
    at = []
    for i in range(2):
        quarter = quarter_of(1 - i, row_flip)
        at += [quarter * per + chunk * take + j for j in range(take)]
    for j in range(take):
        w = jnp.concatenate([w_ref[at[2 * j]], w_ref[at[2 * j + 1]]], axis=1)
        out_ref[:, 2 * lanes * j : 2 * lanes * (j + 1)] = jnp.dot(
            wide_ref[...], w, preferred_element_type=F32
        )


def preacts_of(lefts, weights, row_flip, chunk, chunks):
    tiles, depth2, lanes = weights.shape
    first = len(lefts) > 1
    rows = 4 * lefts[0].shape[0] if first else lefts[0].shape[0] // 2
    units = tiles // 4 // chunks * lanes
    out_shape = [jax.ShapeDtypeStruct((2 * rows, 2 * units), F32)]
    if first:
        out_shape.append(pltpu.VMEM((2 * rows, depth2), BF16))
    return pl.pallas_call(
        functools.partial(preact_kernel, first, row_flip, chunk, chunks),
        in_specs=[VMEM] * (len(lefts) + 1),
        out_specs=[VMEM] * len(out_shape),
        out_shape=out_shape,
        compiler_params=params(4),
        cost_estimate=cost(8 * rows * depth2 * units, 0),
        name="preacts_" + ("sent" if row_flip else "kept"),
    )(*lefts, in_vmem(weights))


def leave_kernel(kept_ref, got_ref, leaves_ref, stays_ref):
    units = stays_ref.shape[1]
    leaves_ref[...] = (kept_ref[:, :units] + got_ref[:, :units]).astype(BF16)
    stays_ref[...] = kept_ref[:, units:] + got_ref[:, units:]


def leave(kept, got):
    rows, units = kept.shape[0], kept.shape[1] // 2
    return pl.pallas_call(
        leave_kernel,
        in_specs=[VMEM] * 2,
        out_specs=[VMEM] * 2,
        out_shape=[
            jax.ShapeDtypeStruct((rows, units), BF16),
            jax.ShapeDtypeStruct((rows, units), F32),
        ],
        compiler_params=params(2),
        name="leave",
    )(kept, got)


def act_kernel(tick_ref, stays_ref, got_ref, *refs):
    del tick_ref
    out_ref = refs[-1]
    rows = out_ref.shape[0]
    gate = stays_ref[:rows, :] + got_ref[:rows, :].astype(F32)
    up = stays_ref[rows:, :] + got_ref[rows:, :].astype(F32)
    hidden = (jax.nn.silu(gate) * up).astype(BF16)
    if len(refs) == 1:
        out_ref[...] = hidden
    else:
        before_ref, part_ref, _ = refs
        done = before_ref.shape[1]
        part_ref[...] = hidden
        out_ref[:, :done] = before_ref[...]
        out_ref[:, done:] = hidden


def act(tick, stays, got, *before):
    rows, units = stays.shape
    shapes = [(rows // 2, units)]
    if before:
        shapes.append((rows // 2, units + before[0].shape[1]))
    return pl.pallas_call(
        act_kernel,
        in_specs=[ANY] + [VMEM] * (2 + len(before)),
        out_specs=[VMEM] * len(shapes),
        out_shape=[jax.ShapeDtypeStruct(shape, BF16) for shape in shapes],
        compiler_params=params(2),
        name="act",
    )(tick, stays, got, *before)


def is_near():
    return (lax.axis_index("col") // 2) == lax.axis_index("expert")


def is_odd():
    return (lax.axis_index("col") % 2) != lax.axis_index("row")


def choose_kernel(n0, n1, far_ref, leaves_ref, joined_ref):
    units = n0.shape[1]
    joined_ref[:, :units] = n0[...]
    joined_ref[:, units:] = n1[...]

    @pl.when(is_near())
    def _():
        leaves_ref[:, :units] = n0[...]
        leaves_ref[:, units:] = n1[...]

    @pl.when(jnp.logical_not(is_near()))
    def _():
        leaves_ref[...] = far_ref[...]


def choose(near_parts, if_far):
    same = jax.ShapeDtypeStruct(if_far.shape, if_far.dtype)
    return pl.pallas_call(
        choose_kernel,
        in_specs=[VMEM] * 3,
        out_specs=[VMEM] * 2,
        out_shape=[same, same],
        compiler_params=params(2),
        name="choose",
    )(*near_parts, if_far)


def pick_kernel(n0, n1, f2, *refs):
    if len(refs) == 3:
        f3, mine_ref, other_ref = refs
    else:
        h0, h1, mine_ref, other_ref, f3 = refs
        units = h0.shape[1]
        f3[:, :units] = h0[...]
        f3[:, units:] = h1[...]
    for near, pair in ((True, (n0, n1)), (False, (f2, f3))):
        for odd in (False, True):

            @pl.when((is_near() == near) & (is_odd() == odd))
            def _():
                mine_ref[...] = pair[int(odd)][...]
                other_ref[...] = pair[1 - int(odd)][...]


def pick(*slots):
    same = jax.ShapeDtypeStruct(slots[0].shape, slots[0].dtype)
    return pl.pallas_call(
        pick_kernel,
        in_specs=[VMEM] * len(slots),
        out_specs=[VMEM] * (len(slots) - 2),
        out_shape=[same] * (len(slots) - 2),
        compiler_params=params(2),
        name="pick",
    )(*slots)


def project_kernel(
    tick_ref, h0, h1, h2, h3, down_ref, own_ref, s1_ref, s2_ref, s3_ref, wide_ref, done_ref, total_ref
):
    del tick_ref
    units = h0.shape[1]
    for k, h_ref in enumerate((h0, h1, h2, h3)):
        at = pl.multiple_of(quarter_of(k % 2, k // 2) * units, units)
        wide_ref[:, pl.ds(at, units)] = h_ref[...]
    done_ref[...] = jnp.zeros_like(done_ref)
    slots, width = own_ref.shape
    cut = 512
    for n in range(width // cut):
        total_ref[:, cut * n : cut * (n + 1)] = jnp.dot(
            wide_ref[...], down_ref[:, cut * n : cut * (n + 1)], preferred_element_type=F32
        )
    here = lax.axis_index("col")
    for slot, out_ref in enumerate((own_ref, s1_ref, s2_ref, s3_ref)):
        at = pl.multiple_of((here ^ slot) * slots, slots)
        out_ref[...] = total_ref[pl.ds(at, slots), :].astype(out_ref.dtype)


def project(tick, quarters, down):
    rows, units = quarters[0].shape
    width = down.shape[1]
    slots = rows // 4
    return pl.pallas_call(
        project_kernel,
        in_specs=[ANY] + [VMEM] * 5,
        out_specs=[VMEM] * 6,
        out_shape=[jax.ShapeDtypeStruct((slots, width), F32)]
        + [jax.ShapeDtypeStruct((slots, width), BF16)] * 3
        + [pltpu.VMEM((rows, 4 * units), BF16), pltpu.VMEM((8, 128), F32)],
        scratch_shapes=[pltpu.VMEM((rows, width), F32)],
        compiler_params=params(4),
        cost_estimate=cost(8 * rows * units * width, 0),
        name="project",
    )(tick, *quarters, in_vmem(down))


def gram_kernel(scale, flips, *refs):
    count = len(flips)
    pieces = refs[1 : 1 + count]
    wide_ref = refs[1 + count]
    out_ref, done_ref, ring_ref, sems = refs[-4:]
    done_ref[...] = jnp.zeros_like(done_ref)
    units = pieces[0].shape[1]
    depth, _, cut = ring_ref.shape
    copies = []
    for (expert_flip, row_flip), a_ref in zip(flips, pieces):
        at = pl.multiple_of(quarter_of(expert_flip, row_flip) * units, units)
        left = a_ref[...].T
        for n in range(4 * units // cut):
            spot = len(copies) % depth
            if len(copies) >= depth:
                copies[-depth].wait()
            ring_ref[spot] = scale * jnp.dot(
                left, wide_ref[:, cut * n : cut * (n + 1)], preferred_element_type=F32
            )
            copy = pltpu.make_async_copy(
                ring_ref.at[spot], out_ref.at[pl.ds(at, units), pl.ds(cut * n, cut)], sems.at[spot]
            )
            copy.start()
            copies.append(copy)
    for copy in copies[-depth:]:
        copy.wait()


def gram_piece(tick, pieces, flips, wide, gram=None):
    rows, units = pieces[0].shape
    cut, depth = 256, 8
    operands = [tick, *pieces, in_vmem(wide)]
    in_specs = [ANY] + [VMEM] * (len(pieces) + 1)
    aliases = {}
    if gram is not None:
        aliases = {len(operands): 0}
        operands.append(gram)
        in_specs.append(HBM)
    return pl.pallas_call(
        functools.partial(gram_kernel, 2.0 / rows, flips),
        in_specs=in_specs,
        out_specs=[HBM, VMEM],
        out_shape=[
            jax.ShapeDtypeStruct((4 * units, 4 * units), F32),
            pltpu.VMEM((8, 128), F32),
        ],
        input_output_aliases=aliases,
        scratch_shapes=[
            pltpu.VMEM((depth, units, cut), F32),
            pltpu.SemaphoreType.DMA((depth,)),
        ],
        compiler_params=params(10),
        cost_estimate=cost(8 * rows * units * units * len(pieces), 16 * units * units * len(pieces)),
        name="gram",
    )(*operands)


def swap(value, axis):
    return lax.ppermute(value, axis, [(0, 1), (1, 0)])


def across(value, slot):
    return lax.ppermute(value, "col", [(i, i ^ slot) for i in range(4)])


def on_device(tokens, routes, route_weight, pad_mask, gate_up, down):
    depth = tokens.shape[1]
    units = gate_up.shape[2]
    lanes = 128
    chunks = 2
    weights = gate_up.reshape(depth, 2, units // lanes, lanes).transpose(0, 2, 1, 3)

    packed, placing, factor = pack(tokens, routes.T, pad_mask[None, :], route_weight.T)
    lefts = [packed] + [across(packed, slot) for slot in (1, 2, 3)]
    grouped = regroup(packed, weights)

    first_sent, wide = preacts_of(lefts, grouped, 1, 0, chunks)
    (last_sent,) = preacts_of([wide], grouped, 1, 1, chunks)
    got = [swap(first_sent, "row"), swap(last_sent, "row")]
    stays, got_x = [], []
    for h in range(chunks):
        (kept,) = preacts_of([wide], grouped, 0, h, chunks)
        leaves, stay = leave(kept, got[h])
        wide, leaves = tie(wide, leaves)
        stays.append(stay)
        got_x.append(swap(leaves, "expert"))
    down_held, tick = fetch(wide, down)
    tick, got_x[0] = tie(tick, got_x[0])
    (hidden_a,) = act(tick, stays[0], got_x[0])

    z2a = across(hidden_a, 2)
    tick, got_x[1], hidden_a = tie(tick, got_x[1], hidden_a)
    hidden_b, hidden = act(tick, stays[1], got_x[1], hidden_a)
    z1 = across(hidden, 1)
    hidden_x = swap(hidden, "expert")
    c_near = swap(hidden, "row")
    tick, z2a, hidden_b = tie(tick, z2a, hidden_b)
    z2b = across(hidden_b, 2)
    z3a = across(z2a, 1)
    tick, z2b, z1, hidden_x, z3a = tie(tick, z2b, z1, hidden_x, z3a)

    leaves, z2 = choose((z2a, z2b), z1)
    tick, z2b, leaves, sent_x = tie(tick, z2b, leaves, hidden_x)
    z3b = across(z2b, 1)
    x2 = swap(leaves, "expert")
    c_far = swap(sent_x, "row")
    own, s1, s2, s3, hidden_c, tick = project(
        tick, [hidden, hidden_x, c_near, c_far], down_held
    )
    returned = [across(value, slot) for slot, value in ((1, s1), (2, s2), (3, s3))]
    tick, z3b = tie(tick, z3b)
    mine, passed, z3 = pick(hidden, z1, z2, z3a, z3b)
    x3 = lax.ppermute(
        z3,
        ("expert", "col"),
        [(ee * 4 + cc, (1 - ee) * 4 + cc) for ee in range(2) for cc in range(4) if cc // 2 == ee],
    )
    mine_near = swap(passed, "row")
    gram, tick = gram_piece(tick, [mine], [(0, 0)], hidden_c)
    tick, x2, x3 = tie(tick, x2, x3)
    mine_x, passed = pick(hidden_x, x2, x2, x3)
    mine_far = swap(passed, "row")
    tick, mine_near = tie(tick, mine_near)
    gram, tick = gram_piece(tick, [mine_near], [(0, 1)], hidden_c, gram)
    tick, mine_far = tie(tick, mine_far)
    gram, tick = gram_piece(tick, [mine_x, mine_far], [(1, 0), (1, 1)], hidden_c, gram)
    return (unpack(tick, placing, factor, own, returned), gram)


def solution(mesh):
    in_specs = (
        P(("parts", "col"), ("expert", "row")),
        P(("parts", "col"), None),
        P(("parts", "col"), None),
        P(("parts", "col")),
        P(("expert", "row"), None, "col"),
        P("col", ("expert", "row")),
    )
    out_specs = (P(("parts", "col"), ("expert", "row")), P(("parts", "expert", "row"), "col"))
    small = mesh.shape["expert"] == 2 and mesh.shape["row"] == 2 and mesh.shape["col"] == 4
    return jax.shard_map(
        on_device if small else on_any_device,
        mesh=mesh,
        in_specs=in_specs,
        out_specs=out_specs,
        check_vma=False,
    )
```

```python
import functools

import jax
import jax.numpy as jnp
from jax import lax
from jax.experimental import pallas as pl
from jax.experimental.pallas import tpu as pltpu
from jax.sharding import PartitionSpec as P

F32 = jnp.float32
BF16 = jnp.bfloat16
MIB = 1 << 20


def spread(value, axis, source):
    kept = jnp.where(lax.axis_index(axis) == source, value, 0).astype(value.dtype)
    return lax.psum(kept, axis)


def activate(preacts):
    return (jax.nn.silu(preacts[:, 0, :]) * preacts[:, 1, :]).astype(jnp.bfloat16)


def on_any_device(tokens, routes, route_weight, pad_mask, gate_up, down):
    group_rows = tokens.shape[0]
    slot_count = group_rows // 4
    names_zero = routes == 0
    routed = jnp.any(names_zero, axis=1)
    live_rows = routed & (pad_mask == 1)
    factor = jnp.sum(
        jnp.where(names_zero, route_weight, jnp.float32(0.0)), axis=1
    ) * live_rows.astype(jnp.float32)
    position = jnp.cumsum(routed.astype(jnp.int32)) - 1
    slot_ids = lax.broadcasted_iota(jnp.int32, (slot_count, group_rows), 0)
    placing = ((position[None, :] == slot_ids) & routed[None, :]).astype(jnp.bfloat16)
    masked = tokens * live_rows.astype(jnp.bfloat16)[:, None]
    packed = jnp.dot(placing, masked, preferred_element_type=jnp.float32).astype(jnp.bfloat16)
    gathered = lax.all_gather(packed, "col", axis=0, tiled=True)
    anchor = lax.axis_index(("expert", "row"))
    preacts = lax.psum(
        jnp.einsum("rd,dgf->rgf", gathered, gate_up, preferred_element_type=jnp.float32),
        ("expert", "row"),
    )
    hidden = activate(preacts)
    mirrored = spread(hidden, "col", anchor)
    gram_block = lax.dot_general(
        mirrored, hidden, (((0,), (0,)), ((), ())), preferred_element_type=jnp.float32
    )
    gram_block = gram_block * jnp.float32(2.0 / hidden.shape[0])
    returned = lax.psum_scatter(
        jnp.dot(hidden, down, preferred_element_type=jnp.float32),
        "col",
        scatter_dimension=0,
        tiled=True,
    )
    unpacked = lax.dot_general(
        placing.astype(jnp.float32),
        returned,
        (((0,), (0,)), ((), ())),
        precision=lax.Precision.HIGHEST,
        preferred_element_type=jnp.float32,
    )
    expert_out = (unpacked * factor[:, None]).astype(jnp.bfloat16)
    return (expert_out, gram_block)


def cost(flops, moved):
    return pl.CostEstimate(flops=int(flops), bytes_accessed=int(moved), transcendentals=0)


def params(mib):
    return pltpu.CompilerParams(vmem_limit_bytes=mib * MIB)


VMEM = pl.BlockSpec(memory_space=pltpu.VMEM)
HBM = pl.BlockSpec(memory_space=pltpu.HBM)
SMEM = pl.BlockSpec(memory_space=pltpu.SMEM)
ANY = pl.BlockSpec(memory_space=pl.ANY)


def in_vmem(value):
    return pltpu.with_memory_space_constraint(value, pltpu.VMEM)


def in_hbm(value):
    return pltpu.with_memory_space_constraint(value, pltpu.HBM)


def quarter_of(expert_flip, row_flip):
    return (lax.axis_index("expert") ^ expert_flip) * 2 + (lax.axis_index("row") ^ row_flip)


def tie(*values):
    return lax.optimization_barrier(values)


def pack_kernel(
    tokens_ref, routes_ref, pad_ref, weight_ref, packed_ref, placing_ref, factor_ref,
    tokens_held, routes_held, pad_held, weight_held, sems,
):
    pairs = (
        (routes_ref, routes_held),
        (pad_ref, pad_held),
        (weight_ref, weight_held),
        (tokens_ref, tokens_held),
    )
    copies = [pltpu.make_async_copy(a, b, sems.at[i]) for i, (a, b) in enumerate(pairs)]
    for copy in copies:
        copy.start()
    slots, rows = placing_ref.shape
    before = lax.broadcasted_iota(jnp.int32, (rows, rows), 0)
    upto = lax.broadcasted_iota(jnp.int32, (rows, rows), 1)
    tri = jnp.where(before <= upto, 1.0, 0.0).astype(BF16)
    slot_ids = lax.broadcasted_iota(jnp.int32, (slots, rows), 0).astype(F32)
    for copy in copies[:3]:
        copy.wait()
    routes_t = routes_held[...]
    routed = (routes_t[0:1, :] == 0) | (routes_t[1:2, :] == 0)
    live = jnp.where(routed & (pad_held[...] == 1), 1.0, 0.0)
    routed_rows = jnp.broadcast_to(jnp.where(routed, 1.0, 0.0), (8, rows)).astype(BF16)
    position = jnp.dot(routed_rows, tri, preferred_element_type=F32)[0:1, :] - 1.0
    placing = jnp.where(position == slot_ids, jnp.broadcast_to(live, (slots, rows)), 0.0)
    placing_ref[...] = placing.astype(BF16)
    weight = jnp.sum(jnp.where(routes_t == 0, weight_held[...], 0.0), axis=0, keepdims=True)
    factor = jnp.sum(placing * weight, axis=1, keepdims=True)
    factor_ref[...] = jnp.broadcast_to(factor, factor_ref.shape)
    copies[3].wait()
    packed_ref[...] = jnp.dot(
        placing.astype(BF16), tokens_held[...], preferred_element_type=F32
    ).astype(BF16)


def pack(tokens, routes_t, pad, weight_t):
    rows, depth = tokens.shape
    slots = rows // 4
    operands = (tokens, routes_t, pad, weight_t)
    return pl.pallas_call(
        pack_kernel,
        in_specs=[HBM] * 4,
        out_specs=[VMEM] * 3,
        out_shape=[
            pltpu.VMEM((slots, depth), BF16),
            pltpu.VMEM((slots, rows), BF16),
            pltpu.VMEM((slots, 128), F32),
        ],
        scratch_shapes=[pltpu.VMEM(x.shape, x.dtype) for x in operands]
        + [pltpu.SemaphoreType.DMA((4,))],
        compiler_params=params(3),
        name="pack",
    )(*(in_hbm(x) for x in operands))


def unpack_kernel(after_ref, placing_ref, factor_ref, own_ref, r1_ref, r2_ref, r3_ref, out_ref):
    del after_ref
    total = own_ref[...] + r1_ref[...].astype(F32) + r2_ref[...].astype(F32) + r3_ref[...].astype(F32)
    scaled = (total * factor_ref[:, 0:1]).astype(BF16)
    out_ref[...] = lax.dot_general(
        placing_ref[...], scaled, (((0,), (0,)), ((), ())), preferred_element_type=F32
    ).astype(BF16)


def unpack(done, placing, factor, own, returned):
    slots, rows = placing.shape
    return pl.pallas_call(
        unpack_kernel,
        in_specs=[ANY] + [VMEM] * 6,
        out_specs=VMEM,
        out_shape=jax.ShapeDtypeStruct((rows, own.shape[1]), BF16),
        compiler_params=params(4),
        name="unpack",
    )(done, placing, factor, own, *returned)


def regroup_kernel(row_flip, after_ref, weights_ref, out_ref, done_ref, sems):
    del after_ref
    per = out_ref.shape[0] // 2
    copies = []
    for i in range(2):
        start = quarter_of(1 - i, row_flip) * per
        for t in range(per):
            copies.append(
                pltpu.make_async_copy(
                    weights_ref.at[:, start + t], out_ref.at[per * i + t], sems.at[per * i + t]
                )
            )
    for copy in copies:
        copy.start()
    done_ref[...] = jnp.zeros_like(done_ref)
    for copy in copies:
        copy.wait()


def regroup(behind, weights, row_flip):
    depth, tiles, two, lanes = weights.shape
    grouped, done = pl.pallas_call(
        functools.partial(regroup_kernel, row_flip),
        in_specs=[ANY, HBM],
        out_specs=[VMEM] * 2,
        out_shape=[
            pltpu.VMEM((tiles // 2, depth, two, lanes), BF16),
            pltpu.VMEM((8, 128), F32),
        ],
        scratch_shapes=[pltpu.SemaphoreType.DMA((tiles // 2,))],
        compiler_params=params(2),
        cost_estimate=cost(0, 2 * weights.size),
        name="regroup",
    )(behind, in_hbm(weights))
    return grouped.reshape(tiles // 2, depth * two, lanes), done


def fetch_kernel(after_ref, down_ref, out_ref, done_ref, sems):
    del after_ref
    parts = sems.shape[0]
    size = down_ref.shape[0] // parts
    copies = [
        pltpu.make_async_copy(
            down_ref.at[pl.ds(size * i, size)], out_ref.at[pl.ds(size * i, size)], sems.at[i]
        )
        for i in range(parts)
    ]
    for copy in copies:
        copy.start()
    done_ref[...] = jnp.zeros_like(done_ref)
    for copy in copies:
        copy.wait()


def fetch(behind, down):
    return pl.pallas_call(
        fetch_kernel,
        in_specs=[ANY, HBM],
        out_specs=[VMEM, VMEM],
        out_shape=[pltpu.VMEM(down.shape, BF16), pltpu.VMEM((8, 128), F32)],
        scratch_shapes=[pltpu.SemaphoreType.DMA((4,))],
        compiler_params=params(4),
        cost_estimate=cost(0, 4 * down.size),
        name="fetch_down",
    )(behind, in_hbm(down))


def widen_tokens(x_refs, wide_ref):
    slots, depth = x_refs[0].shape
    rows = 4 * slots
    here = lax.axis_index("col")
    cut = 256
    into = lax.broadcasted_iota(jnp.int32, (cut, 4 * cut), 1)
    out_of = lax.broadcasted_iota(jnp.int32, (cut, 4 * cut), 0)
    half = jnp.where(into < 2 * cut, 0, 1)
    widen = jnp.where(into - 2 * cut * half == 2 * out_of + half, 1.0, 0.0).astype(BF16)
    for slot, x_ref in enumerate(x_refs):
        stacked = jnp.concatenate(
            [x_ref[:, cut * k : cut * (k + 1)] for k in range(depth // cut)], axis=0
        )
        spaced = jnp.dot(stacked, widen, preferred_element_type=F32).astype(BF16)
        for h in range(2):
            at = pl.multiple_of(h * rows + (here ^ slot) * slots, slots)
            for k in range(depth // cut):
                wide_ref[pl.ds(at, slots), 2 * cut * k : 2 * cut * (k + 1)] = spaced[
                    slots * k : slots * (k + 1), 2 * cut * h : 2 * cut * (h + 1)
                ]


def preact_kernel(first, chunk, chunks, *refs):
    if first:
        x0, x1, x2, x3, w_ref, out_ref, wide_ref = refs
        widen_tokens((x0, x1, x2, x3), wide_ref)
    else:
        wide_ref, w_ref, out_ref = refs
    tiles, _, lanes = w_ref.shape
    per = tiles // 2
    take = per // chunks
    at = [i * per + chunk * take + j for i in range(2) for j in range(take)]
    for j in range(take):
        w = jnp.concatenate([w_ref[at[2 * j]], w_ref[at[2 * j + 1]]], axis=1)
        out_ref[:, 2 * lanes * j : 2 * lanes * (j + 1)] = jnp.dot(
            wide_ref[...], w, preferred_element_type=F32
        )


def preacts_of(lefts, weights, chunk, chunks):
    tiles, depth2, lanes = weights.shape
    first = len(lefts) > 1
    rows = 4 * lefts[0].shape[0] if first else lefts[0].shape[0] // 2
    units = tiles // 2 // chunks * lanes
    out_shape = [jax.ShapeDtypeStruct((2 * rows, 2 * units), F32)]
    if first:
        out_shape.append(pltpu.VMEM((2 * rows, depth2), BF16))
    return pl.pallas_call(
        functools.partial(preact_kernel, first, chunk, chunks),
        in_specs=[VMEM] * (len(lefts) + 1),
        out_specs=[VMEM] * len(out_shape),
        out_shape=out_shape,
        compiler_params=params(4),
        cost_estimate=cost(8 * rows * depth2 * units, 0),
        name="preacts",
    )(*lefts, in_vmem(weights))


def leave_kernel(kept_ref, got_ref, leaves_ref, stays_ref):
    units = stays_ref.shape[1]
    leaves_ref[...] = (kept_ref[:, :units] + got_ref[:, :units]).astype(BF16)
    stays_ref[...] = kept_ref[:, units:] + got_ref[:, units:]


def leave(kept, got):
    rows, units = kept.shape[0], kept.shape[1] // 2
    return pl.pallas_call(
        leave_kernel,
        in_specs=[VMEM] * 2,
        out_specs=[VMEM] * 2,
        out_shape=[
            jax.ShapeDtypeStruct((rows, units), BF16),
            jax.ShapeDtypeStruct((rows, units), F32),
        ],
        compiler_params=params(2),
        name="leave",
    )(kept, got)


def act_kernel(tick_ref, stays_ref, got_ref, *refs):
    del tick_ref
    out_ref = refs[-1]
    rows = out_ref.shape[0]
    gate = stays_ref[:rows, :] + got_ref[:rows, :].astype(F32)
    up = stays_ref[rows:, :] + got_ref[rows:, :].astype(F32)
    hidden = (jax.nn.silu(gate) * up).astype(BF16)
    if len(refs) == 1:
        out_ref[...] = hidden
    else:
        before_ref, part_ref, _ = refs
        done = before_ref.shape[1]
        part_ref[...] = hidden
        out_ref[:, :done] = before_ref[...]
        out_ref[:, done:] = hidden


def act(tick, stays, got, *before):
    rows, units = stays.shape
    shapes = [(rows // 2, units)]
    if before:
        shapes.append((rows // 2, units + before[0].shape[1]))
    return pl.pallas_call(
        act_kernel,
        in_specs=[ANY] + [VMEM] * (2 + len(before)),
        out_specs=[VMEM] * len(shapes),
        out_shape=[jax.ShapeDtypeStruct(shape, BF16) for shape in shapes],
        compiler_params=params(2),
        name="act",
    )(tick, stays, got, *before)


def is_near():
    return (lax.axis_index("col") // 2) == lax.axis_index("expert")


def is_odd():
    return (lax.axis_index("col") % 2) != lax.axis_index("row")


def choose_kernel(n0, n1, far_ref, leaves_ref, joined_ref):
    units = n0.shape[1]
    joined_ref[:, :units] = n0[...]
    joined_ref[:, units:] = n1[...]

    @pl.when(is_near())
    def _():
        leaves_ref[:, :units] = n0[...]
        leaves_ref[:, units:] = n1[...]

    @pl.when(jnp.logical_not(is_near()))
    def _():
        leaves_ref[...] = far_ref[...]


def choose(near_parts, if_far):
    same = jax.ShapeDtypeStruct(if_far.shape, if_far.dtype)
    return pl.pallas_call(
        choose_kernel,
        in_specs=[VMEM] * 3,
        out_specs=[VMEM] * 2,
        out_shape=[same, same],
        compiler_params=params(2),
        name="choose",
    )(*near_parts, if_far)


def pick_kernel(n0, n1, f2, *refs):
    if len(refs) == 3:
        f3, mine_ref, other_ref = refs
    else:
        h0, h1, mine_ref, other_ref, f3 = refs
        units = h0.shape[1]
        f3[:, :units] = h0[...]
        f3[:, units:] = h1[...]
    for near, pair in ((True, (n0, n1)), (False, (f2, f3))):
        for odd in (False, True):

            @pl.when((is_near() == near) & (is_odd() == odd))
            def _():
                mine_ref[...] = pair[int(odd)][...]
                other_ref[...] = pair[1 - int(odd)][...]


def pick(*slots):
    same = jax.ShapeDtypeStruct(slots[0].shape, slots[0].dtype)
    return pl.pallas_call(
        pick_kernel,
        in_specs=[VMEM] * len(slots),
        out_specs=[VMEM] * (len(slots) - 2),
        out_shape=[same] * (len(slots) - 2),
        compiler_params=params(2),
        name="pick",
    )(*slots)


def join_kernel(left_ref, right_ref, out_ref):
    units = left_ref.shape[1]
    out_ref[:, :units] = left_ref[...]
    out_ref[:, units:] = right_ref[...]


def join(left, right):
    rows, units = left.shape
    return pl.pallas_call(
        join_kernel,
        in_specs=[VMEM] * 2,
        out_specs=VMEM,
        out_shape=jax.ShapeDtypeStruct((rows, 2 * units), left.dtype),
        compiler_params=params(2),
        name="join",
    )(left, right)


def project_kernel(
    tick_ref, here_ref, there_ref, down_ref, own_ref, s1_ref, s2_ref, s3_ref, wide_ref, done_ref, total_ref
):
    del tick_ref
    units = here_ref.shape[1] // 2
    for row_flip, pair_ref in enumerate((here_ref, there_ref)):
        for expert_flip in range(2):
            at = pl.multiple_of(quarter_of(expert_flip, row_flip) * units, units)
            wide_ref[:, pl.ds(at, units)] = pair_ref[:, units * expert_flip : units * (expert_flip + 1)]
    done_ref[...] = jnp.zeros_like(done_ref)
    slots, width = own_ref.shape
    cut = 512
    for n in range(width // cut):
        total_ref[:, cut * n : cut * (n + 1)] = jnp.dot(
            wide_ref[...], down_ref[:, cut * n : cut * (n + 1)], preferred_element_type=F32
        )
    here = lax.axis_index("col")
    for slot, out_ref in enumerate((own_ref, s1_ref, s2_ref, s3_ref)):
        at = pl.multiple_of((here ^ slot) * slots, slots)
        out_ref[...] = total_ref[pl.ds(at, slots), :].astype(out_ref.dtype)


def project(tick, here, there, down):
    rows, units = here.shape[0], here.shape[1] // 2
    width = down.shape[1]
    slots = rows // 4
    return pl.pallas_call(
        project_kernel,
        in_specs=[ANY] + [VMEM] * 3,
        out_specs=[VMEM] * 6,
        out_shape=[jax.ShapeDtypeStruct((slots, width), F32)]
        + [jax.ShapeDtypeStruct((slots, width), BF16)] * 3
        + [pltpu.VMEM((rows, 4 * units), BF16), pltpu.VMEM((8, 128), F32)],
        scratch_shapes=[pltpu.VMEM((rows, width), F32)],
        compiler_params=params(4),
        cost_estimate=cost(8 * rows * units * width, 0),
        name="project",
    )(tick, here, there, in_vmem(down))


def gram_kernel(scale, flips, *refs):
    count = len(flips)
    pieces = refs[1 : 1 + count]
    wide_ref = refs[1 + count]
    out_ref, done_ref, ring_ref, sems = refs[-4:]
    done_ref[...] = jnp.zeros_like(done_ref)
    units = pieces[0].shape[1]
    depth, _, cut = ring_ref.shape
    copies = []
    for (expert_flip, row_flip), a_ref in zip(flips, pieces):
        at = pl.multiple_of(quarter_of(expert_flip, row_flip) * units, units)
        left = a_ref[...].T
        for n in range(4 * units // cut):
            spot = len(copies) % depth
            if len(copies) >= depth:
                copies[-depth].wait()
            ring_ref[spot] = scale * jnp.dot(
                left, wide_ref[:, cut * n : cut * (n + 1)], preferred_element_type=F32
            )
            copy = pltpu.make_async_copy(
                ring_ref.at[spot], out_ref.at[pl.ds(at, units), pl.ds(cut * n, cut)], sems.at[spot]
            )
            copy.start()
            copies.append(copy)
    for copy in copies[-depth:]:
        copy.wait()


def gram_piece(tick, pieces, flips, wide, gram=None):
    rows, units = pieces[0].shape
    cut, depth = 512, 4
    operands = [tick, *pieces, in_vmem(wide)]
    in_specs = [ANY] + [VMEM] * (len(pieces) + 1)
    aliases = {}
    if gram is not None:
        aliases = {len(operands): 0}
        operands.append(gram)
        in_specs.append(HBM)
    return pl.pallas_call(
        functools.partial(gram_kernel, 2.0 / rows, flips),
        in_specs=in_specs,
        out_specs=[HBM, VMEM],
        out_shape=[
            jax.ShapeDtypeStruct((4 * units, 4 * units), F32),
            pltpu.VMEM((8, 128), F32),
        ],
        input_output_aliases=aliases,
        scratch_shapes=[
            pltpu.VMEM((depth, units, cut), F32),
            pltpu.SemaphoreType.DMA((depth,)),
        ],
        compiler_params=params(10),
        cost_estimate=cost(8 * rows * units * units * len(pieces), 16 * units * units * len(pieces)),
        name="gram",
    )(*operands)


def swap(value, axis):
    return lax.ppermute(value, axis, [(0, 1), (1, 0)])


def across(value, slot):
    return lax.ppermute(value, "col", [(i, i ^ slot) for i in range(4)])


def on_device(tokens, routes, route_weight, pad_mask, gate_up, down):
    depth = tokens.shape[1]
    units = gate_up.shape[2]
    lanes = 128
    chunks = 2
    weights = gate_up.reshape(depth, 2, units // lanes, lanes).transpose(0, 2, 1, 3)

    packed, placing, factor = pack(tokens, routes.T, pad_mask[None, :], route_weight.T)
    t2 = across(packed, 2)
    t1 = across(packed, 1)
    sent_weights, tick = regroup(packed, weights, 1)
    tick, t2 = tie(tick, t2)
    t3 = across(t2, 1)
    kept_weights, tick = regroup(tick, weights, 0)
    t1, t3, kept_weights = tie(t1, t3, kept_weights)

    first_sent, wide = preacts_of([packed, t1, t2, t3], sent_weights, 0, chunks)
    (last_sent,) = preacts_of([wide], sent_weights, 1, chunks)
    got = [swap(first_sent, "row"), swap(last_sent, "row")]
    stays, got_x = [], []
    for h in range(chunks):
        (kept,) = preacts_of([wide], kept_weights, h, chunks)
        leaves, stay = leave(kept, got[h])
        wide, leaves = tie(wide, leaves)
        stays.append(stay)
        got_x.append(swap(leaves, "expert"))
    down_held, tick = fetch(wide, down)
    tick, got_x[0] = tie(tick, got_x[0])
    (hidden_a,) = act(tick, stays[0], got_x[0])

    z2a = across(hidden_a, 2)
    tick, got_x[1], hidden_a = tie(tick, got_x[1], hidden_a)
    hidden_b, hidden = act(tick, stays[1], got_x[1], hidden_a)
    z2b = across(hidden_b, 2)
    hidden_x = swap(hidden, "expert")
    tick, z2a, leaves = tie(tick, z2a, hidden)
    z3a = across(z2a, 1)
    z1 = across(leaves, 1)
    tick, z2b, z1, hidden_x, z3a = tie(tick, z2b, z1, hidden_x, z3a)

    leaves, z2 = choose((z2a, z2b), z1)
    here = join(hidden, hidden_x)
    tick, z2b, leaves, here = tie(tick, z2b, leaves, here)
    z3b = across(z2b, 1)
    x2 = swap(leaves, "expert")
    there = swap(here, "row")
    tick, there = tie(tick, there)
    own, s1, s2, s3, hidden_c, tick = project(tick, here, there, down_held)
    tick, z3b, s3 = tie(tick, z3b, s3)
    mine, passed, z3 = pick(hidden, z1, z2, z3a, z3b)
    x3 = lax.ppermute(
        z3,
        ("expert", "col"),
        [(ee * 4 + cc, (1 - ee) * 4 + cc) for ee in range(2) for cc in range(4) if cc // 2 == ee],
    )
    mine_near = swap(passed, "row")
    s3 = across(s3, 3)
    gram, tick = gram_piece(tick, [mine], [(0, 0)], hidden_c)
    tick, s3, s2 = tie(tick, s3, s2)
    s2 = across(s2, 2)
    tick, x2, x3 = tie(tick, x2, x3)
    mine_x, passed = pick(hidden_x, x2, x2, x3)
    mine_far = swap(passed, "row")
    tick, mine_near = tie(tick, mine_near)
    gram, tick = gram_piece(tick, [mine_near], [(0, 1)], hidden_c, gram)
    tick, s2, s1 = tie(tick, s2, s1)
    s1 = across(s1, 1)
    tick, mine_far = tie(tick, mine_far)
    gram, tick = gram_piece(tick, [mine_x, mine_far], [(1, 0), (1, 1)], hidden_c, gram)
    return (unpack(tick, placing, factor, own, [s1, s2, s3]), gram)


def solution(mesh):
    in_specs = (
        P(("parts", "col"), ("expert", "row")),
        P(("parts", "col"), None),
        P(("parts", "col"), None),
        P(("parts", "col")),
        P(("expert", "row"), None, "col"),
        P("col", ("expert", "row")),
    )
    out_specs = (P(("parts", "col"), ("expert", "row")), P(("parts", "expert", "row"), "col"))
    small = mesh.shape["expert"] == 2 and mesh.shape["row"] == 2 and mesh.shape["col"] == 4
    return jax.shard_map(
        on_device if small else on_any_device,
        mesh=mesh,
        in_specs=in_specs,
        out_specs=out_specs,
        check_vma=False,
    )
```

```python
import functools

import jax
import jax.numpy as jnp
from jax import lax
from jax.experimental import pallas as pl
from jax.experimental.pallas import tpu as pltpu
from jax.sharding import PartitionSpec as P

F32 = jnp.float32
BF16 = jnp.bfloat16
MIB = 1 << 20


def spread(value, axis, source):
    kept = jnp.where(lax.axis_index(axis) == source, value, 0).astype(value.dtype)
    return lax.psum(kept, axis)


def activate(preacts):
    return (jax.nn.silu(preacts[:, 0, :]) * preacts[:, 1, :]).astype(jnp.bfloat16)


def on_any_device(tokens, routes, route_weight, pad_mask, gate_up, down):
    group_rows = tokens.shape[0]
    slot_count = group_rows // 4
    names_zero = routes == 0
    routed = jnp.any(names_zero, axis=1)
    live_rows = routed & (pad_mask == 1)
    factor = jnp.sum(
        jnp.where(names_zero, route_weight, jnp.float32(0.0)), axis=1
    ) * live_rows.astype(jnp.float32)
    position = jnp.cumsum(routed.astype(jnp.int32)) - 1
    slot_ids = lax.broadcasted_iota(jnp.int32, (slot_count, group_rows), 0)
    placing = ((position[None, :] == slot_ids) & routed[None, :]).astype(jnp.bfloat16)
    masked = tokens * live_rows.astype(jnp.bfloat16)[:, None]
    packed = jnp.dot(placing, masked, preferred_element_type=jnp.float32).astype(jnp.bfloat16)
    gathered = lax.all_gather(packed, "col", axis=0, tiled=True)
    anchor = lax.axis_index(("expert", "row"))
    preacts = lax.psum(
        jnp.einsum("rd,dgf->rgf", gathered, gate_up, preferred_element_type=jnp.float32),
        ("expert", "row"),
    )
    hidden = activate(preacts)
    mirrored = spread(hidden, "col", anchor)
    gram_block = lax.dot_general(
        mirrored, hidden, (((0,), (0,)), ((), ())), preferred_element_type=jnp.float32
    )
    gram_block = gram_block * jnp.float32(2.0 / hidden.shape[0])
    returned = lax.psum_scatter(
        jnp.dot(hidden, down, preferred_element_type=jnp.float32),
        "col",
        scatter_dimension=0,
        tiled=True,
    )
    unpacked = lax.dot_general(
        placing.astype(jnp.float32),
        returned,
        (((0,), (0,)), ((), ())),
        precision=lax.Precision.HIGHEST,
        preferred_element_type=jnp.float32,
    )
    expert_out = (unpacked * factor[:, None]).astype(jnp.bfloat16)
    return (expert_out, gram_block)


def cost(flops, moved):
    return pl.CostEstimate(flops=int(flops), bytes_accessed=int(moved), transcendentals=0)


def params(mib):
    return pltpu.CompilerParams(vmem_limit_bytes=mib * MIB)


VMEM = pl.BlockSpec(memory_space=pltpu.VMEM)
HBM = pl.BlockSpec(memory_space=pltpu.HBM)
SMEM = pl.BlockSpec(memory_space=pltpu.SMEM)
ANY = pl.BlockSpec(memory_space=pl.ANY)


def in_vmem(value):
    return pltpu.with_memory_space_constraint(value, pltpu.VMEM)


def in_hbm(value):
    return pltpu.with_memory_space_constraint(value, pltpu.HBM)


def quarter_of(expert_flip, row_flip):
    return (lax.axis_index("expert") ^ expert_flip) * 2 + (lax.axis_index("row") ^ row_flip)


def tie(*values):
    return lax.optimization_barrier(values)


def pack_kernel(
    tokens_ref, routes_ref, pad_ref, weight_ref, packed_ref, placing_ref, factor_ref,
    tokens_held, routes_held, pad_held, weight_held, sems,
):
    pairs = (
        (routes_ref, routes_held),
        (pad_ref, pad_held),
        (weight_ref, weight_held),
        (tokens_ref, tokens_held),
    )
    copies = [pltpu.make_async_copy(a, b, sems.at[i]) for i, (a, b) in enumerate(pairs)]
    for copy in copies:
        copy.start()
    slots, rows = placing_ref.shape
    before = lax.broadcasted_iota(jnp.int32, (rows, rows), 0)
    upto = lax.broadcasted_iota(jnp.int32, (rows, rows), 1)
    tri = jnp.where(before <= upto, 1.0, 0.0).astype(BF16)
    slot_ids = lax.broadcasted_iota(jnp.int32, (slots, rows), 0).astype(F32)
    for copy in copies[:3]:
        copy.wait()
    routes_t = routes_held[...]
    routed = (routes_t[0:1, :] == 0) | (routes_t[1:2, :] == 0)
    live = jnp.where(routed & (pad_held[...] == 1), 1.0, 0.0)
    routed_rows = jnp.broadcast_to(jnp.where(routed, 1.0, 0.0), (8, rows)).astype(BF16)
    position = jnp.dot(routed_rows, tri, preferred_element_type=F32)[0:1, :] - 1.0
    placing = jnp.where(position == slot_ids, jnp.broadcast_to(live, (slots, rows)), 0.0)
    placing_ref[...] = placing.astype(BF16)
    weight = jnp.sum(jnp.where(routes_t == 0, weight_held[...], 0.0), axis=0, keepdims=True)
    factor = jnp.sum(placing * weight, axis=1, keepdims=True)
    factor_ref[...] = jnp.broadcast_to(factor, factor_ref.shape)
    copies[3].wait()
    packed = jnp.dot(
        placing.astype(BF16), tokens_held[...], preferred_element_type=F32
    ).astype(BF16)
    for i in range(packed_ref.shape[0] // slots):
        packed_ref[slots * i : slots * (i + 1), :] = packed


def pack(tokens, routes_t, pad, weight_t):
    rows, depth = tokens.shape
    slots = rows // 4
    operands = (tokens, routes_t, pad, weight_t)
    return pl.pallas_call(
        pack_kernel,
        in_specs=[HBM] * 4,
        out_specs=[VMEM] * 3,
        out_shape=[
            pltpu.VMEM((4 * slots, depth), BF16),
            pltpu.VMEM((slots, rows), BF16),
            pltpu.VMEM((slots, 128), F32),
        ],
        scratch_shapes=[pltpu.VMEM(x.shape, x.dtype) for x in operands]
        + [pltpu.SemaphoreType.DMA((4,))],
        compiler_params=params(3),
        name="pack",
    )(*(in_hbm(x) for x in operands))


def unpack_kernel(after_ref, placing_ref, factor_ref, own_ref, parts_ref, out_ref):
    del after_ref
    slots = own_ref.shape[0]
    here = lax.axis_index("col")
    total = own_ref[...]
    for slot in range(1, parts_ref.shape[0] // slots):
        at = pl.multiple_of((here ^ slot) * slots, slots)
        total = total + parts_ref[pl.ds(at, slots), :].astype(F32)
    scaled = (total * factor_ref[:, 0:1]).astype(BF16)
    out_ref[...] = lax.dot_general(
        placing_ref[...], scaled, (((0,), (0,)), ((), ())), preferred_element_type=F32
    ).astype(BF16)


def unpack(done, placing, factor, own, parts):
    slots, rows = placing.shape
    return pl.pallas_call(
        unpack_kernel,
        in_specs=[ANY] + [VMEM] * 4,
        out_specs=VMEM,
        out_shape=jax.ShapeDtypeStruct((rows, own.shape[1]), BF16),
        compiler_params=params(4),
        name="unpack",
    )(done, placing, factor, own, parts)


def regroup_kernel(after_ref, weights_ref, out_ref, sems):
    del after_ref
    copies = [
        pltpu.make_async_copy(weights_ref.at[:, t], out_ref.at[t], sems.at[t])
        for t in range(out_ref.shape[0])
    ]
    for copy in copies:
        copy.start()
    for copy in copies:
        copy.wait()


def regroup(behind, weights):
    depth, tiles, two, lanes = weights.shape
    grouped = pl.pallas_call(
        regroup_kernel,
        in_specs=[ANY, HBM],
        out_specs=VMEM,
        out_shape=pltpu.VMEM((tiles, depth, two, lanes), BF16),
        scratch_shapes=[pltpu.SemaphoreType.DMA((tiles,))],
        compiler_params=params(4),
        cost_estimate=cost(0, 4 * weights.size),
        name="regroup",
    )(behind, in_hbm(weights))
    return grouped.reshape(tiles, depth * two, lanes)


def fetch_kernel(after_ref, down_ref, out_ref, done_ref, sems):
    del after_ref
    parts = sems.shape[0]
    size = down_ref.shape[0] // parts
    copies = [
        pltpu.make_async_copy(
            down_ref.at[pl.ds(size * i, size)], out_ref.at[pl.ds(size * i, size)], sems.at[i]
        )
        for i in range(parts)
    ]
    for copy in copies:
        copy.start()
    done_ref[...] = jnp.zeros_like(done_ref)
    for copy in copies:
        copy.wait()


def fetch(behind, down):
    return pl.pallas_call(
        fetch_kernel,
        in_specs=[ANY, HBM],
        out_specs=[VMEM, VMEM],
        out_shape=[pltpu.VMEM(down.shape, BF16), pltpu.VMEM((8, 128), F32)],
        scratch_shapes=[pltpu.SemaphoreType.DMA((4,))],
        compiler_params=params(4),
        cost_estimate=cost(0, 4 * down.size),
        name="fetch_down",
    )(behind, in_hbm(down))


def widen_tokens(x_ref, wide_ref):
    rows, depth = x_ref.shape
    cut = 256
    into = lax.broadcasted_iota(jnp.int32, (cut, 4 * cut), 1)
    out_of = lax.broadcasted_iota(jnp.int32, (cut, 4 * cut), 0)
    half = jnp.where(into < 2 * cut, 0, 1)
    widen = jnp.where(into - 2 * cut * half == 2 * out_of + half, 1.0, 0.0).astype(BF16)
    for k in range(depth // cut):
        spaced = jnp.dot(
            x_ref[:, cut * k : cut * (k + 1)], widen, preferred_element_type=F32
        ).astype(BF16)
        for h in range(2):
            wide_ref[rows * h : rows * (h + 1), 2 * cut * k : 2 * cut * (k + 1)] = spaced[
                :, 2 * cut * h : 2 * cut * (h + 1)
            ]


def preact_kernel(first, row_flip, chunk, chunks, *refs):
    if first:
        x_ref, w_ref, out_ref, wide_ref = refs
        widen_tokens(x_ref, wide_ref)
    else:
        wide_ref, w_ref, out_ref = refs
    tiles, _, lanes = w_ref.shape
    per = tiles // 4
    take = per // chunks
    at = []
    for i in range(2):
        quarter = quarter_of(1 - i, row_flip)
        at += [quarter * per + chunk * take + j for j in range(take)]
    for j in range(take):
        w = jnp.concatenate([w_ref[at[2 * j]], w_ref[at[2 * j + 1]]], axis=1)
        out_ref[:, 2 * lanes * j : 2 * lanes * (j + 1)] = jnp.dot(
            wide_ref[...], w, preferred_element_type=F32
        )


def preacts_of(left, weights, row_flip, chunk, chunks, first=False):
    tiles, depth2, lanes = weights.shape
    rows = left.shape[0] if first else left.shape[0] // 2
    units = tiles // 4 // chunks * lanes
    out_shape = [jax.ShapeDtypeStruct((2 * rows, 2 * units), F32)]
    if first:
        out_shape.append(pltpu.VMEM((2 * rows, depth2), BF16))
    return pl.pallas_call(
        functools.partial(preact_kernel, first, row_flip, chunk, chunks),
        in_specs=[VMEM] * 2,
        out_specs=[VMEM] * len(out_shape),
        out_shape=out_shape,
        compiler_params=params(4),
        cost_estimate=cost(8 * rows * depth2 * units, 0),
        name="preacts_" + ("sent" if row_flip else "kept"),
    )(left, in_vmem(weights))


def leave_kernel(kept_ref, got_ref, leaves_ref, stays_ref):
    units = stays_ref.shape[1]
    leaves_ref[...] = (kept_ref[:, :units] + got_ref[:, :units]).astype(BF16)
    stays_ref[...] = kept_ref[:, units:] + got_ref[:, units:]


def leave(kept, got):
    rows, units = kept.shape[0], kept.shape[1] // 2
    return pl.pallas_call(
        leave_kernel,
        in_specs=[VMEM] * 2,
        out_specs=[VMEM] * 2,
        out_shape=[
            jax.ShapeDtypeStruct((rows, units), BF16),
            jax.ShapeDtypeStruct((rows, units), F32),
        ],
        compiler_params=params(2),
        name="leave",
    )(kept, got)


def act_kernel(tick_ref, stays_ref, got_ref, *refs):
    del tick_ref
    out_ref = refs[-1]
    rows = out_ref.shape[0]
    gate = stays_ref[:rows, :] + got_ref[:rows, :].astype(F32)
    up = stays_ref[rows:, :] + got_ref[rows:, :].astype(F32)
    hidden = (jax.nn.silu(gate) * up).astype(BF16)
    if len(refs) == 1:
        out_ref[...] = hidden
    else:
        before_ref, part_ref, _ = refs
        done = before_ref.shape[1]
        part_ref[...] = hidden
        out_ref[:, :done] = before_ref[...]
        out_ref[:, done:] = hidden


def act(tick, stays, got, *before):
    rows, units = stays.shape
    shapes = [(rows // 2, units)]
    if before:
        shapes.append((rows // 2, units + before[0].shape[1]))
    return pl.pallas_call(
        act_kernel,
        in_specs=[ANY] + [VMEM] * (2 + len(before)),
        out_specs=[VMEM] * len(shapes),
        out_shape=[jax.ShapeDtypeStruct(shape, BF16) for shape in shapes],
        compiler_params=params(2),
        name="act",
    )(tick, stays, got, *before)


def is_near():
    return (lax.axis_index("col") // 2) == lax.axis_index("expert")


def is_odd():
    return (lax.axis_index("col") % 2) != lax.axis_index("row")


def choose_kernel(n0, n1, far_ref, leaves_ref, joined_ref):
    units = n0.shape[1]
    joined_ref[:, :units] = n0[...]
    joined_ref[:, units:] = n1[...]

    @pl.when(is_near())
    def _():
        leaves_ref[:, :units] = n0[...]
        leaves_ref[:, units:] = n1[...]

    @pl.when(jnp.logical_not(is_near()))
    def _():
        leaves_ref[...] = far_ref[...]


def choose(near_parts, if_far):
    same = jax.ShapeDtypeStruct(if_far.shape, if_far.dtype)
    return pl.pallas_call(
        choose_kernel,
        in_specs=[VMEM] * 3,
        out_specs=[VMEM] * 2,
        out_shape=[same, same],
        compiler_params=params(2),
        name="choose",
    )(*near_parts, if_far)


def pick_kernel(n0, n1, f2, *refs):
    if len(refs) == 3:
        f3, mine_ref, other_ref = refs
    else:
        h0, h1, mine_ref, other_ref, f3 = refs
        units = h0.shape[1]
        f3[:, :units] = h0[...]
        f3[:, units:] = h1[...]
    for near, pair in ((True, (n0, n1)), (False, (f2, f3))):
        for odd in (False, True):

            @pl.when((is_near() == near) & (is_odd() == odd))
            def _():
                mine_ref[...] = pair[int(odd)][...]
                other_ref[...] = pair[1 - int(odd)][...]


def pick(*slots):
    same = jax.ShapeDtypeStruct(slots[0].shape, slots[0].dtype)
    return pl.pallas_call(
        pick_kernel,
        in_specs=[VMEM] * len(slots),
        out_specs=[VMEM] * (len(slots) - 2),
        out_shape=[same] * (len(slots) - 2),
        compiler_params=params(2),
        name="pick",
    )(*slots)


def project_kernel(
    tick_ref, h0, h1, h2, h3, down_ref, own_ref, parts_ref, wide_ref, done_ref
):
    del tick_ref
    units = h0.shape[1]
    for k, h_ref in enumerate((h0, h1, h2, h3)):
        at = pl.multiple_of(quarter_of(k % 2, k // 2) * units, units)
        wide_ref[:, pl.ds(at, units)] = h_ref[...]
    done_ref[...] = jnp.zeros_like(done_ref)
    slots, width = own_ref.shape
    cut = 512
    here = lax.axis_index("col")
    for n in range(width // cut):
        columns = slice(cut * n, cut * (n + 1))
        total = jnp.dot(wide_ref[...], down_ref[:, columns], preferred_element_type=F32)
        parts_ref[:, columns] = total.astype(BF16)
        for col in range(parts_ref.shape[0] // slots):

            @pl.when(here == col)
            def _():
                own_ref[:, columns] = total[slots * col : slots * (col + 1), :]


def project(tick, quarters, down):
    rows, units = quarters[0].shape
    width = down.shape[1]
    slots = rows // 4
    return pl.pallas_call(
        project_kernel,
        in_specs=[ANY] + [VMEM] * 5,
        out_specs=[VMEM] * 4,
        out_shape=[
            jax.ShapeDtypeStruct((slots, width), F32),
            jax.ShapeDtypeStruct((rows, width), BF16),
            pltpu.VMEM((rows, 4 * units), BF16),
            pltpu.VMEM((8, 128), F32),
        ],
        compiler_params=params(4),
        cost_estimate=cost(8 * rows * units * width, 0),
        name="project",
    )(tick, *quarters, in_vmem(down))


def gram_kernel(scale, flips, *refs):
    count = len(flips)
    pieces = refs[1 : 1 + count]
    wide_ref = refs[1 + count]
    out_ref, done_ref, ring_ref, sems = refs[-4:]
    done_ref[...] = jnp.zeros_like(done_ref)
    units = pieces[0].shape[1]
    depth, _, cut = ring_ref.shape
    copies = []
    for (expert_flip, row_flip), a_ref in zip(flips, pieces):
        at = pl.multiple_of(quarter_of(expert_flip, row_flip) * units, units)
        left = a_ref[...].T
        for n in range(4 * units // cut):
            spot = len(copies) % depth
            if len(copies) >= depth:
                copies[-depth].wait()
            ring_ref[spot] = scale * jnp.dot(
                left, wide_ref[:, cut * n : cut * (n + 1)], preferred_element_type=F32
            )
            copy = pltpu.make_async_copy(
                ring_ref.at[spot], out_ref.at[pl.ds(at, units), pl.ds(cut * n, cut)], sems.at[spot]
            )
            copy.start()
            copies.append(copy)
    for copy in copies[-depth:]:
        copy.wait()


def gram_piece(tick, pieces, flips, wide, gram=None):
    rows, units = pieces[0].shape
    cut, depth = 512, 4
    operands = [tick, *pieces, in_vmem(wide)]
    in_specs = [ANY] + [VMEM] * (len(pieces) + 1)
    aliases = {}
    if gram is not None:
        aliases = {len(operands): 0}
        operands.append(gram)
        in_specs.append(HBM)
    return pl.pallas_call(
        functools.partial(gram_kernel, 2.0 / rows, flips),
        in_specs=in_specs,
        out_specs=[HBM, VMEM],
        out_shape=[
            jax.ShapeDtypeStruct((4 * units, 4 * units), F32),
            pltpu.VMEM((8, 128), F32),
        ],
        input_output_aliases=aliases,
        scratch_shapes=[
            pltpu.VMEM((depth, units, cut), F32),
            pltpu.SemaphoreType.DMA((depth,)),
        ],
        compiler_params=params(10),
        cost_estimate=cost(8 * rows * units * units * len(pieces), 16 * units * units * len(pieces)),
        name="gram",
    )(*operands)


def swap(value, axis):
    return lax.ppermute(value, axis, [(0, 1), (1, 0)])


def across(value, slot):
    return lax.ppermute(value, "col", [(i, i ^ slot) for i in range(4)])


def on_device(tokens, routes, route_weight, pad_mask, gate_up, down):
    depth = tokens.shape[1]
    units = gate_up.shape[2]
    lanes = 128
    chunks = 2
    weights = gate_up.reshape(depth, 2, units // lanes, lanes).transpose(0, 2, 1, 3)

    packed, placing, factor = pack(tokens, routes.T, pad_mask[None, :], route_weight.T)
    gathered = lax.all_to_all(packed, "col", 0, 0, tiled=True)
    grouped = regroup(packed, weights)

    first_sent, wide = preacts_of(gathered, grouped, 1, 0, chunks, True)
    (last_sent,) = preacts_of(wide, grouped, 1, 1, chunks)
    got = [swap(first_sent, "row"), swap(last_sent, "row")]
    stays, got_x = [], []
    for h in range(chunks):
        (kept,) = preacts_of(wide, grouped, 0, h, chunks)
        leaves, stay = leave(kept, got[h])
        wide, leaves = tie(wide, leaves)
        stays.append(stay)
        got_x.append(swap(leaves, "expert"))
    down_held, tick = fetch(wide, down)
    tick, got_x[0] = tie(tick, got_x[0])
    (hidden_a,) = act(tick, stays[0], got_x[0])

    z2a = across(hidden_a, 2)
    tick, got_x[1], hidden_a = tie(tick, got_x[1], hidden_a)
    hidden_b, hidden = act(tick, stays[1], got_x[1], hidden_a)
    z1 = across(hidden, 1)
    hidden_x = swap(hidden, "expert")
    c_near = swap(hidden, "row")
    tick, z2a, hidden_b = tie(tick, z2a, hidden_b)
    z2b = across(hidden_b, 2)
    z3a = across(z2a, 1)
    tick, z2b, z1, hidden_x, z3a = tie(tick, z2b, z1, hidden_x, z3a)

    leaves, z2 = choose((z2a, z2b), z1)
    tick, z2b, leaves, sent_x = tie(tick, z2b, leaves, hidden_x)
    z3b = across(z2b, 1)
    x2 = swap(leaves, "expert")
    c_far = swap(sent_x, "row")
    own, parts, hidden_c, tick = project(
        tick, [hidden, hidden_x, c_near, c_far], down_held
    )
    returned = lax.all_to_all(parts, "col", 0, 0, tiled=True)
    tick, z3b = tie(tick, z3b)
    mine, passed, z3 = pick(hidden, z1, z2, z3a, z3b)
    x3 = lax.ppermute(
        z3,
        ("expert", "col"),
        [(ee * 4 + cc, (1 - ee) * 4 + cc) for ee in range(2) for cc in range(4) if cc // 2 == ee],
    )
    mine_near = swap(passed, "row")
    gram, tick = gram_piece(tick, [mine], [(0, 0)], hidden_c)
    tick, x2, x3 = tie(tick, x2, x3)
    mine_x, passed = pick(hidden_x, x2, x2, x3)
    mine_far = swap(passed, "row")
    tick, mine_near = tie(tick, mine_near)
    gram, tick = gram_piece(tick, [mine_near], [(0, 1)], hidden_c, gram)
    tick, mine_far = tie(tick, mine_far)
    gram, tick = gram_piece(tick, [mine_x, mine_far], [(1, 0), (1, 1)], hidden_c, gram)
    return (unpack(tick, placing, factor, own, returned), gram)


def solution(mesh):
    in_specs = (
        P(("parts", "col"), ("expert", "row")),
        P(("parts", "col"), None),
        P(("parts", "col"), None),
        P(("parts", "col")),
        P(("expert", "row"), None, "col"),
        P("col", ("expert", "row")),
    )
    out_specs = (P(("parts", "col"), ("expert", "row")), P(("parts", "expert", "row"), "col"))
    small = mesh.shape["expert"] == 2 and mesh.shape["row"] == 2 and mesh.shape["col"] == 4
    return jax.shard_map(
        on_device if small else on_any_device,
        mesh=mesh,
        in_specs=in_specs,
        out_specs=out_specs,
        check_vma=False,
    )
```

```python
import functools

import jax
import jax.numpy as jnp
from jax import lax
from jax.experimental import pallas as pl
from jax.experimental.pallas import tpu as pltpu
from jax.sharding import PartitionSpec as P

F32 = jnp.float32
BF16 = jnp.bfloat16
MIB = 1 << 20


def spread(value, axis, source):
    kept = jnp.where(lax.axis_index(axis) == source, value, 0).astype(value.dtype)
    return lax.psum(kept, axis)


def activate(preacts):
    return (jax.nn.silu(preacts[:, 0, :]) * preacts[:, 1, :]).astype(jnp.bfloat16)


def on_any_device(tokens, routes, route_weight, pad_mask, gate_up, down):
    group_rows = tokens.shape[0]
    slot_count = group_rows // 4
    names_zero = routes == 0
    routed = jnp.any(names_zero, axis=1)
    live_rows = routed & (pad_mask == 1)
    factor = jnp.sum(
        jnp.where(names_zero, route_weight, jnp.float32(0.0)), axis=1
    ) * live_rows.astype(jnp.float32)
    position = jnp.cumsum(routed.astype(jnp.int32)) - 1
    slot_ids = lax.broadcasted_iota(jnp.int32, (slot_count, group_rows), 0)
    placing = ((position[None, :] == slot_ids) & routed[None, :]).astype(jnp.bfloat16)
    masked = tokens * live_rows.astype(jnp.bfloat16)[:, None]
    packed = jnp.dot(placing, masked, preferred_element_type=jnp.float32).astype(jnp.bfloat16)
    gathered = lax.all_gather(packed, "col", axis=0, tiled=True)
    anchor = lax.axis_index(("expert", "row"))
    preacts = lax.psum(
        jnp.einsum("rd,dgf->rgf", gathered, gate_up, preferred_element_type=jnp.float32),
        ("expert", "row"),
    )
    hidden = activate(preacts)
    mirrored = spread(hidden, "col", anchor)
    gram_block = lax.dot_general(
        mirrored, hidden, (((0,), (0,)), ((), ())), preferred_element_type=jnp.float32
    )
    gram_block = gram_block * jnp.float32(2.0 / hidden.shape[0])
    returned = lax.psum_scatter(
        jnp.dot(hidden, down, preferred_element_type=jnp.float32),
        "col",
        scatter_dimension=0,
        tiled=True,
    )
    unpacked = lax.dot_general(
        placing.astype(jnp.float32),
        returned,
        (((0,), (0,)), ((), ())),
        precision=lax.Precision.HIGHEST,
        preferred_element_type=jnp.float32,
    )
    expert_out = (unpacked * factor[:, None]).astype(jnp.bfloat16)
    return (expert_out, gram_block)


def cost(flops, moved):
    return pl.CostEstimate(flops=int(flops), bytes_accessed=int(moved), transcendentals=0)


def params(mib):
    return pltpu.CompilerParams(vmem_limit_bytes=mib * MIB)


VMEM = pl.BlockSpec(memory_space=pltpu.VMEM)
HBM = pl.BlockSpec(memory_space=pltpu.HBM)
SMEM = pl.BlockSpec(memory_space=pltpu.SMEM)
ANY = pl.BlockSpec(memory_space=pl.ANY)


def in_vmem(value):
    return pltpu.with_memory_space_constraint(value, pltpu.VMEM)


def in_hbm(value):
    return pltpu.with_memory_space_constraint(value, pltpu.HBM)


def quarter_of(expert_flip, row_flip):
    return (lax.axis_index("expert") ^ expert_flip) * 2 + (lax.axis_index("row") ^ row_flip)


def tie(*values):
    return lax.optimization_barrier(values)


def pack_kernel(
    tokens_ref, routes_ref, pad_ref, weight_ref, packed_ref, placing_ref, factor_ref,
    tokens_held, routes_held, pad_held, weight_held, sems,
):
    pairs = (
        (routes_ref, routes_held),
        (pad_ref, pad_held),
        (weight_ref, weight_held),
        (tokens_ref, tokens_held),
    )
    copies = [pltpu.make_async_copy(a, b, sems.at[i]) for i, (a, b) in enumerate(pairs)]
    for copy in copies:
        copy.start()
    slots, rows = placing_ref.shape
    before = lax.broadcasted_iota(jnp.int32, (rows, rows), 0)
    upto = lax.broadcasted_iota(jnp.int32, (rows, rows), 1)
    tri = jnp.where(before <= upto, 1.0, 0.0).astype(BF16)
    slot_ids = lax.broadcasted_iota(jnp.int32, (slots, rows), 0).astype(F32)
    for copy in copies[:3]:
        copy.wait()
    routes_t = routes_held[...]
    routed = (routes_t[0:1, :] == 0) | (routes_t[1:2, :] == 0)
    live = jnp.where(routed & (pad_held[...] == 1), 1.0, 0.0)
    routed_rows = jnp.broadcast_to(jnp.where(routed, 1.0, 0.0), (8, rows)).astype(BF16)
    position = jnp.dot(routed_rows, tri, preferred_element_type=F32)[0:1, :] - 1.0
    placing = jnp.where(position == slot_ids, jnp.broadcast_to(live, (slots, rows)), 0.0)
    placing_ref[...] = placing.astype(BF16)
    weight = jnp.sum(jnp.where(routes_t == 0, weight_held[...], 0.0), axis=0, keepdims=True)
    factor = jnp.sum(placing * weight, axis=1, keepdims=True)
    factor_ref[...] = jnp.broadcast_to(factor, factor_ref.shape)
    copies[3].wait()
    packed_ref[...] = jnp.dot(
        placing.astype(BF16), tokens_held[...], preferred_element_type=F32
    ).astype(BF16)


def pack(tokens, routes_t, pad, weight_t):
    rows, depth = tokens.shape
    slots = rows // 4
    operands = (tokens, routes_t, pad, weight_t)
    return pl.pallas_call(
        pack_kernel,
        in_specs=[HBM] * 4,
        out_specs=[VMEM] * 3,
        out_shape=[
            pltpu.VMEM((slots, depth), BF16),
            pltpu.VMEM((slots, rows), BF16),
            pltpu.VMEM((slots, 128), F32),
        ],
        scratch_shapes=[pltpu.VMEM(x.shape, x.dtype) for x in operands]
        + [pltpu.SemaphoreType.DMA((4,))],
        compiler_params=params(3),
        name="pack",
    )(*(in_hbm(x) for x in operands))


def regroup_kernel(after_ref, weights_ref, out_ref, sems):
    del after_ref
    copies = [
        pltpu.make_async_copy(weights_ref.at[:, t], out_ref.at[t], sems.at[t])
        for t in range(out_ref.shape[0])
    ]
    for copy in copies:
        copy.start()
    for copy in copies:
        copy.wait()


def regroup(behind, weights):
    depth, tiles, two, lanes = weights.shape
    grouped = pl.pallas_call(
        regroup_kernel,
        in_specs=[ANY, HBM],
        out_specs=VMEM,
        out_shape=pltpu.VMEM((tiles, depth, two, lanes), BF16),
        scratch_shapes=[pltpu.SemaphoreType.DMA((tiles,))],
        compiler_params=params(4),
        cost_estimate=cost(0, 4 * weights.size),
        name="regroup",
    )(behind, in_hbm(weights))
    return grouped.reshape(tiles, depth * two, lanes)


def fetch_kernel(after_ref, down_ref, out_ref, done_ref, sems):
    del after_ref
    parts = sems.shape[0]
    size = down_ref.shape[0] // parts
    copies = [
        pltpu.make_async_copy(
            down_ref.at[pl.ds(size * i, size)], out_ref.at[pl.ds(size * i, size)], sems.at[i]
        )
        for i in range(parts)
    ]
    for copy in copies:
        copy.start()
    done_ref[...] = jnp.zeros_like(done_ref)
    for copy in copies:
        copy.wait()


def fetch(behind, down):
    return pl.pallas_call(
        fetch_kernel,
        in_specs=[ANY, HBM],
        out_specs=[VMEM, VMEM],
        out_shape=[pltpu.VMEM(down.shape, BF16), pltpu.VMEM((8, 128), F32)],
        scratch_shapes=[pltpu.SemaphoreType.DMA((4,))],
        compiler_params=params(4),
        cost_estimate=cost(0, 4 * down.size),
        name="fetch_down",
    )(behind, in_hbm(down))


def widen_tokens(x_refs, wide_ref):
    slots, depth = x_refs[0].shape
    rows = 4 * slots
    here = lax.axis_index("col")
    cut = 256
    into = lax.broadcasted_iota(jnp.int32, (cut, 4 * cut), 1)
    out_of = lax.broadcasted_iota(jnp.int32, (cut, 4 * cut), 0)
    half = jnp.where(into < 2 * cut, 0, 1)
    widen = jnp.where(into - 2 * cut * half == 2 * out_of + half, 1.0, 0.0).astype(BF16)
    for slot, x_ref in enumerate(x_refs):
        stacked = jnp.concatenate(
            [x_ref[:, cut * k : cut * (k + 1)] for k in range(depth // cut)], axis=0
        )
        spaced = jnp.dot(stacked, widen, preferred_element_type=F32).astype(BF16)
        for h in range(2):
            at = pl.multiple_of(h * rows + (here ^ slot) * slots, slots)
            for k in range(depth // cut):
                wide_ref[pl.ds(at, slots), 2 * cut * k : 2 * cut * (k + 1)] = spaced[
                    slots * k : slots * (k + 1), 2 * cut * h : 2 * cut * (h + 1)
                ]


def preact_kernel(first, row_flip, chunk, chunks, *refs):
    if first:
        x0, x1, x2, x3, w_ref, out_ref, wide_ref = refs
        widen_tokens((x0, x1, x2, x3), wide_ref)
    else:
        wide_ref, w_ref, out_ref = refs
    tiles, _, lanes = w_ref.shape
    per = tiles // 4
    take = per // chunks
    at = []
    for i in range(2):
        quarter = quarter_of(1 - i, row_flip)
        at += [quarter * per + chunk * take + j for j in range(take)]
    for j in range(take):
        w = jnp.concatenate([w_ref[at[2 * j]], w_ref[at[2 * j + 1]]], axis=1)
        out_ref[:, 2 * lanes * j : 2 * lanes * (j + 1)] = jnp.dot(
            wide_ref[...], w, preferred_element_type=F32
        )


def preacts_of(lefts, weights, row_flip, chunk, chunks):
    tiles, depth2, lanes = weights.shape
    first = len(lefts) > 1
    rows = 4 * lefts[0].shape[0] if first else lefts[0].shape[0] // 2
    units = tiles // 4 // chunks * lanes
    out_shape = [jax.ShapeDtypeStruct((2 * rows, 2 * units), F32)]
    if first:
        out_shape.append(pltpu.VMEM((2 * rows, depth2), BF16))
    return pl.pallas_call(
        functools.partial(preact_kernel, first, row_flip, chunk, chunks),
        in_specs=[VMEM] * (len(lefts) + 1),
        out_specs=[VMEM] * len(out_shape),
        out_shape=out_shape,
        compiler_params=params(4),
        cost_estimate=cost(8 * rows * depth2 * units, 0),
        name="preacts_" + ("sent" if row_flip else "kept"),
    )(*lefts, in_vmem(weights))


def leave_kernel(kept_ref, got_ref, leaves_ref, stays_ref):
    units = stays_ref.shape[1]
    leaves_ref[...] = (kept_ref[:, :units] + got_ref[:, :units]).astype(BF16)
    stays_ref[...] = kept_ref[:, units:] + got_ref[:, units:]


def leave(kept, got):
    rows, units = kept.shape[0], kept.shape[1] // 2
    return pl.pallas_call(
        leave_kernel,
        in_specs=[VMEM] * 2,
        out_specs=[VMEM] * 2,
        out_shape=[
            jax.ShapeDtypeStruct((rows, units), BF16),
            jax.ShapeDtypeStruct((rows, units), F32),
        ],
        compiler_params=params(2),
        name="leave",
    )(kept, got)


def act_kernel(tick_ref, stays_ref, got_ref, *refs):
    del tick_ref
    out_ref = refs[-1]
    rows = out_ref.shape[0]
    gate = stays_ref[:rows, :] + got_ref[:rows, :].astype(F32)
    up = stays_ref[rows:, :] + got_ref[rows:, :].astype(F32)
    hidden = (jax.nn.silu(gate) * up).astype(BF16)
    if len(refs) == 1:
        out_ref[...] = hidden
    else:
        before_ref, part_ref, _ = refs
        done = before_ref.shape[1]
        part_ref[...] = hidden
        out_ref[:, :done] = before_ref[...]
        out_ref[:, done:] = hidden


def act(tick, stays, got, *before):
    rows, units = stays.shape
    shapes = [(rows // 2, units)]
    if before:
        shapes.append((rows // 2, units + before[0].shape[1]))
    return pl.pallas_call(
        act_kernel,
        in_specs=[ANY] + [VMEM] * (2 + len(before)),
        out_specs=[VMEM] * len(shapes),
        out_shape=[jax.ShapeDtypeStruct(shape, BF16) for shape in shapes],
        compiler_params=params(2),
        name="act",
    )(tick, stays, got, *before)


def is_near():
    return (lax.axis_index("col") // 2) == lax.axis_index("expert")


def is_odd():
    return (lax.axis_index("col") % 2) != lax.axis_index("row")


def choose_kernel(n0, n1, far_ref, leaves_ref, joined_ref):
    units = n0.shape[1]
    joined_ref[:, :units] = n0[...]
    joined_ref[:, units:] = n1[...]

    @pl.when(is_near())
    def _():
        leaves_ref[:, :units] = n0[...]
        leaves_ref[:, units:] = n1[...]

    @pl.when(jnp.logical_not(is_near()))
    def _():
        leaves_ref[...] = far_ref[...]


def choose(near_parts, if_far):
    same = jax.ShapeDtypeStruct(if_far.shape, if_far.dtype)
    return pl.pallas_call(
        choose_kernel,
        in_specs=[VMEM] * 3,
        out_specs=[VMEM] * 2,
        out_shape=[same, same],
        compiler_params=params(2),
        name="choose",
    )(*near_parts, if_far)


def pick_kernel(n0, n1, f2, *refs):
    if len(refs) == 3:
        f3, mine_ref, other_ref = refs
    else:
        h0, h1, mine_ref, other_ref, f3 = refs
        units = h0.shape[1]
        f3[:, :units] = h0[...]
        f3[:, units:] = h1[...]
    for near, pair in ((True, (n0, n1)), (False, (f2, f3))):
        for odd in (False, True):

            @pl.when((is_near() == near) & (is_odd() == odd))
            def _():
                mine_ref[...] = pair[int(odd)][...]
                other_ref[...] = pair[1 - int(odd)][...]


def pick(*slots):
    same = jax.ShapeDtypeStruct(slots[0].shape, slots[0].dtype)
    return pl.pallas_call(
        pick_kernel,
        in_specs=[VMEM] * len(slots),
        out_specs=[VMEM] * (len(slots) - 2),
        out_shape=[same] * (len(slots) - 2),
        compiler_params=params(2),
        name="pick",
    )(*slots)


def join_kernel(left_ref, right_ref, out_ref):
    units = left_ref.shape[1]
    out_ref[:, :units] = left_ref[...]
    out_ref[:, units:] = right_ref[...]


def join(left, right):
    rows, units = left.shape
    return pl.pallas_call(
        join_kernel,
        in_specs=[VMEM] * 2,
        out_specs=VMEM,
        out_shape=jax.ShapeDtypeStruct((rows, 2 * units), left.dtype),
        compiler_params=params(2),
        name="join",
    )(left, right)


def project_kernel(tick_ref, here_ref, there_ref, down_ref, near_ref, away_ref, wide_ref, done_ref, total_ref):
    del tick_ref
    units = here_ref.shape[1] // 2
    for row_flip, pair_ref in enumerate((here_ref, there_ref)):
        for expert_flip in range(2):
            at = pl.multiple_of(quarter_of(expert_flip, row_flip) * units, units)
            wide_ref[:, pl.ds(at, units)] = pair_ref[:, units * expert_flip : units * (expert_flip + 1)]
    done_ref[...] = jnp.zeros_like(done_ref)
    width = near_ref.shape[1]
    slots = near_ref.shape[0] // 2
    cut = 512
    for n in range(width // cut):
        total_ref[:, cut * n : cut * (n + 1)] = jnp.dot(
            wide_ref[...], down_ref[:, cut * n : cut * (n + 1)], preferred_element_type=F32
        )
    here = lax.axis_index("col")
    for i, (out_ref, slot) in enumerate(((near_ref, 0), (near_ref, 2), (away_ref, 1), (away_ref, 3))):
        at = pl.multiple_of((here ^ slot) * slots, slots)
        row = slots * (i % 2)
        out_ref[row : row + slots, :] = total_ref[pl.ds(at, slots), :].astype(out_ref.dtype)


def project(tick, here, there, down):
    rows, units = here.shape[0], here.shape[1] // 2
    width = down.shape[1]
    return pl.pallas_call(
        project_kernel,
        in_specs=[ANY] + [VMEM] * 3,
        out_specs=[VMEM] * 4,
        out_shape=[
            jax.ShapeDtypeStruct((rows // 2, width), F32),
            jax.ShapeDtypeStruct((rows // 2, width), BF16),
            pltpu.VMEM((rows, 4 * units), BF16),
            pltpu.VMEM((8, 128), F32),
        ],
        scratch_shapes=[pltpu.VMEM((rows, width), F32)],
        compiler_params=params(4),
        cost_estimate=cost(8 * rows * units * width, 0),
        name="project",
    )(tick, here, there, in_vmem(down))


def fold_kernel(near_ref, got_ref, own_ref, onward_ref):
    slots = own_ref.shape[0]
    own_ref[...] = near_ref[:slots, :] + got_ref[:slots, :].astype(F32)
    onward_ref[...] = (near_ref[slots:, :] + got_ref[slots:, :].astype(F32)).astype(BF16)


def fold(near, got):
    slots, width = near.shape[0] // 2, near.shape[1]
    return pl.pallas_call(
        fold_kernel,
        in_specs=[VMEM] * 2,
        out_specs=[VMEM] * 2,
        out_shape=[
            jax.ShapeDtypeStruct((slots, width), F32),
            jax.ShapeDtypeStruct((slots, width), BF16),
        ],
        compiler_params=params(2),
        name="fold",
    )(near, got)


def unpack_rows(placing_ref, factor_ref, own_ref, got_ref):
    total = own_ref[...] + got_ref[...].astype(F32)
    scaled = (total * factor_ref[:, 0:1]).astype(BF16)
    return lax.dot_general(
        placing_ref[...], scaled, (((0,), (0,)), ((), ())), preferred_element_type=F32
    ).astype(BF16)


def gram_kernel(scale, flips, last, *refs):
    count = len(flips)
    pieces = refs[1 : 1 + count]
    wide_ref = refs[1 + count]
    out_ref, done_ref, ring_ref, sems = refs[-4:]
    if not last:
        done_ref[...] = jnp.zeros_like(done_ref)
    units = pieces[0].shape[1]
    depth, _, cut = ring_ref.shape
    copies = []
    for (expert_flip, row_flip), a_ref in zip(flips, pieces):
        at = pl.multiple_of(quarter_of(expert_flip, row_flip) * units, units)
        left = a_ref[...].T
        for n in range(4 * units // cut):
            spot = len(copies) % depth
            if len(copies) >= depth:
                copies[-depth].wait()
            ring_ref[spot] = scale * jnp.dot(
                left, wide_ref[:, cut * n : cut * (n + 1)], preferred_element_type=F32
            )
            copy = pltpu.make_async_copy(
                ring_ref.at[spot], out_ref.at[pl.ds(at, units), pl.ds(cut * n, cut)], sems.at[spot]
            )
            copy.start()
            copies.append(copy)
            if last and len(copies) == depth:
                done_ref[...] = unpack_rows(*refs[2 + count : 6 + count])
    for copy in copies[-depth:]:
        copy.wait()


def gram_piece(tick, pieces, flips, wide, gram=None, outputs=()):
    rows, units = pieces[0].shape
    cut, depth = 512, 4
    operands = [tick, *pieces, in_vmem(wide), *outputs]
    in_specs = [ANY] + [VMEM] * (len(operands) - 1)
    aliases = {}
    if gram is not None:
        aliases = {len(operands): 0}
        operands.append(gram)
        in_specs.append(HBM)
    if outputs:
        placing, _, own, _ = outputs
        second = jax.ShapeDtypeStruct((placing.shape[1], own.shape[1]), BF16)
    else:
        second = pltpu.VMEM((8, 128), F32)
    return pl.pallas_call(
        functools.partial(gram_kernel, 2.0 / rows, flips, bool(outputs)),
        in_specs=in_specs,
        out_specs=[HBM, VMEM],
        out_shape=[jax.ShapeDtypeStruct((4 * units, 4 * units), F32), second],
        input_output_aliases=aliases,
        scratch_shapes=[
            pltpu.VMEM((depth, units, cut), F32),
            pltpu.SemaphoreType.DMA((depth,)),
        ],
        compiler_params=params(12),
        cost_estimate=cost(8 * rows * units * units * len(pieces), 16 * units * units * len(pieces)),
        name="gram",
    )(*operands)


def swap(value, axis):
    return lax.ppermute(value, axis, [(0, 1), (1, 0)])


def across(value, slot):
    return lax.ppermute(value, "col", [(i, i ^ slot) for i in range(4)])


def on_device(tokens, routes, route_weight, pad_mask, gate_up, down):
    depth = tokens.shape[1]
    units = gate_up.shape[2]
    lanes = 128
    chunks = 2
    weights = gate_up.reshape(depth, 2, units // lanes, lanes).transpose(0, 2, 1, 3)

    packed, placing, factor = pack(tokens, routes.T, pad_mask[None, :], route_weight.T)
    lefts = [packed] + [across(packed, slot) for slot in (1, 2, 3)]
    grouped = regroup(packed, weights)

    first_sent, wide = preacts_of(lefts, grouped, 1, 0, chunks)
    (last_sent,) = preacts_of([wide], grouped, 1, 1, chunks)
    got = [swap(first_sent, "row"), swap(last_sent, "row")]
    stays, got_x = [], []
    for h in range(chunks):
        (kept,) = preacts_of([wide], grouped, 0, h, chunks)
        leaves, stay = leave(kept, got[h])
        wide, leaves = tie(wide, leaves)
        stays.append(stay)
        got_x.append(swap(leaves, "expert"))
    down_held, tick = fetch(wide, down)
    tick, got_x[0] = tie(tick, got_x[0])
    (hidden_a,) = act(tick, stays[0], got_x[0])

    z2a = across(hidden_a, 2)
    tick, got_x[1], hidden_a = tie(tick, got_x[1], hidden_a)
    hidden_b, hidden = act(tick, stays[1], got_x[1], hidden_a)
    z1 = across(hidden, 1)
    hidden_x = swap(hidden, "expert")
    tick, z2a, hidden_b = tie(tick, z2a, hidden_b)
    z2b = across(hidden_b, 2)
    z3a = across(z2a, 1)
    tick, z2b, z1, hidden_x, z3a = tie(tick, z2b, z1, hidden_x, z3a)

    leaves, z2 = choose((z2a, z2b), z1)
    here = join(hidden, hidden_x)
    tick, z2b, leaves, here = tie(tick, z2b, leaves, here)
    z3b = across(z2b, 1)
    x2 = swap(leaves, "expert")
    there = swap(here, "row")
    tick, there = tie(tick, there)
    near, away, hidden_c, tick = project(tick, here, there, down_held)
    tick, z3b, away = tie(tick, z3b, away)
    mine, passed, z3 = pick(hidden, z1, z2, z3a, z3b)
    x3 = lax.ppermute(
        z3,
        ("expert", "col"),
        [(ee * 4 + cc, (1 - ee) * 4 + cc) for ee in range(2) for cc in range(4) if cc // 2 == ee],
    )
    mine_near = swap(passed, "row")
    away = across(away, 1)
    gram, tick = gram_piece(tick, [mine], [(0, 0)], hidden_c)
    tick, away = tie(tick, away)
    own, onward = fold(near, away)
    onward = across(onward, 2)
    tick, x2, x3 = tie(tick, x2, x3)
    mine_x, passed = pick(hidden_x, x2, x2, x3)
    mine_far = swap(passed, "row")
    tick, mine_near = tie(tick, mine_near)
    gram, tick = gram_piece(tick, [mine_near], [(0, 1)], hidden_c, gram)
    tick, mine_far = tie(tick, mine_far)
    gram, expert_out = gram_piece(
        tick, [mine_x, mine_far], [(1, 0), (1, 1)], hidden_c, gram, (placing, factor, own, onward)
    )
    return (expert_out, gram)


def solution(mesh):
    in_specs = (
        P(("parts", "col"), ("expert", "row")),
        P(("parts", "col"), None),
        P(("parts", "col"), None),
        P(("parts", "col")),
        P(("expert", "row"), None, "col"),
        P("col", ("expert", "row")),
    )
    out_specs = (P(("parts", "col"), ("expert", "row")), P(("parts", "expert", "row"), "col"))
    small = mesh.shape["expert"] == 2 and mesh.shape["row"] == 2 and mesh.shape["col"] == 4
    return jax.shard_map(
        on_device if small else on_any_device,
        mesh=mesh,
        in_specs=in_specs,
        out_specs=out_specs,
        check_vma=False,
    )
```

```python
import functools

import jax
import jax.numpy as jnp
from jax import lax
from jax.experimental import pallas as pl
from jax.experimental.pallas import tpu as pltpu
from jax.sharding import PartitionSpec as P

F32 = jnp.float32
BF16 = jnp.bfloat16
MIB = 1 << 20


def spread(value, axis, source):
    kept = jnp.where(lax.axis_index(axis) == source, value, 0).astype(value.dtype)
    return lax.psum(kept, axis)


def activate(preacts):
    return (jax.nn.silu(preacts[:, 0, :]) * preacts[:, 1, :]).astype(jnp.bfloat16)


def on_any_device(tokens, routes, route_weight, pad_mask, gate_up, down):
    group_rows = tokens.shape[0]
    slot_count = group_rows // 4
    names_zero = routes == 0
    routed = jnp.any(names_zero, axis=1)
    live_rows = routed & (pad_mask == 1)
    factor = jnp.sum(
        jnp.where(names_zero, route_weight, jnp.float32(0.0)), axis=1
    ) * live_rows.astype(jnp.float32)
    position = jnp.cumsum(routed.astype(jnp.int32)) - 1
    slot_ids = lax.broadcasted_iota(jnp.int32, (slot_count, group_rows), 0)
    placing = ((position[None, :] == slot_ids) & routed[None, :]).astype(jnp.bfloat16)
    masked = tokens * live_rows.astype(jnp.bfloat16)[:, None]
    packed = jnp.dot(placing, masked, preferred_element_type=jnp.float32).astype(jnp.bfloat16)
    gathered = lax.all_gather(packed, "col", axis=0, tiled=True)
    anchor = lax.axis_index(("expert", "row"))
    preacts = lax.psum(
        jnp.einsum("rd,dgf->rgf", gathered, gate_up, preferred_element_type=jnp.float32),
        ("expert", "row"),
    )
    hidden = activate(preacts)
    mirrored = spread(hidden, "col", anchor)
    gram_block = lax.dot_general(
        mirrored, hidden, (((0,), (0,)), ((), ())), preferred_element_type=jnp.float32
    )
    gram_block = gram_block * jnp.float32(2.0 / hidden.shape[0])
    returned = lax.psum_scatter(
        jnp.dot(hidden, down, preferred_element_type=jnp.float32),
        "col",
        scatter_dimension=0,
        tiled=True,
    )
    unpacked = lax.dot_general(
        placing.astype(jnp.float32),
        returned,
        (((0,), (0,)), ((), ())),
        precision=lax.Precision.HIGHEST,
        preferred_element_type=jnp.float32,
    )
    expert_out = (unpacked * factor[:, None]).astype(jnp.bfloat16)
    return (expert_out, gram_block)


def cost(flops, moved):
    return pl.CostEstimate(flops=int(flops), bytes_accessed=int(moved), transcendentals=0)


def params(mib):
    return pltpu.CompilerParams(vmem_limit_bytes=mib * MIB)


VMEM = pl.BlockSpec(memory_space=pltpu.VMEM)
HBM = pl.BlockSpec(memory_space=pltpu.HBM)
SMEM = pl.BlockSpec(memory_space=pltpu.SMEM)
ANY = pl.BlockSpec(memory_space=pl.ANY)


def in_vmem(value):
    return pltpu.with_memory_space_constraint(value, pltpu.VMEM)


def in_hbm(value):
    return pltpu.with_memory_space_constraint(value, pltpu.HBM)


def quarter_of(expert_flip, row_flip):
    return (lax.axis_index("expert") ^ expert_flip) * 2 + (lax.axis_index("row") ^ row_flip)


def tie(*values):
    return lax.optimization_barrier(values)


def pack_kernel(
    tokens_ref, routes_ref, pad_ref, weight_ref, packed_ref, placing_ref, factor_ref,
    tokens_held, routes_held, pad_held, weight_held, sems,
):
    pairs = (
        (routes_ref, routes_held),
        (pad_ref, pad_held),
        (weight_ref, weight_held),
        (tokens_ref, tokens_held),
    )
    copies = [pltpu.make_async_copy(a, b, sems.at[i]) for i, (a, b) in enumerate(pairs)]
    for copy in copies:
        copy.start()
    slots, rows = placing_ref.shape
    before = lax.broadcasted_iota(jnp.int32, (rows, rows), 0)
    upto = lax.broadcasted_iota(jnp.int32, (rows, rows), 1)
    tri = jnp.where(before <= upto, 1.0, 0.0).astype(BF16)
    slot_ids = lax.broadcasted_iota(jnp.int32, (slots, rows), 0).astype(F32)
    for copy in copies[:3]:
        copy.wait()
    routes_t = routes_held[...]
    routed = (routes_t[0:1, :] == 0) | (routes_t[1:2, :] == 0)
    live = jnp.where(routed & (pad_held[...] == 1), 1.0, 0.0)
    routed_rows = jnp.broadcast_to(jnp.where(routed, 1.0, 0.0), (8, rows)).astype(BF16)
    position = jnp.dot(routed_rows, tri, preferred_element_type=F32)[0:1, :] - 1.0
    placing = jnp.where(position == slot_ids, jnp.broadcast_to(live, (slots, rows)), 0.0)
    placing_ref[...] = placing.astype(BF16)
    weight = jnp.sum(jnp.where(routes_t == 0, weight_held[...], 0.0), axis=0, keepdims=True)
    factor = jnp.sum(placing * weight, axis=1, keepdims=True)
    factor_ref[...] = jnp.broadcast_to(factor, factor_ref.shape)
    copies[3].wait()
    packed_ref[...] = jnp.dot(
        placing.astype(BF16), tokens_held[...], preferred_element_type=F32
    ).astype(BF16)


def pack(tokens, routes_t, pad, weight_t):
    rows, depth = tokens.shape
    slots = rows // 4
    operands = (tokens, routes_t, pad, weight_t)
    return pl.pallas_call(
        pack_kernel,
        in_specs=[HBM] * 4,
        out_specs=[VMEM] * 3,
        out_shape=[
            pltpu.VMEM((slots, depth), BF16),
            pltpu.VMEM((slots, rows), BF16),
            pltpu.VMEM((slots, 128), F32),
        ],
        scratch_shapes=[pltpu.VMEM(x.shape, x.dtype) for x in operands]
        + [pltpu.SemaphoreType.DMA((4,))],
        compiler_params=params(3),
        name="pack",
    )(*(in_hbm(x) for x in operands))


def regroup_kernel(after_ref, weights_ref, out_ref, sems):
    del after_ref
    copies = [
        pltpu.make_async_copy(weights_ref.at[:, t], out_ref.at[t], sems.at[t])
        for t in range(out_ref.shape[0])
    ]
    for copy in copies:
        copy.start()
    for copy in copies:
        copy.wait()


def regroup(behind, weights):
    depth, tiles, two, lanes = weights.shape
    grouped = pl.pallas_call(
        regroup_kernel,
        in_specs=[ANY, HBM],
        out_specs=VMEM,
        out_shape=pltpu.VMEM((tiles, depth, two, lanes), BF16),
        scratch_shapes=[pltpu.SemaphoreType.DMA((tiles,))],
        compiler_params=params(4),
        cost_estimate=cost(0, 4 * weights.size),
        name="regroup",
    )(behind, in_hbm(weights))
    return grouped.reshape(tiles, depth * two, lanes)


def fetch_kernel(after_ref, down_ref, out_ref, done_ref, sems):
    del after_ref
    parts = sems.shape[0]
    size = down_ref.shape[0] // parts
    copies = [
        pltpu.make_async_copy(
            down_ref.at[pl.ds(size * i, size)], out_ref.at[pl.ds(size * i, size)], sems.at[i]
        )
        for i in range(parts)
    ]
    for copy in copies:
        copy.start()
    done_ref[...] = jnp.zeros_like(done_ref)
    for copy in copies:
        copy.wait()


def fetch(behind, down):
    return pl.pallas_call(
        fetch_kernel,
        in_specs=[ANY, HBM],
        out_specs=[VMEM, VMEM],
        out_shape=[pltpu.VMEM(down.shape, BF16), pltpu.VMEM((8, 128), F32)],
        scratch_shapes=[pltpu.SemaphoreType.DMA((4,))],
        compiler_params=params(4),
        cost_estimate=cost(0, 4 * down.size),
        name="fetch_down",
    )(behind, in_hbm(down))


def widen_tokens(x_refs, wide_ref):
    slots, depth = x_refs[0].shape
    rows = 4 * slots
    here = lax.axis_index("col")
    cut = 256
    into = lax.broadcasted_iota(jnp.int32, (cut, 4 * cut), 1)
    out_of = lax.broadcasted_iota(jnp.int32, (cut, 4 * cut), 0)
    half = jnp.where(into < 2 * cut, 0, 1)
    widen = jnp.where(into - 2 * cut * half == 2 * out_of + half, 1.0, 0.0).astype(BF16)
    for slot, x_ref in enumerate(x_refs):
        stacked = jnp.concatenate(
            [x_ref[:, cut * k : cut * (k + 1)] for k in range(depth // cut)], axis=0
        )
        spaced = jnp.dot(stacked, widen, preferred_element_type=F32).astype(BF16)
        for h in range(2):
            at = pl.multiple_of(h * rows + (here ^ slot) * slots, slots)
            for k in range(depth // cut):
                wide_ref[pl.ds(at, slots), 2 * cut * k : 2 * cut * (k + 1)] = spaced[
                    slots * k : slots * (k + 1), 2 * cut * h : 2 * cut * (h + 1)
                ]


def preact_kernel(first, row_flip, chunk, chunks, *refs):
    if first:
        x0, x1, x2, x3, w_ref, out_ref, wide_ref = refs
        widen_tokens((x0, x1, x2, x3), wide_ref)
    else:
        wide_ref, w_ref, out_ref = refs
    tiles, _, lanes = w_ref.shape
    per = tiles // 4
    take = per // chunks
    at = []
    for i in range(2):
        quarter = quarter_of(1 - i, row_flip)
        at += [quarter * per + chunk * take + j for j in range(take)]
    for j in range(take):
        w = jnp.concatenate([w_ref[at[2 * j]], w_ref[at[2 * j + 1]]], axis=1)
        out_ref[:, 2 * lanes * j : 2 * lanes * (j + 1)] = jnp.dot(
            wide_ref[...], w, preferred_element_type=F32
        )


def preacts_of(lefts, weights, row_flip, chunk, chunks):
    tiles, depth2, lanes = weights.shape
    first = len(lefts) > 1
    rows = 4 * lefts[0].shape[0] if first else lefts[0].shape[0] // 2
    units = tiles // 4 // chunks * lanes
    out_shape = [jax.ShapeDtypeStruct((2 * rows, 2 * units), F32)]
    if first:
        out_shape.append(pltpu.VMEM((2 * rows, depth2), BF16))
    return pl.pallas_call(
        functools.partial(preact_kernel, first, row_flip, chunk, chunks),
        in_specs=[VMEM] * (len(lefts) + 1),
        out_specs=[VMEM] * len(out_shape),
        out_shape=out_shape,
        compiler_params=params(4),
        cost_estimate=cost(8 * rows * depth2 * units, 0),
        name="preacts_" + ("sent" if row_flip else "kept"),
    )(*lefts, in_vmem(weights))


def leave_kernel(kept_ref, got_ref, leaves_ref, stays_ref):
    units = stays_ref.shape[1]
    leaves_ref[...] = (kept_ref[:, :units] + got_ref[:, :units]).astype(BF16)
    stays_ref[...] = kept_ref[:, units:] + got_ref[:, units:]


def leave(kept, got):
    rows, units = kept.shape[0], kept.shape[1] // 2
    return pl.pallas_call(
        leave_kernel,
        in_specs=[VMEM] * 2,
        out_specs=[VMEM] * 2,
        out_shape=[
            jax.ShapeDtypeStruct((rows, units), BF16),
            jax.ShapeDtypeStruct((rows, units), F32),
        ],
        compiler_params=params(2),
        cost_estimate=cost(0, 1),
        name="leave",
    )(kept, got)


def act_kernel(tick_ref, stays_ref, got_ref, *refs):
    del tick_ref
    out_ref = refs[-1]
    rows = out_ref.shape[0]
    gate = stays_ref[:rows, :] + got_ref[:rows, :].astype(F32)
    up = stays_ref[rows:, :] + got_ref[rows:, :].astype(F32)
    hidden = (jax.nn.silu(gate) * up).astype(BF16)
    if len(refs) == 1:
        out_ref[...] = hidden
    else:
        before_ref, part_ref, _ = refs
        done = before_ref.shape[1]
        part_ref[...] = hidden
        out_ref[:, :done] = before_ref[...]
        out_ref[:, done:] = hidden


def act(tick, stays, got, *before):
    rows, units = stays.shape
    shapes = [(rows // 2, units)]
    if before:
        shapes.append((rows // 2, units + before[0].shape[1]))
    return pl.pallas_call(
        act_kernel,
        in_specs=[ANY] + [VMEM] * (2 + len(before)),
        out_specs=[VMEM] * len(shapes),
        out_shape=[jax.ShapeDtypeStruct(shape, BF16) for shape in shapes],
        compiler_params=params(2),
        cost_estimate=cost(0, 1),
        name="act",
    )(tick, stays, got, *before)


def is_near():
    return (lax.axis_index("col") // 2) == lax.axis_index("expert")


def is_odd():
    return (lax.axis_index("col") % 2) != lax.axis_index("row")


def choose_kernel(n0, n1, f0, f1, leaves_ref, near_ref, far_ref):
    units = n0.shape[1]
    for out_ref, parts in ((near_ref, (n0, n1)), (far_ref, (f0, f1))):
        out_ref[:, :units] = parts[0][...]
        out_ref[:, units:] = parts[1][...]

    @pl.when(is_near())
    def _():
        leaves_ref[...] = near_ref[...]

    @pl.when(jnp.logical_not(is_near()))
    def _():
        leaves_ref[...] = far_ref[...]


def choose(near_parts, far_parts):
    rows, units = near_parts[0].shape
    same = jax.ShapeDtypeStruct((rows, 2 * units), BF16)
    return pl.pallas_call(
        choose_kernel,
        in_specs=[VMEM] * 4,
        out_specs=[VMEM] * 3,
        out_shape=[same] * 3,
        compiler_params=params(2),
        cost_estimate=cost(0, 1),
        name="choose",
    )(*near_parts, *far_parts)


def pick_kernel(n0, n1, f2, *refs):
    if len(refs) == 3:
        f3, mine_ref, other_ref = refs
    else:
        h0, h1, mine_ref, other_ref, f3 = refs
        units = h0.shape[1]
        f3[:, :units] = h0[...]
        f3[:, units:] = h1[...]
    for near, pair in ((True, (n0, n1)), (False, (f2, f3))):
        for odd in (False, True):

            @pl.when((is_near() == near) & (is_odd() == odd))
            def _():
                mine_ref[...] = pair[int(odd)][...]
                other_ref[...] = pair[1 - int(odd)][...]


def pick(*slots):
    same = jax.ShapeDtypeStruct(slots[0].shape, slots[0].dtype)
    return pl.pallas_call(
        pick_kernel,
        in_specs=[VMEM] * len(slots),
        out_specs=[VMEM] * (len(slots) - 2),
        out_shape=[same] * (len(slots) - 2),
        compiler_params=params(2),
        cost_estimate=cost(0, 1),
        name="pick",
    )(*slots)


def join_kernel(left_ref, right_ref, out_ref):
    units = left_ref.shape[1]
    out_ref[:, :units] = left_ref[...]
    out_ref[:, units:] = right_ref[...]


def join(left, right):
    rows, units = left.shape
    return pl.pallas_call(
        join_kernel,
        in_specs=[VMEM] * 2,
        out_specs=VMEM,
        out_shape=jax.ShapeDtypeStruct((rows, 2 * units), left.dtype),
        compiler_params=params(2),
        cost_estimate=cost(0, 1),
        name="join",
    )(left, right)


def project_kernel(tick_ref, here_ref, there_ref, down_ref, near_ref, away_ref, wide_ref, done_ref, total_ref):
    del tick_ref
    units = here_ref.shape[1] // 2
    for row_flip, pair_ref in enumerate((here_ref, there_ref)):
        for expert_flip in range(2):
            at = pl.multiple_of(quarter_of(expert_flip, row_flip) * units, units)
            wide_ref[:, pl.ds(at, units)] = pair_ref[:, units * expert_flip : units * (expert_flip + 1)]
    done_ref[...] = jnp.zeros_like(done_ref)
    width = near_ref.shape[1]
    slots = near_ref.shape[0] // 2
    cut = 512
    for n in range(width // cut):
        total_ref[:, cut * n : cut * (n + 1)] = jnp.dot(
            wide_ref[...], down_ref[:, cut * n : cut * (n + 1)], preferred_element_type=F32
        )
    here = lax.axis_index("col")
    for i, (out_ref, slot) in enumerate(((near_ref, 0), (near_ref, 2), (away_ref, 1), (away_ref, 3))):
        at = pl.multiple_of((here ^ slot) * slots, slots)
        row = slots * (i % 2)
        out_ref[row : row + slots, :] = total_ref[pl.ds(at, slots), :].astype(out_ref.dtype)


def project(tick, here, there, down):
    rows, units = here.shape[0], here.shape[1] // 2
    width = down.shape[1]
    return pl.pallas_call(
        project_kernel,
        in_specs=[ANY] + [VMEM] * 3,
        out_specs=[VMEM] * 4,
        out_shape=[
            jax.ShapeDtypeStruct((rows // 2, width), F32),
            jax.ShapeDtypeStruct((rows // 2, width), BF16),
            pltpu.VMEM((rows, 4 * units), BF16),
            pltpu.VMEM((8, 128), F32),
        ],
        scratch_shapes=[pltpu.VMEM((rows, width), F32)],
        compiler_params=params(4),
        cost_estimate=cost(0, 1),
        name="project",
    )(tick, here, there, in_vmem(down))


def fold_kernel(near_ref, got_ref, own_ref, onward_ref):
    slots = own_ref.shape[0]
    own_ref[...] = near_ref[:slots, :] + got_ref[:slots, :].astype(F32)
    onward_ref[...] = (near_ref[slots:, :] + got_ref[slots:, :].astype(F32)).astype(BF16)


def fold(near, got):
    slots, width = near.shape[0] // 2, near.shape[1]
    return pl.pallas_call(
        fold_kernel,
        in_specs=[VMEM] * 2,
        out_specs=[VMEM] * 2,
        out_shape=[
            jax.ShapeDtypeStruct((slots, width), F32),
            jax.ShapeDtypeStruct((slots, width), BF16),
        ],
        compiler_params=params(2),
        cost_estimate=cost(0, 1),
        name="fold",
    )(near, got)


def unpack_kernel(after_ref, placing_ref, factor_ref, own_ref, got_ref, out_ref):
    del after_ref
    total = own_ref[...] + got_ref[...].astype(F32)
    scaled = (total * factor_ref[:, 0:1]).astype(BF16)
    out_ref[...] = lax.dot_general(
        placing_ref[...], scaled, (((0,), (0,)), ((), ())), preferred_element_type=F32
    ).astype(BF16)


def unpack(done, placing, factor, own, got):
    slots, rows = placing.shape
    return pl.pallas_call(
        unpack_kernel,
        in_specs=[ANY] + [VMEM] * 4,
        out_specs=VMEM,
        out_shape=jax.ShapeDtypeStruct((rows, own.shape[1]), BF16),
        compiler_params=params(4),
        name="unpack",
    )(done, placing, factor, own, got)


def gram_kernel(scale, flips, *refs):
    count = len(flips)
    pieces = refs[1 : 1 + count]
    wide_ref = refs[1 + count]
    out_ref, done_ref, ring_ref, sems = refs[-4:]
    done_ref[...] = jnp.zeros_like(done_ref)
    units = pieces[0].shape[1]
    depth, _, cut = ring_ref.shape
    copies = []
    for (expert_flip, row_flip), a_ref in zip(flips, pieces):
        at = pl.multiple_of(quarter_of(expert_flip, row_flip) * units, units)
        left = a_ref[...].T
        for n in range(4 * units // cut):
            spot = len(copies) % depth
            if len(copies) >= depth:
                copies[-depth].wait()
            ring_ref[spot] = scale * jnp.dot(
                left, wide_ref[:, cut * n : cut * (n + 1)], preferred_element_type=F32
            )
            copy = pltpu.make_async_copy(
                ring_ref.at[spot], out_ref.at[pl.ds(at, units), pl.ds(cut * n, cut)], sems.at[spot]
            )
            copy.start()
            copies.append(copy)
    for copy in copies[-depth:]:
        copy.wait()


def gram_piece(tick, pieces, flips, wide, gram=None):
    rows, units = pieces[0].shape
    cut, depth = 512, 4
    operands = [tick, *pieces, in_vmem(wide)]
    in_specs = [ANY] + [VMEM] * (len(pieces) + 1)
    aliases = {}
    if gram is not None:
        aliases = {len(operands): 0}
        operands.append(gram)
        in_specs.append(HBM)
    return pl.pallas_call(
        functools.partial(gram_kernel, 2.0 / rows, flips),
        in_specs=in_specs,
        out_specs=[HBM, VMEM],
        out_shape=[
            jax.ShapeDtypeStruct((4 * units, 4 * units), F32),
            pltpu.VMEM((8, 128), F32),
        ],
        input_output_aliases=aliases,
        scratch_shapes=[
            pltpu.VMEM((depth, units, cut), F32),
            pltpu.SemaphoreType.DMA((depth,)),
        ],
        compiler_params=params(10),
        cost_estimate=cost(8 * rows * units * units * len(pieces), 16 * units * units * len(pieces)),
        name="gram",
    )(*operands)


def swap(value, axis):
    return lax.ppermute(value, axis, [(0, 1), (1, 0)])


def across(value, slot):
    return lax.ppermute(value, "col", [(i, i ^ slot) for i in range(4)])


def on_device(tokens, routes, route_weight, pad_mask, gate_up, down):
    depth = tokens.shape[1]
    units = gate_up.shape[2]
    lanes = 128
    chunks = 2
    weights = gate_up.reshape(depth, 2, units // lanes, lanes).transpose(0, 2, 1, 3)

    packed, placing, factor = pack(tokens, routes.T, pad_mask[None, :], route_weight.T)
    lefts = [packed] + [across(packed, slot) for slot in (1, 2, 3)]
    grouped = regroup(packed, weights)

    first_sent, wide = preacts_of(lefts, grouped, 1, 0, chunks)
    (last_sent,) = preacts_of([wide], grouped, 1, 1, chunks)
    got = [swap(first_sent, "row"), swap(last_sent, "row")]
    stays, got_x = [], []
    for h in range(chunks):
        (kept,) = preacts_of([wide], grouped, 0, h, chunks)
        leaves, stay = leave(kept, got[h])
        wide, leaves = tie(wide, leaves)
        stays.append(stay)
        got_x.append(swap(leaves, "expert"))
    down_held, tick = fetch(wide, down)
    tick, got_x[0] = tie(tick, got_x[0])
    (hidden_a,) = act(tick, stays[0], got_x[0])

    z2a = across(hidden_a, 2)
    z1a = across(hidden_a, 1)
    tick, got_x[1], hidden_a = tie(tick, got_x[1], hidden_a)
    hidden_b, hidden = act(tick, stays[1], got_x[1], hidden_a)
    hidden_x = swap(hidden, "expert")
    tick, z2a, z1a, hidden_b = tie(tick, z2a, z1a, hidden_b)
    z2b = across(hidden_b, 2)
    z1b = across(hidden_b, 1)
    z3a = across(z2a, 1)
    tick, z2b, z1b, hidden_x, z3a = tie(tick, z2b, z1b, hidden_x, z3a)

    leaves, z2, z1 = choose((z2a, z2b), (z1a, z1b))
    here = join(hidden, hidden_x)
    tick, z2b, leaves, here = tie(tick, z2b, leaves, here)
    z3b = across(z2b, 1)
    x2 = swap(leaves, "expert")
    there = swap(here, "row")
    tick, there, here = tie(tick, there, here)
    near, away, hidden_c, tick = project(tick, here, there, down_held)
    tick, z3b, away, x2 = tie(tick, z3b, away, x2)
    mine, passed, z3 = pick(hidden, z1, z2, z3a, z3b)
    x3 = lax.ppermute(
        z3,
        ("expert", "col"),
        [(ee * 4 + cc, (1 - ee) * 4 + cc) for ee in range(2) for cc in range(4) if cc // 2 == ee],
    )
    mine_near = swap(passed, "row")
    away = across(away, 1)
    tick, mine_near = tie(tick, mine_near)
    gram, tick = gram_piece(tick, [mine, mine_near], [(0, 0), (0, 1)], hidden_c)
    tick, x3 = tie(tick, x3)
    mine_x, passed = pick(hidden_x, x2, x2, x3)
    mine_far = swap(passed, "row")
    tick, away = tie(tick, away)
    own, onward = fold(near, away)
    onward = across(onward, 2)
    tick, mine_far = tie(tick, mine_far)
    gram, tick = gram_piece(tick, [mine_x, mine_far], [(1, 0), (1, 1)], hidden_c, gram)
    return (unpack(tick, placing, factor, own, onward), gram)


def solution(mesh):
    in_specs = (
        P(("parts", "col"), ("expert", "row")),
        P(("parts", "col"), None),
        P(("parts", "col"), None),
        P(("parts", "col")),
        P(("expert", "row"), None, "col"),
        P("col", ("expert", "row")),
    )
    out_specs = (P(("parts", "col"), ("expert", "row")), P(("parts", "expert", "row"), "col"))
    small = mesh.shape["expert"] == 2 and mesh.shape["row"] == 2 and mesh.shape["col"] == 4
    return jax.shard_map(
        on_device if small else on_any_device,
        mesh=mesh,
        in_specs=in_specs,
        out_specs=out_specs,
        check_vma=False,
    )
```

```python
import functools

import jax
import jax.numpy as jnp
from jax import lax
from jax.experimental import pallas as pl
from jax.experimental.pallas import tpu as pltpu
from jax.sharding import PartitionSpec as P

F32 = jnp.float32
BF16 = jnp.bfloat16
MIB = 1 << 20


def spread(value, axis, source):
    kept = jnp.where(lax.axis_index(axis) == source, value, 0).astype(value.dtype)
    return lax.psum(kept, axis)


def activate(preacts):
    return (jax.nn.silu(preacts[:, 0, :]) * preacts[:, 1, :]).astype(jnp.bfloat16)


def on_any_device(tokens, routes, route_weight, pad_mask, gate_up, down):
    group_rows = tokens.shape[0]
    slot_count = group_rows // 4
    names_zero = routes == 0
    routed = jnp.any(names_zero, axis=1)
    live_rows = routed & (pad_mask == 1)
    factor = jnp.sum(
        jnp.where(names_zero, route_weight, jnp.float32(0.0)), axis=1
    ) * live_rows.astype(jnp.float32)
    position = jnp.cumsum(routed.astype(jnp.int32)) - 1
    slot_ids = lax.broadcasted_iota(jnp.int32, (slot_count, group_rows), 0)
    placing = ((position[None, :] == slot_ids) & routed[None, :]).astype(jnp.bfloat16)
    masked = tokens * live_rows.astype(jnp.bfloat16)[:, None]
    packed = jnp.dot(placing, masked, preferred_element_type=jnp.float32).astype(jnp.bfloat16)
    gathered = lax.all_gather(packed, "col", axis=0, tiled=True)
    anchor = lax.axis_index(("expert", "row"))
    preacts = lax.psum(
        jnp.einsum("rd,dgf->rgf", gathered, gate_up, preferred_element_type=jnp.float32),
        ("expert", "row"),
    )
    hidden = activate(preacts)
    mirrored = spread(hidden, "col", anchor)
    gram_block = lax.dot_general(
        mirrored, hidden, (((0,), (0,)), ((), ())), preferred_element_type=jnp.float32
    )
    gram_block = gram_block * jnp.float32(2.0 / hidden.shape[0])
    returned = lax.psum_scatter(
        jnp.dot(hidden, down, preferred_element_type=jnp.float32),
        "col",
        scatter_dimension=0,
        tiled=True,
    )
    unpacked = lax.dot_general(
        placing.astype(jnp.float32),
        returned,
        (((0,), (0,)), ((), ())),
        precision=lax.Precision.HIGHEST,
        preferred_element_type=jnp.float32,
    )
    expert_out = (unpacked * factor[:, None]).astype(jnp.bfloat16)
    return (expert_out, gram_block)


def cost(flops, moved):
    return pl.CostEstimate(flops=int(flops), bytes_accessed=int(moved), transcendentals=0)


def params(mib):
    return pltpu.CompilerParams(vmem_limit_bytes=mib * MIB)


VMEM = pl.BlockSpec(memory_space=pltpu.VMEM)
HBM = pl.BlockSpec(memory_space=pltpu.HBM)
SMEM = pl.BlockSpec(memory_space=pltpu.SMEM)
ANY = pl.BlockSpec(memory_space=pl.ANY)


def in_vmem(value):
    return pltpu.with_memory_space_constraint(value, pltpu.VMEM)


def in_hbm(value):
    return pltpu.with_memory_space_constraint(value, pltpu.HBM)


def quarter_of(expert_flip, row_flip):
    return (lax.axis_index("expert") ^ expert_flip) * 2 + (lax.axis_index("row") ^ row_flip)


def tie(*values):
    return lax.optimization_barrier(values)


def pack_kernel(
    tokens_ref, routes_ref, pad_ref, weight_ref, packed_ref, placing_ref, factor_ref,
    tokens_held, routes_held, pad_held, weight_held, sems,
):
    pairs = (
        (routes_ref, routes_held),
        (pad_ref, pad_held),
        (weight_ref, weight_held),
        (tokens_ref, tokens_held),
    )
    copies = [pltpu.make_async_copy(a, b, sems.at[i]) for i, (a, b) in enumerate(pairs)]
    for copy in copies:
        copy.start()
    slots, rows = placing_ref.shape
    before = lax.broadcasted_iota(jnp.int32, (rows, rows), 0)
    upto = lax.broadcasted_iota(jnp.int32, (rows, rows), 1)
    tri = jnp.where(before <= upto, 1.0, 0.0).astype(BF16)
    slot_ids = lax.broadcasted_iota(jnp.int32, (slots, rows), 0).astype(F32)
    for copy in copies[:3]:
        copy.wait()
    routes_t = routes_held[...]
    routed = (routes_t[0:1, :] == 0) | (routes_t[1:2, :] == 0)
    live = jnp.where(routed & (pad_held[...] == 1), 1.0, 0.0)
    routed_rows = jnp.broadcast_to(jnp.where(routed, 1.0, 0.0), (8, rows)).astype(BF16)
    position = jnp.dot(routed_rows, tri, preferred_element_type=F32)[0:1, :] - 1.0
    placing = jnp.where(position == slot_ids, jnp.broadcast_to(live, (slots, rows)), 0.0)
    placing_ref[...] = placing.astype(BF16)
    weight = jnp.sum(jnp.where(routes_t == 0, weight_held[...], 0.0), axis=0, keepdims=True)
    factor = jnp.sum(placing * weight, axis=1, keepdims=True)
    factor_ref[...] = jnp.broadcast_to(factor, factor_ref.shape)
    copies[3].wait()
    packed_ref[...] = jnp.dot(
        placing.astype(BF16), tokens_held[...], preferred_element_type=F32
    ).astype(BF16)


def pack(tokens, routes_t, pad, weight_t):
    rows, depth = tokens.shape
    slots = rows // 4
    operands = (tokens, routes_t, pad, weight_t)
    return pl.pallas_call(
        pack_kernel,
        in_specs=[HBM] * 4,
        out_specs=[VMEM] * 3,
        out_shape=[
            pltpu.VMEM((slots, depth), BF16),
            pltpu.VMEM((slots, rows), BF16),
            pltpu.VMEM((slots, 128), F32),
        ],
        scratch_shapes=[pltpu.VMEM(x.shape, x.dtype) for x in operands]
        + [pltpu.SemaphoreType.DMA((4,))],
        compiler_params=params(3),
        name="pack",
    )(*(in_hbm(x) for x in operands))


def regroup_kernel(after_ref, weights_ref, out_ref, sems):
    del after_ref
    copies = [
        pltpu.make_async_copy(weights_ref.at[:, t], out_ref.at[t], sems.at[t])
        for t in range(out_ref.shape[0])
    ]
    for copy in copies:
        copy.start()
    for copy in copies:
        copy.wait()


def regroup(behind, weights):
    depth, tiles, two, lanes = weights.shape
    grouped = pl.pallas_call(
        regroup_kernel,
        in_specs=[ANY, HBM],
        out_specs=VMEM,
        out_shape=pltpu.VMEM((tiles, depth, two, lanes), BF16),
        scratch_shapes=[pltpu.SemaphoreType.DMA((tiles,))],
        compiler_params=params(4),
        cost_estimate=cost(0, 4 * weights.size),
        name="regroup",
    )(behind, in_hbm(weights))
    return grouped.reshape(tiles, depth * two, lanes)


def fetch_kernel(after_ref, down_ref, out_ref, done_ref, sems):
    del after_ref
    parts = sems.shape[0]
    size = down_ref.shape[0] // parts
    copies = [
        pltpu.make_async_copy(
            down_ref.at[pl.ds(size * i, size)], out_ref.at[pl.ds(size * i, size)], sems.at[i]
        )
        for i in range(parts)
    ]
    for copy in copies:
        copy.start()
    done_ref[...] = jnp.zeros_like(done_ref)
    for copy in copies:
        copy.wait()


def fetch(behind, down):
    return pl.pallas_call(
        fetch_kernel,
        in_specs=[ANY, HBM],
        out_specs=[VMEM, VMEM],
        out_shape=[pltpu.VMEM(down.shape, BF16), pltpu.VMEM((8, 128), F32)],
        scratch_shapes=[pltpu.SemaphoreType.DMA((4,))],
        compiler_params=params(4),
        cost_estimate=cost(0, 4 * down.size),
        name="fetch_down",
    )(behind, in_hbm(down))


def widen_tokens(x_refs, wide_ref):
    slots, depth = x_refs[0].shape
    rows = 4 * slots
    here = lax.axis_index("col")
    cut = 256
    into = lax.broadcasted_iota(jnp.int32, (cut, 4 * cut), 1)
    out_of = lax.broadcasted_iota(jnp.int32, (cut, 4 * cut), 0)
    half = jnp.where(into < 2 * cut, 0, 1)
    widen = jnp.where(into - 2 * cut * half == 2 * out_of + half, 1.0, 0.0).astype(BF16)
    for slot, x_ref in enumerate(x_refs):
        stacked = jnp.concatenate(
            [x_ref[:, cut * k : cut * (k + 1)] for k in range(depth // cut)], axis=0
        )
        spaced = jnp.dot(stacked, widen, preferred_element_type=F32).astype(BF16)
        for h in range(2):
            at = pl.multiple_of(h * rows + (here ^ slot) * slots, slots)
            for k in range(depth // cut):
                wide_ref[pl.ds(at, slots), 2 * cut * k : 2 * cut * (k + 1)] = spaced[
                    slots * k : slots * (k + 1), 2 * cut * h : 2 * cut * (h + 1)
                ]


def preact_kernel(first, row_flip, chunk, chunks, *refs):
    if first:
        x0, x1, x2, x3, w_ref, out_ref, wide_ref = refs
        widen_tokens((x0, x1, x2, x3), wide_ref)
    else:
        wide_ref, w_ref, out_ref = refs
    tiles, _, lanes = w_ref.shape
    per = tiles // 4
    take = per // chunks
    at = []
    for i in range(2):
        quarter = quarter_of(1 - i, row_flip)
        at += [quarter * per + chunk * take + j for j in range(take)]
    for j in range(take):
        w = jnp.concatenate([w_ref[at[2 * j]], w_ref[at[2 * j + 1]]], axis=1)
        out_ref[:, 2 * lanes * j : 2 * lanes * (j + 1)] = jnp.dot(
            wide_ref[...], w, preferred_element_type=F32
        )


def preacts_of(lefts, weights, row_flip, chunk, chunks):
    tiles, depth2, lanes = weights.shape
    first = len(lefts) > 1
    rows = 4 * lefts[0].shape[0] if first else lefts[0].shape[0] // 2
    units = tiles // 4 // chunks * lanes
    out_shape = [jax.ShapeDtypeStruct((2 * rows, 2 * units), F32)]
    if first:
        out_shape.append(pltpu.VMEM((2 * rows, depth2), BF16))
    return pl.pallas_call(
        functools.partial(preact_kernel, first, row_flip, chunk, chunks),
        in_specs=[VMEM] * (len(lefts) + 1),
        out_specs=[VMEM] * len(out_shape),
        out_shape=out_shape,
        compiler_params=params(4),
        cost_estimate=cost(8 * rows * depth2 * units, 0),
        name="preacts_" + ("sent" if row_flip else "kept"),
    )(*lefts, in_vmem(weights))


def leave_kernel(kept_ref, got_ref, leaves_ref, stays_ref):
    units = stays_ref.shape[1]
    leaves_ref[...] = (kept_ref[:, :units] + got_ref[:, :units]).astype(BF16)
    stays_ref[...] = kept_ref[:, units:] + got_ref[:, units:]


def leave(kept, got):
    rows, units = kept.shape[0], kept.shape[1] // 2
    return pl.pallas_call(
        leave_kernel,
        in_specs=[VMEM] * 2,
        out_specs=[VMEM] * 2,
        out_shape=[
            jax.ShapeDtypeStruct((rows, units), BF16),
            jax.ShapeDtypeStruct((rows, units), F32),
        ],
        compiler_params=params(2),
        cost_estimate=cost(0, 1),
        name="leave",
    )(kept, got)


def act_kernel(tick_ref, stays_ref, got_ref, *refs):
    del tick_ref
    out_ref = refs[-1]
    rows = out_ref.shape[0]
    gate = stays_ref[:rows, :] + got_ref[:rows, :].astype(F32)
    up = stays_ref[rows:, :] + got_ref[rows:, :].astype(F32)
    hidden = (jax.nn.silu(gate) * up).astype(BF16)
    if len(refs) == 1:
        out_ref[...] = hidden
    else:
        before_ref, part_ref, _ = refs
        done = before_ref.shape[1]
        part_ref[...] = hidden
        out_ref[:, :done] = before_ref[...]
        out_ref[:, done:] = hidden


def act(tick, stays, got, *before):
    rows, units = stays.shape
    shapes = [(rows // 2, units)]
    if before:
        shapes.append((rows // 2, units + before[0].shape[1]))
    return pl.pallas_call(
        act_kernel,
        in_specs=[ANY] + [VMEM] * (2 + len(before)),
        out_specs=[VMEM] * len(shapes),
        out_shape=[jax.ShapeDtypeStruct(shape, BF16) for shape in shapes],
        compiler_params=params(2),
        cost_estimate=cost(0, 1),
        name="act",
    )(tick, stays, got, *before)


def is_near():
    return (lax.axis_index("col") // 2) == lax.axis_index("expert")


def is_odd():
    return (lax.axis_index("col") % 2) != lax.axis_index("row")


def choose_kernel(near_ref, far_ref, out_ref):
    @pl.when(is_near())
    def _():
        out_ref[...] = near_ref[...]

    @pl.when(jnp.logical_not(is_near()))
    def _():
        out_ref[...] = far_ref[...]


def choose(if_near, if_far):
    return pl.pallas_call(
        choose_kernel,
        in_specs=[VMEM] * 2,
        out_specs=VMEM,
        out_shape=jax.ShapeDtypeStruct(if_near.shape, if_near.dtype),
        compiler_params=params(2),
        cost_estimate=cost(0, 1),
        name="choose",
    )(if_near, if_far)


def pick_kernel(counts, *refs):
    slots, at = [], 0
    for count in counts:
        slots.append(refs[at : at + count])
        at += count
    mine_ref, other_ref, last_ref = refs[at:]

    def put(out_ref, parts):
        column = 0
        for part in parts:
            out_ref[:, column : column + part.shape[1]] = part[...]
            column += part.shape[1]

    put(last_ref, slots[3])
    for near, pair in ((True, slots[:2]), (False, slots[2:])):
        for odd in (False, True):

            @pl.when((is_near() == near) & (is_odd() == odd))
            def _():
                put(mine_ref, pair[int(odd)])
                put(other_ref, pair[1 - int(odd)])


def pick(*slots):
    parts = [part for slot in slots for part in slot]
    same = jax.ShapeDtypeStruct(slots[0][0].shape, BF16)
    return pl.pallas_call(
        functools.partial(pick_kernel, [len(slot) for slot in slots]),
        in_specs=[VMEM] * len(parts),
        out_specs=[VMEM] * 3,
        out_shape=[same] * 3,
        compiler_params=params(2),
        cost_estimate=cost(0, 1),
        name="pick",
    )(*parts)


def join_kernel(left_ref, right_ref, out_ref):
    units = left_ref.shape[1]
    out_ref[:, :units] = left_ref[...]
    out_ref[:, units:] = right_ref[...]


def join(left, right):
    rows, units = left.shape
    return pl.pallas_call(
        join_kernel,
        in_specs=[VMEM] * 2,
        out_specs=VMEM,
        out_shape=jax.ShapeDtypeStruct((rows, 2 * units), left.dtype),
        compiler_params=params(2),
        cost_estimate=cost(0, 1),
        name="join",
    )(left, right)


def project_kernel(tick_ref, here_ref, there_ref, down_ref, near_ref, away_ref, wide_ref, done_ref, total_ref):
    del tick_ref
    units = here_ref.shape[1] // 2
    for row_flip, pair_ref in enumerate((here_ref, there_ref)):
        for expert_flip in range(2):
            at = pl.multiple_of(quarter_of(expert_flip, row_flip) * units, units)
            wide_ref[:, pl.ds(at, units)] = pair_ref[:, units * expert_flip : units * (expert_flip + 1)]
    done_ref[...] = jnp.zeros_like(done_ref)
    width = near_ref.shape[1]
    slots = near_ref.shape[0] // 2
    cut = 512
    for n in range(width // cut):
        total_ref[:, cut * n : cut * (n + 1)] = jnp.dot(
            wide_ref[...], down_ref[:, cut * n : cut * (n + 1)], preferred_element_type=F32
        )
    here = lax.axis_index("col")
    for i, (out_ref, slot) in enumerate(((near_ref, 0), (near_ref, 2), (away_ref, 1), (away_ref, 3))):
        at = pl.multiple_of((here ^ slot) * slots, slots)
        row = slots * (i % 2)
        out_ref[row : row + slots, :] = total_ref[pl.ds(at, slots), :].astype(out_ref.dtype)


def project(tick, here, there, down):
    rows, units = here.shape[0], here.shape[1] // 2
    width = down.shape[1]
    return pl.pallas_call(
        project_kernel,
        in_specs=[ANY] + [VMEM] * 3,
        out_specs=[VMEM] * 4,
        out_shape=[
            jax.ShapeDtypeStruct((rows // 2, width), F32),
            jax.ShapeDtypeStruct((rows // 2, width), BF16),
            pltpu.VMEM((rows, 4 * units), BF16),
            pltpu.VMEM((8, 128), F32),
        ],
        scratch_shapes=[pltpu.VMEM((rows, width), F32)],
        compiler_params=params(4),
        cost_estimate=cost(0, 1),
        name="project",
    )(tick, here, there, in_vmem(down))


def fold_kernel(near_ref, got_ref, own_ref, onward_ref):
    slots = own_ref.shape[0]
    own_ref[...] = near_ref[:slots, :] + got_ref[:slots, :].astype(F32)
    onward_ref[...] = (near_ref[slots:, :] + got_ref[slots:, :].astype(F32)).astype(BF16)


def fold(near, got):
    slots, width = near.shape[0] // 2, near.shape[1]
    return pl.pallas_call(
        fold_kernel,
        in_specs=[VMEM] * 2,
        out_specs=[VMEM] * 2,
        out_shape=[
            jax.ShapeDtypeStruct((slots, width), F32),
            jax.ShapeDtypeStruct((slots, width), BF16),
        ],
        compiler_params=params(2),
        cost_estimate=cost(0, 1),
        name="fold",
    )(near, got)


def unpack_kernel(after_ref, placing_ref, factor_ref, own_ref, got_ref, out_ref):
    del after_ref
    total = own_ref[...] + got_ref[...].astype(F32)
    scaled = (total * factor_ref[:, 0:1]).astype(BF16)
    out_ref[...] = lax.dot_general(
        placing_ref[...], scaled, (((0,), (0,)), ((), ())), preferred_element_type=F32
    ).astype(BF16)


def unpack(done, placing, factor, own, got):
    slots, rows = placing.shape
    return pl.pallas_call(
        unpack_kernel,
        in_specs=[ANY] + [VMEM] * 4,
        out_specs=VMEM,
        out_shape=jax.ShapeDtypeStruct((rows, own.shape[1]), BF16),
        compiler_params=params(4),
        name="unpack",
    )(done, placing, factor, own, got)


def gram_kernel(scale, flips, *refs):
    count = len(flips)
    pieces = refs[1 : 1 + count]
    wide_ref = refs[1 + count]
    out_ref, done_ref, ring_ref, sems = refs[-4:]
    done_ref[...] = jnp.zeros_like(done_ref)
    units = pieces[0].shape[1]
    depth, _, cut = ring_ref.shape
    copies = []
    for (expert_flip, row_flip), a_ref in zip(flips, pieces):
        at = pl.multiple_of(quarter_of(expert_flip, row_flip) * units, units)
        left = a_ref[...].T
        for n in range(4 * units // cut):
            spot = len(copies) % depth
            if len(copies) >= depth:
                copies[-depth].wait()
            ring_ref[spot] = scale * jnp.dot(
                left, wide_ref[:, cut * n : cut * (n + 1)], preferred_element_type=F32
            )
            copy = pltpu.make_async_copy(
                ring_ref.at[spot], out_ref.at[pl.ds(at, units), pl.ds(cut * n, cut)], sems.at[spot]
            )
            copy.start()
            copies.append(copy)
    for copy in copies[-depth:]:
        copy.wait()


def gram_piece(tick, pieces, flips, wide, gram=None):
    rows, units = pieces[0].shape
    cut, depth = 512, 4
    operands = [tick, *pieces, in_vmem(wide)]
    in_specs = [ANY] + [VMEM] * (len(pieces) + 1)
    aliases = {}
    if gram is not None:
        aliases = {len(operands): 0}
        operands.append(gram)
        in_specs.append(HBM)
    return pl.pallas_call(
        functools.partial(gram_kernel, 2.0 / rows, flips),
        in_specs=in_specs,
        out_specs=[HBM, VMEM],
        out_shape=[
            jax.ShapeDtypeStruct((4 * units, 4 * units), F32),
            pltpu.VMEM((8, 128), F32),
        ],
        input_output_aliases=aliases,
        scratch_shapes=[
            pltpu.VMEM((depth, units, cut), F32),
            pltpu.SemaphoreType.DMA((depth,)),
        ],
        compiler_params=params(10),
        cost_estimate=cost(8 * rows * units * units * len(pieces), 16 * units * units * len(pieces)),
        name="gram",
    )(*operands)


def swap(value, axis):
    return lax.ppermute(value, axis, [(0, 1), (1, 0)])


def across(value, slot):
    return lax.ppermute(value, "col", [(i, i ^ slot) for i in range(4)])


def on_device(tokens, routes, route_weight, pad_mask, gate_up, down):
    depth = tokens.shape[1]
    units = gate_up.shape[2]
    lanes = 128
    chunks = 2
    weights = gate_up.reshape(depth, 2, units // lanes, lanes).transpose(0, 2, 1, 3)

    packed, placing, factor = pack(tokens, routes.T, pad_mask[None, :], route_weight.T)
    lefts = [packed] + [across(packed, slot) for slot in (1, 2, 3)]
    grouped = regroup(packed, weights)

    first_sent, wide = preacts_of(lefts, grouped, 1, 0, chunks)
    (last_sent,) = preacts_of([wide], grouped, 1, 1, chunks)
    got = [swap(first_sent, "row"), swap(last_sent, "row")]
    stays, got_x = [], []
    for h in range(chunks):
        (kept,) = preacts_of([wide], grouped, 0, h, chunks)
        leaves, stay = leave(kept, got[h])
        wide, leaves = tie(wide, leaves)
        stays.append(stay)
        got_x.append(swap(leaves, "expert"))
    down_held, tick = fetch(wide, down)
    tick, got_x[0] = tie(tick, got_x[0])
    (hidden_a,) = act(tick, stays[0], got_x[0])

    z2a = across(hidden_a, 2)
    z1a = across(hidden_a, 1)
    tick, got_x[1], hidden_a = tie(tick, got_x[1], hidden_a)
    hidden_b, hidden = act(tick, stays[1], got_x[1], hidden_a)
    hidden_x = swap(hidden, "expert")
    tick, z2a, z1a, hidden_b = tie(tick, z2a, z1a, hidden_b)
    z2b = across(hidden_b, 2)
    z3a = across(z2a, 1)
    z1b = across(hidden_b, 1)
    x2a = swap(choose(z2a, z1a), "expert")
    tick, z2b = tie(tick, z2b)
    tick, z3a = tie(tick, z3a)
    tick, z1b = tie(tick, z1b)
    tick, hidden_x = tie(tick, hidden_x)
    tick, x2a = tie(tick, x2a)
    here = join(hidden, hidden_x)
    tick, z2b, leaves, here = tie(tick, z2b, choose(z2b, z1b), here)
    z3b = across(z2b, 1)
    x2b = swap(leaves, "expert")
    there = swap(here, "row")
    tick, there, here = tie(tick, there, here)
    near, away, hidden_c, tick = project(tick, here, there, down_held)
    tick, z3b, away = tie(tick, z3b, away)
    tick, x2b, z3b = tie(tick, x2b, z3b)
    mine, passed, z3 = pick([hidden], [z1a, z1b], [z2a, z2b], [z3a, z3b])
    x3 = lax.ppermute(
        z3,
        ("expert", "col"),
        [(ee * 4 + cc, (1 - ee) * 4 + cc) for ee in range(2) for cc in range(4) if cc // 2 == ee],
    )
    mine_near = swap(passed, "row")
    away = across(away, 1)
    tick, mine_near = tie(tick, mine_near)
    gram, tick = gram_piece(tick, [mine, mine_near], [(0, 0), (0, 1)], hidden_c)
    tick, x3 = tie(tick, x3)
    mine_x, passed, _ = pick([hidden_x], [x2a, x2b], [x2a, x2b], [x3])
    mine_far = swap(passed, "row")
    tick, away = tie(tick, away)
    own, onward = fold(near, away)
    onward = across(onward, 2)
    tick, mine_far = tie(tick, mine_far)
    gram, tick = gram_piece(tick, [mine_x, mine_far], [(1, 0), (1, 1)], hidden_c, gram)
    return (unpack(tick, placing, factor, own, onward), gram)


def solution(mesh):
    in_specs = (
        P(("parts", "col"), ("expert", "row")),
        P(("parts", "col"), None),
        P(("parts", "col"), None),
        P(("parts", "col")),
        P(("expert", "row"), None, "col"),
        P("col", ("expert", "row")),
    )
    out_specs = (P(("parts", "col"), ("expert", "row")), P(("parts", "expert", "row"), "col"))
    small = mesh.shape["expert"] == 2 and mesh.shape["row"] == 2 and mesh.shape["col"] == 4
    return jax.shard_map(
        on_device if small else on_any_device,
        mesh=mesh,
        in_specs=in_specs,
        out_specs=out_specs,
        check_vma=False,
    )
```

```python
import functools

import jax
import jax.numpy as jnp
from jax import lax
from jax.experimental import pallas as pl
from jax.experimental.pallas import tpu as pltpu
from jax.sharding import PartitionSpec as P

F32 = jnp.float32
BF16 = jnp.bfloat16
MIB = 1 << 20


def spread(value, axis, source):
    kept = jnp.where(lax.axis_index(axis) == source, value, 0).astype(value.dtype)
    return lax.psum(kept, axis)


def activate(preacts):
    return (jax.nn.silu(preacts[:, 0, :]) * preacts[:, 1, :]).astype(jnp.bfloat16)


def on_any_device(tokens, routes, route_weight, pad_mask, gate_up, down):
    group_rows = tokens.shape[0]
    slot_count = group_rows // 4
    names_zero = routes == 0
    routed = jnp.any(names_zero, axis=1)
    live_rows = routed & (pad_mask == 1)
    factor = jnp.sum(
        jnp.where(names_zero, route_weight, jnp.float32(0.0)), axis=1
    ) * live_rows.astype(jnp.float32)
    position = jnp.cumsum(routed.astype(jnp.int32)) - 1
    slot_ids = lax.broadcasted_iota(jnp.int32, (slot_count, group_rows), 0)
    placing = ((position[None, :] == slot_ids) & routed[None, :]).astype(jnp.bfloat16)
    masked = tokens * live_rows.astype(jnp.bfloat16)[:, None]
    packed = jnp.dot(placing, masked, preferred_element_type=jnp.float32).astype(jnp.bfloat16)
    gathered = lax.all_gather(packed, "col", axis=0, tiled=True)
    anchor = lax.axis_index(("expert", "row"))
    preacts = lax.psum(
        jnp.einsum("rd,dgf->rgf", gathered, gate_up, preferred_element_type=jnp.float32),
        ("expert", "row"),
    )
    hidden = activate(preacts)
    mirrored = spread(hidden, "col", anchor)
    gram_block = lax.dot_general(
        mirrored, hidden, (((0,), (0,)), ((), ())), preferred_element_type=jnp.float32
    )
    gram_block = gram_block * jnp.float32(2.0 / hidden.shape[0])
    returned = lax.psum_scatter(
        jnp.dot(hidden, down, preferred_element_type=jnp.float32),
        "col",
        scatter_dimension=0,
        tiled=True,
    )
    unpacked = lax.dot_general(
        placing.astype(jnp.float32),
        returned,
        (((0,), (0,)), ((), ())),
        precision=lax.Precision.HIGHEST,
        preferred_element_type=jnp.float32,
    )
    expert_out = (unpacked * factor[:, None]).astype(jnp.bfloat16)
    return (expert_out, gram_block)


def cost(flops, moved):
    return pl.CostEstimate(flops=int(flops), bytes_accessed=int(moved), transcendentals=0)


def params(mib):
    return pltpu.CompilerParams(vmem_limit_bytes=mib * MIB)


VMEM = pl.BlockSpec(memory_space=pltpu.VMEM)
HBM = pl.BlockSpec(memory_space=pltpu.HBM)
SMEM = pl.BlockSpec(memory_space=pltpu.SMEM)
ANY = pl.BlockSpec(memory_space=pl.ANY)


def in_vmem(value):
    return pltpu.with_memory_space_constraint(value, pltpu.VMEM)


def in_hbm(value):
    return pltpu.with_memory_space_constraint(value, pltpu.HBM)


def quarter_of(expert_flip, row_flip):
    return (lax.axis_index("expert") ^ expert_flip) * 2 + (lax.axis_index("row") ^ row_flip)


def tie(*values):
    return lax.optimization_barrier(values)


def pack_kernel(
    tokens_ref, routes_ref, pad_ref, weight_ref, packed_ref, placing_ref, factor_ref,
    tokens_held, routes_held, pad_held, weight_held, sems,
):
    pairs = (
        (routes_ref, routes_held),
        (pad_ref, pad_held),
        (weight_ref, weight_held),
        (tokens_ref, tokens_held),
    )
    copies = [pltpu.make_async_copy(a, b, sems.at[i]) for i, (a, b) in enumerate(pairs)]
    for copy in copies:
        copy.start()
    slots, rows = placing_ref.shape
    before = lax.broadcasted_iota(jnp.int32, (rows, rows), 0)
    upto = lax.broadcasted_iota(jnp.int32, (rows, rows), 1)
    tri = jnp.where(before <= upto, 1.0, 0.0).astype(BF16)
    slot_ids = lax.broadcasted_iota(jnp.int32, (slots, rows), 0).astype(F32)
    for copy in copies[:3]:
        copy.wait()
    routes_t = routes_held[...]
    routed = (routes_t[0:1, :] == 0) | (routes_t[1:2, :] == 0)
    live = jnp.where(routed & (pad_held[...] == 1), 1.0, 0.0)
    routed_rows = jnp.broadcast_to(jnp.where(routed, 1.0, 0.0), (8, rows)).astype(BF16)
    position = jnp.dot(routed_rows, tri, preferred_element_type=F32)[0:1, :] - 1.0
    placing = jnp.where(position == slot_ids, jnp.broadcast_to(live, (slots, rows)), 0.0)
    placing_ref[...] = placing.astype(BF16)
    weight = jnp.sum(jnp.where(routes_t == 0, weight_held[...], 0.0), axis=0, keepdims=True)
    factor = jnp.sum(placing * weight, axis=1, keepdims=True)
    factor_ref[...] = jnp.broadcast_to(factor, factor_ref.shape)
    copies[3].wait()
    packed_ref[...] = jnp.dot(
        placing.astype(BF16), tokens_held[...], preferred_element_type=F32
    ).astype(BF16)


def pack(tokens, routes_t, pad, weight_t):
    rows, depth = tokens.shape
    slots = rows // 4
    operands = (tokens, routes_t, pad, weight_t)
    return pl.pallas_call(
        pack_kernel,
        in_specs=[HBM] * 4,
        out_specs=[VMEM] * 3,
        out_shape=[
            pltpu.VMEM((slots, depth), BF16),
            pltpu.VMEM((slots, rows), BF16),
            pltpu.VMEM((slots, 128), F32),
        ],
        scratch_shapes=[pltpu.VMEM(x.shape, x.dtype) for x in operands]
        + [pltpu.SemaphoreType.DMA((4,))],
        compiler_params=params(3),
        name="pack",
    )(*(in_hbm(x) for x in operands))


def regroup_kernel(after_ref, weights_ref, out_ref, sems):
    del after_ref
    copies = [
        pltpu.make_async_copy(weights_ref.at[:, t], out_ref.at[t], sems.at[t])
        for t in range(out_ref.shape[0])
    ]
    for copy in copies:
        copy.start()
    for copy in copies:
        copy.wait()


def regroup(behind, weights):
    depth, tiles, two, lanes = weights.shape
    grouped = pl.pallas_call(
        regroup_kernel,
        in_specs=[ANY, HBM],
        out_specs=VMEM,
        out_shape=pltpu.VMEM((tiles, depth, two, lanes), BF16),
        scratch_shapes=[pltpu.SemaphoreType.DMA((tiles,))],
        compiler_params=params(4),
        cost_estimate=cost(0, 4 * weights.size),
        name="regroup",
    )(behind, in_hbm(weights))
    return grouped.reshape(tiles, depth * two, lanes)


def fetch_kernel(after_ref, down_ref, out_ref, done_ref, sems):
    del after_ref
    parts = sems.shape[0]
    size = down_ref.shape[0] // parts
    copies = [
        pltpu.make_async_copy(
            down_ref.at[pl.ds(size * i, size)], out_ref.at[pl.ds(size * i, size)], sems.at[i]
        )
        for i in range(parts)
    ]
    for copy in copies:
        copy.start()
    done_ref[...] = jnp.zeros_like(done_ref)
    for copy in copies:
        copy.wait()


def fetch(behind, down):
    return pl.pallas_call(
        fetch_kernel,
        in_specs=[ANY, HBM],
        out_specs=[VMEM, VMEM],
        out_shape=[pltpu.VMEM(down.shape, BF16), pltpu.VMEM((8, 128), F32)],
        scratch_shapes=[pltpu.SemaphoreType.DMA((4,))],
        compiler_params=params(4),
        cost_estimate=cost(0, 4 * down.size),
        name="fetch_down",
    )(behind, in_hbm(down))


def widen_tokens(x_refs, wide_ref):
    slots, depth = x_refs[0].shape
    rows = 4 * slots
    here = lax.axis_index("col")
    cut = 256
    into = lax.broadcasted_iota(jnp.int32, (cut, 4 * cut), 1)
    out_of = lax.broadcasted_iota(jnp.int32, (cut, 4 * cut), 0)
    half = jnp.where(into < 2 * cut, 0, 1)
    widen = jnp.where(into - 2 * cut * half == 2 * out_of + half, 1.0, 0.0).astype(BF16)
    for slot, x_ref in enumerate(x_refs):
        stacked = jnp.concatenate(
            [x_ref[:, cut * k : cut * (k + 1)] for k in range(depth // cut)], axis=0
        )
        spaced = jnp.dot(stacked, widen, preferred_element_type=F32).astype(BF16)
        for h in range(2):
            at = pl.multiple_of(h * rows + (here ^ slot) * slots, slots)
            for k in range(depth // cut):
                wide_ref[pl.ds(at, slots), 2 * cut * k : 2 * cut * (k + 1)] = spaced[
                    slots * k : slots * (k + 1), 2 * cut * h : 2 * cut * (h + 1)
                ]


def preact_kernel(first, row_flip, chunk, chunks, *refs):
    if first:
        x0, x1, x2, x3, w_ref, out_ref, wide_ref = refs
        widen_tokens((x0, x1, x2, x3), wide_ref)
    else:
        wide_ref, w_ref, out_ref = refs
    tiles, _, lanes = w_ref.shape
    per = tiles // 4
    take = per // chunks
    at = []
    for i in range(2):
        quarter = quarter_of(1 - i, row_flip)
        at += [quarter * per + chunk * take + j for j in range(take)]
    for j in range(take):
        w = jnp.concatenate([w_ref[at[2 * j]], w_ref[at[2 * j + 1]]], axis=1)
        out_ref[:, 2 * lanes * j : 2 * lanes * (j + 1)] = jnp.dot(
            wide_ref[...], w, preferred_element_type=F32
        )


def preacts_of(lefts, weights, row_flip, chunk, chunks):
    tiles, depth2, lanes = weights.shape
    first = len(lefts) > 1
    rows = 4 * lefts[0].shape[0] if first else lefts[0].shape[0] // 2
    units = tiles // 4 // chunks * lanes
    out_shape = [jax.ShapeDtypeStruct((2 * rows, 2 * units), F32)]
    if first:
        out_shape.append(pltpu.VMEM((2 * rows, depth2), BF16))
    return pl.pallas_call(
        functools.partial(preact_kernel, first, row_flip, chunk, chunks),
        in_specs=[VMEM] * (len(lefts) + 1),
        out_specs=[VMEM] * len(out_shape),
        out_shape=out_shape,
        compiler_params=params(4),
        cost_estimate=cost(8 * rows * depth2 * units, 0),
        name="preacts_" + ("sent" if row_flip else "kept"),
    )(*lefts, in_vmem(weights))


def leave_kernel(kept_ref, got_ref, leaves_ref, stays_ref):
    units = stays_ref.shape[1]
    leaves_ref[...] = (kept_ref[:, :units] + got_ref[:, :units]).astype(BF16)
    stays_ref[...] = kept_ref[:, units:] + got_ref[:, units:]


def leave(kept, got):
    rows, units = kept.shape[0], kept.shape[1] // 2
    return pl.pallas_call(
        leave_kernel,
        in_specs=[VMEM] * 2,
        out_specs=[VMEM] * 2,
        out_shape=[
            jax.ShapeDtypeStruct((rows, units), BF16),
            jax.ShapeDtypeStruct((rows, units), F32),
        ],
        compiler_params=params(2),
        cost_estimate=cost(0, 1),
        name="leave",
    )(kept, got)


def act_kernel(tick_ref, stays_ref, got_ref, *refs):
    del tick_ref
    out_ref = refs[-1]
    rows = out_ref.shape[0]
    gate = stays_ref[:rows, :] + got_ref[:rows, :].astype(F32)
    up = stays_ref[rows:, :] + got_ref[rows:, :].astype(F32)
    hidden = (jax.nn.silu(gate) * up).astype(BF16)
    if len(refs) == 1:
        out_ref[...] = hidden
    else:
        before_ref, part_ref, _ = refs
        done = before_ref.shape[1]
        part_ref[...] = hidden
        out_ref[:, :done] = before_ref[...]
        out_ref[:, done:] = hidden


def act(tick, stays, got, *before):
    rows, units = stays.shape
    shapes = [(rows // 2, units)]
    if before:
        shapes.append((rows // 2, units + before[0].shape[1]))
    return pl.pallas_call(
        act_kernel,
        in_specs=[ANY] + [VMEM] * (2 + len(before)),
        out_specs=[VMEM] * len(shapes),
        out_shape=[jax.ShapeDtypeStruct(shape, BF16) for shape in shapes],
        compiler_params=params(2),
        cost_estimate=cost(0, 1),
        name="act",
    )(tick, stays, got, *before)


def is_near():
    return (lax.axis_index("col") // 2) == lax.axis_index("expert")


def is_odd():
    return (lax.axis_index("col") % 2) != lax.axis_index("row")


def choose_kernel(near_ref, far_ref, out_ref):
    @pl.when(is_near())
    def _():
        out_ref[...] = near_ref[...]

    @pl.when(jnp.logical_not(is_near()))
    def _():
        out_ref[...] = far_ref[...]


def choose(if_near, if_far):
    return pl.pallas_call(
        choose_kernel,
        in_specs=[VMEM] * 2,
        out_specs=VMEM,
        out_shape=jax.ShapeDtypeStruct(if_near.shape, if_near.dtype),
        compiler_params=params(2),
        cost_estimate=cost(0, 1),
        name="choose",
    )(if_near, if_far)


def put(out_ref, parts):
    column = 0
    for part in parts:
        out_ref[:, column : column + part.shape[1]] = part[...]
        column += part.shape[1]


def pick_kernel(counts, *refs):
    slots, at = [], 0
    for count in counts:
        slots.append(refs[at : at + count])
        at += count
    mine_ref, other_ref = refs[at : at + 2]
    for near, pair in ((True, slots[:2]), (False, slots[2:])):
        for odd in (False, True):

            @pl.when((is_near() == near) & (is_odd() == odd))
            def _():
                put(mine_ref, pair[int(odd)])
                put(other_ref, pair[1 - int(odd)])

        if len(refs) > at + 2:

            @pl.when(is_near() == near)
            def _():
                put(refs[-1], (slots[2][-1] if near else slots[1][-1], *slots[3]))


def pick(*slots, leaves=False):
    parts = [part for slot in slots for part in slot]
    rows, units = slots[0][0].shape
    shapes = [(rows, units)] * 2
    if leaves:
        shapes.append((rows, units + slots[1][-1].shape[1]))
    return pl.pallas_call(
        functools.partial(pick_kernel, [len(slot) for slot in slots]),
        in_specs=[VMEM] * len(parts),
        out_specs=[VMEM] * len(shapes),
        out_shape=[jax.ShapeDtypeStruct(shape, BF16) for shape in shapes],
        compiler_params=params(2),
        cost_estimate=cost(0, 1),
        name="pick",
    )(*parts)


def pick_far_kernel(own_ref, first_ref, rest_ref, mine_ref, other_ref):
    units = first_ref.shape[1]

    def fill(out_ref, slot):
        if slot == 0:
            out_ref[...] = own_ref[...]
        elif slot == 3:
            out_ref[...] = rest_ref[:, units:]
        else:
            out_ref[:, :units] = first_ref[...]
            out_ref[:, units:] = rest_ref[:, :units]

    for near, pair in ((True, (0, 1)), (False, (2, 3))):
        for odd in (False, True):

            @pl.when((is_near() == near) & (is_odd() == odd))
            def _():
                fill(mine_ref, pair[int(odd)])
                fill(other_ref, pair[1 - int(odd)])


def pick_far(own, first, rest):
    same = jax.ShapeDtypeStruct(own.shape, BF16)
    return pl.pallas_call(
        pick_far_kernel,
        in_specs=[VMEM] * 3,
        out_specs=[VMEM] * 2,
        out_shape=[same] * 2,
        compiler_params=params(2),
        cost_estimate=cost(0, 1),
        name="pick_far",
    )(own, first, rest)


def join_kernel(left_ref, right_ref, out_ref):
    units = left_ref.shape[1]
    out_ref[:, :units] = left_ref[...]
    out_ref[:, units:] = right_ref[...]


def join(left, right):
    rows, units = left.shape
    return pl.pallas_call(
        join_kernel,
        in_specs=[VMEM] * 2,
        out_specs=VMEM,
        out_shape=jax.ShapeDtypeStruct((rows, 2 * units), left.dtype),
        compiler_params=params(2),
        cost_estimate=cost(0, 1),
        name="join",
    )(left, right)


def project_kernel(tick_ref, here_ref, there_ref, down_ref, near_ref, away_ref, wide_ref, done_ref, total_ref):
    del tick_ref
    units = here_ref.shape[1] // 2
    for row_flip, pair_ref in enumerate((here_ref, there_ref)):
        for expert_flip in range(2):
            at = pl.multiple_of(quarter_of(expert_flip, row_flip) * units, units)
            wide_ref[:, pl.ds(at, units)] = pair_ref[:, units * expert_flip : units * (expert_flip + 1)]
    done_ref[...] = jnp.zeros_like(done_ref)
    width = near_ref.shape[1]
    slots = near_ref.shape[0] // 2
    cut = 512
    for n in range(width // cut):
        total_ref[:, cut * n : cut * (n + 1)] = jnp.dot(
            wide_ref[...], down_ref[:, cut * n : cut * (n + 1)], preferred_element_type=F32
        )
    here = lax.axis_index("col")
    for i, (out_ref, slot) in enumerate(((near_ref, 0), (near_ref, 2), (away_ref, 1), (away_ref, 3))):
        at = pl.multiple_of((here ^ slot) * slots, slots)
        row = slots * (i % 2)
        out_ref[row : row + slots, :] = total_ref[pl.ds(at, slots), :].astype(out_ref.dtype)


def project(tick, here, there, down):
    rows, units = here.shape[0], here.shape[1] // 2
    width = down.shape[1]
    return pl.pallas_call(
        project_kernel,
        in_specs=[ANY] + [VMEM] * 3,
        out_specs=[VMEM] * 4,
        out_shape=[
            jax.ShapeDtypeStruct((rows // 2, width), F32),
            jax.ShapeDtypeStruct((rows // 2, width), BF16),
            pltpu.VMEM((rows, 4 * units), BF16),
            pltpu.VMEM((8, 128), F32),
        ],
        scratch_shapes=[pltpu.VMEM((rows, width), F32)],
        compiler_params=params(4),
        cost_estimate=cost(0, 1),
        name="project",
    )(tick, here, there, in_vmem(down))


def fold_kernel(near_ref, got_ref, own_ref, onward_ref):
    slots = own_ref.shape[0]
    own_ref[...] = near_ref[:slots, :] + got_ref[:slots, :].astype(F32)
    onward_ref[...] = (near_ref[slots:, :] + got_ref[slots:, :].astype(F32)).astype(BF16)


def fold(near, got):
    slots, width = near.shape[0] // 2, near.shape[1]
    return pl.pallas_call(
        fold_kernel,
        in_specs=[VMEM] * 2,
        out_specs=[VMEM] * 2,
        out_shape=[
            jax.ShapeDtypeStruct((slots, width), F32),
            jax.ShapeDtypeStruct((slots, width), BF16),
        ],
        compiler_params=params(2),
        cost_estimate=cost(0, 1),
        name="fold",
    )(near, got)


def unpack_kernel(after_ref, placing_ref, factor_ref, own_ref, got_ref, out_ref):
    del after_ref
    total = own_ref[...] + got_ref[...].astype(F32)
    scaled = (total * factor_ref[:, 0:1]).astype(BF16)
    out_ref[...] = lax.dot_general(
        placing_ref[...], scaled, (((0,), (0,)), ((), ())), preferred_element_type=F32
    ).astype(BF16)


def unpack(done, placing, factor, own, got):
    slots, rows = placing.shape
    return pl.pallas_call(
        unpack_kernel,
        in_specs=[ANY] + [VMEM] * 4,
        out_specs=VMEM,
        out_shape=jax.ShapeDtypeStruct((rows, own.shape[1]), BF16),
        compiler_params=params(4),
        name="unpack",
    )(done, placing, factor, own, got)


def gram_kernel(scale, flips, *refs):
    count = len(flips)
    pieces = refs[1 : 1 + count]
    wide_ref = refs[1 + count]
    out_ref, done_ref, ring_ref, sems = refs[-4:]
    done_ref[...] = jnp.zeros_like(done_ref)
    units = pieces[0].shape[1]
    depth, _, cut = ring_ref.shape
    copies = []
    for (expert_flip, row_flip), a_ref in zip(flips, pieces):
        at = pl.multiple_of(quarter_of(expert_flip, row_flip) * units, units)
        left = a_ref[...].T
        for n in range(4 * units // cut):
            spot = len(copies) % depth
            if len(copies) >= depth:
                copies[-depth].wait()
            ring_ref[spot] = scale * jnp.dot(
                left, wide_ref[:, cut * n : cut * (n + 1)], preferred_element_type=F32
            )
            copy = pltpu.make_async_copy(
                ring_ref.at[spot], out_ref.at[pl.ds(at, units), pl.ds(cut * n, cut)], sems.at[spot]
            )
            copy.start()
            copies.append(copy)
    for copy in copies[-depth:]:
        copy.wait()


def gram_piece(tick, pieces, flips, wide, gram=None):
    rows, units = pieces[0].shape
    cut, depth = 512, 4
    operands = [tick, *pieces, in_vmem(wide)]
    in_specs = [ANY] + [VMEM] * (len(pieces) + 1)
    aliases = {}
    if gram is not None:
        aliases = {len(operands): 0}
        operands.append(gram)
        in_specs.append(HBM)
    return pl.pallas_call(
        functools.partial(gram_kernel, 2.0 / rows, flips),
        in_specs=in_specs,
        out_specs=[HBM, VMEM],
        out_shape=[
            jax.ShapeDtypeStruct((4 * units, 4 * units), F32),
            pltpu.VMEM((8, 128), F32),
        ],
        input_output_aliases=aliases,
        scratch_shapes=[
            pltpu.VMEM((depth, units, cut), F32),
            pltpu.SemaphoreType.DMA((depth,)),
        ],
        compiler_params=params(10),
        cost_estimate=cost(8 * rows * units * units * len(pieces), 16 * units * units * len(pieces)),
        name="gram",
    )(*operands)


def swap(value, axis):
    return lax.ppermute(value, axis, [(0, 1), (1, 0)])


def across(value, slot):
    return lax.ppermute(value, "col", [(i, i ^ slot) for i in range(4)])


def on_device(tokens, routes, route_weight, pad_mask, gate_up, down):
    depth = tokens.shape[1]
    units = gate_up.shape[2]
    lanes = 128
    chunks = 2
    weights = gate_up.reshape(depth, 2, units // lanes, lanes).transpose(0, 2, 1, 3)

    packed, placing, factor = pack(tokens, routes.T, pad_mask[None, :], route_weight.T)
    lefts = [packed] + [across(packed, slot) for slot in (1, 2, 3)]
    grouped = regroup(packed, weights)

    first_sent, wide = preacts_of(lefts, grouped, 1, 0, chunks)
    (last_sent,) = preacts_of([wide], grouped, 1, 1, chunks)
    got = [swap(first_sent, "row"), swap(last_sent, "row")]
    stays, got_x = [], []
    for h in range(chunks):
        (kept,) = preacts_of([wide], grouped, 0, h, chunks)
        leaves, stay = leave(kept, got[h])
        wide, leaves = tie(wide, leaves)
        stays.append(stay)
        got_x.append(swap(leaves, "expert"))
    down_held, tick = fetch(wide, down)
    tick, got_x[0] = tie(tick, got_x[0])
    (hidden_a,) = act(tick, stays[0], got_x[0])

    z2a = across(hidden_a, 2)
    z1a = across(hidden_a, 1)
    tick, got_x[1], hidden_a = tie(tick, got_x[1], hidden_a)
    hidden_b, hidden = act(tick, stays[1], got_x[1], hidden_a)
    hidden_x = swap(hidden, "expert")
    tick, z2a, z1a, hidden_b = tie(tick, z2a, z1a, hidden_b)
    z2b = across(hidden_b, 2)
    z3a = across(z2a, 1)
    z1b = across(hidden_b, 1)
    x2a = swap(choose(z2a, z1a), "expert")
    tick, z2b = tie(tick, z2b)
    tick, z3a = tie(tick, z3a)
    tick, z1b = tie(tick, z1b)
    tick, hidden_x = tie(tick, hidden_x)
    tick, x2a = tie(tick, x2a)
    here = join(hidden, hidden_x)
    tick, z2b, here = tie(tick, z2b, here)
    z3b = across(z2b, 1)
    there = swap(here, "row")
    tick, there, here = tie(tick, there, here)
    near, away, hidden_c, tick = project(tick, here, there, down_held)
    tick, z3b, away = tie(tick, z3b, away)
    mine, passed, leaves = pick([hidden], [z1a, z1b], [z2a, z2b], [z3a, z3b], leaves=True)
    rest = swap(leaves, "expert")
    mine_near = swap(passed, "row")
    away = across(away, 1)
    tick, mine_near = tie(tick, mine_near)
    gram, tick = gram_piece(tick, [mine, mine_near], [(0, 0), (0, 1)], hidden_c)
    tick, rest = tie(tick, rest)
    mine_x, passed = pick_far(hidden_x, x2a, rest)
    mine_far = swap(passed, "row")
    tick, away = tie(tick, away)
    own, onward = fold(near, away)
    onward = across(onward, 2)
    tick, mine_far = tie(tick, mine_far)
    gram, tick = gram_piece(tick, [mine_x, mine_far], [(1, 0), (1, 1)], hidden_c, gram)
    return (unpack(tick, placing, factor, own, onward), gram)


def solution(mesh):
    in_specs = (
        P(("parts", "col"), ("expert", "row")),
        P(("parts", "col"), None),
        P(("parts", "col"), None),
        P(("parts", "col")),
        P(("expert", "row"), None, "col"),
        P("col", ("expert", "row")),
    )
    out_specs = (P(("parts", "col"), ("expert", "row")), P(("parts", "expert", "row"), "col"))
    small = mesh.shape["expert"] == 2 and mesh.shape["row"] == 2 and mesh.shape["col"] == 4
    return jax.shard_map(
        on_device if small else on_any_device,
        mesh=mesh,
        in_specs=in_specs,
        out_specs=out_specs,
        check_vma=False,
    )
```

```python
import functools

import jax
import jax.numpy as jnp
from jax import lax
from jax.experimental import pallas as pl
from jax.experimental.pallas import tpu as pltpu
from jax.sharding import PartitionSpec as P

F32 = jnp.float32
BF16 = jnp.bfloat16
MIB = 1 << 20


def spread(value, axis, source):
    kept = jnp.where(lax.axis_index(axis) == source, value, 0).astype(value.dtype)
    return lax.psum(kept, axis)


def activate(preacts):
    return (jax.nn.silu(preacts[:, 0, :]) * preacts[:, 1, :]).astype(jnp.bfloat16)


def on_any_device(tokens, routes, route_weight, pad_mask, gate_up, down):
    group_rows = tokens.shape[0]
    slot_count = group_rows // 4
    names_zero = routes == 0
    routed = jnp.any(names_zero, axis=1)
    live_rows = routed & (pad_mask == 1)
    factor = jnp.sum(
        jnp.where(names_zero, route_weight, jnp.float32(0.0)), axis=1
    ) * live_rows.astype(jnp.float32)
    position = jnp.cumsum(routed.astype(jnp.int32)) - 1
    slot_ids = lax.broadcasted_iota(jnp.int32, (slot_count, group_rows), 0)
    placing = ((position[None, :] == slot_ids) & routed[None, :]).astype(jnp.bfloat16)
    masked = tokens * live_rows.astype(jnp.bfloat16)[:, None]
    packed = jnp.dot(placing, masked, preferred_element_type=jnp.float32).astype(jnp.bfloat16)
    gathered = lax.all_gather(packed, "col", axis=0, tiled=True)
    anchor = lax.axis_index(("expert", "row"))
    preacts = lax.psum(
        jnp.einsum("rd,dgf->rgf", gathered, gate_up, preferred_element_type=jnp.float32),
        ("expert", "row"),
    )
    hidden = activate(preacts)
    mirrored = spread(hidden, "col", anchor)
    gram_block = lax.dot_general(
        mirrored, hidden, (((0,), (0,)), ((), ())), preferred_element_type=jnp.float32
    )
    gram_block = gram_block * jnp.float32(2.0 / hidden.shape[0])
    returned = lax.psum_scatter(
        jnp.dot(hidden, down, preferred_element_type=jnp.float32),
        "col",
        scatter_dimension=0,
        tiled=True,
    )
    unpacked = lax.dot_general(
        placing.astype(jnp.float32),
        returned,
        (((0,), (0,)), ((), ())),
        precision=lax.Precision.HIGHEST,
        preferred_element_type=jnp.float32,
    )
    expert_out = (unpacked * factor[:, None]).astype(jnp.bfloat16)
    return (expert_out, gram_block)


def cost(flops, moved):
    return pl.CostEstimate(flops=int(flops), bytes_accessed=int(moved), transcendentals=0)


def params(mib):
    return pltpu.CompilerParams(vmem_limit_bytes=mib * MIB)


VMEM = pl.BlockSpec(memory_space=pltpu.VMEM)
HBM = pl.BlockSpec(memory_space=pltpu.HBM)
SMEM = pl.BlockSpec(memory_space=pltpu.SMEM)
ANY = pl.BlockSpec(memory_space=pl.ANY)


def in_vmem(value):
    return pltpu.with_memory_space_constraint(value, pltpu.VMEM)


def in_hbm(value):
    return pltpu.with_memory_space_constraint(value, pltpu.HBM)


def quarter_of(expert_flip, row_flip):
    return (lax.axis_index("expert") ^ expert_flip) * 2 + (lax.axis_index("row") ^ row_flip)


def tie(*values):
    return lax.optimization_barrier(values)


def pack_kernel(
    tokens_ref, routes_ref, pad_ref, weight_ref, packed_ref, placing_ref, factor_ref,
    tokens_held, routes_held, pad_held, weight_held, sems,
):
    pairs = (
        (routes_ref, routes_held),
        (pad_ref, pad_held),
        (weight_ref, weight_held),
        (tokens_ref, tokens_held),
    )
    copies = [pltpu.make_async_copy(a, b, sems.at[i]) for i, (a, b) in enumerate(pairs)]
    for copy in copies:
        copy.start()
    slots, rows = placing_ref.shape
    before = lax.broadcasted_iota(jnp.int32, (rows, rows), 0)
    upto = lax.broadcasted_iota(jnp.int32, (rows, rows), 1)
    tri = jnp.where(before <= upto, 1.0, 0.0).astype(BF16)
    slot_ids = lax.broadcasted_iota(jnp.int32, (slots, rows), 0).astype(F32)
    for copy in copies[:3]:
        copy.wait()
    routes_t = routes_held[...]
    routed = (routes_t[0:1, :] == 0) | (routes_t[1:2, :] == 0)
    live = jnp.where(routed & (pad_held[...] == 1), 1.0, 0.0)
    routed_rows = jnp.broadcast_to(jnp.where(routed, 1.0, 0.0), (8, rows)).astype(BF16)
    position = jnp.dot(routed_rows, tri, preferred_element_type=F32)[0:1, :] - 1.0
    placing = jnp.where(position == slot_ids, jnp.broadcast_to(live, (slots, rows)), 0.0)
    placing_ref[...] = placing.astype(BF16)
    weight = jnp.sum(jnp.where(routes_t == 0, weight_held[...], 0.0), axis=0, keepdims=True)
    factor = jnp.sum(placing * weight, axis=1, keepdims=True)
    factor_ref[...] = jnp.broadcast_to(factor, factor_ref.shape)
    copies[3].wait()
    packed_ref[...] = jnp.dot(
        placing.astype(BF16), tokens_held[...], preferred_element_type=F32
    ).astype(BF16)


def pack(tokens, routes_t, pad, weight_t):
    rows, depth = tokens.shape
    slots = rows // 4
    operands = (tokens, routes_t, pad, weight_t)
    return pl.pallas_call(
        pack_kernel,
        in_specs=[HBM] * 4,
        out_specs=[VMEM] * 3,
        out_shape=[
            pltpu.VMEM((slots, depth), BF16),
            pltpu.VMEM((slots, rows), BF16),
            pltpu.VMEM((slots, 128), F32),
        ],
        scratch_shapes=[pltpu.VMEM(x.shape, x.dtype) for x in operands]
        + [pltpu.SemaphoreType.DMA((4,))],
        compiler_params=params(3),
        name="pack",
    )(*(in_hbm(x) for x in operands))


def regroup_kernel(after_ref, weights_ref, out_ref, sems):
    del after_ref
    copies = [
        pltpu.make_async_copy(weights_ref.at[:, t], out_ref.at[t], sems.at[t])
        for t in range(out_ref.shape[0])
    ]
    for copy in copies:
        copy.start()
    for copy in copies:
        copy.wait()


def regroup(behind, weights):
    depth, tiles, two, lanes = weights.shape
    grouped = pl.pallas_call(
        regroup_kernel,
        in_specs=[ANY, HBM],
        out_specs=VMEM,
        out_shape=pltpu.VMEM((tiles, depth, two, lanes), BF16),
        scratch_shapes=[pltpu.SemaphoreType.DMA((tiles,))],
        compiler_params=params(4),
        cost_estimate=cost(0, 4 * weights.size),
        name="regroup",
    )(behind, in_hbm(weights))
    return grouped.reshape(tiles, depth * two, lanes)


def fetch_kernel(after_ref, down_ref, out_ref, done_ref, sems):
    del after_ref
    parts = sems.shape[0]
    size = down_ref.shape[0] // parts
    copies = [
        pltpu.make_async_copy(
            down_ref.at[pl.ds(size * i, size)], out_ref.at[pl.ds(size * i, size)], sems.at[i]
        )
        for i in range(parts)
    ]
    for copy in copies:
        copy.start()
    done_ref[...] = jnp.zeros_like(done_ref)
    for copy in copies:
        copy.wait()


def fetch(behind, down):
    return pl.pallas_call(
        fetch_kernel,
        in_specs=[ANY, HBM],
        out_specs=[VMEM, VMEM],
        out_shape=[pltpu.VMEM(down.shape, BF16), pltpu.VMEM((8, 128), F32)],
        scratch_shapes=[pltpu.SemaphoreType.DMA((4,))],
        compiler_params=params(4),
        cost_estimate=cost(0, 4 * down.size),
        name="fetch_down",
    )(behind, in_hbm(down))


def widen_tokens(x_refs, wide_ref):
    slots, depth = x_refs[0].shape
    rows = 4 * slots
    here = lax.axis_index("col")
    cut = 256
    into = lax.broadcasted_iota(jnp.int32, (cut, 4 * cut), 1)
    out_of = lax.broadcasted_iota(jnp.int32, (cut, 4 * cut), 0)
    half = jnp.where(into < 2 * cut, 0, 1)
    widen = jnp.where(into - 2 * cut * half == 2 * out_of + half, 1.0, 0.0).astype(BF16)
    for slot, x_ref in enumerate(x_refs):
        stacked = jnp.concatenate(
            [x_ref[:, cut * k : cut * (k + 1)] for k in range(depth // cut)], axis=0
        )
        spaced = jnp.dot(stacked, widen, preferred_element_type=F32).astype(BF16)
        for h in range(2):
            at = pl.multiple_of(h * rows + (here ^ slot) * slots, slots)
            for k in range(depth // cut):
                wide_ref[pl.ds(at, slots), 2 * cut * k : 2 * cut * (k + 1)] = spaced[
                    slots * k : slots * (k + 1), 2 * cut * h : 2 * cut * (h + 1)
                ]


def preact_kernel(first, row_flip, chunk, chunks, *refs):
    if first:
        x0, x1, x2, x3, w_ref, out_ref, wide_ref = refs
        widen_tokens((x0, x1, x2, x3), wide_ref)
    else:
        wide_ref, w_ref, out_ref = refs
    tiles, _, lanes = w_ref.shape
    per = tiles // 4
    take = per // chunks
    at = []
    for i in range(2):
        quarter = quarter_of(1 - i, row_flip)
        at += [quarter * per + chunk * take + j for j in range(take)]
    for j in range(take):
        w = jnp.concatenate([w_ref[at[2 * j]], w_ref[at[2 * j + 1]]], axis=1)
        out_ref[:, 2 * lanes * j : 2 * lanes * (j + 1)] = jnp.dot(
            wide_ref[...], w, preferred_element_type=F32
        )


def preacts_of(lefts, weights, row_flip, chunk, chunks):
    tiles, depth2, lanes = weights.shape
    first = len(lefts) > 1
    rows = 4 * lefts[0].shape[0] if first else lefts[0].shape[0] // 2
    units = tiles // 4 // chunks * lanes
    out_shape = [jax.ShapeDtypeStruct((2 * rows, 2 * units), F32)]
    if first:
        out_shape.append(pltpu.VMEM((2 * rows, depth2), BF16))
    return pl.pallas_call(
        functools.partial(preact_kernel, first, row_flip, chunk, chunks),
        in_specs=[VMEM] * (len(lefts) + 1),
        out_specs=[VMEM] * len(out_shape),
        out_shape=out_shape,
        compiler_params=params(4),
        cost_estimate=cost(8 * rows * depth2 * units, 0),
        name="preacts_" + ("sent" if row_flip else "kept"),
    )(*lefts, in_vmem(weights))


def leave_kernel(kept_ref, got_ref, leaves_ref, stays_ref):
    units = stays_ref.shape[1]
    leaves_ref[...] = (kept_ref[:, :units] + got_ref[:, :units]).astype(BF16)
    stays_ref[...] = kept_ref[:, units:] + got_ref[:, units:]


def leave(kept, got):
    rows, units = kept.shape[0], kept.shape[1] // 2
    return pl.pallas_call(
        leave_kernel,
        in_specs=[VMEM] * 2,
        out_specs=[VMEM] * 2,
        out_shape=[
            jax.ShapeDtypeStruct((rows, units), BF16),
            jax.ShapeDtypeStruct((rows, units), F32),
        ],
        compiler_params=params(2),
        cost_estimate=cost(0, 1),
        name="leave",
    )(kept, got)


def act_kernel(tick_ref, stays_ref, got_ref, *refs):
    del tick_ref
    out_ref = refs[-1]
    rows = out_ref.shape[0]
    gate = stays_ref[:rows, :] + got_ref[:rows, :].astype(F32)
    up = stays_ref[rows:, :] + got_ref[rows:, :].astype(F32)
    hidden = (jax.nn.silu(gate) * up).astype(BF16)
    if len(refs) == 1:
        out_ref[...] = hidden
    else:
        before_ref, part_ref, _ = refs
        done = before_ref.shape[1]
        part_ref[...] = hidden
        out_ref[:, :done] = before_ref[...]
        out_ref[:, done:] = hidden


def act(tick, stays, got, *before):
    rows, units = stays.shape
    shapes = [(rows // 2, units)]
    if before:
        shapes.append((rows // 2, units + before[0].shape[1]))
    return pl.pallas_call(
        act_kernel,
        in_specs=[ANY] + [VMEM] * (2 + len(before)),
        out_specs=[VMEM] * len(shapes),
        out_shape=[jax.ShapeDtypeStruct(shape, BF16) for shape in shapes],
        compiler_params=params(2),
        cost_estimate=cost(0, 1),
        name="act",
    )(tick, stays, got, *before)


def is_near():
    return (lax.axis_index("col") // 2) == lax.axis_index("expert")


def is_odd():
    return (lax.axis_index("col") % 2) != lax.axis_index("row")


def choose_kernel(near_ref, far_ref, out_ref):
    @pl.when(is_near())
    def _():
        out_ref[...] = near_ref[...]

    @pl.when(jnp.logical_not(is_near()))
    def _():
        out_ref[...] = far_ref[...]


def choose(if_near, if_far):
    return pl.pallas_call(
        choose_kernel,
        in_specs=[VMEM] * 2,
        out_specs=VMEM,
        out_shape=jax.ShapeDtypeStruct(if_near.shape, if_near.dtype),
        compiler_params=params(2),
        cost_estimate=cost(0, 1),
        name="choose",
    )(if_near, if_far)


def put(out_ref, parts):
    column = 0
    for part in parts:
        out_ref[:, column : column + part.shape[1]] = part[...]
        column += part.shape[1]


def pick_kernel(counts, *refs):
    slots, at = [], 0
    for count in counts:
        slots.append(refs[at : at + count])
        at += count
    mine_ref, other_ref = refs[at : at + 2]
    for near, pair in ((True, slots[:2]), (False, slots[2:])):
        for odd in (False, True):

            @pl.when((is_near() == near) & (is_odd() == odd))
            def _():
                put(mine_ref, pair[int(odd)])
                put(other_ref, pair[1 - int(odd)])

        if len(refs) > at + 2:

            @pl.when(is_near() == near)
            def _():
                put(refs[-1], (slots[2][-1] if near else slots[1][-1], *slots[3]))


def pick(*slots, leaves=False):
    parts = [part for slot in slots for part in slot]
    rows, units = slots[0][0].shape
    shapes = [(rows, units)] * 2
    if leaves:
        shapes.append((rows, units + slots[1][-1].shape[1]))
    return pl.pallas_call(
        functools.partial(pick_kernel, [len(slot) for slot in slots]),
        in_specs=[VMEM] * len(parts),
        out_specs=[VMEM] * len(shapes),
        out_shape=[jax.ShapeDtypeStruct(shape, BF16) for shape in shapes],
        compiler_params=params(2),
        cost_estimate=cost(0, 1),
        name="pick",
    )(*parts)


def pick_far_kernel(own_ref, first_ref, rest_ref, mine_ref, other_ref):
    units = first_ref.shape[1]

    def fill(out_ref, slot):
        if slot == 0:
            out_ref[...] = own_ref[...]
        elif slot == 3:
            out_ref[...] = rest_ref[:, units:]
        else:
            out_ref[:, :units] = first_ref[...]
            out_ref[:, units:] = rest_ref[:, :units]

    for near, pair in ((True, (0, 1)), (False, (2, 3))):
        for odd in (False, True):

            @pl.when((is_near() == near) & (is_odd() == odd))
            def _():
                fill(mine_ref, pair[int(odd)])
                fill(other_ref, pair[1 - int(odd)])


def pick_far(own, first, rest):
    same = jax.ShapeDtypeStruct(own.shape, BF16)
    return pl.pallas_call(
        pick_far_kernel,
        in_specs=[VMEM] * 3,
        out_specs=[VMEM] * 2,
        out_shape=[same] * 2,
        compiler_params=params(2),
        cost_estimate=cost(0, 1),
        name="pick_far",
    )(own, first, rest)


def join_kernel(left_ref, right_ref, out_ref):
    units = left_ref.shape[1]
    out_ref[:, :units] = left_ref[...]
    out_ref[:, units:] = right_ref[...]


def join(left, right):
    rows, units = left.shape
    return pl.pallas_call(
        join_kernel,
        in_specs=[VMEM] * 2,
        out_specs=VMEM,
        out_shape=jax.ShapeDtypeStruct((rows, 2 * units), left.dtype),
        compiler_params=params(2),
        cost_estimate=cost(0, 1),
        name="join",
    )(left, right)


def project_kernel(tick_ref, here_ref, there_ref, down_ref, near_ref, away_ref, wide_ref, done_ref, total_ref):
    del tick_ref
    units = here_ref.shape[1] // 2
    for row_flip, pair_ref in enumerate((here_ref, there_ref)):
        for expert_flip in range(2):
            at = pl.multiple_of(quarter_of(expert_flip, row_flip) * units, units)
            wide_ref[:, pl.ds(at, units)] = pair_ref[:, units * expert_flip : units * (expert_flip + 1)]
    done_ref[...] = jnp.zeros_like(done_ref)
    width = near_ref.shape[1]
    slots = near_ref.shape[0] // 2
    cut = 512
    for n in range(width // cut):
        total_ref[:, cut * n : cut * (n + 1)] = jnp.dot(
            wide_ref[...], down_ref[:, cut * n : cut * (n + 1)], preferred_element_type=F32
        )
    here = lax.axis_index("col")
    for i, (out_ref, slot) in enumerate(((near_ref, 0), (near_ref, 2), (away_ref, 1), (away_ref, 3))):
        at = pl.multiple_of((here ^ slot) * slots, slots)
        row = slots * (i % 2)
        out_ref[row : row + slots, :] = total_ref[pl.ds(at, slots), :].astype(out_ref.dtype)


def project(tick, here, there, down):
    rows, units = here.shape[0], here.shape[1] // 2
    width = down.shape[1]
    return pl.pallas_call(
        project_kernel,
        in_specs=[ANY] + [VMEM] * 3,
        out_specs=[VMEM] * 4,
        out_shape=[
            jax.ShapeDtypeStruct((rows // 2, width), F32),
            jax.ShapeDtypeStruct((rows // 2, width), BF16),
            pltpu.VMEM((rows, 4 * units), BF16),
            pltpu.VMEM((8, 128), F32),
        ],
        scratch_shapes=[pltpu.VMEM((rows, width), F32)],
        compiler_params=params(4),
        cost_estimate=cost(0, 1),
        name="project",
    )(tick, here, there, in_vmem(down))


def fold_kernel(near_ref, got_ref, own_ref, onward_ref):
    slots = own_ref.shape[0]
    own_ref[...] = near_ref[:slots, :] + got_ref[:slots, :].astype(F32)
    onward_ref[...] = (near_ref[slots:, :] + got_ref[slots:, :].astype(F32)).astype(BF16)


def fold(near, got):
    slots, width = near.shape[0] // 2, near.shape[1]
    return pl.pallas_call(
        fold_kernel,
        in_specs=[VMEM] * 2,
        out_specs=[VMEM] * 2,
        out_shape=[
            jax.ShapeDtypeStruct((slots, width), F32),
            jax.ShapeDtypeStruct((slots, width), BF16),
        ],
        compiler_params=params(2),
        cost_estimate=cost(0, 1),
        name="fold",
    )(near, got)


def unpack_kernel(after_ref, placing_ref, factor_ref, own_ref, got_ref, out_ref):
    del after_ref
    total = own_ref[...] + got_ref[...].astype(F32)
    scaled = (total * factor_ref[:, 0:1]).astype(BF16)
    out_ref[...] = lax.dot_general(
        placing_ref[...], scaled, (((0,), (0,)), ((), ())), preferred_element_type=F32
    ).astype(BF16)


def unpack(done, placing, factor, own, got):
    slots, rows = placing.shape
    return pl.pallas_call(
        unpack_kernel,
        in_specs=[ANY] + [VMEM] * 4,
        out_specs=VMEM,
        out_shape=jax.ShapeDtypeStruct((rows, own.shape[1]), BF16),
        compiler_params=params(4),
        name="unpack",
    )(done, placing, factor, own, got)


def gram_kernel(scale, flips, *refs):
    count = len(flips)
    pieces = refs[1 : 1 + count]
    wide_ref = refs[1 + count]
    out_ref, done_ref, ring_ref, sems = refs[-4:]
    done_ref[...] = jnp.zeros_like(done_ref)
    units = pieces[0].shape[1]
    depth, _, cut = ring_ref.shape
    copies = []
    for (expert_flip, row_flip), a_ref in zip(flips, pieces):
        at = pl.multiple_of(quarter_of(expert_flip, row_flip) * units, units)
        left = a_ref[...].T
        for n in range(4 * units // cut):
            spot = len(copies) % depth
            if len(copies) >= depth:
                copies[-depth].wait()
            ring_ref[spot] = scale * jnp.dot(
                left, wide_ref[:, cut * n : cut * (n + 1)], preferred_element_type=F32
            )
            copy = pltpu.make_async_copy(
                ring_ref.at[spot], out_ref.at[pl.ds(at, units), pl.ds(cut * n, cut)], sems.at[spot]
            )
            copy.start()
            copies.append(copy)
    for copy in copies[-depth:]:
        copy.wait()


def gram_piece(tick, pieces, flips, wide, gram=None):
    rows, units = pieces[0].shape
    cut, depth = 512, 4
    operands = [tick, *pieces, in_vmem(wide)]
    in_specs = [ANY] + [VMEM] * (len(pieces) + 1)
    aliases = {}
    if gram is not None:
        aliases = {len(operands): 0}
        operands.append(gram)
        in_specs.append(HBM)
    return pl.pallas_call(
        functools.partial(gram_kernel, 2.0 / rows, flips),
        in_specs=in_specs,
        out_specs=[HBM, VMEM],
        out_shape=[
            jax.ShapeDtypeStruct((4 * units, 4 * units), F32),
            pltpu.VMEM((8, 128), F32),
        ],
        input_output_aliases=aliases,
        scratch_shapes=[
            pltpu.VMEM((depth, units, cut), F32),
            pltpu.SemaphoreType.DMA((depth,)),
        ],
        compiler_params=params(10),
        cost_estimate=cost(8 * rows * units * units * len(pieces), 16 * units * units * len(pieces)),
        name="gram",
    )(*operands)


def swap(value, axis):
    return lax.ppermute(value, axis, [(0, 1), (1, 0)])


def across(value, slot):
    return lax.ppermute(value, "col", [(i, i ^ slot) for i in range(4)])


def on_device(tokens, routes, route_weight, pad_mask, gate_up, down):
    depth = tokens.shape[1]
    units = gate_up.shape[2]
    lanes = 128
    chunks = 2
    weights = gate_up.reshape(depth, 2, units // lanes, lanes).transpose(0, 2, 1, 3)

    packed, placing, factor = pack(tokens, routes.T, pad_mask[None, :], route_weight.T)
    lefts = [packed] + [across(packed, slot) for slot in (1, 2, 3)]
    grouped = regroup(packed, weights)

    first_sent, wide = preacts_of(lefts, grouped, 1, 0, chunks)
    (last_sent,) = preacts_of([wide], grouped, 1, 1, chunks)
    got = [swap(first_sent, "row"), swap(last_sent, "row")]
    stays, got_x = [], []
    for h in range(chunks):
        (kept,) = preacts_of([wide], grouped, 0, h, chunks)
        leaves, stay = leave(kept, got[h])
        wide, leaves = tie(wide, leaves)
        stays.append(stay)
        got_x.append(swap(leaves, "expert"))
    down_held, tick = fetch(wide, down)
    tick, got_x[0] = tie(tick, got_x[0])
    (hidden_a,) = act(tick, stays[0], got_x[0])

    z2a = across(hidden_a, 2)
    z1a = across(hidden_a, 1)
    tick, got_x[1], hidden_a = tie(tick, got_x[1], hidden_a)
    hidden_b, hidden = act(tick, stays[1], got_x[1], hidden_a)
    hidden_x = swap(hidden, "expert")
    z2b = across(hidden_b, 2)
    tick, z2a = tie(tick, z2a)
    z3a = across(z2a, 1)
    tick, z1a, hidden_b = tie(tick, z1a, hidden_b)
    z1b = across(hidden_b, 1)
    x2a = swap(choose(z2a, z1a), "expert")
    tick, z2b = tie(tick, z2b)
    tick, z3a = tie(tick, z3a)
    tick, z1b = tie(tick, z1b)
    tick, hidden_x = tie(tick, hidden_x)
    tick, x2a = tie(tick, x2a)
    here = join(hidden, hidden_x)
    tick, z2b, here = tie(tick, z2b, here)
    z3b = across(z2b, 1)
    there = swap(here, "row")
    tick, there, here = tie(tick, there, here)
    near, away, hidden_c, tick = project(tick, here, there, down_held)
    tick, z3b, away = tie(tick, z3b, away)
    mine, passed, leaves = pick([hidden], [z1a, z1b], [z2a, z2b], [z3a, z3b], leaves=True)
    rest = swap(leaves, "expert")
    mine_near = swap(passed, "row")
    away = across(away, 1)
    tick, mine_near = tie(tick, mine_near)
    gram, tick = gram_piece(tick, [mine, mine_near], [(0, 0), (0, 1)], hidden_c)
    tick, rest = tie(tick, rest)
    mine_x, passed = pick_far(hidden_x, x2a, rest)
    mine_far = swap(passed, "row")
    tick, away = tie(tick, away)
    own, onward = fold(near, away)
    onward = across(onward, 2)
    tick, mine_far = tie(tick, mine_far)
    gram, tick = gram_piece(tick, [mine_x, mine_far], [(1, 0), (1, 1)], hidden_c, gram)
    return (unpack(tick, placing, factor, own, onward), gram)


def solution(mesh):
    in_specs = (
        P(("parts", "col"), ("expert", "row")),
        P(("parts", "col"), None),
        P(("parts", "col"), None),
        P(("parts", "col")),
        P(("expert", "row"), None, "col"),
        P("col", ("expert", "row")),
    )
    out_specs = (P(("parts", "col"), ("expert", "row")), P(("parts", "expert", "row"), "col"))
    small = mesh.shape["expert"] == 2 and mesh.shape["row"] == 2 and mesh.shape["col"] == 4
    return jax.shard_map(
        on_device if small else on_any_device,
        mesh=mesh,
        in_specs=in_specs,
        out_specs=out_specs,
        check_vma=False,
    )
```

```python
import functools

import jax
import jax.numpy as jnp
from jax import lax
from jax.experimental import pallas as pl
from jax.experimental.pallas import tpu as pltpu
from jax.sharding import PartitionSpec as P

F32 = jnp.float32
BF16 = jnp.bfloat16
MIB = 1 << 20


def spread(value, axis, source):
    kept = jnp.where(lax.axis_index(axis) == source, value, 0).astype(value.dtype)
    return lax.psum(kept, axis)


def activate(preacts):
    return (jax.nn.silu(preacts[:, 0, :]) * preacts[:, 1, :]).astype(jnp.bfloat16)


def on_any_device(tokens, routes, route_weight, pad_mask, gate_up, down):
    group_rows = tokens.shape[0]
    slot_count = group_rows // 4
    names_zero = routes == 0
    routed = jnp.any(names_zero, axis=1)
    live_rows = routed & (pad_mask == 1)
    factor = jnp.sum(
        jnp.where(names_zero, route_weight, jnp.float32(0.0)), axis=1
    ) * live_rows.astype(jnp.float32)
    position = jnp.cumsum(routed.astype(jnp.int32)) - 1
    slot_ids = lax.broadcasted_iota(jnp.int32, (slot_count, group_rows), 0)
    placing = ((position[None, :] == slot_ids) & routed[None, :]).astype(jnp.bfloat16)
    masked = tokens * live_rows.astype(jnp.bfloat16)[:, None]
    packed = jnp.dot(placing, masked, preferred_element_type=jnp.float32).astype(jnp.bfloat16)
    gathered = lax.all_gather(packed, "col", axis=0, tiled=True)
    anchor = lax.axis_index(("expert", "row"))
    preacts = lax.psum(
        jnp.einsum("rd,dgf->rgf", gathered, gate_up, preferred_element_type=jnp.float32),
        ("expert", "row"),
    )
    hidden = activate(preacts)
    mirrored = spread(hidden, "col", anchor)
    gram_block = lax.dot_general(
        mirrored, hidden, (((0,), (0,)), ((), ())), preferred_element_type=jnp.float32
    )
    gram_block = gram_block * jnp.float32(2.0 / hidden.shape[0])
    returned = lax.psum_scatter(
        jnp.dot(hidden, down, preferred_element_type=jnp.float32),
        "col",
        scatter_dimension=0,
        tiled=True,
    )
    unpacked = lax.dot_general(
        placing.astype(jnp.float32),
        returned,
        (((0,), (0,)), ((), ())),
        precision=lax.Precision.HIGHEST,
        preferred_element_type=jnp.float32,
    )
    expert_out = (unpacked * factor[:, None]).astype(jnp.bfloat16)
    return (expert_out, gram_block)


def cost(flops, moved):
    return pl.CostEstimate(flops=int(flops), bytes_accessed=int(moved), transcendentals=0)


def params(mib):
    return pltpu.CompilerParams(vmem_limit_bytes=mib * MIB)


VMEM = pl.BlockSpec(memory_space=pltpu.VMEM)
HBM = pl.BlockSpec(memory_space=pltpu.HBM)
SMEM = pl.BlockSpec(memory_space=pltpu.SMEM)
ANY = pl.BlockSpec(memory_space=pl.ANY)


def in_vmem(value):
    return pltpu.with_memory_space_constraint(value, pltpu.VMEM)


def in_hbm(value):
    return pltpu.with_memory_space_constraint(value, pltpu.HBM)


def quarter_of(expert_flip, row_flip):
    return (lax.axis_index("expert") ^ expert_flip) * 2 + (lax.axis_index("row") ^ row_flip)


def tie(*values):
    return lax.optimization_barrier(values)


def pack_kernel(
    tokens_ref, routes_ref, pad_ref, weight_ref, packed_ref, placing_ref, factor_ref,
    tokens_held, routes_held, pad_held, weight_held, sems,
):
    pairs = (
        (routes_ref, routes_held),
        (pad_ref, pad_held),
        (weight_ref, weight_held),
        (tokens_ref, tokens_held),
    )
    copies = [pltpu.make_async_copy(a, b, sems.at[i]) for i, (a, b) in enumerate(pairs)]
    for copy in copies:
        copy.start()
    slots, rows = placing_ref.shape
    before = lax.broadcasted_iota(jnp.int32, (rows, rows), 0)
    upto = lax.broadcasted_iota(jnp.int32, (rows, rows), 1)
    tri = jnp.where(before <= upto, 1.0, 0.0).astype(BF16)
    slot_ids = lax.broadcasted_iota(jnp.int32, (slots, rows), 0).astype(F32)
    for copy in copies[:3]:
        copy.wait()
    routes_t = routes_held[...]
    routed = (routes_t[0:1, :] == 0) | (routes_t[1:2, :] == 0)
    live = jnp.where(routed & (pad_held[...] == 1), 1.0, 0.0)
    routed_rows = jnp.broadcast_to(jnp.where(routed, 1.0, 0.0), (8, rows)).astype(BF16)
    position = jnp.dot(routed_rows, tri, preferred_element_type=F32)[0:1, :] - 1.0
    placing = jnp.where(position == slot_ids, jnp.broadcast_to(live, (slots, rows)), 0.0)
    placing_ref[...] = placing.astype(BF16)
    weight = jnp.sum(jnp.where(routes_t == 0, weight_held[...], 0.0), axis=0, keepdims=True)
    factor = jnp.sum(placing * weight, axis=1, keepdims=True)
    factor_ref[...] = jnp.broadcast_to(factor, factor_ref.shape)
    copies[3].wait()
    packed_ref[...] = jnp.dot(
        placing.astype(BF16), tokens_held[...], preferred_element_type=F32
    ).astype(BF16)


def pack(tokens, routes_t, pad, weight_t):
    rows, depth = tokens.shape
    slots = rows // 4
    operands = (tokens, routes_t, pad, weight_t)
    return pl.pallas_call(
        pack_kernel,
        in_specs=[HBM] * 4,
        out_specs=[VMEM] * 3,
        out_shape=[
            pltpu.VMEM((slots, depth), BF16),
            pltpu.VMEM((slots, rows), BF16),
            pltpu.VMEM((slots, 128), F32),
        ],
        scratch_shapes=[pltpu.VMEM(x.shape, x.dtype) for x in operands]
        + [pltpu.SemaphoreType.DMA((4,))],
        compiler_params=params(3),
        name="pack",
    )(*(in_hbm(x) for x in operands))


def regroup_kernel(after_ref, weights_ref, out_ref, sems):
    del after_ref
    copies = [
        pltpu.make_async_copy(weights_ref.at[:, t], out_ref.at[t], sems.at[t])
        for t in range(out_ref.shape[0])
    ]
    for copy in copies:
        copy.start()
    for copy in copies:
        copy.wait()


def regroup(behind, weights):
    depth, tiles, two, lanes = weights.shape
    grouped = pl.pallas_call(
        regroup_kernel,
        in_specs=[ANY, HBM],
        out_specs=VMEM,
        out_shape=pltpu.VMEM((tiles, depth, two, lanes), BF16),
        scratch_shapes=[pltpu.SemaphoreType.DMA((tiles,))],
        compiler_params=params(4),
        cost_estimate=cost(0, 4 * weights.size),
        name="regroup",
    )(behind, in_hbm(weights))
    return grouped.reshape(tiles, depth * two, lanes)


def fetch_kernel(after_ref, down_ref, out_ref, done_ref, sems):
    del after_ref
    parts = sems.shape[0]
    size = down_ref.shape[0] // parts
    copies = [
        pltpu.make_async_copy(
            down_ref.at[pl.ds(size * i, size)], out_ref.at[pl.ds(size * i, size)], sems.at[i]
        )
        for i in range(parts)
    ]
    for copy in copies:
        copy.start()
    done_ref[...] = jnp.zeros_like(done_ref)
    for copy in copies:
        copy.wait()


def fetch(behind, down):
    return pl.pallas_call(
        fetch_kernel,
        in_specs=[ANY, HBM],
        out_specs=[VMEM, VMEM],
        out_shape=[pltpu.VMEM(down.shape, BF16), pltpu.VMEM((8, 128), F32)],
        scratch_shapes=[pltpu.SemaphoreType.DMA((4,))],
        compiler_params=params(4),
        cost_estimate=cost(0, 4 * down.size),
        name="fetch_down",
    )(behind, in_hbm(down))


def widen_tokens(x_refs, wide_ref):
    slots, depth = x_refs[0].shape
    rows = 4 * slots
    here = lax.axis_index("col")
    cut = 256
    into = lax.broadcasted_iota(jnp.int32, (cut, 4 * cut), 1)
    out_of = lax.broadcasted_iota(jnp.int32, (cut, 4 * cut), 0)
    half = jnp.where(into < 2 * cut, 0, 1)
    widen = jnp.where(into - 2 * cut * half == 2 * out_of + half, 1.0, 0.0).astype(BF16)
    for slot, x_ref in enumerate(x_refs):
        stacked = jnp.concatenate(
            [x_ref[:, cut * k : cut * (k + 1)] for k in range(depth // cut)], axis=0
        )
        spaced = jnp.dot(stacked, widen, preferred_element_type=F32).astype(BF16)
        for h in range(2):
            at = pl.multiple_of(h * rows + (here ^ slot) * slots, slots)
            for k in range(depth // cut):
                wide_ref[pl.ds(at, slots), 2 * cut * k : 2 * cut * (k + 1)] = spaced[
                    slots * k : slots * (k + 1), 2 * cut * h : 2 * cut * (h + 1)
                ]


def preact_kernel(first, row_flip, chunk, chunks, *refs):
    if first:
        x0, x1, x2, x3, w_ref, out_ref, wide_ref = refs
        widen_tokens((x0, x1, x2, x3), wide_ref)
    else:
        wide_ref, w_ref, out_ref = refs
    tiles, _, lanes = w_ref.shape
    per = tiles // 4
    take = per // chunks
    at = []
    for i in range(2):
        quarter = quarter_of(1 - i, row_flip)
        at += [quarter * per + chunk * take + j for j in range(take)]
    for j in range(take):
        w = jnp.concatenate([w_ref[at[2 * j]], w_ref[at[2 * j + 1]]], axis=1)
        out_ref[:, 2 * lanes * j : 2 * lanes * (j + 1)] = jnp.dot(
            wide_ref[...], w, preferred_element_type=F32
        )


def preacts_of(lefts, weights, row_flip, chunk, chunks):
    tiles, depth2, lanes = weights.shape
    first = len(lefts) > 1
    rows = 4 * lefts[0].shape[0] if first else lefts[0].shape[0] // 2
    units = tiles // 4 // chunks * lanes
    out_shape = [jax.ShapeDtypeStruct((2 * rows, 2 * units), F32)]
    if first:
        out_shape.append(pltpu.VMEM((2 * rows, depth2), BF16))
    return pl.pallas_call(
        functools.partial(preact_kernel, first, row_flip, chunk, chunks),
        in_specs=[VMEM] * (len(lefts) + 1),
        out_specs=[VMEM] * len(out_shape),
        out_shape=out_shape,
        compiler_params=params(4),
        cost_estimate=cost(8 * rows * depth2 * units, 0),
        name="preacts_" + ("sent" if row_flip else "kept"),
    )(*lefts, in_vmem(weights))


def leave_kernel(kept_ref, got_ref, leaves_ref, stays_ref):
    units = stays_ref.shape[1]
    leaves_ref[...] = (kept_ref[:, :units] + got_ref[:, :units]).astype(BF16)
    stays_ref[...] = kept_ref[:, units:] + got_ref[:, units:]


def leave(kept, got):
    rows, units = kept.shape[0], kept.shape[1] // 2
    return pl.pallas_call(
        leave_kernel,
        in_specs=[VMEM] * 2,
        out_specs=[VMEM] * 2,
        out_shape=[
            jax.ShapeDtypeStruct((rows, units), BF16),
            jax.ShapeDtypeStruct((rows, units), F32),
        ],
        compiler_params=params(2),
        cost_estimate=cost(0, 1),
        name="leave",
    )(kept, got)


def act_kernel(tick_ref, stays_ref, got_ref, *refs):
    del tick_ref
    out_ref = refs[-1]
    rows = out_ref.shape[0]
    gate = stays_ref[:rows, :] + got_ref[:rows, :].astype(F32)
    up = stays_ref[rows:, :] + got_ref[rows:, :].astype(F32)
    hidden = (jax.nn.silu(gate) * up).astype(BF16)
    if len(refs) == 1:
        out_ref[...] = hidden
    else:
        before_ref, part_ref, _ = refs
        done = before_ref.shape[1]
        part_ref[...] = hidden
        out_ref[:, :done] = before_ref[...]
        out_ref[:, done:] = hidden


def act(tick, stays, got, *before):
    rows, units = stays.shape
    shapes = [(rows // 2, units)]
    if before:
        shapes.append((rows // 2, units + before[0].shape[1]))
    return pl.pallas_call(
        act_kernel,
        in_specs=[ANY] + [VMEM] * (2 + len(before)),
        out_specs=[VMEM] * len(shapes),
        out_shape=[jax.ShapeDtypeStruct(shape, BF16) for shape in shapes],
        compiler_params=params(2),
        cost_estimate=cost(0, 1),
        name="act",
    )(tick, stays, got, *before)


def relay_kernel(in_ref, out_ref):
    out_ref[...] = in_ref[...]


def relay(value):
    return pl.pallas_call(
        relay_kernel,
        in_specs=[VMEM],
        out_specs=VMEM,
        out_shape=jax.ShapeDtypeStruct(value.shape, value.dtype),
        compiler_params=params(2),
        cost_estimate=cost(1e10, 1),
        name="relay",
    )(value)


def is_near():
    return (lax.axis_index("col") // 2) == lax.axis_index("expert")


def is_odd():
    return (lax.axis_index("col") % 2) != lax.axis_index("row")


def choose_kernel(near_ref, far_ref, out_ref):
    @pl.when(is_near())
    def _():
        out_ref[...] = near_ref[...]

    @pl.when(jnp.logical_not(is_near()))
    def _():
        out_ref[...] = far_ref[...]


def choose(if_near, if_far):
    return pl.pallas_call(
        choose_kernel,
        in_specs=[VMEM] * 2,
        out_specs=VMEM,
        out_shape=jax.ShapeDtypeStruct(if_near.shape, if_near.dtype),
        compiler_params=params(2),
        cost_estimate=cost(1e10, 1),
        name="choose",
    )(if_near, if_far)


def put(out_ref, parts):
    column = 0
    for part in parts:
        out_ref[:, column : column + part.shape[1]] = part[...]
        column += part.shape[1]


def pick_kernel(counts, *refs):
    slots, at = [], 0
    for count in counts:
        slots.append(refs[at : at + count])
        at += count
    mine_ref, other_ref = refs[at : at + 2]
    for near, pair in ((True, slots[:2]), (False, slots[2:])):
        for odd in (False, True):

            @pl.when((is_near() == near) & (is_odd() == odd))
            def _():
                put(mine_ref, pair[int(odd)])
                put(other_ref, pair[1 - int(odd)])

        if len(refs) > at + 2:

            @pl.when(is_near() == near)
            def _():
                put(refs[-1], (slots[2][-1] if near else slots[1][-1], *slots[3]))


def pick(*slots, leaves=False):
    parts = [part for slot in slots for part in slot]
    rows, units = slots[0][0].shape
    shapes = [(rows, units)] * 2
    if leaves:
        shapes.append((rows, units + slots[1][-1].shape[1]))
    return pl.pallas_call(
        functools.partial(pick_kernel, [len(slot) for slot in slots]),
        in_specs=[VMEM] * len(parts),
        out_specs=[VMEM] * len(shapes),
        out_shape=[jax.ShapeDtypeStruct(shape, BF16) for shape in shapes],
        compiler_params=params(2),
        cost_estimate=cost(0, 1),
        name="pick",
    )(*parts)


def pick_far_kernel(own_ref, first_ref, rest_ref, mine_ref, other_ref):
    units = first_ref.shape[1]

    def fill(out_ref, slot):
        if slot == 0:
            out_ref[...] = own_ref[...]
        elif slot == 3:
            out_ref[...] = rest_ref[:, units:]
        else:
            out_ref[:, :units] = first_ref[...]
            out_ref[:, units:] = rest_ref[:, :units]

    for near, pair in ((True, (0, 1)), (False, (2, 3))):
        for odd in (False, True):

            @pl.when((is_near() == near) & (is_odd() == odd))
            def _():
                fill(mine_ref, pair[int(odd)])
                fill(other_ref, pair[1 - int(odd)])


def pick_far(own, first, rest):
    same = jax.ShapeDtypeStruct(own.shape, BF16)
    return pl.pallas_call(
        pick_far_kernel,
        in_specs=[VMEM] * 3,
        out_specs=[VMEM] * 2,
        out_shape=[same] * 2,
        compiler_params=params(2),
        cost_estimate=cost(0, 1),
        name="pick_far",
    )(own, first, rest)


def join_kernel(left_ref, right_ref, out_ref):
    units = left_ref.shape[1]
    out_ref[:, :units] = left_ref[...]
    out_ref[:, units:] = right_ref[...]


def join(left, right):
    rows, units = left.shape
    return pl.pallas_call(
        join_kernel,
        in_specs=[VMEM] * 2,
        out_specs=VMEM,
        out_shape=jax.ShapeDtypeStruct((rows, 2 * units), left.dtype),
        compiler_params=params(2),
        cost_estimate=cost(0, 1),
        name="join",
    )(left, right)


def project_kernel(tick_ref, here_ref, there_ref, down_ref, near_ref, away_ref, wide_ref, done_ref, total_ref):
    del tick_ref
    units = here_ref.shape[1] // 2
    for row_flip, pair_ref in enumerate((here_ref, there_ref)):
        for expert_flip in range(2):
            at = pl.multiple_of(quarter_of(expert_flip, row_flip) * units, units)
            wide_ref[:, pl.ds(at, units)] = pair_ref[:, units * expert_flip : units * (expert_flip + 1)]
    done_ref[...] = jnp.zeros_like(done_ref)
    width = near_ref.shape[1]
    slots = near_ref.shape[0] // 2
    cut = 512
    for n in range(width // cut):
        total_ref[:, cut * n : cut * (n + 1)] = jnp.dot(
            wide_ref[...], down_ref[:, cut * n : cut * (n + 1)], preferred_element_type=F32
        )
    here = lax.axis_index("col")
    for i, (out_ref, slot) in enumerate(((near_ref, 0), (near_ref, 2), (away_ref, 1), (away_ref, 3))):
        at = pl.multiple_of((here ^ slot) * slots, slots)
        row = slots * (i % 2)
        out_ref[row : row + slots, :] = total_ref[pl.ds(at, slots), :].astype(out_ref.dtype)


def project(tick, here, there, down):
    rows, units = here.shape[0], here.shape[1] // 2
    width = down.shape[1]
    return pl.pallas_call(
        project_kernel,
        in_specs=[ANY] + [VMEM] * 3,
        out_specs=[VMEM] * 4,
        out_shape=[
            jax.ShapeDtypeStruct((rows // 2, width), F32),
            jax.ShapeDtypeStruct((rows // 2, width), BF16),
            pltpu.VMEM((rows, 4 * units), BF16),
            pltpu.VMEM((8, 128), F32),
        ],
        scratch_shapes=[pltpu.VMEM((rows, width), F32)],
        compiler_params=params(4),
        cost_estimate=cost(0, 1),
        name="project",
    )(tick, here, there, in_vmem(down))


def fold_kernel(near_ref, got_ref, own_ref, onward_ref):
    slots = own_ref.shape[0]
    own_ref[...] = near_ref[:slots, :] + got_ref[:slots, :].astype(F32)
    onward_ref[...] = (near_ref[slots:, :] + got_ref[slots:, :].astype(F32)).astype(BF16)


def fold(near, got):
    slots, width = near.shape[0] // 2, near.shape[1]
    return pl.pallas_call(
        fold_kernel,
        in_specs=[VMEM] * 2,
        out_specs=[VMEM] * 2,
        out_shape=[
            jax.ShapeDtypeStruct((slots, width), F32),
            jax.ShapeDtypeStruct((slots, width), BF16),
        ],
        compiler_params=params(2),
        cost_estimate=cost(0, 1),
        name="fold",
    )(near, got)


def unpack_kernel(after_ref, placing_ref, factor_ref, own_ref, got_ref, out_ref):
    del after_ref
    total = own_ref[...] + got_ref[...].astype(F32)
    scaled = (total * factor_ref[:, 0:1]).astype(BF16)
    out_ref[...] = lax.dot_general(
        placing_ref[...], scaled, (((0,), (0,)), ((), ())), preferred_element_type=F32
    ).astype(BF16)


def unpack(done, placing, factor, own, got):
    slots, rows = placing.shape
    return pl.pallas_call(
        unpack_kernel,
        in_specs=[ANY] + [VMEM] * 4,
        out_specs=VMEM,
        out_shape=jax.ShapeDtypeStruct((rows, own.shape[1]), BF16),
        compiler_params=params(4),
        name="unpack",
    )(done, placing, factor, own, got)


def gram_kernel(scale, flips, *refs):
    count = len(flips)
    pieces = refs[1 : 1 + count]
    wide_ref = refs[1 + count]
    out_ref, done_ref, ring_ref, sems = refs[-4:]
    done_ref[...] = jnp.zeros_like(done_ref)
    units = pieces[0].shape[1]
    depth, _, cut = ring_ref.shape
    copies = []
    for (expert_flip, row_flip), a_ref in zip(flips, pieces):
        at = pl.multiple_of(quarter_of(expert_flip, row_flip) * units, units)
        left = a_ref[...].T
        for n in range(4 * units // cut):
            spot = len(copies) % depth
            if len(copies) >= depth:
                copies[-depth].wait()
            ring_ref[spot] = scale * jnp.dot(
                left, wide_ref[:, cut * n : cut * (n + 1)], preferred_element_type=F32
            )
            copy = pltpu.make_async_copy(
                ring_ref.at[spot], out_ref.at[pl.ds(at, units), pl.ds(cut * n, cut)], sems.at[spot]
            )
            copy.start()
            copies.append(copy)
    for copy in copies[-depth:]:
        copy.wait()


def gram_piece(tick, pieces, flips, wide, gram=None):
    rows, units = pieces[0].shape
    cut, depth = 512, 4
    operands = [tick, *pieces, in_vmem(wide)]
    in_specs = [ANY] + [VMEM] * (len(pieces) + 1)
    aliases = {}
    if gram is not None:
        aliases = {len(operands): 0}
        operands.append(gram)
        in_specs.append(HBM)
    return pl.pallas_call(
        functools.partial(gram_kernel, 2.0 / rows, flips),
        in_specs=in_specs,
        out_specs=[HBM, VMEM],
        out_shape=[
            jax.ShapeDtypeStruct((4 * units, 4 * units), F32),
            pltpu.VMEM((8, 128), F32),
        ],
        input_output_aliases=aliases,
        scratch_shapes=[
            pltpu.VMEM((depth, units, cut), F32),
            pltpu.SemaphoreType.DMA((depth,)),
        ],
        compiler_params=params(10),
        cost_estimate=cost(8 * rows * units * units * len(pieces), 16 * units * units * len(pieces)),
        name="gram",
    )(*operands)


def swap(value, axis):
    return lax.ppermute(value, axis, [(0, 1), (1, 0)])


def across(value, slot):
    return lax.ppermute(value, "col", [(i, i ^ slot) for i in range(4)])


def on_device(tokens, routes, route_weight, pad_mask, gate_up, down):
    depth = tokens.shape[1]
    units = gate_up.shape[2]
    lanes = 128
    chunks = 2
    weights = gate_up.reshape(depth, 2, units // lanes, lanes).transpose(0, 2, 1, 3)

    packed, placing, factor = pack(tokens, routes.T, pad_mask[None, :], route_weight.T)
    lefts = [packed] + [across(packed, slot) for slot in (1, 2, 3)]
    grouped = regroup(packed, weights)

    first_sent, wide = preacts_of(lefts, grouped, 1, 0, chunks)
    (last_sent,) = preacts_of([wide], grouped, 1, 1, chunks)
    got = [swap(first_sent, "row"), swap(last_sent, "row")]
    stays, got_x = [], []
    for h in range(chunks):
        (kept,) = preacts_of([wide], grouped, 0, h, chunks)
        leaves, stay = leave(kept, got[h])
        wide, leaves = tie(wide, leaves)
        stays.append(stay)
        got_x.append(swap(leaves, "expert"))
    down_held, tick = fetch(wide, down)
    tick, got_x[0] = tie(tick, got_x[0])
    (hidden_a,) = act(tick, stays[0], got_x[0])

    z2a = across(hidden_a, 2)
    z1a = across(hidden_a, 1)
    tick, got_x[1], hidden_a = tie(tick, got_x[1], hidden_a)
    hidden_b, hidden = act(tick, stays[1], got_x[1], hidden_a)
    hidden_x = swap(hidden, "expert")
    z2b = across(hidden_b, 2)
    tick, z2a = tie(tick, z2a)
    z3a = across(relay(z2a), 1)
    tick, z1a, hidden_b = tie(tick, z1a, hidden_b)
    z1b = across(hidden_b, 1)
    x2a = swap(choose(z2a, z1a), "expert")
    tick, z2b = tie(tick, z2b)
    z3b = across(z2b, 1)
    tick, z3a = tie(tick, z3a)
    tick, z1b = tie(tick, z1b)
    here = join(hidden, hidden_x)
    there = swap(here, "row")
    tick, there, here = tie(tick, there, here)
    near, away, hidden_c, tick = project(tick, here, there, down_held)
    tick, x2a = tie(tick, x2a)
    tick, z3b = tie(tick, z3b)
    mine, passed, leaves = pick([hidden], [z1a, z1b], [z2a, z2b], [z3a, z3b], leaves=True)
    rest = swap(leaves, "expert")
    mine_near = swap(passed, "row")
    away = across(away, 1)
    tick, mine_near = tie(tick, mine_near)
    gram, tick = gram_piece(tick, [mine, mine_near], [(0, 0), (0, 1)], hidden_c)
    tick, rest = tie(tick, rest)
    mine_x, passed = pick_far(hidden_x, x2a, rest)
    mine_far = swap(passed, "row")
    tick, away = tie(tick, away)
    own, onward = fold(near, away)
    onward = across(onward, 2)
    tick, mine_far = tie(tick, mine_far)
    gram, tick = gram_piece(tick, [mine_x, mine_far], [(1, 0), (1, 1)], hidden_c, gram)
    return (unpack(tick, placing, factor, own, onward), gram)


def solution(mesh):
    in_specs = (
        P(("parts", "col"), ("expert", "row")),
        P(("parts", "col"), None),
        P(("parts", "col"), None),
        P(("parts", "col")),
        P(("expert", "row"), None, "col"),
        P("col", ("expert", "row")),
    )
    out_specs = (P(("parts", "col"), ("expert", "row")), P(("parts", "expert", "row"), "col"))
    small = mesh.shape["expert"] == 2 and mesh.shape["row"] == 2 and mesh.shape["col"] == 4
    return jax.shard_map(
        on_device if small else on_any_device,
        mesh=mesh,
        in_specs=in_specs,
        out_specs=out_specs,
        check_vma=False,
    )
```

```python
import functools

import jax
import jax.numpy as jnp
from jax import lax
from jax.experimental import pallas as pl
from jax.experimental.pallas import tpu as pltpu
from jax.sharding import PartitionSpec as P

F32 = jnp.float32
BF16 = jnp.bfloat16
MIB = 1 << 20


def spread(value, axis, source):
    kept = jnp.where(lax.axis_index(axis) == source, value, 0).astype(value.dtype)
    return lax.psum(kept, axis)


def activate(preacts):
    return (jax.nn.silu(preacts[:, 0, :]) * preacts[:, 1, :]).astype(jnp.bfloat16)


def on_any_device(tokens, routes, route_weight, pad_mask, gate_up, down):
    group_rows = tokens.shape[0]
    slot_count = group_rows // 4
    names_zero = routes == 0
    routed = jnp.any(names_zero, axis=1)
    live_rows = routed & (pad_mask == 1)
    factor = jnp.sum(
        jnp.where(names_zero, route_weight, jnp.float32(0.0)), axis=1
    ) * live_rows.astype(jnp.float32)
    position = jnp.cumsum(routed.astype(jnp.int32)) - 1
    slot_ids = lax.broadcasted_iota(jnp.int32, (slot_count, group_rows), 0)
    placing = ((position[None, :] == slot_ids) & routed[None, :]).astype(jnp.bfloat16)
    masked = tokens * live_rows.astype(jnp.bfloat16)[:, None]
    packed = jnp.dot(placing, masked, preferred_element_type=jnp.float32).astype(jnp.bfloat16)
    gathered = lax.all_gather(packed, "col", axis=0, tiled=True)
    anchor = lax.axis_index(("expert", "row"))
    preacts = lax.psum(
        jnp.einsum("rd,dgf->rgf", gathered, gate_up, preferred_element_type=jnp.float32),
        ("expert", "row"),
    )
    hidden = activate(preacts)
    mirrored = spread(hidden, "col", anchor)
    gram_block = lax.dot_general(
        mirrored, hidden, (((0,), (0,)), ((), ())), preferred_element_type=jnp.float32
    )
    gram_block = gram_block * jnp.float32(2.0 / hidden.shape[0])
    returned = lax.psum_scatter(
        jnp.dot(hidden, down, preferred_element_type=jnp.float32),
        "col",
        scatter_dimension=0,
        tiled=True,
    )
    unpacked = lax.dot_general(
        placing.astype(jnp.float32),
        returned,
        (((0,), (0,)), ((), ())),
        precision=lax.Precision.HIGHEST,
        preferred_element_type=jnp.float32,
    )
    expert_out = (unpacked * factor[:, None]).astype(jnp.bfloat16)
    return (expert_out, gram_block)


def cost(flops, moved):
    return pl.CostEstimate(flops=int(flops), bytes_accessed=int(moved), transcendentals=0)


def params(mib):
    return pltpu.CompilerParams(vmem_limit_bytes=mib * MIB)


VMEM = pl.BlockSpec(memory_space=pltpu.VMEM)
HBM = pl.BlockSpec(memory_space=pltpu.HBM)
SMEM = pl.BlockSpec(memory_space=pltpu.SMEM)
ANY = pl.BlockSpec(memory_space=pl.ANY)


def in_vmem(value):
    return pltpu.with_memory_space_constraint(value, pltpu.VMEM)


def in_hbm(value):
    return pltpu.with_memory_space_constraint(value, pltpu.HBM)


def quarter_of(expert_flip, row_flip):
    return (lax.axis_index("expert") ^ expert_flip) * 2 + (lax.axis_index("row") ^ row_flip)


def tie(*values):
    return lax.optimization_barrier(values)


def pack_kernel(
    tokens_ref, routes_ref, pad_ref, weight_ref, packed_ref, placing_ref, factor_ref,
    tokens_held, routes_held, pad_held, weight_held, sems,
):
    pairs = (
        (routes_ref, routes_held),
        (pad_ref, pad_held),
        (weight_ref, weight_held),
        (tokens_ref, tokens_held),
    )
    copies = [pltpu.make_async_copy(a, b, sems.at[i]) for i, (a, b) in enumerate(pairs)]
    for copy in copies:
        copy.start()
    slots, rows = placing_ref.shape
    before = lax.broadcasted_iota(jnp.int32, (rows, rows), 0)
    upto = lax.broadcasted_iota(jnp.int32, (rows, rows), 1)
    tri = jnp.where(before <= upto, 1.0, 0.0).astype(BF16)
    slot_ids = lax.broadcasted_iota(jnp.int32, (slots, rows), 0).astype(F32)
    for copy in copies[:3]:
        copy.wait()
    routes_t = routes_held[...]
    routed = (routes_t[0:1, :] == 0) | (routes_t[1:2, :] == 0)
    live = jnp.where(routed & (pad_held[...] == 1), 1.0, 0.0)
    routed_rows = jnp.broadcast_to(jnp.where(routed, 1.0, 0.0), (8, rows)).astype(BF16)
    position = jnp.dot(routed_rows, tri, preferred_element_type=F32)[0:1, :] - 1.0
    placing = jnp.where(position == slot_ids, jnp.broadcast_to(live, (slots, rows)), 0.0)
    placing_ref[...] = placing.astype(BF16)
    weight = jnp.sum(jnp.where(routes_t == 0, weight_held[...], 0.0), axis=0, keepdims=True)
    factor = jnp.sum(placing * weight, axis=1, keepdims=True)
    factor_ref[...] = jnp.broadcast_to(factor, factor_ref.shape)
    copies[3].wait()
    packed_ref[...] = jnp.dot(
        placing.astype(BF16), tokens_held[...], preferred_element_type=F32
    ).astype(BF16)


def pack(tokens, routes_t, pad, weight_t):
    rows, depth = tokens.shape
    slots = rows // 4
    operands = (tokens, routes_t, pad, weight_t)
    return pl.pallas_call(
        pack_kernel,
        in_specs=[HBM] * 4,
        out_specs=[VMEM] * 3,
        out_shape=[
            pltpu.VMEM((slots, depth), BF16),
            pltpu.VMEM((slots, rows), BF16),
            pltpu.VMEM((slots, 128), F32),
        ],
        scratch_shapes=[pltpu.VMEM(x.shape, x.dtype) for x in operands]
        + [pltpu.SemaphoreType.DMA((4,))],
        compiler_params=params(3),
        name="pack",
    )(*(in_hbm(x) for x in operands))


def regroup_kernel(after_ref, weights_ref, out_ref, sems):
    del after_ref
    copies = [
        pltpu.make_async_copy(weights_ref.at[:, t], out_ref.at[t], sems.at[t])
        for t in range(out_ref.shape[0])
    ]
    for copy in copies:
        copy.start()
    for copy in copies:
        copy.wait()


def regroup(behind, weights):
    depth, tiles, two, lanes = weights.shape
    grouped = pl.pallas_call(
        regroup_kernel,
        in_specs=[ANY, HBM],
        out_specs=VMEM,
        out_shape=pltpu.VMEM((tiles, depth, two, lanes), BF16),
        scratch_shapes=[pltpu.SemaphoreType.DMA((tiles,))],
        compiler_params=params(4),
        cost_estimate=cost(0, 4 * weights.size),
        name="regroup",
    )(behind, in_hbm(weights))
    return grouped.reshape(tiles, depth * two, lanes)


def fetch_kernel(after_ref, down_ref, out_ref, done_ref, sems):
    del after_ref
    parts = sems.shape[0]
    size = down_ref.shape[0] // parts
    copies = [
        pltpu.make_async_copy(
            down_ref.at[pl.ds(size * i, size)], out_ref.at[pl.ds(size * i, size)], sems.at[i]
        )
        for i in range(parts)
    ]
    for copy in copies:
        copy.start()
    done_ref[...] = jnp.zeros_like(done_ref)
    for copy in copies:
        copy.wait()


def fetch(behind, down):
    return pl.pallas_call(
        fetch_kernel,
        in_specs=[ANY, HBM],
        out_specs=[VMEM, VMEM],
        out_shape=[pltpu.VMEM(down.shape, BF16), pltpu.VMEM((8, 128), F32)],
        scratch_shapes=[pltpu.SemaphoreType.DMA((4,))],
        compiler_params=params(4),
        cost_estimate=cost(0, 4 * down.size),
        name="fetch_down",
    )(behind, in_hbm(down))


def widen_tokens(x_refs, wide_ref):
    slots, depth = x_refs[0].shape
    rows = 4 * slots
    here = lax.axis_index("col")
    cut = 256
    into = lax.broadcasted_iota(jnp.int32, (cut, 4 * cut), 1)
    out_of = lax.broadcasted_iota(jnp.int32, (cut, 4 * cut), 0)
    half = jnp.where(into < 2 * cut, 0, 1)
    widen = jnp.where(into - 2 * cut * half == 2 * out_of + half, 1.0, 0.0).astype(BF16)
    for slot, x_ref in enumerate(x_refs):
        stacked = jnp.concatenate(
            [x_ref[:, cut * k : cut * (k + 1)] for k in range(depth // cut)], axis=0
        )
        spaced = jnp.dot(stacked, widen, preferred_element_type=F32).astype(BF16)
        for h in range(2):
            at = pl.multiple_of(h * rows + (here ^ slot) * slots, slots)
            for k in range(depth // cut):
                wide_ref[pl.ds(at, slots), 2 * cut * k : 2 * cut * (k + 1)] = spaced[
                    slots * k : slots * (k + 1), 2 * cut * h : 2 * cut * (h + 1)
                ]


def preact_kernel(first, row_flip, chunk, chunks, *refs):
    if first:
        x0, x1, x2, x3, w_ref, out_ref, wide_ref = refs
        widen_tokens((x0, x1, x2, x3), wide_ref)
    else:
        wide_ref, w_ref, out_ref = refs
    tiles, _, lanes = w_ref.shape
    per = tiles // 4
    take = per // chunks
    at = []
    for i in range(2):
        quarter = quarter_of(1 - i, row_flip)
        at += [quarter * per + chunk * take + j for j in range(take)]
    for j in range(take):
        w = jnp.concatenate([w_ref[at[2 * j]], w_ref[at[2 * j + 1]]], axis=1)
        out_ref[:, 2 * lanes * j : 2 * lanes * (j + 1)] = jnp.dot(
            wide_ref[...], w, preferred_element_type=F32
        )


def preacts_of(lefts, weights, row_flip, chunk, chunks):
    tiles, depth2, lanes = weights.shape
    first = len(lefts) > 1
    rows = 4 * lefts[0].shape[0] if first else lefts[0].shape[0] // 2
    units = tiles // 4 // chunks * lanes
    out_shape = [jax.ShapeDtypeStruct((2 * rows, 2 * units), F32)]
    if first:
        out_shape.append(pltpu.VMEM((2 * rows, depth2), BF16))
    return pl.pallas_call(
        functools.partial(preact_kernel, first, row_flip, chunk, chunks),
        in_specs=[VMEM] * (len(lefts) + 1),
        out_specs=[VMEM] * len(out_shape),
        out_shape=out_shape,
        compiler_params=params(4),
        cost_estimate=cost(8 * rows * depth2 * units, 0),
        name="preacts_" + ("sent" if row_flip else "kept"),
    )(*lefts, in_vmem(weights))


def leave_kernel(kept_ref, got_ref, leaves_ref, stays_ref):
    units = stays_ref.shape[1]
    leaves_ref[...] = (kept_ref[:, :units] + got_ref[:, :units]).astype(BF16)
    stays_ref[...] = kept_ref[:, units:] + got_ref[:, units:]


def leave(kept, got):
    rows, units = kept.shape[0], kept.shape[1] // 2
    return pl.pallas_call(
        leave_kernel,
        in_specs=[VMEM] * 2,
        out_specs=[VMEM] * 2,
        out_shape=[
            jax.ShapeDtypeStruct((rows, units), BF16),
            jax.ShapeDtypeStruct((rows, units), F32),
        ],
        compiler_params=params(2),
        cost_estimate=cost(0, 1),
        name="leave",
    )(kept, got)


def act_kernel(tick_ref, stays_ref, got_ref, *refs):
    del tick_ref
    out_ref = refs[-1]
    rows = out_ref.shape[0]
    gate = stays_ref[:rows, :] + got_ref[:rows, :].astype(F32)
    up = stays_ref[rows:, :] + got_ref[rows:, :].astype(F32)
    hidden = (jax.nn.silu(gate) * up).astype(BF16)
    if len(refs) == 1:
        out_ref[...] = hidden
    else:
        before_ref, part_ref, _ = refs
        done = before_ref.shape[1]
        part_ref[...] = hidden
        out_ref[:, :done] = before_ref[...]
        out_ref[:, done:] = hidden


def act(tick, stays, got, *before):
    rows, units = stays.shape
    shapes = [(rows // 2, units)]
    if before:
        shapes.append((rows // 2, units + before[0].shape[1]))
    return pl.pallas_call(
        act_kernel,
        in_specs=[ANY] + [VMEM] * (2 + len(before)),
        out_specs=[VMEM] * len(shapes),
        out_shape=[jax.ShapeDtypeStruct(shape, BF16) for shape in shapes],
        compiler_params=params(2),
        cost_estimate=cost(0, 1),
        name="act",
    )(tick, stays, got, *before)


def relay_kernel(in_ref, out_ref):
    out_ref[...] = in_ref[...]


def relay(value):
    return pl.pallas_call(
        relay_kernel,
        in_specs=[VMEM],
        out_specs=VMEM,
        out_shape=jax.ShapeDtypeStruct(value.shape, value.dtype),
        compiler_params=params(2),
        cost_estimate=cost(1e10, 1),
        name="relay",
    )(value)


def is_near():
    return (lax.axis_index("col") // 2) == lax.axis_index("expert")


def is_odd():
    return (lax.axis_index("col") % 2) != lax.axis_index("row")


def choose_kernel(near_ref, far_ref, out_ref):
    @pl.when(is_near())
    def _():
        out_ref[...] = near_ref[...]

    @pl.when(jnp.logical_not(is_near()))
    def _():
        out_ref[...] = far_ref[...]


def choose(if_near, if_far):
    return pl.pallas_call(
        choose_kernel,
        in_specs=[VMEM] * 2,
        out_specs=VMEM,
        out_shape=jax.ShapeDtypeStruct(if_near.shape, if_near.dtype),
        compiler_params=params(2),
        cost_estimate=cost(1e10, 1),
        name="choose",
    )(if_near, if_far)


def put(out_ref, parts):
    column = 0
    for part in parts:
        out_ref[:, column : column + part.shape[1]] = part[...]
        column += part.shape[1]


def pick_kernel(counts, *refs):
    slots, at = [], 0
    for count in counts:
        slots.append(refs[at : at + count])
        at += count
    mine_ref, other_ref = refs[at : at + 2]
    for near, pair in ((True, slots[:2]), (False, slots[2:])):
        for odd in (False, True):

            @pl.when((is_near() == near) & (is_odd() == odd))
            def _():
                put(mine_ref, pair[int(odd)])
                put(other_ref, pair[1 - int(odd)])

        if len(refs) > at + 2:

            @pl.when(is_near() == near)
            def _():
                put(refs[-1], (slots[2][-1] if near else slots[1][-1], *slots[3]))


def pick(*slots, leaves=False):
    parts = [part for slot in slots for part in slot]
    rows, units = slots[0][0].shape
    shapes = [(rows, units)] * 2
    if leaves:
        shapes.append((rows, units + slots[1][-1].shape[1]))
    return pl.pallas_call(
        functools.partial(pick_kernel, [len(slot) for slot in slots]),
        in_specs=[VMEM] * len(parts),
        out_specs=[VMEM] * len(shapes),
        out_shape=[jax.ShapeDtypeStruct(shape, BF16) for shape in shapes],
        compiler_params=params(2),
        cost_estimate=cost(0, 1),
        name="pick",
    )(*parts)


def pick_far_kernel(own_ref, first_ref, rest_ref, mine_ref, other_ref):
    units = first_ref.shape[1]

    def fill(out_ref, slot):
        if slot == 0:
            out_ref[...] = own_ref[...]
        elif slot == 3:
            out_ref[...] = rest_ref[:, units:]
        else:
            out_ref[:, :units] = first_ref[...]
            out_ref[:, units:] = rest_ref[:, :units]

    for near, pair in ((True, (0, 1)), (False, (2, 3))):
        for odd in (False, True):

            @pl.when((is_near() == near) & (is_odd() == odd))
            def _():
                fill(mine_ref, pair[int(odd)])
                fill(other_ref, pair[1 - int(odd)])


def pick_far(own, first, rest):
    same = jax.ShapeDtypeStruct(own.shape, BF16)
    return pl.pallas_call(
        pick_far_kernel,
        in_specs=[VMEM] * 3,
        out_specs=[VMEM] * 2,
        out_shape=[same] * 2,
        compiler_params=params(2),
        cost_estimate=cost(0, 1),
        name="pick_far",
    )(own, first, rest)


def join_kernel(left_ref, right_ref, out_ref):
    units = left_ref.shape[1]
    out_ref[:, :units] = left_ref[...]
    out_ref[:, units:] = right_ref[...]


def join(left, right):
    rows, units = left.shape
    return pl.pallas_call(
        join_kernel,
        in_specs=[VMEM] * 2,
        out_specs=VMEM,
        out_shape=jax.ShapeDtypeStruct((rows, 2 * units), left.dtype),
        compiler_params=params(2),
        cost_estimate=cost(0, 1),
        name="join",
    )(left, right)


def project_kernel(tick_ref, here_ref, there_ref, down_ref, near_ref, away_ref, wide_ref, done_ref, total_ref):
    del tick_ref
    units = here_ref.shape[1] // 2
    for row_flip, pair_ref in enumerate((here_ref, there_ref)):
        for expert_flip in range(2):
            at = pl.multiple_of(quarter_of(expert_flip, row_flip) * units, units)
            wide_ref[:, pl.ds(at, units)] = pair_ref[:, units * expert_flip : units * (expert_flip + 1)]
    done_ref[...] = jnp.zeros_like(done_ref)
    width = near_ref.shape[1]
    slots = near_ref.shape[0] // 2
    cut = 512
    for n in range(width // cut):
        total_ref[:, cut * n : cut * (n + 1)] = jnp.dot(
            wide_ref[...], down_ref[:, cut * n : cut * (n + 1)], preferred_element_type=F32
        )
    here = lax.axis_index("col")
    for i, (out_ref, slot) in enumerate(((near_ref, 0), (near_ref, 2), (away_ref, 1), (away_ref, 3))):
        at = pl.multiple_of((here ^ slot) * slots, slots)
        row = slots * (i % 2)
        out_ref[row : row + slots, :] = total_ref[pl.ds(at, slots), :].astype(out_ref.dtype)


def project(tick, here, there, down):
    rows, units = here.shape[0], here.shape[1] // 2
    width = down.shape[1]
    return pl.pallas_call(
        project_kernel,
        in_specs=[ANY] + [VMEM] * 3,
        out_specs=[VMEM] * 4,
        out_shape=[
            jax.ShapeDtypeStruct((rows // 2, width), F32),
            jax.ShapeDtypeStruct((rows // 2, width), BF16),
            pltpu.VMEM((rows, 4 * units), BF16),
            pltpu.VMEM((8, 128), F32),
        ],
        scratch_shapes=[pltpu.VMEM((rows, width), F32)],
        compiler_params=params(4),
        cost_estimate=cost(0, 1),
        name="project",
    )(tick, here, there, in_vmem(down))


def fold_kernel(near_ref, got_ref, own_ref, onward_ref):
    slots = own_ref.shape[0]
    own_ref[...] = near_ref[:slots, :] + got_ref[:slots, :].astype(F32)
    onward_ref[...] = (near_ref[slots:, :] + got_ref[slots:, :].astype(F32)).astype(BF16)


def fold(near, got):
    slots, width = near.shape[0] // 2, near.shape[1]
    return pl.pallas_call(
        fold_kernel,
        in_specs=[VMEM] * 2,
        out_specs=[VMEM] * 2,
        out_shape=[
            jax.ShapeDtypeStruct((slots, width), F32),
            jax.ShapeDtypeStruct((slots, width), BF16),
        ],
        compiler_params=params(2),
        cost_estimate=cost(0, 1),
        name="fold",
    )(near, got)


def unpack_kernel(after_ref, placing_ref, factor_ref, own_ref, got_ref, out_ref):
    del after_ref
    total = own_ref[...] + got_ref[...].astype(F32)
    scaled = (total * factor_ref[:, 0:1]).astype(BF16)
    out_ref[...] = lax.dot_general(
        placing_ref[...], scaled, (((0,), (0,)), ((), ())), preferred_element_type=F32
    ).astype(BF16)


def unpack(done, placing, factor, own, got):
    slots, rows = placing.shape
    return pl.pallas_call(
        unpack_kernel,
        in_specs=[ANY] + [VMEM] * 4,
        out_specs=VMEM,
        out_shape=jax.ShapeDtypeStruct((rows, own.shape[1]), BF16),
        compiler_params=params(4),
        name="unpack",
    )(done, placing, factor, own, got)


def gram_kernel(scale, flips, *refs):
    count = len(flips)
    pieces = refs[1 : 1 + count]
    wide_ref = refs[1 + count]
    out_ref, done_ref, ring_ref, sems = refs[-4:]
    done_ref[...] = jnp.zeros_like(done_ref)
    units = pieces[0].shape[1]
    depth, height, cut = ring_ref.shape
    half = cut // 2
    copies = []
    for (expert_flip, row_flip), a_ref in zip(flips, pieces):
        start = quarter_of(expert_flip, row_flip) * units
        for m in range(units // height):
            rows = pl.ds(pl.multiple_of(start + height * m, height), height)
            left = a_ref[:, height * m : height * (m + 1)].T
            for n in range(4 * units // cut):
                spot = len(copies) % depth
                if len(copies) >= depth:
                    copies[-depth].wait()
                for i in range(2):
                    column = cut * n + half * i
                    ring_ref[spot, :, half * i : half * (i + 1)] = scale * jnp.dot(
                        left, wide_ref[:, column : column + half], preferred_element_type=F32
                    )
                copy = pltpu.make_async_copy(
                    ring_ref.at[spot], out_ref.at[rows, pl.ds(cut * n, cut)], sems.at[spot]
                )
                copy.start()
                copies.append(copy)
    for copy in copies[-depth:]:
        copy.wait()


def gram_piece(tick, pieces, flips, wide, gram=None):
    rows, units = pieces[0].shape
    cut, height, depth = 1024, 256, 6
    operands = [tick, *pieces, in_vmem(wide)]
    in_specs = [ANY] + [VMEM] * (len(pieces) + 1)
    aliases = {}
    if gram is not None:
        aliases = {len(operands): 0}
        operands.append(gram)
        in_specs.append(HBM)
    return pl.pallas_call(
        functools.partial(gram_kernel, 2.0 / rows, flips),
        in_specs=in_specs,
        out_specs=[HBM, VMEM],
        out_shape=[
            jax.ShapeDtypeStruct((4 * units, 4 * units), F32),
            pltpu.VMEM((8, 128), F32),
        ],
        input_output_aliases=aliases,
        scratch_shapes=[
            pltpu.VMEM((depth, height, cut), F32),
            pltpu.SemaphoreType.DMA((depth,)),
        ],
        compiler_params=params(10),
        cost_estimate=cost(8 * rows * units * units * len(pieces), 16 * units * units * len(pieces)),
        name="gram",
    )(*operands)


def swap(value, axis):
    return lax.ppermute(value, axis, [(0, 1), (1, 0)])


def across(value, slot):
    return lax.ppermute(value, "col", [(i, i ^ slot) for i in range(4)])


def on_device(tokens, routes, route_weight, pad_mask, gate_up, down):
    depth = tokens.shape[1]
    units = gate_up.shape[2]
    lanes = 128
    chunks = 2
    weights = gate_up.reshape(depth, 2, units // lanes, lanes).transpose(0, 2, 1, 3)

    packed, placing, factor = pack(tokens, routes.T, pad_mask[None, :], route_weight.T)
    lefts = [packed] + [across(packed, slot) for slot in (1, 2, 3)]
    grouped = regroup(packed, weights)

    first_sent, wide = preacts_of(lefts, grouped, 1, 0, chunks)
    (last_sent,) = preacts_of([wide], grouped, 1, 1, chunks)
    got = [swap(first_sent, "row"), swap(last_sent, "row")]
    stays, got_x = [], []
    for h in range(chunks):
        (kept,) = preacts_of([wide], grouped, 0, h, chunks)
        leaves, stay = leave(kept, got[h])
        wide, leaves = tie(wide, leaves)
        stays.append(stay)
        got_x.append(swap(leaves, "expert"))
    down_held, tick = fetch(wide, down)
    tick, got_x[0] = tie(tick, got_x[0])
    (hidden_a,) = act(tick, stays[0], got_x[0])

    z2a = across(hidden_a, 2)
    z1a = across(hidden_a, 1)
    tick, got_x[1], hidden_a = tie(tick, got_x[1], hidden_a)
    hidden_b, hidden = act(tick, stays[1], got_x[1], hidden_a)
    hidden_x = swap(hidden, "expert")
    z2b = across(hidden_b, 2)
    tick, z2a = tie(tick, z2a)
    z3a = across(relay(z2a), 1)
    tick, z1a, hidden_b = tie(tick, z1a, hidden_b)
    z1b = across(hidden_b, 1)
    x2a = swap(choose(z2a, z1a), "expert")
    tick, z2b = tie(tick, z2b)
    z3b = across(z2b, 1)
    tick, z3a = tie(tick, z3a)
    tick, z1b = tie(tick, z1b)
    here = join(hidden, hidden_x)
    there = swap(here, "row")
    tick, there, here = tie(tick, there, here)
    near, away, hidden_c, tick = project(tick, here, there, down_held)
    tick, x2a = tie(tick, x2a)
    tick, z3b = tie(tick, z3b)
    mine, passed, leaves = pick([hidden], [z1a, z1b], [z2a, z2b], [z3a, z3b], leaves=True)
    rest = swap(leaves, "expert")
    mine_near = swap(passed, "row")
    away = across(away, 1)
    tick, mine_near = tie(tick, mine_near)
    gram, tick = gram_piece(tick, [mine, mine_near], [(0, 0), (0, 1)], hidden_c)
    tick, rest = tie(tick, rest)
    mine_x, passed = pick_far(hidden_x, x2a, rest)
    mine_far = swap(passed, "row")
    tick, away = tie(tick, away)
    own, onward = fold(near, away)
    onward = across(onward, 2)
    tick, mine_far = tie(tick, mine_far)
    gram, tick = gram_piece(tick, [mine_x, mine_far], [(1, 0), (1, 1)], hidden_c, gram)
    return (unpack(tick, placing, factor, own, onward), gram)


def solution(mesh):
    in_specs = (
        P(("parts", "col"), ("expert", "row")),
        P(("parts", "col"), None),
        P(("parts", "col"), None),
        P(("parts", "col")),
        P(("expert", "row"), None, "col"),
        P("col", ("expert", "row")),
    )
    out_specs = (P(("parts", "col"), ("expert", "row")), P(("parts", "expert", "row"), "col"))
    small = mesh.shape["expert"] == 2 and mesh.shape["row"] == 2 and mesh.shape["col"] == 4
    return jax.shard_map(
        on_device if small else on_any_device,
        mesh=mesh,
        in_specs=in_specs,
        out_specs=out_specs,
        check_vma=False,
    )
```

```python
import functools

import jax
import jax.numpy as jnp
from jax import lax
from jax.experimental import pallas as pl
from jax.experimental.pallas import tpu as pltpu
from jax.sharding import PartitionSpec as P

F32 = jnp.float32
BF16 = jnp.bfloat16
MIB = 1 << 20


def spread(value, axis, source):
    kept = jnp.where(lax.axis_index(axis) == source, value, 0).astype(value.dtype)
    return lax.psum(kept, axis)


def activate(preacts):
    return (jax.nn.silu(preacts[:, 0, :]) * preacts[:, 1, :]).astype(jnp.bfloat16)


def on_any_device(tokens, routes, route_weight, pad_mask, gate_up, down):
    group_rows = tokens.shape[0]
    slot_count = group_rows // 4
    names_zero = routes == 0
    routed = jnp.any(names_zero, axis=1)
    live_rows = routed & (pad_mask == 1)
    factor = jnp.sum(
        jnp.where(names_zero, route_weight, jnp.float32(0.0)), axis=1
    ) * live_rows.astype(jnp.float32)
    position = jnp.cumsum(routed.astype(jnp.int32)) - 1
    slot_ids = lax.broadcasted_iota(jnp.int32, (slot_count, group_rows), 0)
    placing = ((position[None, :] == slot_ids) & routed[None, :]).astype(jnp.bfloat16)
    masked = tokens * live_rows.astype(jnp.bfloat16)[:, None]
    packed = jnp.dot(placing, masked, preferred_element_type=jnp.float32).astype(jnp.bfloat16)
    gathered = lax.all_gather(packed, "col", axis=0, tiled=True)
    anchor = lax.axis_index(("expert", "row"))
    preacts = lax.psum(
        jnp.einsum("rd,dgf->rgf", gathered, gate_up, preferred_element_type=jnp.float32),
        ("expert", "row"),
    )
    hidden = activate(preacts)
    mirrored = spread(hidden, "col", anchor)
    gram_block = lax.dot_general(
        mirrored, hidden, (((0,), (0,)), ((), ())), preferred_element_type=jnp.float32
    )
    gram_block = gram_block * jnp.float32(2.0 / hidden.shape[0])
    returned = lax.psum_scatter(
        jnp.dot(hidden, down, preferred_element_type=jnp.float32),
        "col",
        scatter_dimension=0,
        tiled=True,
    )
    unpacked = lax.dot_general(
        placing.astype(jnp.float32),
        returned,
        (((0,), (0,)), ((), ())),
        precision=lax.Precision.HIGHEST,
        preferred_element_type=jnp.float32,
    )
    expert_out = (unpacked * factor[:, None]).astype(jnp.bfloat16)
    return (expert_out, gram_block)


def cost(flops, moved):
    return pl.CostEstimate(flops=int(flops), bytes_accessed=int(moved), transcendentals=0)


def params(mib):
    return pltpu.CompilerParams(vmem_limit_bytes=mib * MIB)


VMEM = pl.BlockSpec(memory_space=pltpu.VMEM)
HBM = pl.BlockSpec(memory_space=pltpu.HBM)
SMEM = pl.BlockSpec(memory_space=pltpu.SMEM)
ANY = pl.BlockSpec(memory_space=pl.ANY)


def in_vmem(value):
    return pltpu.with_memory_space_constraint(value, pltpu.VMEM)


def in_hbm(value):
    return pltpu.with_memory_space_constraint(value, pltpu.HBM)


def quarter_of(expert_flip, row_flip):
    return (lax.axis_index("expert") ^ expert_flip) * 2 + (lax.axis_index("row") ^ row_flip)


def tie(*values):
    return lax.optimization_barrier(values)


def pack_kernel(
    tokens_ref, routes_ref, pad_ref, weight_ref, packed_ref, placing_ref, factor_ref,
    tokens_held, routes_held, pad_held, weight_held, sems,
):
    pairs = (
        (routes_ref, routes_held),
        (pad_ref, pad_held),
        (weight_ref, weight_held),
        (tokens_ref, tokens_held),
    )
    copies = [pltpu.make_async_copy(a, b, sems.at[i]) for i, (a, b) in enumerate(pairs)]
    for copy in copies:
        copy.start()
    slots, rows = placing_ref.shape
    before = lax.broadcasted_iota(jnp.int32, (rows, rows), 0)
    upto = lax.broadcasted_iota(jnp.int32, (rows, rows), 1)
    tri = jnp.where(before <= upto, 1.0, 0.0).astype(BF16)
    slot_ids = lax.broadcasted_iota(jnp.int32, (slots, rows), 0).astype(F32)
    for copy in copies[:3]:
        copy.wait()
    routes_t = routes_held[...]
    routed = (routes_t[0:1, :] == 0) | (routes_t[1:2, :] == 0)
    live = jnp.where(routed & (pad_held[...] == 1), 1.0, 0.0)
    routed_rows = jnp.broadcast_to(jnp.where(routed, 1.0, 0.0), (8, rows)).astype(BF16)
    position = jnp.dot(routed_rows, tri, preferred_element_type=F32)[0:1, :] - 1.0
    placing = jnp.where(position == slot_ids, jnp.broadcast_to(live, (slots, rows)), 0.0)
    placing_ref[...] = placing.astype(BF16)
    weight = jnp.sum(jnp.where(routes_t == 0, weight_held[...], 0.0), axis=0, keepdims=True)
    factor = jnp.sum(placing * weight, axis=1, keepdims=True)
    factor_ref[...] = jnp.broadcast_to(factor, factor_ref.shape)
    copies[3].wait()
    packed_ref[...] = jnp.dot(
        placing.astype(BF16), tokens_held[...], preferred_element_type=F32
    ).astype(BF16)


def pack(tokens, routes_t, pad, weight_t):
    rows, depth = tokens.shape
    slots = rows // 4
    operands = (tokens, routes_t, pad, weight_t)
    return pl.pallas_call(
        pack_kernel,
        in_specs=[HBM] * 4,
        out_specs=[VMEM] * 3,
        out_shape=[
            pltpu.VMEM((slots, depth), BF16),
            pltpu.VMEM((slots, rows), BF16),
            pltpu.VMEM((slots, 128), F32),
        ],
        scratch_shapes=[pltpu.VMEM(x.shape, x.dtype) for x in operands]
        + [pltpu.SemaphoreType.DMA((4,))],
        compiler_params=params(3),
        name="pack",
    )(*(in_hbm(x) for x in operands))


def regroup_kernel(after_ref, weights_ref, out_ref, widen_ref, sems):
    del after_ref
    copies = [
        pltpu.make_async_copy(weights_ref.at[:, t], out_ref.at[t], sems.at[t])
        for t in range(out_ref.shape[0])
    ]
    for copy in copies:
        copy.start()
    cut = widen_ref.shape[0]
    into = lax.broadcasted_iota(jnp.int32, (cut, 4 * cut), 1)
    out_of = lax.broadcasted_iota(jnp.int32, (cut, 4 * cut), 0)
    half = jnp.where(into < 2 * cut, 0, 1)
    widen_ref[...] = jnp.where(into - 2 * cut * half == 2 * out_of + half, 1.0, 0.0).astype(BF16)
    for copy in copies:
        copy.wait()


def regroup(behind, weights):
    depth, tiles, two, lanes = weights.shape
    grouped, widen = pl.pallas_call(
        regroup_kernel,
        in_specs=[ANY, HBM],
        out_specs=[VMEM] * 2,
        out_shape=[
            pltpu.VMEM((tiles, depth, two, lanes), BF16),
            pltpu.VMEM((256, 1024), BF16),
        ],
        scratch_shapes=[pltpu.SemaphoreType.DMA((tiles,))],
        compiler_params=params(4),
        cost_estimate=cost(0, 4 * weights.size),
        name="regroup",
    )(behind, in_hbm(weights))
    return grouped.reshape(tiles, depth * two, lanes), widen


def fetch_kernel(after_ref, down_ref, out_ref, done_ref, sems):
    del after_ref
    parts = sems.shape[0]
    size = down_ref.shape[0] // parts
    copies = [
        pltpu.make_async_copy(
            down_ref.at[pl.ds(size * i, size)], out_ref.at[pl.ds(size * i, size)], sems.at[i]
        )
        for i in range(parts)
    ]
    for copy in copies:
        copy.start()
    done_ref[...] = jnp.zeros_like(done_ref)
    for copy in copies:
        copy.wait()


def fetch(behind, down):
    return pl.pallas_call(
        fetch_kernel,
        in_specs=[ANY, HBM],
        out_specs=[VMEM, VMEM],
        out_shape=[pltpu.VMEM(down.shape, BF16), pltpu.VMEM((8, 128), F32)],
        scratch_shapes=[pltpu.SemaphoreType.DMA((4,))],
        compiler_params=params(4),
        cost_estimate=cost(0, 4 * down.size),
        name="fetch_down",
    )(behind, in_hbm(down))


def widen_tokens(x_refs, widen_ref, wide_ref):
    slots, depth = x_refs[0].shape
    rows = 4 * slots
    here = lax.axis_index("col")
    cut = widen_ref.shape[0]
    parts = depth // cut
    stacked = jnp.concatenate(
        [x_ref[:, cut * k : cut * (k + 1)] for x_ref in x_refs for k in range(parts)], axis=0
    )
    spaced = jnp.dot(stacked, widen_ref[...], preferred_element_type=F32).astype(BF16)
    for slot in range(len(x_refs)):
        for h in range(2):
            at = pl.multiple_of(h * rows + (here ^ slot) * slots, slots)
            for k in range(parts):
                row = slots * (slot * parts + k)
                wide_ref[pl.ds(at, slots), 2 * cut * k : 2 * cut * (k + 1)] = spaced[
                    row : row + slots, 2 * cut * h : 2 * cut * (h + 1)
                ]


def preact_kernel(first, row_flip, chunk, chunks, *refs):
    if first:
        x0, x1, x2, x3, widen_ref, w_ref, out_ref, wide_ref = refs
        widen_tokens((x0, x1, x2, x3), widen_ref, wide_ref)
    else:
        wide_ref, w_ref, out_ref = refs
    tiles, _, lanes = w_ref.shape
    per = tiles // 4
    take = per // chunks
    at = []
    for i in range(2):
        quarter = quarter_of(1 - i, row_flip)
        at += [quarter * per + chunk * take + j for j in range(take)]
    for j in range(take):
        w = jnp.concatenate([w_ref[at[2 * j]], w_ref[at[2 * j + 1]]], axis=1)
        out_ref[:, 2 * lanes * j : 2 * lanes * (j + 1)] = jnp.dot(
            wide_ref[...], w, preferred_element_type=F32
        )


def preacts_of(lefts, weights, row_flip, chunk, chunks):
    tiles, depth2, lanes = weights.shape
    first = len(lefts) > 1
    rows = 4 * lefts[0].shape[0] if first else lefts[0].shape[0] // 2
    units = tiles // 4 // chunks * lanes
    out_shape = [jax.ShapeDtypeStruct((2 * rows, 2 * units), F32)]
    if first:
        out_shape.append(pltpu.VMEM((2 * rows, depth2), BF16))
    return pl.pallas_call(
        functools.partial(preact_kernel, first, row_flip, chunk, chunks),
        in_specs=[VMEM] * (len(lefts) + 1),
        out_specs=[VMEM] * len(out_shape),
        out_shape=out_shape,
        compiler_params=params(4),
        cost_estimate=cost(8 * rows * depth2 * units, 0),
        name="preacts_" + ("sent" if row_flip else "kept"),
    )(*lefts, in_vmem(weights))


def leave_kernel(kept_ref, got_ref, leaves_ref, stays_ref):
    units = stays_ref.shape[1]
    leaves_ref[...] = (kept_ref[:, :units] + got_ref[:, :units]).astype(BF16)
    stays_ref[...] = kept_ref[:, units:] + got_ref[:, units:]


def leave(kept, got):
    rows, units = kept.shape[0], kept.shape[1] // 2
    return pl.pallas_call(
        leave_kernel,
        in_specs=[VMEM] * 2,
        out_specs=[VMEM] * 2,
        out_shape=[
            jax.ShapeDtypeStruct((rows, units), BF16),
            jax.ShapeDtypeStruct((rows, units), F32),
        ],
        compiler_params=params(2),
        cost_estimate=cost(0, 1),
        name="leave",
    )(kept, got)


def act_kernel(tick_ref, stays_ref, got_ref, *refs):
    del tick_ref
    out_ref = refs[-1]
    rows = out_ref.shape[0]
    gate = stays_ref[:rows, :] + got_ref[:rows, :].astype(F32)
    up = stays_ref[rows:, :] + got_ref[rows:, :].astype(F32)
    hidden = (jax.nn.silu(gate) * up).astype(BF16)
    if len(refs) == 1:
        out_ref[...] = hidden
    else:
        before_ref, part_ref, _ = refs
        done = before_ref.shape[1]
        part_ref[...] = hidden
        out_ref[:, :done] = before_ref[...]
        out_ref[:, done:] = hidden


def act(tick, stays, got, *before):
    rows, units = stays.shape
    shapes = [(rows // 2, units)]
    if before:
        shapes.append((rows // 2, units + before[0].shape[1]))
    return pl.pallas_call(
        act_kernel,
        in_specs=[ANY] + [VMEM] * (2 + len(before)),
        out_specs=[VMEM] * len(shapes),
        out_shape=[jax.ShapeDtypeStruct(shape, BF16) for shape in shapes],
        compiler_params=params(2),
        cost_estimate=cost(0, 1),
        name="act",
    )(tick, stays, got, *before)


def relay_kernel(in_ref, out_ref):
    out_ref[...] = in_ref[...]


def relay(value):
    return pl.pallas_call(
        relay_kernel,
        in_specs=[VMEM],
        out_specs=VMEM,
        out_shape=jax.ShapeDtypeStruct(value.shape, value.dtype),
        compiler_params=params(2),
        cost_estimate=cost(1e10, 1),
        name="relay",
    )(value)


def is_near():
    return (lax.axis_index("col") // 2) == lax.axis_index("expert")


def is_odd():
    return (lax.axis_index("col") % 2) != lax.axis_index("row")


def choose_kernel(near_ref, far_ref, out_ref):
    @pl.when(is_near())
    def _():
        out_ref[...] = near_ref[...]

    @pl.when(jnp.logical_not(is_near()))
    def _():
        out_ref[...] = far_ref[...]


def choose(if_near, if_far):
    return pl.pallas_call(
        choose_kernel,
        in_specs=[VMEM] * 2,
        out_specs=VMEM,
        out_shape=jax.ShapeDtypeStruct(if_near.shape, if_near.dtype),
        compiler_params=params(2),
        cost_estimate=cost(1e10, 1),
        name="choose",
    )(if_near, if_far)


def put(out_ref, parts):
    column = 0
    for part in parts:
        out_ref[:, column : column + part.shape[1]] = part[...]
        column += part.shape[1]


def pick_kernel(counts, *refs):
    slots, at = [], 0
    for count in counts:
        slots.append(refs[at : at + count])
        at += count
    mine_ref, other_ref = refs[at : at + 2]
    for near, pair in ((True, slots[:2]), (False, slots[2:])):
        for odd in (False, True):

            @pl.when((is_near() == near) & (is_odd() == odd))
            def _():
                put(mine_ref, pair[int(odd)])
                put(other_ref, pair[1 - int(odd)])

        if len(refs) > at + 2:

            @pl.when(is_near() == near)
            def _():
                put(refs[-1], (slots[2][-1] if near else slots[1][-1], *slots[3]))


def pick(*slots, leaves=False):
    parts = [part for slot in slots for part in slot]
    rows, units = slots[0][0].shape
    shapes = [(rows, units)] * 2
    if leaves:
        shapes.append((rows, units + slots[1][-1].shape[1]))
    return pl.pallas_call(
        functools.partial(pick_kernel, [len(slot) for slot in slots]),
        in_specs=[VMEM] * len(parts),
        out_specs=[VMEM] * len(shapes),
        out_shape=[jax.ShapeDtypeStruct(shape, BF16) for shape in shapes],
        compiler_params=params(2),
        cost_estimate=cost(0, 1),
        name="pick",
    )(*parts)


def pick_far_kernel(own_ref, first_ref, rest_ref, mine_ref, other_ref):
    units = first_ref.shape[1]

    def fill(out_ref, slot):
        if slot == 0:
            out_ref[...] = own_ref[...]
        elif slot == 3:
            out_ref[...] = rest_ref[:, units:]
        else:
            out_ref[:, :units] = first_ref[...]
            out_ref[:, units:] = rest_ref[:, :units]

    for near, pair in ((True, (0, 1)), (False, (2, 3))):
        for odd in (False, True):

            @pl.when((is_near() == near) & (is_odd() == odd))
            def _():
                fill(mine_ref, pair[int(odd)])
                fill(other_ref, pair[1 - int(odd)])


def pick_far(own, first, rest):
    same = jax.ShapeDtypeStruct(own.shape, BF16)
    return pl.pallas_call(
        pick_far_kernel,
        in_specs=[VMEM] * 3,
        out_specs=[VMEM] * 2,
        out_shape=[same] * 2,
        compiler_params=params(2),
        cost_estimate=cost(0, 1),
        name="pick_far",
    )(own, first, rest)


def join_kernel(left_ref, right_ref, out_ref):
    units = left_ref.shape[1]
    out_ref[:, :units] = left_ref[...]
    out_ref[:, units:] = right_ref[...]


def join(left, right):
    rows, units = left.shape
    return pl.pallas_call(
        join_kernel,
        in_specs=[VMEM] * 2,
        out_specs=VMEM,
        out_shape=jax.ShapeDtypeStruct((rows, 2 * units), left.dtype),
        compiler_params=params(2),
        cost_estimate=cost(0, 1),
        name="join",
    )(left, right)


def project_kernel(tick_ref, here_ref, there_ref, down_ref, near_ref, away_ref, wide_ref, done_ref, total_ref):
    del tick_ref
    units = here_ref.shape[1] // 2
    for row_flip, pair_ref in enumerate((here_ref, there_ref)):
        for expert_flip in range(2):
            at = pl.multiple_of(quarter_of(expert_flip, row_flip) * units, units)
            wide_ref[:, pl.ds(at, units)] = pair_ref[:, units * expert_flip : units * (expert_flip + 1)]
    done_ref[...] = jnp.zeros_like(done_ref)
    width = near_ref.shape[1]
    slots = near_ref.shape[0] // 2
    cut = 512
    for n in range(width // cut):
        total_ref[:, cut * n : cut * (n + 1)] = jnp.dot(
            wide_ref[...], down_ref[:, cut * n : cut * (n + 1)], preferred_element_type=F32
        )
    here = lax.axis_index("col")
    for i, (out_ref, slot) in enumerate(((near_ref, 0), (near_ref, 2), (away_ref, 1), (away_ref, 3))):
        at = pl.multiple_of((here ^ slot) * slots, slots)
        row = slots * (i % 2)
        out_ref[row : row + slots, :] = total_ref[pl.ds(at, slots), :].astype(out_ref.dtype)


def project(tick, here, there, down):
    rows, units = here.shape[0], here.shape[1] // 2
    width = down.shape[1]
    return pl.pallas_call(
        project_kernel,
        in_specs=[ANY] + [VMEM] * 3,
        out_specs=[VMEM] * 4,
        out_shape=[
            jax.ShapeDtypeStruct((rows // 2, width), F32),
            jax.ShapeDtypeStruct((rows // 2, width), BF16),
            pltpu.VMEM((rows, 4 * units), BF16),
            pltpu.VMEM((8, 128), F32),
        ],
        scratch_shapes=[pltpu.VMEM((rows, width), F32)],
        compiler_params=params(4),
        cost_estimate=cost(0, 1),
        name="project",
    )(tick, here, there, in_vmem(down))


def fold_kernel(near_ref, got_ref, own_ref, onward_ref):
    slots = own_ref.shape[0]
    own_ref[...] = near_ref[:slots, :] + got_ref[:slots, :].astype(F32)
    onward_ref[...] = (near_ref[slots:, :] + got_ref[slots:, :].astype(F32)).astype(BF16)


def fold(near, got):
    slots, width = near.shape[0] // 2, near.shape[1]
    return pl.pallas_call(
        fold_kernel,
        in_specs=[VMEM] * 2,
        out_specs=[VMEM] * 2,
        out_shape=[
            jax.ShapeDtypeStruct((slots, width), F32),
            jax.ShapeDtypeStruct((slots, width), BF16),
        ],
        compiler_params=params(2),
        cost_estimate=cost(0, 1),
        name="fold",
    )(near, got)


def unpack_kernel(after_ref, placing_ref, factor_ref, own_ref, got_ref, out_ref):
    del after_ref
    total = own_ref[...] + got_ref[...].astype(F32)
    scaled = (total * factor_ref[:, 0:1]).astype(BF16)
    out_ref[...] = lax.dot_general(
        placing_ref[...], scaled, (((0,), (0,)), ((), ())), preferred_element_type=F32
    ).astype(BF16)


def unpack(done, placing, factor, own, got):
    slots, rows = placing.shape
    return pl.pallas_call(
        unpack_kernel,
        in_specs=[ANY] + [VMEM] * 4,
        out_specs=VMEM,
        out_shape=jax.ShapeDtypeStruct((rows, own.shape[1]), BF16),
        compiler_params=params(4),
        name="unpack",
    )(done, placing, factor, own, got)


def gram_kernel(scale, flips, *refs):
    count = len(flips)
    pieces = refs[1 : 1 + count]
    wide_ref = refs[1 + count]
    out_ref, done_ref, ring_ref, sems = refs[-4:]
    done_ref[...] = jnp.zeros_like(done_ref)
    units = pieces[0].shape[1]
    depth, height, cut = ring_ref.shape
    half = cut // 2
    copies = []
    for (expert_flip, row_flip), a_ref in zip(flips, pieces):
        start = quarter_of(expert_flip, row_flip) * units
        for m in range(units // height):
            rows = pl.ds(pl.multiple_of(start + height * m, height), height)
            left = a_ref[:, height * m : height * (m + 1)].T
            for n in range(4 * units // cut):
                spot = len(copies) % depth
                if len(copies) >= depth:
                    copies[-depth].wait()
                for i in range(2):
                    column = cut * n + half * i
                    ring_ref[spot, :, half * i : half * (i + 1)] = scale * jnp.dot(
                        left, wide_ref[:, column : column + half], preferred_element_type=F32
                    )
                copy = pltpu.make_async_copy(
                    ring_ref.at[spot], out_ref.at[rows, pl.ds(cut * n, cut)], sems.at[spot]
                )
                copy.start()
                copies.append(copy)
    for copy in copies[-depth:]:
        copy.wait()


def gram_piece(tick, pieces, flips, wide, gram=None):
    rows, units = pieces[0].shape
    cut, height, depth = 1024, 256, 6
    operands = [tick, *pieces, in_vmem(wide)]
    in_specs = [ANY] + [VMEM] * (len(pieces) + 1)
    aliases = {}
    if gram is not None:
        aliases = {len(operands): 0}
        operands.append(gram)
        in_specs.append(HBM)
    return pl.pallas_call(
        functools.partial(gram_kernel, 2.0 / rows, flips),
        in_specs=in_specs,
        out_specs=[HBM, VMEM],
        out_shape=[
            jax.ShapeDtypeStruct((4 * units, 4 * units), F32),
            pltpu.VMEM((8, 128), F32),
        ],
        input_output_aliases=aliases,
        scratch_shapes=[
            pltpu.VMEM((depth, height, cut), F32),
            pltpu.SemaphoreType.DMA((depth,)),
        ],
        compiler_params=params(10),
        cost_estimate=cost(8 * rows * units * units * len(pieces), 16 * units * units * len(pieces)),
        name="gram",
    )(*operands)


def swap(value, axis):
    return lax.ppermute(value, axis, [(0, 1), (1, 0)])


def across(value, slot):
    return lax.ppermute(value, "col", [(i, i ^ slot) for i in range(4)])


def on_device(tokens, routes, route_weight, pad_mask, gate_up, down):
    depth = tokens.shape[1]
    units = gate_up.shape[2]
    lanes = 128
    chunks = 2
    weights = gate_up.reshape(depth, 2, units // lanes, lanes).transpose(0, 2, 1, 3)

    packed, placing, factor = pack(tokens, routes.T, pad_mask[None, :], route_weight.T)
    lefts = [packed] + [across(packed, slot) for slot in (1, 2, 3)]
    grouped, widen = regroup(packed, weights)

    first_sent, wide = preacts_of([*lefts, widen], grouped, 1, 0, chunks)
    (last_sent,) = preacts_of([wide], grouped, 1, 1, chunks)
    got = [swap(first_sent, "row"), swap(last_sent, "row")]
    stays, got_x = [], []
    for h in range(chunks):
        (kept,) = preacts_of([wide], grouped, 0, h, chunks)
        leaves, stay = leave(kept, got[h])
        wide, leaves = tie(wide, leaves)
        stays.append(stay)
        got_x.append(swap(leaves, "expert"))
    down_held, tick = fetch(wide, down)
    tick, got_x[0] = tie(tick, got_x[0])
    (hidden_a,) = act(tick, stays[0], got_x[0])

    z2a = across(hidden_a, 2)
    z1a = across(hidden_a, 1)
    tick, got_x[1], hidden_a = tie(tick, got_x[1], hidden_a)
    hidden_b, hidden = act(tick, stays[1], got_x[1], hidden_a)
    hidden_x = swap(hidden, "expert")
    z2b = across(hidden_b, 2)
    tick, z2a = tie(tick, z2a)
    z3a = across(relay(z2a), 1)
    tick, z1a, hidden_b = tie(tick, z1a, hidden_b)
    z1b = across(hidden_b, 1)
    x2a = swap(choose(z2a, z1a), "expert")
    tick, z2b = tie(tick, z2b)
    z3b = across(z2b, 1)
    tick, z3a = tie(tick, z3a)
    tick, z1b = tie(tick, z1b)
    here = join(hidden, hidden_x)
    there = swap(here, "row")
    tick, there, here = tie(tick, there, here)
    near, away, hidden_c, tick = project(tick, here, there, down_held)
    tick, x2a = tie(tick, x2a)
    tick, z3b = tie(tick, z3b)
    mine, passed, leaves = pick([hidden], [z1a, z1b], [z2a, z2b], [z3a, z3b], leaves=True)
    rest = swap(leaves, "expert")
    mine_near = swap(passed, "row")
    away = across(away, 1)
    tick, mine_near = tie(tick, mine_near)
    gram, tick = gram_piece(tick, [mine, mine_near], [(0, 0), (0, 1)], hidden_c)
    tick, rest = tie(tick, rest)
    mine_x, passed = pick_far(hidden_x, x2a, rest)
    mine_far = swap(passed, "row")
    tick, away = tie(tick, away)
    own, onward = fold(near, away)
    onward = across(onward, 2)
    tick, mine_far = tie(tick, mine_far)
    gram, tick = gram_piece(tick, [mine_x, mine_far], [(1, 0), (1, 1)], hidden_c, gram)
    return (unpack(tick, placing, factor, own, onward), gram)


def solution(mesh):
    in_specs = (
        P(("parts", "col"), ("expert", "row")),
        P(("parts", "col"), None),
        P(("parts", "col"), None),
        P(("parts", "col")),
        P(("expert", "row"), None, "col"),
        P("col", ("expert", "row")),
    )
    out_specs = (P(("parts", "col"), ("expert", "row")), P(("parts", "expert", "row"), "col"))
    small = mesh.shape["expert"] == 2 and mesh.shape["row"] == 2 and mesh.shape["col"] == 4
    return jax.shard_map(
        on_device if small else on_any_device,
        mesh=mesh,
        in_specs=in_specs,
        out_specs=out_specs,
        check_vma=False,
    )
```

```python
import functools

import jax
import jax.numpy as jnp
from jax import lax
from jax.experimental import pallas as pl
from jax.experimental.pallas import tpu as pltpu
from jax.sharding import PartitionSpec as P

F32 = jnp.float32
BF16 = jnp.bfloat16
MIB = 1 << 20


def spread(value, axis, source):
    kept = jnp.where(lax.axis_index(axis) == source, value, 0).astype(value.dtype)
    return lax.psum(kept, axis)


def activate(preacts):
    return (jax.nn.silu(preacts[:, 0, :]) * preacts[:, 1, :]).astype(jnp.bfloat16)


def on_any_device(tokens, routes, route_weight, pad_mask, gate_up, down):
    group_rows = tokens.shape[0]
    slot_count = group_rows // 4
    names_zero = routes == 0
    routed = jnp.any(names_zero, axis=1)
    live_rows = routed & (pad_mask == 1)
    factor = jnp.sum(
        jnp.where(names_zero, route_weight, jnp.float32(0.0)), axis=1
    ) * live_rows.astype(jnp.float32)
    position = jnp.cumsum(routed.astype(jnp.int32)) - 1
    slot_ids = lax.broadcasted_iota(jnp.int32, (slot_count, group_rows), 0)
    placing = ((position[None, :] == slot_ids) & routed[None, :]).astype(jnp.bfloat16)
    masked = tokens * live_rows.astype(jnp.bfloat16)[:, None]
    packed = jnp.dot(placing, masked, preferred_element_type=jnp.float32).astype(jnp.bfloat16)
    gathered = lax.all_gather(packed, "col", axis=0, tiled=True)
    anchor = lax.axis_index(("expert", "row"))
    preacts = lax.psum(
        jnp.einsum("rd,dgf->rgf", gathered, gate_up, preferred_element_type=jnp.float32),
        ("expert", "row"),
    )
    hidden = activate(preacts)
    mirrored = spread(hidden, "col", anchor)
    gram_block = lax.dot_general(
        mirrored, hidden, (((0,), (0,)), ((), ())), preferred_element_type=jnp.float32
    )
    gram_block = gram_block * jnp.float32(2.0 / hidden.shape[0])
    returned = lax.psum_scatter(
        jnp.dot(hidden, down, preferred_element_type=jnp.float32),
        "col",
        scatter_dimension=0,
        tiled=True,
    )
    unpacked = lax.dot_general(
        placing.astype(jnp.float32),
        returned,
        (((0,), (0,)), ((), ())),
        precision=lax.Precision.HIGHEST,
        preferred_element_type=jnp.float32,
    )
    expert_out = (unpacked * factor[:, None]).astype(jnp.bfloat16)
    return (expert_out, gram_block)


def cost(flops, moved):
    return pl.CostEstimate(flops=int(flops), bytes_accessed=int(moved), transcendentals=0)


def params(mib):
    return pltpu.CompilerParams(vmem_limit_bytes=mib * MIB)


VMEM = pl.BlockSpec(memory_space=pltpu.VMEM)
HBM = pl.BlockSpec(memory_space=pltpu.HBM)
SMEM = pl.BlockSpec(memory_space=pltpu.SMEM)
ANY = pl.BlockSpec(memory_space=pl.ANY)


def in_vmem(value):
    return pltpu.with_memory_space_constraint(value, pltpu.VMEM)


def in_hbm(value):
    return pltpu.with_memory_space_constraint(value, pltpu.HBM)


def quarter_of(expert_flip, row_flip):
    return (lax.axis_index("expert") ^ expert_flip) * 2 + (lax.axis_index("row") ^ row_flip)


def tie(*values):
    return lax.optimization_barrier(values)


def pack_kernel(
    tokens_ref, routes_ref, pad_ref, weight_ref, packed_ref, placing_ref, factor_ref,
    tokens_held, routes_held, pad_held, weight_held, sems,
):
    pairs = (
        (routes_ref, routes_held),
        (pad_ref, pad_held),
        (weight_ref, weight_held),
        (tokens_ref, tokens_held),
    )
    copies = [pltpu.make_async_copy(a, b, sems.at[i]) for i, (a, b) in enumerate(pairs)]
    for copy in copies:
        copy.start()
    slots, rows = placing_ref.shape
    before = lax.broadcasted_iota(jnp.int32, (rows, rows), 0)
    upto = lax.broadcasted_iota(jnp.int32, (rows, rows), 1)
    tri = jnp.where(before <= upto, 1.0, 0.0).astype(BF16)
    slot_ids = lax.broadcasted_iota(jnp.int32, (slots, rows), 0).astype(F32)
    for copy in copies[:3]:
        copy.wait()
    routes_t = routes_held[...]
    routed = (routes_t[0:1, :] == 0) | (routes_t[1:2, :] == 0)
    live = jnp.where(routed & (pad_held[...] == 1), 1.0, 0.0)
    routed_rows = jnp.broadcast_to(jnp.where(routed, 1.0, 0.0), (8, rows)).astype(BF16)
    position = jnp.dot(routed_rows, tri, preferred_element_type=F32)[0:1, :] - 1.0
    placing = jnp.where(position == slot_ids, jnp.broadcast_to(live, (slots, rows)), 0.0)
    placing_ref[...] = placing.astype(BF16)
    weight = jnp.sum(jnp.where(routes_t == 0, weight_held[...], 0.0), axis=0, keepdims=True)
    factor = jnp.sum(placing * weight, axis=1, keepdims=True)
    factor_ref[...] = jnp.broadcast_to(factor, factor_ref.shape)
    copies[3].wait()
    packed_ref[...] = jnp.dot(
        placing.astype(BF16), tokens_held[...], preferred_element_type=F32
    ).astype(BF16)


def pack(tokens, routes_t, pad, weight_t):
    rows, depth = tokens.shape
    slots = rows // 4
    operands = (tokens, routes_t, pad, weight_t)
    return pl.pallas_call(
        pack_kernel,
        in_specs=[HBM] * 4,
        out_specs=[VMEM] * 3,
        out_shape=[
            pltpu.VMEM((slots, depth), BF16),
            pltpu.VMEM((slots, rows), BF16),
            pltpu.VMEM((slots, 128), F32),
        ],
        scratch_shapes=[pltpu.VMEM(x.shape, x.dtype) for x in operands]
        + [pltpu.SemaphoreType.DMA((4,))],
        compiler_params=params(3),
        name="pack",
    )(*(in_hbm(x) for x in operands))


def regroup_kernel(after_ref, weights_ref, out_ref, widen_ref, sems):
    del after_ref
    copies = [
        pltpu.make_async_copy(weights_ref.at[:, t], out_ref.at[t], sems.at[t])
        for t in range(out_ref.shape[0])
    ]
    for copy in copies:
        copy.start()
    cut = widen_ref.shape[0]
    into = lax.broadcasted_iota(jnp.int32, (cut, 4 * cut), 1)
    out_of = lax.broadcasted_iota(jnp.int32, (cut, 4 * cut), 0)
    half = jnp.where(into < 2 * cut, 0, 1)
    widen_ref[...] = jnp.where(into - 2 * cut * half == 2 * out_of + half, 1.0, 0.0).astype(BF16)
    for copy in copies:
        copy.wait()


def regroup(behind, weights):
    depth, tiles, two, lanes = weights.shape
    grouped, widen = pl.pallas_call(
        regroup_kernel,
        in_specs=[ANY, HBM],
        out_specs=[VMEM] * 2,
        out_shape=[
            pltpu.VMEM((tiles, depth, two, lanes), BF16),
            pltpu.VMEM((256, 1024), BF16),
        ],
        scratch_shapes=[pltpu.SemaphoreType.DMA((tiles,))],
        compiler_params=params(4),
        cost_estimate=cost(0, 4 * weights.size),
        name="regroup",
    )(behind, in_hbm(weights))
    return grouped.reshape(tiles, depth * two, lanes), widen


def fetch_kernel(after_ref, down_ref, out_ref, done_ref, sems):
    del after_ref
    parts = sems.shape[0]
    size = down_ref.shape[0] // parts
    copies = [
        pltpu.make_async_copy(
            down_ref.at[pl.ds(size * i, size)], out_ref.at[pl.ds(size * i, size)], sems.at[i]
        )
        for i in range(parts)
    ]
    for copy in copies:
        copy.start()
    done_ref[...] = jnp.zeros_like(done_ref)
    for copy in copies:
        copy.wait()


def fetch(behind, down):
    return pl.pallas_call(
        fetch_kernel,
        in_specs=[ANY, HBM],
        out_specs=[VMEM, VMEM],
        out_shape=[pltpu.VMEM(down.shape, BF16), pltpu.VMEM((8, 128), F32)],
        scratch_shapes=[pltpu.SemaphoreType.DMA((4,))],
        compiler_params=params(4),
        cost_estimate=cost(0, 4 * down.size),
        name="fetch_down",
    )(behind, in_hbm(down))


def widen_tokens(x_refs, widen_ref, wide_ref):
    slots, depth = x_refs[0].shape
    rows = 4 * slots
    here = lax.axis_index("col")
    cut = widen_ref.shape[0]
    parts = depth // cut
    for slot, x_ref in enumerate(x_refs):
        stacked = jnp.concatenate(
            [x_ref[:, cut * k : cut * (k + 1)] for k in range(parts)], axis=0
        )
        spaced = jnp.dot(stacked, widen_ref[...], preferred_element_type=F32).astype(BF16)
        for h in range(2):
            at = pl.multiple_of(h * rows + (here ^ slot) * slots, slots)
            for k in range(parts):
                wide_ref[pl.ds(at, slots), 2 * cut * k : 2 * cut * (k + 1)] = spaced[
                    slots * k : slots * (k + 1), 2 * cut * h : 2 * cut * (h + 1)
                ]


def preact_kernel(first, row_flip, chunk, chunks, *refs):
    if first:
        x0, x1, x2, x3, widen_ref, w_ref, out_ref, wide_ref = refs
        widen_tokens((x0, x1, x2, x3), widen_ref, wide_ref)
    else:
        wide_ref, w_ref, out_ref = refs
    tiles, _, lanes = w_ref.shape
    per = tiles // 4
    take = per // chunks
    at = []
    for i in range(2):
        quarter = quarter_of(1 - i, row_flip)
        at += [quarter * per + chunk * take + j for j in range(take)]
    for j in range(take):
        w = jnp.concatenate([w_ref[at[2 * j]], w_ref[at[2 * j + 1]]], axis=1)
        out_ref[:, 2 * lanes * j : 2 * lanes * (j + 1)] = jnp.dot(
            wide_ref[...], w, preferred_element_type=F32
        )


def preacts_of(lefts, weights, row_flip, chunk, chunks):
    tiles, depth2, lanes = weights.shape
    first = len(lefts) > 1
    rows = 4 * lefts[0].shape[0] if first else lefts[0].shape[0] // 2
    units = tiles // 4 // chunks * lanes
    out_shape = [jax.ShapeDtypeStruct((2 * rows, 2 * units), F32)]
    if first:
        out_shape.append(pltpu.VMEM((2 * rows, depth2), BF16))
    return pl.pallas_call(
        functools.partial(preact_kernel, first, row_flip, chunk, chunks),
        in_specs=[VMEM] * (len(lefts) + 1),
        out_specs=[VMEM] * len(out_shape),
        out_shape=out_shape,
        compiler_params=params(4),
        cost_estimate=cost(8 * rows * depth2 * units, 0),
        name="preacts_" + ("sent" if row_flip else "kept"),
    )(*lefts, in_vmem(weights))


def leave_kernel(kept_ref, got_ref, leaves_ref, stays_ref):
    units = stays_ref.shape[1]
    leaves_ref[...] = (kept_ref[:, :units] + got_ref[:, :units]).astype(BF16)
    stays_ref[...] = kept_ref[:, units:] + got_ref[:, units:]


def leave(kept, got):
    rows, units = kept.shape[0], kept.shape[1] // 2
    return pl.pallas_call(
        leave_kernel,
        in_specs=[VMEM] * 2,
        out_specs=[VMEM] * 2,
        out_shape=[
            jax.ShapeDtypeStruct((rows, units), BF16),
            jax.ShapeDtypeStruct((rows, units), F32),
        ],
        compiler_params=params(2),
        cost_estimate=cost(0, 1),
        name="leave",
    )(kept, got)


def act_kernel(tick_ref, stays_ref, got_ref, *refs):
    del tick_ref
    out_ref = refs[-1]
    rows = out_ref.shape[0]
    gate = stays_ref[:rows, :] + got_ref[:rows, :].astype(F32)
    up = stays_ref[rows:, :] + got_ref[rows:, :].astype(F32)
    hidden = (jax.nn.silu(gate) * up).astype(BF16)
    if len(refs) == 1:
        out_ref[...] = hidden
    else:
        before_ref, part_ref, _ = refs
        done = before_ref.shape[1]
        part_ref[...] = hidden
        out_ref[:, :done] = before_ref[...]
        out_ref[:, done:] = hidden


def act(tick, stays, got, *before):
    rows, units = stays.shape
    shapes = [(rows // 2, units)]
    if before:
        shapes.append((rows // 2, units + before[0].shape[1]))
    return pl.pallas_call(
        act_kernel,
        in_specs=[ANY] + [VMEM] * (2 + len(before)),
        out_specs=[VMEM] * len(shapes),
        out_shape=[jax.ShapeDtypeStruct(shape, BF16) for shape in shapes],
        compiler_params=params(2),
        cost_estimate=cost(0, 1),
        name="act",
    )(tick, stays, got, *before)


def relay_kernel(in_ref, out_ref):
    out_ref[...] = in_ref[...]


def relay(value):
    return pl.pallas_call(
        relay_kernel,
        in_specs=[VMEM],
        out_specs=VMEM,
        out_shape=jax.ShapeDtypeStruct(value.shape, value.dtype),
        compiler_params=params(2),
        cost_estimate=cost(1e10, 1),
        name="relay",
    )(value)


def is_near():
    return (lax.axis_index("col") // 2) == lax.axis_index("expert")


def is_odd():
    return (lax.axis_index("col") % 2) != lax.axis_index("row")


def choose_kernel(near_ref, far_ref, out_ref):
    @pl.when(is_near())
    def _():
        out_ref[...] = near_ref[...]

    @pl.when(jnp.logical_not(is_near()))
    def _():
        out_ref[...] = far_ref[...]


def choose(if_near, if_far):
    return pl.pallas_call(
        choose_kernel,
        in_specs=[VMEM] * 2,
        out_specs=VMEM,
        out_shape=jax.ShapeDtypeStruct(if_near.shape, if_near.dtype),
        compiler_params=params(2),
        cost_estimate=cost(1e10, 1),
        name="choose",
    )(if_near, if_far)


def put(out_ref, parts):
    column = 0
    for part in parts:
        out_ref[:, column : column + part.shape[1]] = part[...]
        column += part.shape[1]


def pick_kernel(counts, *refs):
    slots, at = [], 0
    for count in counts:
        slots.append(refs[at : at + count])
        at += count
    mine_ref, other_ref = refs[at : at + 2]
    for near, pair in ((True, slots[:2]), (False, slots[2:])):
        for odd in (False, True):

            @pl.when((is_near() == near) & (is_odd() == odd))
            def _():
                put(mine_ref, pair[int(odd)])
                put(other_ref, pair[1 - int(odd)])

        if len(refs) > at + 2:

            @pl.when(is_near() == near)
            def _():
                put(refs[-1], (slots[2][-1] if near else slots[1][-1], *slots[3]))


def pick(*slots, leaves=False):
    parts = [part for slot in slots for part in slot]
    rows, units = slots[0][0].shape
    shapes = [(rows, units)] * 2
    if leaves:
        shapes.append((rows, units + slots[1][-1].shape[1]))
    return pl.pallas_call(
        functools.partial(pick_kernel, [len(slot) for slot in slots]),
        in_specs=[VMEM] * len(parts),
        out_specs=[VMEM] * len(shapes),
        out_shape=[jax.ShapeDtypeStruct(shape, BF16) for shape in shapes],
        compiler_params=params(2),
        cost_estimate=cost(0, 1),
        name="pick",
    )(*parts)


def pick_far_kernel(own_ref, first_ref, rest_ref, mine_ref, other_ref):
    units = first_ref.shape[1]

    def fill(out_ref, slot):
        if slot == 0:
            out_ref[...] = own_ref[...]
        elif slot == 3:
            out_ref[...] = rest_ref[:, units:]
        else:
            out_ref[:, :units] = first_ref[...]
            out_ref[:, units:] = rest_ref[:, :units]

    for near, pair in ((True, (0, 1)), (False, (2, 3))):
        for odd in (False, True):

            @pl.when((is_near() == near) & (is_odd() == odd))
            def _():
                fill(mine_ref, pair[int(odd)])
                fill(other_ref, pair[1 - int(odd)])


def pick_far(own, first, rest):
    same = jax.ShapeDtypeStruct(own.shape, BF16)
    return pl.pallas_call(
        pick_far_kernel,
        in_specs=[VMEM] * 3,
        out_specs=[VMEM] * 2,
        out_shape=[same] * 2,
        compiler_params=params(2),
        cost_estimate=cost(0, 1),
        name="pick_far",
    )(own, first, rest)


def join_kernel(left_ref, right_ref, out_ref):
    units = left_ref.shape[1]
    out_ref[:, :units] = left_ref[...]
    out_ref[:, units:] = right_ref[...]


def join(left, right):
    rows, units = left.shape
    return pl.pallas_call(
        join_kernel,
        in_specs=[VMEM] * 2,
        out_specs=VMEM,
        out_shape=jax.ShapeDtypeStruct((rows, 2 * units), left.dtype),
        compiler_params=params(2),
        cost_estimate=cost(0, 1),
        name="join",
    )(left, right)


def project_kernel(tick_ref, here_ref, there_ref, down_ref, near_ref, away_ref, wide_ref, done_ref, total_ref):
    del tick_ref
    units = here_ref.shape[1] // 2
    for row_flip, pair_ref in enumerate((here_ref, there_ref)):
        for expert_flip in range(2):
            at = pl.multiple_of(quarter_of(expert_flip, row_flip) * units, units)
            wide_ref[:, pl.ds(at, units)] = pair_ref[:, units * expert_flip : units * (expert_flip + 1)]
    done_ref[...] = jnp.zeros_like(done_ref)
    width = near_ref.shape[1]
    slots = near_ref.shape[0] // 2
    cut = 512
    for n in range(width // cut):
        total_ref[:, cut * n : cut * (n + 1)] = jnp.dot(
            wide_ref[...], down_ref[:, cut * n : cut * (n + 1)], preferred_element_type=F32
        )
    here = lax.axis_index("col")
    for i, (out_ref, slot) in enumerate(((near_ref, 0), (near_ref, 2), (away_ref, 1), (away_ref, 3))):
        at = pl.multiple_of((here ^ slot) * slots, slots)
        row = slots * (i % 2)
        out_ref[row : row + slots, :] = total_ref[pl.ds(at, slots), :].astype(out_ref.dtype)


def project(tick, here, there, down):
    rows, units = here.shape[0], here.shape[1] // 2
    width = down.shape[1]
    return pl.pallas_call(
        project_kernel,
        in_specs=[ANY] + [VMEM] * 3,
        out_specs=[VMEM] * 4,
        out_shape=[
            jax.ShapeDtypeStruct((rows // 2, width), F32),
            jax.ShapeDtypeStruct((rows // 2, width), BF16),
            pltpu.VMEM((rows, 4 * units), BF16),
            pltpu.VMEM((8, 128), F32),
        ],
        scratch_shapes=[pltpu.VMEM((rows, width), F32)],
        compiler_params=params(4),
        cost_estimate=cost(0, 1),
        name="project",
    )(tick, here, there, in_vmem(down))


def fold_kernel(near_ref, got_ref, own_ref, onward_ref):
    slots = own_ref.shape[0]
    own_ref[...] = near_ref[:slots, :] + got_ref[:slots, :].astype(F32)
    onward_ref[...] = (near_ref[slots:, :] + got_ref[slots:, :].astype(F32)).astype(BF16)


def fold(near, got):
    slots, width = near.shape[0] // 2, near.shape[1]
    return pl.pallas_call(
        fold_kernel,
        in_specs=[VMEM] * 2,
        out_specs=[VMEM] * 2,
        out_shape=[
            jax.ShapeDtypeStruct((slots, width), F32),
            jax.ShapeDtypeStruct((slots, width), BF16),
        ],
        compiler_params=params(2),
        cost_estimate=cost(0, 1),
        name="fold",
    )(near, got)


def unpack_kernel(after_ref, placing_ref, factor_ref, own_ref, got_ref, out_ref):
    del after_ref
    total = own_ref[...] + got_ref[...].astype(F32)
    scaled = (total * factor_ref[:, 0:1]).astype(BF16)
    out_ref[...] = lax.dot_general(
        placing_ref[...], scaled, (((0,), (0,)), ((), ())), preferred_element_type=F32
    ).astype(BF16)


def unpack(done, placing, factor, own, got):
    slots, rows = placing.shape
    return pl.pallas_call(
        unpack_kernel,
        in_specs=[ANY] + [VMEM] * 4,
        out_specs=VMEM,
        out_shape=jax.ShapeDtypeStruct((rows, own.shape[1]), BF16),
        compiler_params=params(4),
        name="unpack",
    )(done, placing, factor, own, got)


def gram_kernel(scale, flips, *refs):
    count = len(flips)
    pieces = refs[1 : 1 + count]
    wide_ref = refs[1 + count]
    out_ref, done_ref, ring_ref, sems = refs[-4:]
    done_ref[...] = jnp.zeros_like(done_ref)
    units = pieces[0].shape[1]
    depth, height, cut = ring_ref.shape
    half = cut // 2
    copies = []
    for (expert_flip, row_flip), a_ref in zip(flips, pieces):
        start = quarter_of(expert_flip, row_flip) * units
        for m in range(units // height):
            rows = pl.ds(pl.multiple_of(start + height * m, height), height)
            left = a_ref[:, height * m : height * (m + 1)].T
            for n in range(4 * units // cut):
                spot = len(copies) % depth
                if len(copies) >= depth:
                    copies[-depth].wait()
                for i in range(2):
                    column = cut * n + half * i
                    ring_ref[spot, :, half * i : half * (i + 1)] = scale * jnp.dot(
                        left, wide_ref[:, column : column + half], preferred_element_type=F32
                    )
                copy = pltpu.make_async_copy(
                    ring_ref.at[spot], out_ref.at[rows, pl.ds(cut * n, cut)], sems.at[spot]
                )
                copy.start()
                copies.append(copy)
    for copy in copies[-depth:]:
        copy.wait()


def gram_piece(tick, pieces, flips, wide, gram=None):
    rows, units = pieces[0].shape
    cut, height, depth = 1024, 256, 6
    operands = [tick, *pieces, in_vmem(wide)]
    in_specs = [ANY] + [VMEM] * (len(pieces) + 1)
    aliases = {}
    if gram is not None:
        aliases = {len(operands): 0}
        operands.append(gram)
        in_specs.append(HBM)
    return pl.pallas_call(
        functools.partial(gram_kernel, 2.0 / rows, flips),
        in_specs=in_specs,
        out_specs=[HBM, VMEM],
        out_shape=[
            jax.ShapeDtypeStruct((4 * units, 4 * units), F32),
            pltpu.VMEM((8, 128), F32),
        ],
        input_output_aliases=aliases,
        scratch_shapes=[
            pltpu.VMEM((depth, height, cut), F32),
            pltpu.SemaphoreType.DMA((depth,)),
        ],
        compiler_params=params(10),
        cost_estimate=cost(8 * rows * units * units * len(pieces), 16 * units * units * len(pieces)),
        name="gram",
    )(*operands)


def swap(value, axis):
    return lax.ppermute(value, axis, [(0, 1), (1, 0)])


def across(value, slot):
    return lax.ppermute(value, "col", [(i, i ^ slot) for i in range(4)])


def on_device(tokens, routes, route_weight, pad_mask, gate_up, down):
    depth = tokens.shape[1]
    units = gate_up.shape[2]
    lanes = 128
    chunks = 2
    weights = gate_up.reshape(depth, 2, units // lanes, lanes).transpose(0, 2, 1, 3)

    packed, placing, factor = pack(tokens, routes.T, pad_mask[None, :], route_weight.T)
    lefts = [packed] + [across(packed, slot) for slot in (1, 2, 3)]
    grouped, widen = regroup(packed, weights)

    first_sent, wide = preacts_of([*lefts, widen], grouped, 1, 0, chunks)
    (last_sent,) = preacts_of([wide], grouped, 1, 1, chunks)
    got = [swap(first_sent, "row"), swap(last_sent, "row")]
    stays, got_x = [], []
    for h in range(chunks):
        (kept,) = preacts_of([wide], grouped, 0, h, chunks)
        leaves, stay = leave(kept, got[h])
        wide, leaves = tie(wide, leaves)
        stays.append(stay)
        got_x.append(swap(leaves, "expert"))
    down_held, tick = fetch(wide, down)
    tick, got_x[0] = tie(tick, got_x[0])
    (hidden_a,) = act(tick, stays[0], got_x[0])

    z2a = across(hidden_a, 2)
    z1a = across(hidden_a, 1)
    tick, got_x[1], hidden_a = tie(tick, got_x[1], hidden_a)
    hidden_b, hidden = act(tick, stays[1], got_x[1], hidden_a)
    hidden_x = swap(hidden, "expert")
    z2b = across(hidden_b, 2)
    tick, z2a = tie(tick, z2a)
    z3a = across(relay(z2a), 1)
    tick, z1a, hidden_b = tie(tick, z1a, hidden_b)
    z1b = across(hidden_b, 1)
    x2a = swap(choose(z2a, z1a), "expert")
    tick, z2b = tie(tick, z2b)
    z3b = across(z2b, 1)
    tick, z3a = tie(tick, z3a)
    tick, z1b = tie(tick, z1b)
    here = join(hidden, hidden_x)
    there = swap(here, "row")
    tick, there, here = tie(tick, there, here)
    near, away, hidden_c, tick = project(tick, here, there, down_held)
    tick, x2a = tie(tick, x2a)
    tick, z3b = tie(tick, z3b)
    mine, passed, leaves = pick([hidden], [z1a, z1b], [z2a, z2b], [z3a, z3b], leaves=True)
    rest = swap(leaves, "expert")
    mine_near = swap(passed, "row")
    away = across(away, 1)
    tick, mine_near = tie(tick, mine_near)
    gram, tick = gram_piece(tick, [mine, mine_near], [(0, 0), (0, 1)], hidden_c)
    tick, rest = tie(tick, rest)
    mine_x, passed = pick_far(hidden_x, x2a, rest)
    mine_far = swap(passed, "row")
    tick, away = tie(tick, away)
    own, onward = fold(near, away)
    onward = across(onward, 2)
    tick, mine_far = tie(tick, mine_far)
    gram, tick = gram_piece(tick, [mine_x, mine_far], [(1, 0), (1, 1)], hidden_c, gram)
    return (unpack(tick, placing, factor, own, onward), gram)


def solution(mesh):
    in_specs = (
        P(("parts", "col"), ("expert", "row")),
        P(("parts", "col"), None),
        P(("parts", "col"), None),
        P(("parts", "col")),
        P(("expert", "row"), None, "col"),
        P("col", ("expert", "row")),
    )
    out_specs = (P(("parts", "col"), ("expert", "row")), P(("parts", "expert", "row"), "col"))
    small = mesh.shape["expert"] == 2 and mesh.shape["row"] == 2 and mesh.shape["col"] == 4
    return jax.shard_map(
        on_device if small else on_any_device,
        mesh=mesh,
        in_specs=in_specs,
        out_specs=out_specs,
        check_vma=False,
    )
```

```python
import functools

import jax
import jax.numpy as jnp
from jax import lax
from jax.experimental import pallas as pl
from jax.experimental.pallas import tpu as pltpu
from jax.sharding import PartitionSpec as P

F32 = jnp.float32
BF16 = jnp.bfloat16
MIB = 1 << 20


def spread(value, axis, source):
    kept = jnp.where(lax.axis_index(axis) == source, value, 0).astype(value.dtype)
    return lax.psum(kept, axis)


def activate(preacts):
    return (jax.nn.silu(preacts[:, 0, :]) * preacts[:, 1, :]).astype(jnp.bfloat16)


def on_any_device(tokens, routes, route_weight, pad_mask, gate_up, down):
    group_rows = tokens.shape[0]
    slot_count = group_rows // 4
    names_zero = routes == 0
    routed = jnp.any(names_zero, axis=1)
    live_rows = routed & (pad_mask == 1)
    factor = jnp.sum(
        jnp.where(names_zero, route_weight, jnp.float32(0.0)), axis=1
    ) * live_rows.astype(jnp.float32)
    position = jnp.cumsum(routed.astype(jnp.int32)) - 1
    slot_ids = lax.broadcasted_iota(jnp.int32, (slot_count, group_rows), 0)
    placing = ((position[None, :] == slot_ids) & routed[None, :]).astype(jnp.bfloat16)
    masked = tokens * live_rows.astype(jnp.bfloat16)[:, None]
    packed = jnp.dot(placing, masked, preferred_element_type=jnp.float32).astype(jnp.bfloat16)
    gathered = lax.all_gather(packed, "col", axis=0, tiled=True)
    anchor = lax.axis_index(("expert", "row"))
    preacts = lax.psum(
        jnp.einsum("rd,dgf->rgf", gathered, gate_up, preferred_element_type=jnp.float32),
        ("expert", "row"),
    )
    hidden = activate(preacts)
    mirrored = spread(hidden, "col", anchor)
    gram_block = lax.dot_general(
        mirrored, hidden, (((0,), (0,)), ((), ())), preferred_element_type=jnp.float32
    )
    gram_block = gram_block * jnp.float32(2.0 / hidden.shape[0])
    returned = lax.psum_scatter(
        jnp.dot(hidden, down, preferred_element_type=jnp.float32),
        "col",
        scatter_dimension=0,
        tiled=True,
    )
    unpacked = lax.dot_general(
        placing.astype(jnp.float32),
        returned,
        (((0,), (0,)), ((), ())),
        precision=lax.Precision.HIGHEST,
        preferred_element_type=jnp.float32,
    )
    expert_out = (unpacked * factor[:, None]).astype(jnp.bfloat16)
    return (expert_out, gram_block)


def cost(flops, moved):
    return pl.CostEstimate(flops=int(flops), bytes_accessed=int(moved), transcendentals=0)


def params(mib):
    return pltpu.CompilerParams(vmem_limit_bytes=mib * MIB)


VMEM = pl.BlockSpec(memory_space=pltpu.VMEM)
HBM = pl.BlockSpec(memory_space=pltpu.HBM)
SMEM = pl.BlockSpec(memory_space=pltpu.SMEM)
ANY = pl.BlockSpec(memory_space=pl.ANY)


def in_vmem(value):
    return pltpu.with_memory_space_constraint(value, pltpu.VMEM)


def in_hbm(value):
    return pltpu.with_memory_space_constraint(value, pltpu.HBM)


def quarter_of(expert_flip, row_flip):
    return (lax.axis_index("expert") ^ expert_flip) * 2 + (lax.axis_index("row") ^ row_flip)


def tie(*values):
    return lax.optimization_barrier(values)


def pack_kernel(
    tokens_ref, routes_ref, pad_ref, weight_ref, packed_ref, placing_ref, factor_ref,
    tokens_held, routes_held, pad_held, weight_held, sems,
):
    pairs = (
        (routes_ref, routes_held),
        (pad_ref, pad_held),
        (weight_ref, weight_held),
        (tokens_ref, tokens_held),
    )
    copies = [pltpu.make_async_copy(a, b, sems.at[i]) for i, (a, b) in enumerate(pairs)]
    for copy in copies:
        copy.start()
    slots, rows = placing_ref.shape
    before = lax.broadcasted_iota(jnp.int32, (rows, rows), 0)
    upto = lax.broadcasted_iota(jnp.int32, (rows, rows), 1)
    tri = jnp.where(before <= upto, 1.0, 0.0).astype(BF16)
    slot_ids = lax.broadcasted_iota(jnp.int32, (slots, rows), 0).astype(F32)
    for copy in copies[:3]:
        copy.wait()
    routes_t = routes_held[...]
    routed = (routes_t[0:1, :] == 0) | (routes_t[1:2, :] == 0)
    live = jnp.where(routed & (pad_held[...] == 1), 1.0, 0.0)
    routed_rows = jnp.broadcast_to(jnp.where(routed, 1.0, 0.0), (8, rows)).astype(BF16)
    position = jnp.dot(routed_rows, tri, preferred_element_type=F32)[0:1, :] - 1.0
    placing = jnp.where(position == slot_ids, jnp.broadcast_to(live, (slots, rows)), 0.0)
    placing_ref[...] = placing.astype(BF16)
    weight = jnp.sum(jnp.where(routes_t == 0, weight_held[...], 0.0), axis=0, keepdims=True)
    factor = jnp.sum(placing * weight, axis=1, keepdims=True)
    factor_ref[...] = jnp.broadcast_to(factor, factor_ref.shape)
    copies[3].wait()
    packed_ref[...] = jnp.dot(
        placing.astype(BF16), tokens_held[...], preferred_element_type=F32
    ).astype(BF16)


def pack(tokens, routes_t, pad, weight_t):
    rows, depth = tokens.shape
    slots = rows // 4
    operands = (tokens, routes_t, pad, weight_t)
    return pl.pallas_call(
        pack_kernel,
        in_specs=[HBM] * 4,
        out_specs=[VMEM] * 3,
        out_shape=[
            pltpu.VMEM((slots, depth), BF16),
            pltpu.VMEM((slots, rows), BF16),
            pltpu.VMEM((slots, 128), F32),
        ],
        scratch_shapes=[pltpu.VMEM(x.shape, x.dtype) for x in operands]
        + [pltpu.SemaphoreType.DMA((4,))],
        compiler_params=params(3),
        name="pack",
    )(*(in_hbm(x) for x in operands))


def regroup_kernel(after_ref, weights_ref, out_ref, widen_ref, sems):
    del after_ref
    copies = [
        pltpu.make_async_copy(weights_ref.at[:, t], out_ref.at[t], sems.at[t])
        for t in range(out_ref.shape[0])
    ]
    for copy in copies:
        copy.start()
    cut = widen_ref.shape[0]
    into = lax.broadcasted_iota(jnp.int32, (cut, 4 * cut), 1)
    out_of = lax.broadcasted_iota(jnp.int32, (cut, 4 * cut), 0)
    half = jnp.where(into < 2 * cut, 0, 1)
    widen_ref[...] = jnp.where(into - 2 * cut * half == 2 * out_of + half, 1.0, 0.0).astype(BF16)
    for copy in copies:
        copy.wait()


def regroup(behind, weights):
    depth, tiles, two, lanes = weights.shape
    grouped, widen = pl.pallas_call(
        regroup_kernel,
        in_specs=[ANY, HBM],
        out_specs=[VMEM] * 2,
        out_shape=[
            pltpu.VMEM((tiles, depth, two, lanes), BF16),
            pltpu.VMEM((256, 1024), BF16),
        ],
        scratch_shapes=[pltpu.SemaphoreType.DMA((tiles,))],
        compiler_params=params(4),
        cost_estimate=cost(0, 4 * weights.size),
        name="regroup",
    )(behind, in_hbm(weights))
    return grouped.reshape(tiles, depth * two, lanes), widen


def fetch_kernel(after_ref, down_ref, out_ref, done_ref, sems):
    del after_ref
    parts = sems.shape[0]
    size = down_ref.shape[0] // parts
    copies = [
        pltpu.make_async_copy(
            down_ref.at[pl.ds(size * i, size)], out_ref.at[pl.ds(size * i, size)], sems.at[i]
        )
        for i in range(parts)
    ]
    for copy in copies:
        copy.start()
    done_ref[...] = jnp.zeros_like(done_ref)
    for copy in copies:
        copy.wait()


def fetch(behind, down):
    return pl.pallas_call(
        fetch_kernel,
        in_specs=[ANY, HBM],
        out_specs=[VMEM, VMEM],
        out_shape=[pltpu.VMEM(down.shape, BF16), pltpu.VMEM((8, 128), F32)],
        scratch_shapes=[pltpu.SemaphoreType.DMA((4,))],
        compiler_params=params(4),
        cost_estimate=cost(0, 4 * down.size),
        name="fetch_down",
    )(behind, in_hbm(down))


def widen_tokens(x_refs, widen_ref, wide_ref):
    slots, depth = x_refs[0].shape
    rows = 4 * slots
    here = lax.axis_index("col")
    cut = widen_ref.shape[0]
    parts = depth // cut
    for slot, x_ref in enumerate(x_refs):
        stacked = jnp.concatenate(
            [x_ref[:, cut * k : cut * (k + 1)] for k in range(parts)], axis=0
        )
        spaced = jnp.dot(stacked, widen_ref[...], preferred_element_type=F32).astype(BF16)
        for h in range(2):
            at = pl.multiple_of(h * rows + (here ^ slot) * slots, slots)
            for k in range(parts):
                wide_ref[pl.ds(at, slots), 2 * cut * k : 2 * cut * (k + 1)] = spaced[
                    slots * k : slots * (k + 1), 2 * cut * h : 2 * cut * (h + 1)
                ]


def preact_kernel(first, row_flip, chunk, chunks, *refs):
    if first:
        x0, x1, x2, x3, widen_ref, w_ref, out_ref, wide_ref = refs
        widen_tokens((x0, x1, x2, x3), widen_ref, wide_ref)
    else:
        wide_ref, w_ref, out_ref = refs
    tiles, _, lanes = w_ref.shape
    per = tiles // 4
    take = per // chunks
    at = []
    for i in range(2):
        quarter = quarter_of(1 - i, row_flip)
        at += [quarter * per + chunk * take + j for j in range(take)]
    for j in range(take):
        w = jnp.concatenate([w_ref[at[2 * j]], w_ref[at[2 * j + 1]]], axis=1)
        out_ref[:, 2 * lanes * j : 2 * lanes * (j + 1)] = jnp.dot(
            wide_ref[...], w, preferred_element_type=F32
        )


def preacts_of(lefts, weights, row_flip, chunk, chunks):
    tiles, depth2, lanes = weights.shape
    first = len(lefts) > 1
    rows = 4 * lefts[0].shape[0] if first else lefts[0].shape[0] // 2
    units = tiles // 4 // chunks * lanes
    out_shape = [jax.ShapeDtypeStruct((2 * rows, 2 * units), F32)]
    if first:
        out_shape.append(pltpu.VMEM((2 * rows, depth2), BF16))
    return pl.pallas_call(
        functools.partial(preact_kernel, first, row_flip, chunk, chunks),
        in_specs=[VMEM] * (len(lefts) + 1),
        out_specs=[VMEM] * len(out_shape),
        out_shape=out_shape,
        compiler_params=params(4),
        cost_estimate=cost(8 * rows * depth2 * units, 0),
        name="preacts_" + ("sent" if row_flip else "kept"),
    )(*lefts, in_vmem(weights))


def leave_kernel(kept_ref, got_ref, leaves_ref, stays_ref):
    units = stays_ref.shape[1]
    leaves_ref[...] = (kept_ref[:, :units] + got_ref[:, :units]).astype(BF16)
    stays_ref[...] = kept_ref[:, units:] + got_ref[:, units:]


def leave(kept, got):
    rows, units = kept.shape[0], kept.shape[1] // 2
    return pl.pallas_call(
        leave_kernel,
        in_specs=[VMEM] * 2,
        out_specs=[VMEM] * 2,
        out_shape=[
            jax.ShapeDtypeStruct((rows, units), BF16),
            jax.ShapeDtypeStruct((rows, units), F32),
        ],
        compiler_params=params(2),
        cost_estimate=cost(0, 1),
        name="leave",
    )(kept, got)


def act_kernel(tick_ref, stays_ref, got_ref, *refs):
    del tick_ref
    out_ref = refs[-1]
    rows = out_ref.shape[0]
    gate = stays_ref[:rows, :] + got_ref[:rows, :].astype(F32)
    up = stays_ref[rows:, :] + got_ref[rows:, :].astype(F32)
    hidden = (jax.nn.silu(gate) * up).astype(BF16)
    if len(refs) == 1:
        out_ref[...] = hidden
    else:
        before_ref, part_ref, _ = refs
        done = before_ref.shape[1]
        part_ref[...] = hidden
        out_ref[:, :done] = before_ref[...]
        out_ref[:, done:] = hidden


def act(tick, stays, got, *before):
    rows, units = stays.shape
    shapes = [(rows // 2, units)]
    if before:
        shapes.append((rows // 2, units + before[0].shape[1]))
    return pl.pallas_call(
        act_kernel,
        in_specs=[ANY] + [VMEM] * (2 + len(before)),
        out_specs=[VMEM] * len(shapes),
        out_shape=[jax.ShapeDtypeStruct(shape, BF16) for shape in shapes],
        compiler_params=params(2),
        cost_estimate=cost(0, 1),
        name="act",
    )(tick, stays, got, *before)


def relay_kernel(in_ref, out_ref):
    out_ref[...] = in_ref[...]


def relay(value):
    return pl.pallas_call(
        relay_kernel,
        in_specs=[VMEM],
        out_specs=VMEM,
        out_shape=jax.ShapeDtypeStruct(value.shape, value.dtype),
        compiler_params=params(2),
        cost_estimate=cost(1e10, 1),
        name="relay",
    )(value)


def is_near():
    return (lax.axis_index("col") // 2) == lax.axis_index("expert")


def is_odd():
    return (lax.axis_index("col") % 2) != lax.axis_index("row")


def choose_kernel(near_ref, far_ref, out_ref):
    @pl.when(is_near())
    def _():
        out_ref[...] = near_ref[...]

    @pl.when(jnp.logical_not(is_near()))
    def _():
        out_ref[...] = far_ref[...]


def choose(if_near, if_far):
    return pl.pallas_call(
        choose_kernel,
        in_specs=[VMEM] * 2,
        out_specs=VMEM,
        out_shape=jax.ShapeDtypeStruct(if_near.shape, if_near.dtype),
        compiler_params=params(2),
        cost_estimate=cost(1e10, 1),
        name="choose",
    )(if_near, if_far)


def put(out_ref, parts):
    column = 0
    for part in parts:
        out_ref[:, column : column + part.shape[1]] = part[...]
        column += part.shape[1]


def pick_kernel(counts, *refs):
    slots, at = [], 0
    for count in counts:
        slots.append(refs[at : at + count])
        at += count
    mine_ref, other_ref = refs[at : at + 2]
    for near, pair in ((True, slots[:2]), (False, slots[2:])):
        for odd in (False, True):

            @pl.when((is_near() == near) & (is_odd() == odd))
            def _():
                put(mine_ref, pair[int(odd)])
                put(other_ref, pair[1 - int(odd)])

        if len(refs) > at + 2:

            @pl.when(is_near() == near)
            def _():
                put(refs[-1], (slots[2][-1] if near else slots[1][-1], *slots[3]))


def pick(*slots, leaves=False):
    parts = [part for slot in slots for part in slot]
    rows, units = slots[0][0].shape
    shapes = [(rows, units)] * 2
    if leaves:
        shapes.append((rows, units + slots[1][-1].shape[1]))
    return pl.pallas_call(
        functools.partial(pick_kernel, [len(slot) for slot in slots]),
        in_specs=[VMEM] * len(parts),
        out_specs=[VMEM] * len(shapes),
        out_shape=[jax.ShapeDtypeStruct(shape, BF16) for shape in shapes],
        compiler_params=params(2),
        cost_estimate=cost(0, 1),
        name="pick",
    )(*parts)


def pick_far_kernel(own_ref, first_ref, rest_ref, mine_ref, other_ref):
    units = first_ref.shape[1]

    def fill(out_ref, slot):
        if slot == 0:
            out_ref[...] = own_ref[...]
        elif slot == 3:
            out_ref[...] = rest_ref[:, units:]
        else:
            out_ref[:, :units] = first_ref[...]
            out_ref[:, units:] = rest_ref[:, :units]

    for near, pair in ((True, (0, 1)), (False, (2, 3))):
        for odd in (False, True):

            @pl.when((is_near() == near) & (is_odd() == odd))
            def _():
                fill(mine_ref, pair[int(odd)])
                fill(other_ref, pair[1 - int(odd)])


def pick_far(own, first, rest):
    same = jax.ShapeDtypeStruct(own.shape, BF16)
    return pl.pallas_call(
        pick_far_kernel,
        in_specs=[VMEM] * 3,
        out_specs=[VMEM] * 2,
        out_shape=[same] * 2,
        compiler_params=params(2),
        cost_estimate=cost(0, 1),
        name="pick_far",
    )(own, first, rest)


def join_kernel(left_ref, right_ref, out_ref):
    units = left_ref.shape[1]
    out_ref[:, :units] = left_ref[...]
    out_ref[:, units:] = right_ref[...]


def join(left, right):
    rows, units = left.shape
    return pl.pallas_call(
        join_kernel,
        in_specs=[VMEM] * 2,
        out_specs=VMEM,
        out_shape=jax.ShapeDtypeStruct((rows, 2 * units), left.dtype),
        compiler_params=params(2),
        cost_estimate=cost(0, 1),
        name="join",
    )(left, right)


def project_kernel(tick_ref, here_ref, there_ref, down_ref, near_ref, away_ref, wide_ref, done_ref, total_ref):
    del tick_ref
    units = here_ref.shape[1] // 2
    for row_flip, pair_ref in enumerate((here_ref, there_ref)):
        for expert_flip in range(2):
            at = pl.multiple_of(quarter_of(expert_flip, row_flip) * units, units)
            wide_ref[:, pl.ds(at, units)] = pair_ref[:, units * expert_flip : units * (expert_flip + 1)]
    done_ref[...] = jnp.zeros_like(done_ref)
    width = near_ref.shape[1]
    slots = near_ref.shape[0] // 2
    cut = 512
    for n in range(width // cut):
        total_ref[:, cut * n : cut * (n + 1)] = jnp.dot(
            wide_ref[...], down_ref[:, cut * n : cut * (n + 1)], preferred_element_type=F32
        )
    here = lax.axis_index("col")
    for i, (out_ref, slot) in enumerate(((near_ref, 0), (near_ref, 2), (away_ref, 1), (away_ref, 3))):
        at = pl.multiple_of((here ^ slot) * slots, slots)
        row = slots * (i % 2)
        out_ref[row : row + slots, :] = total_ref[pl.ds(at, slots), :].astype(out_ref.dtype)


def project(tick, here, there, down):
    rows, units = here.shape[0], here.shape[1] // 2
    width = down.shape[1]
    return pl.pallas_call(
        project_kernel,
        in_specs=[ANY] + [VMEM] * 3,
        out_specs=[VMEM] * 4,
        out_shape=[
            jax.ShapeDtypeStruct((rows // 2, width), F32),
            jax.ShapeDtypeStruct((rows // 2, width), BF16),
            pltpu.VMEM((rows, 4 * units), BF16),
            pltpu.VMEM((8, 128), F32),
        ],
        scratch_shapes=[pltpu.VMEM((rows, width), F32)],
        compiler_params=params(4),
        cost_estimate=cost(0, 1),
        name="project",
    )(tick, here, there, in_vmem(down))


def fold_kernel(near_ref, got_ref, own_ref, onward_ref):
    slots = own_ref.shape[0]
    own_ref[...] = near_ref[:slots, :] + got_ref[:slots, :].astype(F32)
    onward_ref[...] = (near_ref[slots:, :] + got_ref[slots:, :].astype(F32)).astype(BF16)


def fold(near, got):
    slots, width = near.shape[0] // 2, near.shape[1]
    return pl.pallas_call(
        fold_kernel,
        in_specs=[VMEM] * 2,
        out_specs=[VMEM] * 2,
        out_shape=[
            jax.ShapeDtypeStruct((slots, width), F32),
            jax.ShapeDtypeStruct((slots, width), BF16),
        ],
        compiler_params=params(2),
        cost_estimate=cost(0, 1),
        name="fold",
    )(near, got)


def unpack_kernel(
    after_ref, placing_ref, factor_ref, own_ref, got_ref, out_ref, held_ref, sems
):
    del after_ref
    parts, _, cut = held_ref.shape
    copies = []
    for n in range(parts):
        columns = slice(cut * n, cut * (n + 1))
        total = own_ref[:, columns] + got_ref[:, columns].astype(F32)
        scaled = (total * factor_ref[:, 0:1]).astype(BF16)
        held_ref[n] = lax.dot_general(
            placing_ref[...], scaled, (((0,), (0,)), ((), ())), preferred_element_type=F32
        ).astype(BF16)
        copy = pltpu.make_async_copy(
            held_ref.at[n], out_ref.at[:, pl.ds(cut * n, cut)], sems.at[n]
        )
        copy.start()
        copies.append(copy)
    for copy in copies:
        copy.wait()


def unpack(done, placing, factor, own, got):
    slots, rows = placing.shape
    width = own.shape[1]
    parts = 3
    return pl.pallas_call(
        unpack_kernel,
        in_specs=[ANY] + [VMEM] * 4,
        out_specs=HBM,
        out_shape=jax.ShapeDtypeStruct((rows, width), BF16),
        scratch_shapes=[
            pltpu.VMEM((parts, rows, width // parts), BF16),
            pltpu.SemaphoreType.DMA((parts,)),
        ],
        compiler_params=params(4),
        name="unpack",
    )(done, placing, factor, own, got)


def gram_kernel(scale, flips, *refs):
    count = len(flips)
    pieces = refs[1 : 1 + count]
    wide_ref = refs[1 + count]
    out_ref, done_ref, ring_ref, sems = refs[-4:]
    done_ref[...] = jnp.zeros_like(done_ref)
    units = pieces[0].shape[1]
    depth, height, cut = ring_ref.shape
    half = cut // 2
    copies = []
    for (expert_flip, row_flip), a_ref in zip(flips, pieces):
        start = quarter_of(expert_flip, row_flip) * units
        for m in range(units // height):
            rows = pl.ds(pl.multiple_of(start + height * m, height), height)
            left = a_ref[:, height * m : height * (m + 1)].T
            for n in range(4 * units // cut):
                spot = len(copies) % depth
                if len(copies) >= depth:
                    copies[-depth].wait()
                for i in range(2):
                    column = cut * n + half * i
                    ring_ref[spot, :, half * i : half * (i + 1)] = scale * jnp.dot(
                        left, wide_ref[:, column : column + half], preferred_element_type=F32
                    )
                copy = pltpu.make_async_copy(
                    ring_ref.at[spot], out_ref.at[rows, pl.ds(cut * n, cut)], sems.at[spot]
                )
                copy.start()
                copies.append(copy)
    for copy in copies[-depth:]:
        copy.wait()


def gram_piece(tick, pieces, flips, wide, gram=None):
    rows, units = pieces[0].shape
    cut, height, depth = 1024, 256, 6
    operands = [tick, *pieces, in_vmem(wide)]
    in_specs = [ANY] + [VMEM] * (len(pieces) + 1)
    aliases = {}
    if gram is not None:
        aliases = {len(operands): 0}
        operands.append(gram)
        in_specs.append(HBM)
    return pl.pallas_call(
        functools.partial(gram_kernel, 2.0 / rows, flips),
        in_specs=in_specs,
        out_specs=[HBM, VMEM],
        out_shape=[
            jax.ShapeDtypeStruct((4 * units, 4 * units), F32),
            pltpu.VMEM((8, 128), F32),
        ],
        input_output_aliases=aliases,
        scratch_shapes=[
            pltpu.VMEM((depth, height, cut), F32),
            pltpu.SemaphoreType.DMA((depth,)),
        ],
        compiler_params=params(10),
        cost_estimate=cost(8 * rows * units * units * len(pieces), 16 * units * units * len(pieces)),
        name="gram",
    )(*operands)


def swap(value, axis):
    return lax.ppermute(value, axis, [(0, 1), (1, 0)])


def across(value, slot):
    return lax.ppermute(value, "col", [(i, i ^ slot) for i in range(4)])


def on_device(tokens, routes, route_weight, pad_mask, gate_up, down):
    depth = tokens.shape[1]
    units = gate_up.shape[2]
    lanes = 128
    chunks = 2
    weights = gate_up.reshape(depth, 2, units // lanes, lanes).transpose(0, 2, 1, 3)

    packed, placing, factor = pack(tokens, routes.T, pad_mask[None, :], route_weight.T)
    lefts = [packed] + [across(packed, slot) for slot in (1, 2, 3)]
    grouped, widen = regroup(packed, weights)

    first_sent, wide = preacts_of([*lefts, widen], grouped, 1, 0, chunks)
    (last_sent,) = preacts_of([wide], grouped, 1, 1, chunks)
    got = [swap(first_sent, "row"), swap(last_sent, "row")]
    stays, got_x = [], []
    for h in range(chunks):
        (kept,) = preacts_of([wide], grouped, 0, h, chunks)
        leaves, stay = leave(kept, got[h])
        wide, leaves = tie(wide, leaves)
        stays.append(stay)
        got_x.append(swap(leaves, "expert"))
    down_held, tick = fetch(wide, down)
    tick, got_x[0] = tie(tick, got_x[0])
    (hidden_a,) = act(tick, stays[0], got_x[0])

    z2a = across(hidden_a, 2)
    z1a = across(hidden_a, 1)
    tick, got_x[1], hidden_a = tie(tick, got_x[1], hidden_a)
    hidden_b, hidden = act(tick, stays[1], got_x[1], hidden_a)
    hidden_x = swap(hidden, "expert")
    z2b = across(hidden_b, 2)
    tick, z2a = tie(tick, z2a)
    z3a = across(relay(z2a), 1)
    tick, z1a, hidden_b = tie(tick, z1a, hidden_b)
    z1b = across(hidden_b, 1)
    x2a = swap(choose(z2a, z1a), "expert")
    tick, z2b = tie(tick, z2b)
    z3b = across(z2b, 1)
    tick, z3a = tie(tick, z3a)
    tick, z1b = tie(tick, z1b)
    here = join(hidden, hidden_x)
    there = swap(here, "row")
    tick, there, here = tie(tick, there, here)
    near, away, hidden_c, tick = project(tick, here, there, down_held)
    tick, x2a = tie(tick, x2a)
    tick, z3b = tie(tick, z3b)
    mine, passed, leaves = pick([hidden], [z1a, z1b], [z2a, z2b], [z3a, z3b], leaves=True)
    rest = swap(leaves, "expert")
    mine_near = swap(passed, "row")
    away = across(away, 1)
    tick, mine_near = tie(tick, mine_near)
    gram, tick = gram_piece(tick, [mine, mine_near], [(0, 0), (0, 1)], hidden_c)
    tick, rest = tie(tick, rest)
    mine_x, passed = pick_far(hidden_x, x2a, rest)
    mine_far = swap(passed, "row")
    tick, away = tie(tick, away)
    own, onward = fold(near, away)
    onward = across(onward, 2)
    tick, mine_far = tie(tick, mine_far)
    gram, tick = gram_piece(tick, [mine_x, mine_far], [(1, 0), (1, 1)], hidden_c, gram)
    return (unpack(tick, placing, factor, own, onward), gram)


def solution(mesh):
    in_specs = (
        P(("parts", "col"), ("expert", "row")),
        P(("parts", "col"), None),
        P(("parts", "col"), None),
        P(("parts", "col")),
        P(("expert", "row"), None, "col"),
        P("col", ("expert", "row")),
    )
    out_specs = (P(("parts", "col"), ("expert", "row")), P(("parts", "expert", "row"), "col"))
    small = mesh.shape["expert"] == 2 and mesh.shape["row"] == 2 and mesh.shape["col"] == 4
    return jax.shard_map(
        on_device if small else on_any_device,
        mesh=mesh,
        in_specs=in_specs,
        out_specs=out_specs,
        check_vma=False,
    )
```

```python
import functools

import jax
import jax.numpy as jnp
from jax import lax
from jax.experimental import pallas as pl
from jax.experimental.pallas import tpu as pltpu
from jax.sharding import PartitionSpec as P

F32 = jnp.float32
BF16 = jnp.bfloat16
MIB = 1 << 20


def spread(value, axis, source):
    kept = jnp.where(lax.axis_index(axis) == source, value, 0).astype(value.dtype)
    return lax.psum(kept, axis)


def activate(preacts):
    return (jax.nn.silu(preacts[:, 0, :]) * preacts[:, 1, :]).astype(jnp.bfloat16)


def on_any_device(tokens, routes, route_weight, pad_mask, gate_up, down):
    group_rows = tokens.shape[0]
    slot_count = group_rows // 4
    names_zero = routes == 0
    routed = jnp.any(names_zero, axis=1)
    live_rows = routed & (pad_mask == 1)
    factor = jnp.sum(
        jnp.where(names_zero, route_weight, jnp.float32(0.0)), axis=1
    ) * live_rows.astype(jnp.float32)
    position = jnp.cumsum(routed.astype(jnp.int32)) - 1
    slot_ids = lax.broadcasted_iota(jnp.int32, (slot_count, group_rows), 0)
    placing = ((position[None, :] == slot_ids) & routed[None, :]).astype(jnp.bfloat16)
    masked = tokens * live_rows.astype(jnp.bfloat16)[:, None]
    packed = jnp.dot(placing, masked, preferred_element_type=jnp.float32).astype(jnp.bfloat16)
    gathered = lax.all_gather(packed, "col", axis=0, tiled=True)
    anchor = lax.axis_index(("expert", "row"))
    preacts = lax.psum(
        jnp.einsum("rd,dgf->rgf", gathered, gate_up, preferred_element_type=jnp.float32),
        ("expert", "row"),
    )
    hidden = activate(preacts)
    mirrored = spread(hidden, "col", anchor)
    gram_block = lax.dot_general(
        mirrored, hidden, (((0,), (0,)), ((), ())), preferred_element_type=jnp.float32
    )
    gram_block = gram_block * jnp.float32(2.0 / hidden.shape[0])
    returned = lax.psum_scatter(
        jnp.dot(hidden, down, preferred_element_type=jnp.float32),
        "col",
        scatter_dimension=0,
        tiled=True,
    )
    unpacked = lax.dot_general(
        placing.astype(jnp.float32),
        returned,
        (((0,), (0,)), ((), ())),
        precision=lax.Precision.HIGHEST,
        preferred_element_type=jnp.float32,
    )
    expert_out = (unpacked * factor[:, None]).astype(jnp.bfloat16)
    return (expert_out, gram_block)


def cost(flops, moved):
    return pl.CostEstimate(flops=int(flops), bytes_accessed=int(moved), transcendentals=0)


def params(mib):
    return pltpu.CompilerParams(vmem_limit_bytes=mib * MIB)


VMEM = pl.BlockSpec(memory_space=pltpu.VMEM)
HBM = pl.BlockSpec(memory_space=pltpu.HBM)
SMEM = pl.BlockSpec(memory_space=pltpu.SMEM)
ANY = pl.BlockSpec(memory_space=pl.ANY)


def in_vmem(value):
    return pltpu.with_memory_space_constraint(value, pltpu.VMEM)


def in_hbm(value):
    return pltpu.with_memory_space_constraint(value, pltpu.HBM)


def quarter_of(expert_flip, row_flip):
    return (lax.axis_index("expert") ^ expert_flip) * 2 + (lax.axis_index("row") ^ row_flip)


def tie(*values):
    return lax.optimization_barrier(values)


def pack_kernel(
    tokens_ref, routes_ref, pad_ref, weight_ref, packed_ref, placing_ref, factor_ref,
    tokens_held, routes_held, pad_held, weight_held, sems,
):
    pairs = (
        (routes_ref, routes_held),
        (pad_ref, pad_held),
        (weight_ref, weight_held),
        (tokens_ref, tokens_held),
    )
    copies = [pltpu.make_async_copy(a, b, sems.at[i]) for i, (a, b) in enumerate(pairs)]
    for copy in copies:
        copy.start()
    slots, rows = placing_ref.shape
    before = lax.broadcasted_iota(jnp.int32, (rows, rows), 0)
    upto = lax.broadcasted_iota(jnp.int32, (rows, rows), 1)
    tri = jnp.where(before <= upto, 1.0, 0.0).astype(BF16)
    slot_ids = lax.broadcasted_iota(jnp.int32, (slots, rows), 0).astype(F32)
    for copy in copies[:3]:
        copy.wait()
    routes_t = routes_held[...]
    routed = (routes_t[0:1, :] == 0) | (routes_t[1:2, :] == 0)
    live = jnp.where(routed & (pad_held[...] == 1), 1.0, 0.0)
    routed_rows = jnp.broadcast_to(jnp.where(routed, 1.0, 0.0), (8, rows)).astype(BF16)
    position = jnp.dot(routed_rows, tri, preferred_element_type=F32)[0:1, :] - 1.0
    placing = jnp.where(position == slot_ids, jnp.broadcast_to(live, (slots, rows)), 0.0)
    placing_ref[...] = placing.astype(BF16)
    weight = jnp.sum(jnp.where(routes_t == 0, weight_held[...], 0.0), axis=0, keepdims=True)
    factor = jnp.sum(placing * weight, axis=1, keepdims=True)
    factor_ref[...] = jnp.broadcast_to(factor, factor_ref.shape)
    copies[3].wait()
    packed_ref[...] = jnp.dot(
        placing.astype(BF16), tokens_held[...], preferred_element_type=F32
    ).astype(BF16)


def pack(tokens, routes_t, pad, weight_t):
    rows, depth = tokens.shape
    slots = rows // 4
    operands = (tokens, routes_t, pad, weight_t)
    return pl.pallas_call(
        pack_kernel,
        in_specs=[HBM] * 4,
        out_specs=[VMEM] * 3,
        out_shape=[
            pltpu.VMEM((slots, depth), BF16),
            pltpu.VMEM((slots, rows), BF16),
            pltpu.VMEM((slots, 128), F32),
        ],
        scratch_shapes=[pltpu.VMEM(x.shape, x.dtype) for x in operands]
        + [pltpu.SemaphoreType.DMA((4,))],
        compiler_params=params(3),
        name="pack",
    )(*(in_hbm(x) for x in operands))


def regroup_kernel(after_ref, weights_ref, out_ref, widen_ref, sems):
    del after_ref
    copies = [
        pltpu.make_async_copy(weights_ref.at[:, t], out_ref.at[t], sems.at[t])
        for t in range(out_ref.shape[0])
    ]
    for copy in copies:
        copy.start()
    cut = widen_ref.shape[0]
    into = lax.broadcasted_iota(jnp.int32, (cut, 4 * cut), 1)
    out_of = lax.broadcasted_iota(jnp.int32, (cut, 4 * cut), 0)
    half = jnp.where(into < 2 * cut, 0, 1)
    widen_ref[...] = jnp.where(into - 2 * cut * half == 2 * out_of + half, 1.0, 0.0).astype(BF16)
    for copy in copies:
        copy.wait()


def regroup(behind, weights):
    depth, tiles, two, lanes = weights.shape
    grouped, widen = pl.pallas_call(
        regroup_kernel,
        in_specs=[ANY, HBM],
        out_specs=[VMEM] * 2,
        out_shape=[
            pltpu.VMEM((tiles, depth, two, lanes), BF16),
            pltpu.VMEM((256, 1024), BF16),
        ],
        scratch_shapes=[pltpu.SemaphoreType.DMA((tiles,))],
        compiler_params=params(4),
        cost_estimate=cost(0, 4 * weights.size),
        name="regroup",
    )(behind, in_hbm(weights))
    return grouped.reshape(tiles, depth * two, lanes), widen


def fetch_kernel(after_ref, down_ref, out_ref, done_ref, sems):
    del after_ref
    parts = sems.shape[0]
    size = down_ref.shape[0] // parts
    copies = [
        pltpu.make_async_copy(
            down_ref.at[pl.ds(size * i, size)], out_ref.at[pl.ds(size * i, size)], sems.at[i]
        )
        for i in range(parts)
    ]
    for copy in copies:
        copy.start()
    done_ref[...] = jnp.zeros_like(done_ref)
    for copy in copies:
        copy.wait()


def fetch(behind, down):
    return pl.pallas_call(
        fetch_kernel,
        in_specs=[ANY, HBM],
        out_specs=[VMEM, VMEM],
        out_shape=[pltpu.VMEM(down.shape, BF16), pltpu.VMEM((8, 128), F32)],
        scratch_shapes=[pltpu.SemaphoreType.DMA((4,))],
        compiler_params=params(4),
        cost_estimate=cost(0, 4 * down.size),
        name="fetch_down",
    )(behind, in_hbm(down))


def widen_tokens(x_refs, widen_ref, wide_ref):
    slots, depth = x_refs[0].shape
    rows = 4 * slots
    here = lax.axis_index("col")
    cut = widen_ref.shape[0]
    parts = depth // cut
    for slot, x_ref in enumerate(x_refs):
        stacked = jnp.concatenate(
            [x_ref[:, cut * k : cut * (k + 1)] for k in range(parts)], axis=0
        )
        spaced = jnp.dot(stacked, widen_ref[...], preferred_element_type=F32).astype(BF16)
        for h in range(2):
            at = pl.multiple_of(h * rows + (here ^ slot) * slots, slots)
            for k in range(parts):
                wide_ref[pl.ds(at, slots), 2 * cut * k : 2 * cut * (k + 1)] = spaced[
                    slots * k : slots * (k + 1), 2 * cut * h : 2 * cut * (h + 1)
                ]


def preact_kernel(first, row_flip, chunk, chunks, *refs):
    if first:
        x0, x1, x2, x3, widen_ref, w_ref, out_ref, wide_ref = refs
        widen_tokens((x0, x1, x2, x3), widen_ref, wide_ref)
    else:
        wide_ref, w_ref, out_ref = refs
    tiles, _, lanes = w_ref.shape
    per = tiles // 4
    take = per // chunks
    at = []
    for i in range(2):
        quarter = quarter_of(1 - i, row_flip)
        at += [quarter * per + chunk * take + j for j in range(take)]
    for j in range(take):
        w = jnp.concatenate([w_ref[at[2 * j]], w_ref[at[2 * j + 1]]], axis=1)
        out_ref[:, 2 * lanes * j : 2 * lanes * (j + 1)] = jnp.dot(
            wide_ref[...], w, preferred_element_type=F32
        )


def preacts_of(lefts, weights, row_flip, chunk, chunks):
    tiles, depth2, lanes = weights.shape
    first = len(lefts) > 1
    rows = 4 * lefts[0].shape[0] if first else lefts[0].shape[0] // 2
    units = tiles // 4 // chunks * lanes
    out_shape = [jax.ShapeDtypeStruct((2 * rows, 2 * units), F32)]
    if first:
        out_shape.append(pltpu.VMEM((2 * rows, depth2), BF16))
    return pl.pallas_call(
        functools.partial(preact_kernel, first, row_flip, chunk, chunks),
        in_specs=[VMEM] * (len(lefts) + 1),
        out_specs=[VMEM] * len(out_shape),
        out_shape=out_shape,
        compiler_params=params(4),
        cost_estimate=cost(8 * rows * depth2 * units, 0),
        name="preacts_" + ("sent" if row_flip else "kept"),
    )(*lefts, in_vmem(weights))


def leave_kernel(kept_ref, got_ref, leaves_ref, stays_ref):
    units = stays_ref.shape[1]
    leaves_ref[...] = (kept_ref[:, :units] + got_ref[:, :units]).astype(BF16)
    stays_ref[...] = kept_ref[:, units:] + got_ref[:, units:]


def leave(kept, got):
    rows, units = kept.shape[0], kept.shape[1] // 2
    return pl.pallas_call(
        leave_kernel,
        in_specs=[VMEM] * 2,
        out_specs=[VMEM] * 2,
        out_shape=[
            jax.ShapeDtypeStruct((rows, units), BF16),
            jax.ShapeDtypeStruct((rows, units), F32),
        ],
        compiler_params=params(2),
        cost_estimate=cost(0, 1),
        name="leave",
    )(kept, got)


def act_kernel(tick_ref, stays_ref, got_ref, *refs):
    del tick_ref
    out_ref = refs[-1]
    rows = out_ref.shape[0]
    gate = stays_ref[:rows, :] + got_ref[:rows, :].astype(F32)
    up = stays_ref[rows:, :] + got_ref[rows:, :].astype(F32)
    hidden = (jax.nn.silu(gate) * up).astype(BF16)
    if len(refs) == 1:
        out_ref[...] = hidden
    else:
        before_ref, part_ref, _ = refs
        done = before_ref.shape[1]
        part_ref[...] = hidden
        out_ref[:, :done] = before_ref[...]
        out_ref[:, done:] = hidden


def act(tick, stays, got, *before):
    rows, units = stays.shape
    shapes = [(rows // 2, units)]
    if before:
        shapes.append((rows // 2, units + before[0].shape[1]))
    return pl.pallas_call(
        act_kernel,
        in_specs=[ANY] + [VMEM] * (2 + len(before)),
        out_specs=[VMEM] * len(shapes),
        out_shape=[jax.ShapeDtypeStruct(shape, BF16) for shape in shapes],
        compiler_params=params(2),
        cost_estimate=cost(0, 1),
        name="act",
    )(tick, stays, got, *before)


def relay_kernel(in_ref, out_ref):
    out_ref[...] = in_ref[...]


def relay(value):
    return pl.pallas_call(
        relay_kernel,
        in_specs=[VMEM],
        out_specs=VMEM,
        out_shape=jax.ShapeDtypeStruct(value.shape, value.dtype),
        compiler_params=params(2),
        cost_estimate=cost(1e10, 1),
        name="relay",
    )(value)


def is_near():
    return (lax.axis_index("col") // 2) == lax.axis_index("expert")


def is_odd():
    return (lax.axis_index("col") % 2) != lax.axis_index("row")


def choose_kernel(near_ref, far_ref, out_ref):
    @pl.when(is_near())
    def _():
        out_ref[...] = near_ref[...]

    @pl.when(jnp.logical_not(is_near()))
    def _():
        out_ref[...] = far_ref[...]


def choose(if_near, if_far):
    return pl.pallas_call(
        choose_kernel,
        in_specs=[VMEM] * 2,
        out_specs=VMEM,
        out_shape=jax.ShapeDtypeStruct(if_near.shape, if_near.dtype),
        compiler_params=params(2),
        cost_estimate=cost(1e10, 1),
        name="choose",
    )(if_near, if_far)


def put(out_ref, parts):
    column = 0
    for part in parts:
        out_ref[:, column : column + part.shape[1]] = part[...]
        column += part.shape[1]


def pick_kernel(counts, *refs):
    slots, at = [], 0
    for count in counts:
        slots.append(refs[at : at + count])
        at += count
    mine_ref, other_ref = refs[at : at + 2]
    for near, pair in ((True, slots[:2]), (False, slots[2:])):
        for odd in (False, True):

            @pl.when((is_near() == near) & (is_odd() == odd))
            def _():
                put(mine_ref, pair[int(odd)])
                put(other_ref, pair[1 - int(odd)])

        if len(refs) > at + 2:

            @pl.when(is_near() == near)
            def _():
                put(refs[-1], (slots[2][-1] if near else slots[1][-1], *slots[3]))


def pick(*slots, leaves=False):
    parts = [part for slot in slots for part in slot]
    rows, units = slots[0][0].shape
    shapes = [(rows, units)] * 2
    if leaves:
        shapes.append((rows, units + slots[1][-1].shape[1]))
    return pl.pallas_call(
        functools.partial(pick_kernel, [len(slot) for slot in slots]),
        in_specs=[VMEM] * len(parts),
        out_specs=[VMEM] * len(shapes),
        out_shape=[jax.ShapeDtypeStruct(shape, BF16) for shape in shapes],
        compiler_params=params(2),
        cost_estimate=cost(0, 1),
        name="pick",
    )(*parts)


def pick_far_kernel(own_ref, first_ref, rest_ref, mine_ref, other_ref):
    units = first_ref.shape[1]

    def fill(out_ref, slot):
        if slot == 0:
            out_ref[...] = own_ref[...]
        elif slot == 3:
            out_ref[...] = rest_ref[:, units:]
        else:
            out_ref[:, :units] = first_ref[...]
            out_ref[:, units:] = rest_ref[:, :units]

    for near, pair in ((True, (0, 1)), (False, (2, 3))):
        for odd in (False, True):

            @pl.when((is_near() == near) & (is_odd() == odd))
            def _():
                fill(mine_ref, pair[int(odd)])
                fill(other_ref, pair[1 - int(odd)])


def pick_far(own, first, rest):
    same = jax.ShapeDtypeStruct(own.shape, BF16)
    return pl.pallas_call(
        pick_far_kernel,
        in_specs=[VMEM] * 3,
        out_specs=[VMEM] * 2,
        out_shape=[same] * 2,
        compiler_params=params(2),
        cost_estimate=cost(0, 1),
        name="pick_far",
    )(own, first, rest)


def join_kernel(left_ref, right_ref, out_ref):
    units = left_ref.shape[1]
    out_ref[:, :units] = left_ref[...]
    out_ref[:, units:] = right_ref[...]


def join(left, right):
    rows, units = left.shape
    return pl.pallas_call(
        join_kernel,
        in_specs=[VMEM] * 2,
        out_specs=VMEM,
        out_shape=jax.ShapeDtypeStruct((rows, 2 * units), left.dtype),
        compiler_params=params(2),
        cost_estimate=cost(0, 1),
        name="join",
    )(left, right)


def project_kernel(tick_ref, here_ref, there_ref, down_ref, near_ref, away_ref, wide_ref, done_ref, total_ref):
    del tick_ref
    units = here_ref.shape[1] // 2
    for row_flip, pair_ref in enumerate((here_ref, there_ref)):
        for expert_flip in range(2):
            at = pl.multiple_of(quarter_of(expert_flip, row_flip) * units, units)
            wide_ref[:, pl.ds(at, units)] = pair_ref[:, units * expert_flip : units * (expert_flip + 1)]
    done_ref[...] = jnp.zeros_like(done_ref)
    width = near_ref.shape[1]
    slots = near_ref.shape[0] // 2
    cut = 512
    for n in range(width // cut):
        total_ref[:, cut * n : cut * (n + 1)] = jnp.dot(
            wide_ref[...], down_ref[:, cut * n : cut * (n + 1)], preferred_element_type=F32
        )
    here = lax.axis_index("col")
    for i, (out_ref, slot) in enumerate(((near_ref, 0), (near_ref, 2), (away_ref, 1), (away_ref, 3))):
        at = pl.multiple_of((here ^ slot) * slots, slots)
        row = slots * (i % 2)
        out_ref[row : row + slots, :] = total_ref[pl.ds(at, slots), :].astype(out_ref.dtype)


def project(tick, here, there, down):
    rows, units = here.shape[0], here.shape[1] // 2
    width = down.shape[1]
    return pl.pallas_call(
        project_kernel,
        in_specs=[ANY] + [VMEM] * 3,
        out_specs=[VMEM] * 4,
        out_shape=[
            jax.ShapeDtypeStruct((rows // 2, width), F32),
            jax.ShapeDtypeStruct((rows // 2, width), BF16),
            pltpu.VMEM((rows, 4 * units), BF16),
            pltpu.VMEM((8, 128), F32),
        ],
        scratch_shapes=[pltpu.VMEM((rows, width), F32)],
        compiler_params=params(4),
        cost_estimate=cost(0, 1),
        name="project",
    )(tick, here, there, in_vmem(down))


def fold_kernel(near_ref, got_ref, own_ref, onward_ref):
    slots = own_ref.shape[0]
    own_ref[...] = near_ref[:slots, :] + got_ref[:slots, :].astype(F32)
    onward_ref[...] = (near_ref[slots:, :] + got_ref[slots:, :].astype(F32)).astype(BF16)


def fold(near, got):
    slots, width = near.shape[0] // 2, near.shape[1]
    return pl.pallas_call(
        fold_kernel,
        in_specs=[VMEM] * 2,
        out_specs=[VMEM] * 2,
        out_shape=[
            jax.ShapeDtypeStruct((slots, width), F32),
            jax.ShapeDtypeStruct((slots, width), BF16),
        ],
        compiler_params=params(2),
        cost_estimate=cost(0, 1),
        name="fold",
    )(near, got)


def unpack_kernel(after_ref, placing_ref, factor_ref, own_ref, got_ref, out_ref):
    del after_ref
    total = own_ref[...] + got_ref[...].astype(F32)
    scaled = (total * factor_ref[:, 0:1]).astype(BF16)
    out_ref[...] = lax.dot_general(
        placing_ref[...], scaled, (((0,), (0,)), ((), ())), preferred_element_type=F32
    ).astype(BF16)


def unpack(done, placing, factor, own, got):
    slots, rows = placing.shape
    return pl.pallas_call(
        unpack_kernel,
        in_specs=[ANY] + [VMEM] * 4,
        out_specs=VMEM,
        out_shape=jax.ShapeDtypeStruct((rows, own.shape[1]), BF16),
        compiler_params=params(4),
        name="unpack",
    )(done, placing, factor, own, got)


def gram_kernel(scale, flips, *refs):
    count = len(flips)
    pieces = refs[1 : 1 + count]
    wide_ref = refs[1 + count]
    out_ref, done_ref, ring_ref, sems = refs[-4:]
    done_ref[...] = jnp.zeros_like(done_ref)
    units = pieces[0].shape[1]
    depth, height, cut = ring_ref.shape
    half = cut // 2
    copies = []
    for (expert_flip, row_flip), a_ref in zip(flips, pieces):
        start = quarter_of(expert_flip, row_flip) * units
        for m in range(units // height):
            rows = pl.ds(pl.multiple_of(start + height * m, height), height)
            left = a_ref[:, height * m : height * (m + 1)].T
            for n in range(4 * units // cut):
                spot = len(copies) % depth
                if len(copies) >= depth:
                    copies[-depth].wait()
                for i in range(2):
                    column = cut * n + half * i
                    ring_ref[spot, :, half * i : half * (i + 1)] = scale * jnp.dot(
                        left, wide_ref[:, column : column + half], preferred_element_type=F32
                    )
                copy = pltpu.make_async_copy(
                    ring_ref.at[spot], out_ref.at[rows, pl.ds(cut * n, cut)], sems.at[spot]
                )
                copy.start()
                copies.append(copy)
    for copy in copies[-depth:]:
        copy.wait()


def gram_piece(tick, pieces, flips, wide, gram=None):
    rows, units = pieces[0].shape
    cut, height, depth = 512, 256, 12
    operands = [tick, *pieces, in_vmem(wide)]
    in_specs = [ANY] + [VMEM] * (len(pieces) + 1)
    aliases = {}
    if gram is not None:
        aliases = {len(operands): 0}
        operands.append(gram)
        in_specs.append(HBM)
    return pl.pallas_call(
        functools.partial(gram_kernel, 2.0 / rows, flips),
        in_specs=in_specs,
        out_specs=[HBM, VMEM],
        out_shape=[
            jax.ShapeDtypeStruct((4 * units, 4 * units), F32),
            pltpu.VMEM((8, 128), F32),
        ],
        input_output_aliases=aliases,
        scratch_shapes=[
            pltpu.VMEM((depth, height, cut), F32),
            pltpu.SemaphoreType.DMA((depth,)),
        ],
        compiler_params=params(10),
        cost_estimate=cost(8 * rows * units * units * len(pieces), 16 * units * units * len(pieces)),
        name="gram",
    )(*operands)


def swap(value, axis):
    return lax.ppermute(value, axis, [(0, 1), (1, 0)])


def across(value, slot):
    return lax.ppermute(value, "col", [(i, i ^ slot) for i in range(4)])


def on_device(tokens, routes, route_weight, pad_mask, gate_up, down):
    depth = tokens.shape[1]
    units = gate_up.shape[2]
    lanes = 128
    chunks = 2
    weights = gate_up.reshape(depth, 2, units // lanes, lanes).transpose(0, 2, 1, 3)

    packed, placing, factor = pack(tokens, routes.T, pad_mask[None, :], route_weight.T)
    lefts = [packed] + [across(packed, slot) for slot in (1, 2, 3)]
    grouped, widen = regroup(packed, weights)

    first_sent, wide = preacts_of([*lefts, widen], grouped, 1, 0, chunks)
    (last_sent,) = preacts_of([wide], grouped, 1, 1, chunks)
    got = [swap(first_sent, "row"), swap(last_sent, "row")]
    stays, got_x = [], []
    for h in range(chunks):
        (kept,) = preacts_of([wide], grouped, 0, h, chunks)
        leaves, stay = leave(kept, got[h])
        wide, leaves = tie(wide, leaves)
        stays.append(stay)
        got_x.append(swap(leaves, "expert"))
    down_held, tick = fetch(wide, down)
    tick, got_x[0] = tie(tick, got_x[0])
    (hidden_a,) = act(tick, stays[0], got_x[0])

    z2a = across(hidden_a, 2)
    z1a = across(hidden_a, 1)
    tick, got_x[1], hidden_a = tie(tick, got_x[1], hidden_a)
    hidden_b, hidden = act(tick, stays[1], got_x[1], hidden_a)
    hidden_x = swap(hidden, "expert")
    z2b = across(hidden_b, 2)
    tick, z2a = tie(tick, z2a)
    z3a = across(relay(z2a), 1)
    tick, z1a, hidden_b = tie(tick, z1a, hidden_b)
    z1b = across(hidden_b, 1)
    x2a = swap(choose(z2a, z1a), "expert")
    tick, z2b = tie(tick, z2b)
    z3b = across(z2b, 1)
    tick, z3a = tie(tick, z3a)
    tick, z1b = tie(tick, z1b)
    here = join(hidden, hidden_x)
    there = swap(here, "row")
    tick, there, here = tie(tick, there, here)
    near, away, hidden_c, tick = project(tick, here, there, down_held)
    tick, x2a = tie(tick, x2a)
    tick, z3b = tie(tick, z3b)
    mine, passed, leaves = pick([hidden], [z1a, z1b], [z2a, z2b], [z3a, z3b], leaves=True)
    rest = swap(leaves, "expert")
    mine_near = swap(passed, "row")
    away = across(away, 1)
    tick, mine_near = tie(tick, mine_near)
    gram, tick = gram_piece(tick, [mine, mine_near], [(0, 0), (0, 1)], hidden_c)
    tick, rest = tie(tick, rest)
    mine_x, passed = pick_far(hidden_x, x2a, rest)
    mine_far = swap(passed, "row")
    tick, away = tie(tick, away)
    own, onward = fold(near, away)
    onward = across(onward, 2)
    tick, mine_far = tie(tick, mine_far)
    gram, tick = gram_piece(tick, [mine_x, mine_far], [(1, 0), (1, 1)], hidden_c, gram)
    return (unpack(tick, placing, factor, own, onward), gram)


def solution(mesh):
    in_specs = (
        P(("parts", "col"), ("expert", "row")),
        P(("parts", "col"), None),
        P(("parts", "col"), None),
        P(("parts", "col")),
        P(("expert", "row"), None, "col"),
        P("col", ("expert", "row")),
    )
    out_specs = (P(("parts", "col"), ("expert", "row")), P(("parts", "expert", "row"), "col"))
    small = mesh.shape["expert"] == 2 and mesh.shape["row"] == 2 and mesh.shape["col"] == 4
    return jax.shard_map(
        on_device if small else on_any_device,
        mesh=mesh,
        in_specs=in_specs,
        out_specs=out_specs,
        check_vma=False,
    )
```
